32 devices in a mesh: groups: 2 (over y), space: 8 (over z, x), modes: 2 (over core).
Axes of the slice: x: 2, y: 2, z: 4, core: 2. Of those that a mesh axis runs over, the one named last changes fastest.
Arguments:
- modes: bfloat16 [256, 3, 16, 8, 128], P('modes', None, ('groups', 'space')), parts along dimension 2, may hold values from -6 to 6
- weight_ids: int32 [16, 8, 128], P(('groups', 'space')), parts along dimension 0, may hold values from 0 to 15
- weight_table: float32 [16], replicated, may hold values from 0.2 to 2
- j_block: int32 [2], P('groups'), parts along dimension 0, may hold values from 0 to 63
Outputs:
- galerkin: float32 [512, 4, 256], P(('groups', 'space'), None, 'modes'), parts along dimension 0
The draws below stay inside these ranges and needn't reach their ends.
There are 2 independent parts, one for each index of `groups`. The reference program is written for one: setup_inputs(seed, part) draws one part's arguments, and reference() takes and returns one part's arrays. A program takes and returns all parts, laid end to end along the dimension named above; an argument that names none is the same for every part. Nothing has to cross between parts.
All inputs are finite; a program needn't handle non-finite values.
Results may differ from the reference program's by a relative error of at most 0.005.
Values may be sent and summed in bfloat16 or wider, within the bound.
No kernel may reach another device: no remote copies, remote signals or barrier semaphores. Data moves between devices by JAX's collectives and lax.ppermute only.
A program may use at most 64 MiB of HBM per device.

```python
import math
import jax
import jax.numpy as jnp
from jax import lax

MODES = 256
JB = 4
PL = 1
NX = 8
NZ = 128
NW = 16
NY = 8


def with_ends(entries, rng, smallest, top_value):
    spot = [jax.random.randint(jax.random.fold_in(rng, axis), (), 0, length) for axis, length in enumerate(entries.shape)]
    longest = entries.shape.index(max(entries.shape))
    neighbour = spot[:longest] + [(spot[longest] + 1) % entries.shape[longest]] + spot[longest + 1:]
    return entries.at[tuple(spot)].set(smallest).at[tuple(neighbour)].set(top_value)


def spiked(entries, own_key, source, target, parts, factor):
    def block_of(axis_at):
        return (jnp.arange(entries.shape[axis_at]) // (entries.shape[axis_at] // parts)).reshape((-1,) + (1,) * (entries.ndim - 1 - axis_at))

    one_side = jax.random.permutation(own_key, parts)[block_of(target)]
    second = (block_of(target) + parts // 2) % parts
    return jnp.where((block_of(source) == one_side) | (block_of(source) == second), factor * entries, entries)


def block_scale(own_key, extent, pieces, low, top_value):
    factor_of, own = 1.0, jax.random.fold_in(own_key, 6)
    for axis_at, blocks in pieces:
        draws = jnp.exp(jax.random.uniform(jax.random.fold_in(own, axis_at), (blocks,), jnp.float32, low / len(pieces), top_value / len(pieces)))
        factor_of = factor_of * jnp.repeat(draws, extent[axis_at] // blocks).reshape([-1 if axis == axis_at else 1 for axis in range(len(extent))])
    return factor_of


def gaussian_with(rng, dims, spread, bound, cuts, heavy, kind=jnp.bfloat16):
    values = spread * jax.random.normal(rng, dims, jnp.float32)
    if cuts:
        values = values * block_scale(rng, dims, cuts, -0.22, 0.18)
    return jnp.clip(spiked(values, jax.random.fold_in(rng, 3), *heavy), -bound, bound).astype(kind)


def setup_inputs(seed: int = 0, part: int = 0) -> dict:
    keys = jax.random.split(jax.random.key(seed), 5)
    own_keys = jax.random.split(jax.random.fold_in(keys[4], part), 5)
    modes = gaussian_with(own_keys[0], (MODES, 3, NY, NX, NZ), 1.0, 6.0, ((0, 2), (2, 8)), (2, 0, 8, 2.0))
    weight_ids = with_ends(jax.random.randint(own_keys[1], (NY, NX, NZ), 0, NW), jax.random.fold_in(own_keys[1], 1), 0, NW - 1).astype(jnp.int32)
    weight_table = jnp.clip(jnp.exp(jax.random.uniform(keys[2], (NW,), jnp.float32, math.log(0.2), math.log(2.0))), 0.2, 2.0)
    j_block = jax.random.randint(own_keys[3], (1,), 0, MODES // JB).astype(jnp.int32)
    return dict(modes=modes, weight_ids=weight_ids, weight_table=weight_table, j_block=j_block)


def derivs(padded):
    core = padded[:, :, 1:-1]
    along_x = 0.5 * (jnp.roll(core, -1, 3) - jnp.roll(core, 1, 3))
    along_y = 0.5 * (padded[:, :, 2:] - padded[:, :, :-2])
    along_z = 0.5 * (jnp.roll(core, -1, 4) - jnp.roll(core, 1, 4))
    return jnp.stack([along_x, along_y, along_z], 2)


def advect_all(phij, grads):
    total = phij[:, 0][:, None, None, :] * grads[None, :, :, 0].astype(jnp.float32)
    total = total + phij[:, 1][:, None, None, :] * grads[None, :, :, 1].astype(jnp.float32)
    total = total + phij[:, 2][:, None, None, :] * grads[None, :, :, 2].astype(jnp.float32)
    return total.astype(jnp.bfloat16)


def reference(modes, weight_ids, weight_table, j_block):
    first = (j_block[0] * JB).astype(jnp.int32)
    jmodes = lax.dynamic_slice_in_dim(modes, first, JB, 0)
    weight = jnp.zeros(weight_ids.shape, jnp.float32)
    for entry in range(NW):
        weight = jnp.where(weight_ids == entry, weight_table[entry], weight)
    points = PL * NX * NZ

    def step(total, block):
        start = (block * PL).astype(jnp.int32)
        core = lax.dynamic_slice_in_dim(modes, start, PL, 2)
        lower = lax.dynamic_slice_in_dim(modes, jnp.maximum(start - 1, 0).astype(jnp.int32), 1, 2)
        upper = lax.dynamic_slice_in_dim(modes, jnp.minimum(start + PL, NY - 1).astype(jnp.int32), 1, 2)
        lower = jnp.where(start > 0, lower, jnp.zeros_like(lower))
        upper = jnp.where(start + PL < NY, upper, jnp.zeros_like(upper))
        padded = jnp.concatenate([lower, core, upper], 2).astype(jnp.float32)
        grads = derivs(padded).astype(jnp.bfloat16).reshape(MODES, 3, 3, points)
        wblock = lax.dynamic_slice_in_dim(weight, start, PL, 0)
        weighted = (wblock[None, None] * core.astype(jnp.float32)).astype(jnp.bfloat16).reshape(MODES, 3, points)
        phij = lax.dynamic_slice_in_dim(jmodes, start, PL, 2).astype(jnp.float32).reshape(JB, 3, points)
        advect = advect_all(phij, grads)
        total = total + jnp.einsum('jkcp,icp->kji', advect.astype(jnp.float32), weighted.astype(jnp.float32))
        return total, None

    total, unused = lax.scan(step, jnp.zeros((MODES, JB, MODES), jnp.float32), jnp.arange(NY // PL, dtype=jnp.int32))
    return total
```

```python
import functools

import jax
import jax.numpy as jnp
from jax import lax
from jax.experimental import pallas as pl
from jax.experimental.pallas import tpu as pltpu
from jax.sharding import PartitionSpec as P

JB = 4
NW = 16
IDROWS = 16
VMEM_LIMIT = 48 * 1024 * 1024


def prep_kernel(modes_ref, ids_ref, own_ref, core_ref, xs_ref, xc_ref, zs_ref, zc_ref, tr):
    m = lax.axis_index("modes")
    q = lax.rem(lax.axis_index("space"), 2)
    nk, comps, _, nx, nz = modes_ref.shape
    for c in range(comps):
        value = modes_ref[:, c, 0].astype(jnp.float32)
        tr[:, c] = jnp.swapaxes(value, 0, 1).astype(jnp.bfloat16)
    quarter = nx // 4
    for r in range(nx // 2 + 2):
        own_ref[r] = tr[lax.rem(nx // 2 * m + nx - 1 + r, nx)]
        core_ref[r] = tr[lax.rem(nx // 2 * (1 - m) + nx - 1 + r, nx)]
    for ref, at, with_ids in (
        (xs_ref, 2 * m + 1 - q, True),
        (xc_ref, 2 * (1 - m) + 1 - q, False),
        (zs_ref, 2 * m + q, True),
        (zc_ref, 2 * (1 - m) + q, False),
    ):
        for row in range(quarter):
            for c in range(comps):
                ref[pl.ds((row * comps + c) * nk, nk), :] = tr[at * quarter + row, c]
        if with_ids:
            ids = [
                jnp.broadcast_to(ids_ref[0, pl.ds(at * quarter + row, 1), :], (IDROWS // quarter, nz))
                for row in range(quarter)
            ]
            rows = jnp.concatenate(ids, axis=0).astype(jnp.float32).astype(jnp.bfloat16)
            ref[pl.ds(quarter * comps * nk, IDROWS), :] = rows


def picks(jb_ref, m, nk):
    first = jb_ref[0] * JB
    row = lax.broadcasted_iota(jnp.int32, (16, nk), 0)
    col = lax.broadcasted_iota(jnp.int32, (16, nk), 1)
    want = jnp.where(row < JB, first + row, -1)
    own = (want == col + m * nk).astype(jnp.float32).astype(jnp.bfloat16)
    other = (want == col + (1 - m) * nk).astype(jnp.float32).astype(jnp.bfloat16)
    return own, other


def picked(pick, own, other):
    return jnp.dot(pick[0], own, preferred_element_type=jnp.float32) + jnp.dot(
        pick[1], other, preferred_element_type=jnp.float32
    )


def weights_of(ids, table_ref):
    weight = jnp.zeros(ids.shape, jnp.float32)
    for entry in range(NW):
        weight = jnp.where(ids == entry, table_ref[entry], weight)
    return weight


def dot_nt(a, b):
    return lax.dot_general(a, b, (((1,), (1,)), ((), ())), preferred_element_type=jnp.float32)


def local_kernel(own_ref, other_ref, ids_ref, table_ref, jb_ref, acc_ref, adv, wts, wscr):
    m = lax.axis_index("modes")
    rows, comps, nk, nz = own_ref.shape
    rows -= 2
    pick = picks(jb_ref, m, nk)
    wscr[...] = weights_of(ids_ref[0], table_ref)
    for r in range(rows):
        phi = [picked(pick, own_ref[r + 1, d], other_ref[r + 1, d]) for d in range(comps)]
        weight = wscr[pl.ds(rows * m + r, 1), :]
        for c in range(comps):
            at = pl.ds((r * comps + c) * nz, nz)
            for half, ref in enumerate((own_ref, other_ref)):
                block = pl.ds(half * nk, nk)
                here = ref[r + 1, c].astype(jnp.float32)
                gx = 0.5 * (ref[r + 2, c].astype(jnp.float32) - ref[r, c].astype(jnp.float32))
                gz = 0.5 * (pltpu.roll(here, nz - 1, 1) - pltpu.roll(here, 1, 1))
                gx = gx.astype(jnp.bfloat16).astype(jnp.float32)
                gz = gz.astype(jnp.bfloat16).astype(jnp.float32)
                wts[block, at] = (weight * here).astype(jnp.bfloat16)
                for j in range(JB):
                    total = phi[0][j : j + 1] * gx + phi[2][j : j + 1] * gz
                    adv[j, block, at] = total.astype(jnp.bfloat16)
    for j in range(JB):
        acc_ref[j] = dot_nt(adv[j], wts[...])


def cross_kernel(
    chunk, own_ref, other_ref, xs_ref, xc_ref, zs_ref, zc_ref, ids_ref, table_ref, jb_ref, acc_ref,
    keep_ref, send_ref, adv, wts, wscr,
):
    m = lax.axis_index("modes")
    q = lax.rem(lax.axis_index("space"), 2)
    sigma = jnp.where(q == 0, 0.5, -0.5)
    rows, comps, nk, nz = own_ref.shape
    rows -= 2
    quarter = rows // 2
    span = quarter * comps * nz
    pick = picks(jb_ref, m, nk)
    wscr[...] = weights_of(ids_ref[0], table_ref)
    w1 = weights_of(xs_ref[pl.ds(span, IDROWS), :].astype(jnp.float32), table_ref)
    w2 = weights_of(zs_ref[pl.ds(span, IDROWS), :].astype(jnp.float32), table_ref)
    for r in range(quarter):
        row0 = 1 + quarter * q + r
        weight0 = wscr[pl.ds(rows * m + quarter * q + r, 1), :]
        idrow = IDROWS // quarter * r
        weight1, weight2 = w1[idrow : idrow + 1], w2[idrow : idrow + 1]
        along = pl.ds((r * comps + 1) * nk, nk)
        phi0 = sigma * picked(pick, own_ref[row0, 1], other_ref[row0, 1])
        phi1 = picked(pick, xs_ref[along, :], xc_ref[along, :])
        phi2 = -sigma * picked(pick, zs_ref[along, :], zc_ref[along, :])
        for c in range(comps):
            lane = (r * comps + c) * nz
            src = pl.ds((r * comps + c) * nk, nk)
            for half, (p0, p1, p2) in enumerate(
                ((own_ref, xs_ref, zs_ref), (other_ref, xc_ref, zc_ref))
            ):
                block = pl.ds(half * nk, nk)
                f0 = p0[row0, c].astype(jnp.float32)
                f1 = p1[src, :].astype(jnp.float32)
                f2 = p2[src, :].astype(jnp.float32)
                gy = (sigma * (f2 - f0)).astype(jnp.bfloat16).astype(jnp.float32)
                for part, (field, weight) in enumerate(((f0, weight0), (f1, weight1), (f2, weight2))):
                    wts[block, pl.ds(part * span + lane, nz)] = (weight * field).astype(jnp.bfloat16)
                for j in range(JB):
                    for part, (phi, field) in enumerate(((phi0, f1), (phi1, gy), (phi2, f1))):
                        adv[j, block, pl.ds(part * span + lane, nz)] = (
                            phi[j : j + 1] * field
                        ).astype(jnp.bfloat16)
    per_half = nk // chunk
    for j in range(JB):
        total = acc_ref[j] + dot_nt(adv[j], wts[...])
        for half in range(2):
            first = per_half * (m if half == 0 else 1 - m)
            for part in range(per_half):
                piece = total[half * nk + part * chunk : half * nk + (part + 1) * chunk]
                keep_ref[first + part, j] = piece[:, :nk]
                send_ref[first + part, j] = piece[:, nk:]


def on_device(n, modes, weight_ids, weight_table, j_block):
    nk, comps, _, nx, nz = modes.shape
    bf16, f32 = jnp.bfloat16, jnp.float32
    vmem = pl.BlockSpec(memory_space=pltpu.VMEM)
    smem = pl.BlockSpec(memory_space=pltpu.SMEM)
    params = pltpu.CompilerParams(vmem_limit_bytes=VMEM_LIMIT)
    six = nx // 2 + 2
    body = nx // 4 * comps * nk
    own, to_core, xs, xc, zs, zc = pl.pallas_call(
        prep_kernel,
        out_shape=[
            jax.ShapeDtypeStruct((six, comps, nk, nz), bf16),
            jax.ShapeDtypeStruct((six, comps, nk, nz), bf16),
            jax.ShapeDtypeStruct((body + IDROWS, nz), bf16),
            jax.ShapeDtypeStruct((body, nz), bf16),
            jax.ShapeDtypeStruct((body + IDROWS, nz), bf16),
            jax.ShapeDtypeStruct((body, nz), bf16),
        ],
        in_specs=[vmem, vmem],
        out_specs=[vmem] * 6,
        scratch_shapes=[pltpu.VMEM((nx, comps, nk, nz), bf16)],
        compiler_params=params,
        name="prep",
    )(modes, weight_ids)

    both = ("space", "modes")
    x_pairs = [(s, s ^ 1) for s in range(n)]
    z_pairs = [(s, s - 2) for s in range(2, n, 2)] + [(s, s + 2) for s in range(1, n - 2, 2)]
    same = lambda pairs: [(2 * a + m, 2 * b + m) for a, b in pairs for m in range(2)]
    cross = lambda pairs: [(2 * a + m, 2 * b + 1 - m) for a, b in pairs for m in range(2)]
    other = lax.ppermute(to_core, "modes", [(0, 1), (1, 0)])
    xs = lax.ppermute(xs, both, same(x_pairs))
    zs = lax.ppermute(zs, both, same(z_pairs))
    xc = lax.ppermute(xc, both, cross(x_pairs))
    zc = lax.ppermute(zc, both, cross(z_pairs))

    acc = pl.pallas_call(
        local_kernel,
        out_shape=jax.ShapeDtypeStruct((JB, 2 * nk, 2 * nk), f32),
        in_specs=[vmem, vmem, vmem, smem, smem],
        out_specs=vmem,
        scratch_shapes=[
            pltpu.VMEM((JB, 2 * nk, nx // 2 * comps * nz), bf16),
            pltpu.VMEM((2 * nk, nx // 2 * comps * nz), bf16),
            pltpu.VMEM((nx, nz), f32),
        ],
        compiler_params=params,
        cost_estimate=pl.CostEstimate(flops=900_000_000, bytes_accessed=2_400_000, transcendentals=0),
        name="local",
    )(own, other, weight_ids, weight_table, j_block)

    per_target = 2 * nk // n
    chunk = max(16, per_target)
    pieces = 2 * nk // chunk
    keep, send = pl.pallas_call(
        functools.partial(cross_kernel, chunk),
        out_shape=[jax.ShapeDtypeStruct((pieces, JB, chunk, nk), f32)] * 2,
        in_specs=[vmem] * 7 + [smem, smem, vmem],
        out_specs=[vmem] * 2,
        scratch_shapes=[
            pltpu.VMEM((JB, 2 * nk, 3 * nx // 4 * comps * nz), bf16),
            pltpu.VMEM((2 * nk, 3 * nx // 4 * comps * nz), bf16),
            pltpu.VMEM((nx, nz), f32),
        ],
        compiler_params=params,
        cost_estimate=pl.CostEstimate(flops=1_300_000_000, bytes_accessed=4_000_000, transcendentals=0),
        name="cross",
    )(own, other, xs, xc, zs, zc, weight_ids, weight_table, j_block, acc)

    got = lax.ppermute(send, "modes", [(0, 1), (1, 0)])
    share = (keep + got).astype(bf16)
    if chunk != per_target:
        share = share.reshape(pieces, JB, chunk // per_target, per_target, nk)
        share = share.transpose(0, 2, 1, 3, 4).reshape(n, JB, per_target, nk)
    parts = lax.all_to_all(share, "space", 0, 0, tiled=True)
    return jnp.sum(parts.astype(f32), axis=0).transpose(1, 0, 2)


def solution(mesh):
    return jax.shard_map(
        functools.partial(on_device, mesh.shape["space"]),
        mesh=mesh,
        in_specs=(
            P("modes", None, ("groups", "space"), None, None),
            P(("groups", "space"), None, None),
            P(),
            P("groups"),
        ),
        out_specs=P(("groups", "space"), None, "modes"),
        check_vma=False,
    )
```

```python
import functools

import jax
import jax.numpy as jnp
from jax import lax
from jax.experimental import pallas as pl
from jax.experimental.pallas import tpu as pltpu
from jax.sharding import PartitionSpec as P

JB = 4
NW = 16
IDROWS = 16
LOADS = 4
VMEM_LIMIT = 48 * 1024 * 1024


def prep_kernel(
    modes_hbm, ids_hbm, own_ref, core_ref, xs_ref, xc_ref, zs_ref, zc_ref, modes_ref, ids_ref, tr, sems
):
    m = lax.axis_index("modes")
    q = lax.rem(lax.axis_index("space"), 2)
    nk, comps, _, nx, nz = modes_hbm.shape
    step = nk // LOADS
    copies = [
        pltpu.make_async_copy(
            modes_hbm.at[pl.ds(p * step, step)], modes_ref.at[pl.ds(p * step, step)], sems.at[p]
        )
        for p in range(LOADS)
    ]
    copies.append(pltpu.make_async_copy(ids_hbm, ids_ref, sems.at[LOADS]))
    for copy in copies:
        copy.start()
    for p in range(LOADS):
        copies[p].wait()
        block = pl.ds(p * step, step)
        for c in range(comps):
            value = modes_ref[block, c, 0].astype(jnp.float32)
            tr[:, c, block] = jnp.swapaxes(value, 0, 1).astype(jnp.bfloat16)
    copies[LOADS].wait()
    quarter = nx // 4
    for r in range(nx // 2 + 2):
        own_ref[r] = tr[lax.rem(nx // 2 * m + nx - 1 + r, nx)]
        core_ref[r] = tr[lax.rem(nx // 2 * (1 - m) + nx - 1 + r, nx)]
    for ref, at, with_ids in (
        (xs_ref, 2 * m + 1 - q, True),
        (xc_ref, 2 * (1 - m) + 1 - q, False),
        (zs_ref, 2 * m + q, True),
        (zc_ref, 2 * (1 - m) + q, False),
    ):
        for row in range(quarter):
            for c in range(comps):
                ref[pl.ds((row * comps + c) * nk, nk), :] = tr[at * quarter + row, c]
        if with_ids:
            ids = [
                jnp.broadcast_to(ids_ref[0, pl.ds(at * quarter + row, 1), :], (IDROWS // quarter, nz))
                for row in range(quarter)
            ]
            rows = jnp.concatenate(ids, axis=0).astype(jnp.float32).astype(jnp.bfloat16)
            ref[pl.ds(quarter * comps * nk, IDROWS), :] = rows


def picks(jb_ref, m, nk):
    first = jb_ref[0] * JB
    row = lax.broadcasted_iota(jnp.int32, (16, nk), 0)
    col = lax.broadcasted_iota(jnp.int32, (16, nk), 1)
    want = jnp.where(row < JB, first + row, -1)
    own = (want == col + m * nk).astype(jnp.float32).astype(jnp.bfloat16)
    other = (want == col + (1 - m) * nk).astype(jnp.float32).astype(jnp.bfloat16)
    return own, other


def picked(pick, own, other):
    return jnp.dot(pick[0], own, preferred_element_type=jnp.float32) + jnp.dot(
        pick[1], other, preferred_element_type=jnp.float32
    )


def weights_of(ids, table_ref):
    weight = jnp.zeros(ids.shape, jnp.float32)
    for entry in range(NW):
        weight = jnp.where(ids == entry, table_ref[entry], weight)
    return weight


def dot_nt(a, b):
    return lax.dot_general(a, b, (((1,), (1,)), ((), ())), preferred_element_type=jnp.float32)


def local_kernel(own_ref, other_ref, ids_ref, table_ref, jb_ref, acc_ref, adv, wts, wscr):
    m = lax.axis_index("modes")
    rows, comps, nk, nz = own_ref.shape
    rows -= 2
    pick = picks(jb_ref, m, nk)
    wscr[...] = weights_of(ids_ref[0], table_ref)
    for r in range(rows):
        phi = [picked(pick, own_ref[r + 1, d], other_ref[r + 1, d]) for d in range(comps)]
        weight = wscr[pl.ds(rows * m + r, 1), :]
        for c in range(comps):
            at = pl.ds((r * comps + c) * nz, nz)
            for half, ref in enumerate((own_ref, other_ref)):
                block = pl.ds(half * nk, nk)
                here = ref[r + 1, c].astype(jnp.float32)
                gx = 0.5 * (ref[r + 2, c].astype(jnp.float32) - ref[r, c].astype(jnp.float32))
                gz = 0.5 * (pltpu.roll(here, nz - 1, 1) - pltpu.roll(here, 1, 1))
                gx = gx.astype(jnp.bfloat16).astype(jnp.float32)
                gz = gz.astype(jnp.bfloat16).astype(jnp.float32)
                wts[block, at] = (weight * here).astype(jnp.bfloat16)
                for j in range(JB):
                    total = phi[0][j : j + 1] * gx + phi[2][j : j + 1] * gz
                    adv[j, block, at] = total.astype(jnp.bfloat16)
    for j in range(JB):
        acc_ref[j] = dot_nt(adv[j], wts[...])


def cross_kernel(
    chunk, planes, own_ref, other_ref, xs_ref, xc_ref, zs_ref, zc_ref, ids_ref, table_ref, jb_ref, acc_ref,
    keep_ref, send_ref, adv, wts, wscr,
):
    m = lax.axis_index("modes")
    plane = lax.axis_index("space")
    q = lax.rem(plane, 2)
    inside = jnp.where(jnp.logical_or(plane == 1, plane == planes - 2), 0.0, 1.0)
    sigma = jnp.where(q == 0, 0.5, -0.5)
    rows, comps, nk, nz = own_ref.shape
    rows -= 2
    quarter = rows // 2
    span = quarter * comps * nz
    pick = picks(jb_ref, m, nk)
    wscr[...] = weights_of(ids_ref[0], table_ref)
    w1 = weights_of(xs_ref[pl.ds(span, IDROWS), :].astype(jnp.float32), table_ref)
    w2 = weights_of(zs_ref[pl.ds(span, IDROWS), :].astype(jnp.float32), table_ref)
    for r in range(quarter):
        row0 = 1 + quarter * q + r
        weight0 = wscr[pl.ds(rows * m + quarter * q + r, 1), :]
        idrow = IDROWS // quarter * r
        weight1, weight2 = w1[idrow : idrow + 1], w2[idrow : idrow + 1]
        along = pl.ds((r * comps + 1) * nk, nk)
        phi0 = sigma * picked(pick, own_ref[row0, 1], other_ref[row0, 1])
        phi1 = picked(pick, xs_ref[along, :], xc_ref[along, :])
        phi2 = -sigma * picked(pick, zs_ref[along, :], zc_ref[along, :])
        for c in range(comps):
            lane = (r * comps + c) * nz
            src = pl.ds((r * comps + c) * nk, nk)
            for half, (p0, p1, p2) in enumerate(
                ((own_ref, xs_ref, zs_ref), (other_ref, xc_ref, zc_ref))
            ):
                block = pl.ds(half * nk, nk)
                f0 = p0[row0, c].astype(jnp.float32)
                f1 = p1[src, :].astype(jnp.float32)
                f2 = inside * p2[src, :].astype(jnp.float32)
                gy = (sigma * (f2 - f0)).astype(jnp.bfloat16).astype(jnp.float32)
                for part, (field, weight) in enumerate(((f0, weight0), (f1, weight1), (f2, weight2))):
                    wts[block, pl.ds(part * span + lane, nz)] = (weight * field).astype(jnp.bfloat16)
                for j in range(JB):
                    for part, (phi, field) in enumerate(((phi0, f1), (phi1, gy), (phi2, f1))):
                        adv[j, block, pl.ds(part * span + lane, nz)] = (
                            phi[j : j + 1] * field
                        ).astype(jnp.bfloat16)
    per_half = nk // chunk
    for j in range(JB):
        total = acc_ref[j] + dot_nt(adv[j], wts[...])
        for half in range(2):
            first = per_half * (m if half == 0 else 1 - m)
            for part in range(per_half):
                piece = total[half * nk + part * chunk : half * nk + (part + 1) * chunk]
                keep_ref[first + part, j] = piece[:, :nk]
                send_ref[first + part, j] = piece[:, nk:].astype(jnp.bfloat16)


def share_kernel(keep_ref, got_ref, mine_ref, *out_refs):
    s = lax.axis_index("space")
    mine_ref[...] = keep_ref[s] + got_ref[s].astype(jnp.float32)
    for step, ref in enumerate(out_refs, 1):
        to = jnp.bitwise_xor(s, step)
        ref[...] = (keep_ref[to] + got_ref[to].astype(jnp.float32)).astype(jnp.bfloat16)


def total_kernel(mine_ref, *refs):
    *parts, out_ref = refs
    total = mine_ref[...]
    for ref in parts:
        total = total + ref[...].astype(jnp.float32)
    for j in range(JB):
        out_ref[:, j, :] = total[j]


def on_device(n, modes, weight_ids, weight_table, j_block):
    nk, comps, _, nx, nz = modes.shape
    bf16, f32 = jnp.bfloat16, jnp.float32
    vmem = pl.BlockSpec(memory_space=pltpu.VMEM)
    smem = pl.BlockSpec(memory_space=pltpu.SMEM)
    hbm = pl.BlockSpec(memory_space=pl.ANY)
    params = pltpu.CompilerParams(vmem_limit_bytes=VMEM_LIMIT)
    six = nx // 2 + 2
    body = nx // 4 * comps * nk
    own, to_core, xs, xc, zs, zc = pl.pallas_call(
        prep_kernel,
        out_shape=[
            jax.ShapeDtypeStruct((six, comps, nk, nz), bf16),
            jax.ShapeDtypeStruct((six, comps, nk, nz), bf16),
            jax.ShapeDtypeStruct((body + IDROWS, nz), bf16),
            jax.ShapeDtypeStruct((body, nz), bf16),
            jax.ShapeDtypeStruct((body + IDROWS, nz), bf16),
            jax.ShapeDtypeStruct((body, nz), bf16),
        ],
        in_specs=[hbm, hbm],
        out_specs=[vmem] * 6,
        scratch_shapes=[
            pltpu.VMEM(modes.shape, bf16),
            pltpu.VMEM(weight_ids.shape, jnp.int32),
            pltpu.VMEM((nx, comps, nk, nz), bf16),
            pltpu.SemaphoreType.DMA((LOADS + 1,)),
        ],
        compiler_params=params,
        name="prep",
    )(modes, weight_ids)

    both = ("space", "modes")
    x_pairs = [(s, s ^ 1) for s in range(n)]
    z_pairs = [(s, (s + (2 if s % 2 else -2)) % n) for s in range(n)]
    same = lambda pairs: [(2 * a + m, 2 * b + m) for a, b in pairs for m in range(2)]
    cross = lambda pairs: [(2 * a + m, 2 * b + 1 - m) for a, b in pairs for m in range(2)]
    other = lax.ppermute(to_core, "modes", [(0, 1), (1, 0)])
    xs = lax.ppermute(xs, both, same(x_pairs))
    zs = lax.ppermute(zs, both, same(z_pairs))
    xc = lax.ppermute(xc, both, cross(x_pairs))
    zc = lax.ppermute(zc, both, cross(z_pairs))

    acc = pl.pallas_call(
        local_kernel,
        out_shape=jax.ShapeDtypeStruct((JB, 2 * nk, 2 * nk), f32),
        in_specs=[vmem, vmem, vmem, smem, smem],
        out_specs=vmem,
        scratch_shapes=[
            pltpu.VMEM((JB, 2 * nk, nx // 2 * comps * nz), bf16),
            pltpu.VMEM((2 * nk, nx // 2 * comps * nz), bf16),
            pltpu.VMEM((nx, nz), f32),
        ],
        compiler_params=params,
        cost_estimate=pl.CostEstimate(flops=900_000_000, bytes_accessed=2_400_000, transcendentals=0),
        name="local",
    )(own, other, weight_ids, weight_table, j_block)

    per_target = 2 * nk // n
    chunk = max(16, per_target)
    pieces = 2 * nk // chunk
    keep, send = pl.pallas_call(
        functools.partial(cross_kernel, chunk, n),
        out_shape=[
            jax.ShapeDtypeStruct((pieces, JB, chunk, nk), f32),
            jax.ShapeDtypeStruct((pieces, JB, chunk, nk), bf16),
        ],
        in_specs=[vmem] * 7 + [smem, smem, vmem],
        out_specs=[vmem] * 2,
        scratch_shapes=[
            pltpu.VMEM((JB, 2 * nk, 3 * nx // 4 * comps * nz), bf16),
            pltpu.VMEM((2 * nk, 3 * nx // 4 * comps * nz), bf16),
            pltpu.VMEM((nx, nz), f32),
        ],
        compiler_params=params,
        cost_estimate=pl.CostEstimate(flops=1_300_000_000, bytes_accessed=4_000_000, transcendentals=0),
        name="cross",
    )(own, other, xs, xc, zs, zc, weight_ids, weight_table, j_block, acc)

    got = lax.ppermute(send, "modes", [(0, 1), (1, 0)])
    if n in (2, 4, 8):
        piece = (JB, chunk, nk)
        mine, *shares = pl.pallas_call(
            share_kernel,
            out_shape=[jax.ShapeDtypeStruct(piece, f32)] + [jax.ShapeDtypeStruct(piece, bf16)] * (n - 1),
            in_specs=[vmem] * 2,
            out_specs=[vmem] * n,
            compiler_params=params,
            name="share",
        )(keep, got)
        parts = [
            lax.ppermute(part, "space", [(s, s ^ step) for s in range(n)])
            for step, part in enumerate(shares, 1)
        ]
        return pl.pallas_call(
            total_kernel,
            out_shape=jax.ShapeDtypeStruct((chunk, JB, nk), f32),
            in_specs=[vmem] * n,
            out_specs=vmem,
            compiler_params=params,
            name="total",
        )(mine, *parts)
    share = (keep + got).astype(bf16)
    if chunk != per_target:
        share = share.reshape(pieces, JB, chunk // per_target, per_target, nk)
        share = share.transpose(0, 2, 1, 3, 4).reshape(n, JB, per_target, nk)
    parts = lax.all_to_all(share, "space", 0, 0, tiled=True)
    return jnp.sum(parts.astype(f32), axis=0).transpose(1, 0, 2)


def solution(mesh):
    return jax.shard_map(
        functools.partial(on_device, mesh.shape["space"]),
        mesh=mesh,
        in_specs=(
            P("modes", None, ("groups", "space"), None, None),
            P(("groups", "space"), None, None),
            P(),
            P("groups"),
        ),
        out_specs=P(("groups", "space"), None, "modes"),
        check_vma=False,
    )
```

```python
import functools

import jax
import jax.numpy as jnp
from jax import lax
from jax.experimental import pallas as pl
from jax.experimental.pallas import tpu as pltpu
from jax.sharding import PartitionSpec as P

JB = 4
NW = 16
IDROWS = 16
LOADS = 4
NEAR = 4
VMEM_LIMIT = 48 * 1024 * 1024


def prep_kernel(
    modes_hbm, ids_hbm, own_ref, core_ref, xs_ref, xc_ref, zs_ref, zc_ref, modes_ref, ids_ref, tr, sems
):
    m = lax.axis_index("modes")
    q = lax.rem(lax.axis_index("space"), 2)
    nk, comps, _, nx, nz = modes_hbm.shape
    step = nk // LOADS
    copies = [
        pltpu.make_async_copy(
            modes_hbm.at[pl.ds(p * step, step)], modes_ref.at[pl.ds(p * step, step)], sems.at[p]
        )
        for p in range(LOADS)
    ]
    copies.append(pltpu.make_async_copy(ids_hbm, ids_ref, sems.at[LOADS]))
    for copy in copies:
        copy.start()
    for p in range(LOADS):
        copies[p].wait()
        block = pl.ds(p * step, step)
        for c in range(comps):
            value = modes_ref[block, c, 0].astype(jnp.float32)
            tr[:, c, block] = jnp.swapaxes(value, 0, 1).astype(jnp.bfloat16)
    copies[LOADS].wait()
    quarter = nx // 4
    for r in range(nx // 2 + 2):
        own_ref[r] = tr[lax.rem(nx // 2 * m + nx - 1 + r, nx)]
        core_ref[r] = tr[lax.rem(nx // 2 * (1 - m) + nx - 1 + r, nx)]
    for ref, at, with_ids in (
        (xs_ref, 2 * m + 1 - q, True),
        (xc_ref, 2 * (1 - m) + 1 - q, False),
        (zs_ref, 2 * m + q, True),
        (zc_ref, 2 * (1 - m) + q, False),
    ):
        for row in range(quarter):
            for c in range(comps):
                ref[pl.ds((row * comps + c) * nk, nk), :] = tr[at * quarter + row, c]
        if with_ids:
            ids = [
                jnp.broadcast_to(ids_ref[0, pl.ds(at * quarter + row, 1), :], (IDROWS // quarter, nz))
                for row in range(quarter)
            ]
            rows = jnp.concatenate(ids, axis=0).astype(jnp.float32).astype(jnp.bfloat16)
            ref[pl.ds(quarter * comps * nk, IDROWS), :] = rows


def picks(jb_ref, m, nk):
    first = jb_ref[0] * JB
    row = lax.broadcasted_iota(jnp.int32, (16, nk), 0)
    col = lax.broadcasted_iota(jnp.int32, (16, nk), 1)
    want = jnp.where(row < JB, first + row, -1)
    own = (want == col + m * nk).astype(jnp.float32).astype(jnp.bfloat16)
    other = (want == col + (1 - m) * nk).astype(jnp.float32).astype(jnp.bfloat16)
    return own, other


def picked(pick, own, other):
    return jnp.dot(pick[0], own, preferred_element_type=jnp.float32) + jnp.dot(
        pick[1], other, preferred_element_type=jnp.float32
    )


def weights_of(ids, table_ref):
    weight = jnp.zeros(ids.shape, jnp.float32)
    for entry in range(NW):
        weight = jnp.where(ids == entry, table_ref[entry], weight)
    return weight


def dot_nt(a, b):
    return lax.dot_general(a, b, (((1,), (1,)), ((), ())), preferred_element_type=jnp.float32)


def local_kernel(own_ref, other_ref, ids_ref, table_ref, jb_ref, acc_ref, adv, wts, wscr):
    m = lax.axis_index("modes")
    rows, comps, nk, nz = own_ref.shape
    rows -= 2
    pick = picks(jb_ref, m, nk)
    wscr[...] = weights_of(ids_ref[0], table_ref)
    for r in range(rows):
        phi = [picked(pick, own_ref[r + 1, d], other_ref[r + 1, d]) for d in range(comps)]
        weight = wscr[pl.ds(rows * m + r, 1), :]
        for c in range(comps):
            at = pl.ds((r * comps + c) * nz, nz)
            for half, ref in enumerate((own_ref, other_ref)):
                block = pl.ds(half * nk, nk)
                here = ref[r + 1, c].astype(jnp.float32)
                gx = 0.5 * (ref[r + 2, c].astype(jnp.float32) - ref[r, c].astype(jnp.float32))
                gz = 0.5 * (pltpu.roll(here, nz - 1, 1) - pltpu.roll(here, 1, 1))
                gx = gx.astype(jnp.bfloat16).astype(jnp.float32)
                gz = gz.astype(jnp.bfloat16).astype(jnp.float32)
                wts[block, at] = (weight * here).astype(jnp.bfloat16)
                for j in range(JB):
                    total = phi[0][j : j + 1] * gx + phi[2][j : j + 1] * gz
                    adv[j, block, at] = total.astype(jnp.bfloat16)
    for j in range(JB):
        acc_ref[j] = dot_nt(adv[j], wts[...])


def cross_kernel(
    chunk, planes, own_ref, other_ref, xs_ref, xc_ref, zs_ref, zc_ref, ids_ref, table_ref, jb_ref, acc_ref,
    keep_ref, send_ref, adv, wts, wscr,
):
    m = lax.axis_index("modes")
    plane = lax.axis_index("space")
    q = lax.rem(plane, 2)
    inside = jnp.where(jnp.logical_or(plane == 1, plane == planes - 2), 0.0, 1.0)
    inside = inside.astype(jnp.bfloat16)
    sigma = jnp.where(q == 0, 0.5, -0.5)
    rows, comps, nk, nz = own_ref.shape
    rows -= 2
    quarter = rows // 2
    span = quarter * comps * nz
    pick = picks(jb_ref, m, nk)
    wscr[...] = weights_of(ids_ref[0], table_ref)
    w1 = weights_of(xs_ref[pl.ds(span, IDROWS), :].astype(jnp.float32), table_ref)
    w2 = weights_of(zs_ref[pl.ds(span, IDROWS), :].astype(jnp.float32), table_ref)
    for r in range(quarter):
        row0 = 1 + quarter * q + r
        weight0 = wscr[pl.ds(rows * m + quarter * q + r, 1), :]
        idrow = IDROWS // quarter * r
        weight1, weight2 = w1[idrow : idrow + 1], w2[idrow : idrow + 1]
        along = pl.ds((r * comps + 1) * nk, nk)
        phi0 = (sigma * picked(pick, own_ref[row0, 1], other_ref[row0, 1])).astype(jnp.bfloat16)
        phi1 = (sigma * picked(pick, xs_ref[along, :], xc_ref[along, :])).astype(jnp.bfloat16)
        phi2 = (-sigma * picked(pick, zs_ref[along, :], zc_ref[along, :])).astype(jnp.bfloat16)
        for c in range(comps):
            lane = (r * comps + c) * nz
            src = pl.ds((r * comps + c) * nk, nk)
            for half, (p0, p1, p2) in enumerate(
                ((own_ref, xs_ref, zs_ref), (other_ref, xc_ref, zc_ref))
            ):
                block = pl.ds(half * nk, nk)
                f0 = p0[row0, c]
                f1 = p1[src, :]
                f2 = inside * p2[src, :]
                gy = f2 - f0
                for part, (field, weight) in enumerate(((f0, weight0), (f1, weight1), (f2, weight2))):
                    wts[block, pl.ds(part * span + lane, nz)] = (
                        weight * field.astype(jnp.float32)
                    ).astype(jnp.bfloat16)
                for j in range(JB):
                    for part, (phi, field) in enumerate(((phi0, f1), (phi1, gy), (phi2, f1))):
                        adv[j, block, pl.ds(part * span + lane, nz)] = phi[j : j + 1] * field
    per_half = nk // chunk
    for j in range(JB):
        total = acc_ref[j] + dot_nt(adv[j], wts[...])
        for half in range(2):
            first = per_half * (m if half == 0 else 1 - m)
            for part in range(per_half):
                piece = total[half * nk + part * chunk : half * nk + (part + 1) * chunk]
                keep_ref[first + part, j] = piece[:, :nk]
                send_ref[first + part, j] = piece[:, nk:].astype(jnp.bfloat16)


def near_kernel(keep_ref, got_ref, mine_ref, *out_refs):
    s = lax.axis_index("space")
    low = lax.rem(s, NEAR)
    for step, ref in enumerate((mine_ref,) + out_refs):
        for level in range(mine_ref.shape[0]):
            to = NEAR * level + jnp.bitwise_xor(low, step)
            ref[level] = (keep_ref[to] + got_ref[to].astype(jnp.float32)).astype(ref.dtype)


def far_kernel(mine_ref, *refs):
    *parts, keep_ref, send_ref = refs
    level = lax.div(lax.axis_index("space"), NEAR)
    for ref, at in ((keep_ref, level), (send_ref, 1 - level)):
        total = mine_ref[at]
        for part in parts:
            total = total + part[at].astype(jnp.float32)
        ref[...] = total.astype(ref.dtype)


def total_kernel(keep_ref, got_ref, out_ref):
    total = keep_ref[...] + got_ref[...].astype(jnp.float32)
    for j in range(JB):
        out_ref[:, j, :] = total[j]


def on_device(n, modes, weight_ids, weight_table, j_block):
    nk, comps, _, nx, nz = modes.shape
    bf16, f32 = jnp.bfloat16, jnp.float32
    vmem = pl.BlockSpec(memory_space=pltpu.VMEM)
    smem = pl.BlockSpec(memory_space=pltpu.SMEM)
    hbm = pl.BlockSpec(memory_space=pltpu.HBM)
    params = pltpu.CompilerParams(vmem_limit_bytes=VMEM_LIMIT)
    six = nx // 2 + 2
    body = nx // 4 * comps * nk
    own, to_core, xs, xc, zs, zc = pl.pallas_call(
        prep_kernel,
        out_shape=[
            jax.ShapeDtypeStruct((six, comps, nk, nz), bf16),
            jax.ShapeDtypeStruct((six, comps, nk, nz), bf16),
            jax.ShapeDtypeStruct((body + IDROWS, nz), bf16),
            jax.ShapeDtypeStruct((body, nz), bf16),
            jax.ShapeDtypeStruct((body + IDROWS, nz), bf16),
            jax.ShapeDtypeStruct((body, nz), bf16),
        ],
        in_specs=[hbm, hbm],
        out_specs=[vmem] * 6,
        scratch_shapes=[
            pltpu.VMEM(modes.shape, bf16),
            pltpu.VMEM(weight_ids.shape, jnp.int32),
            pltpu.VMEM((nx, comps, nk, nz), bf16),
            pltpu.SemaphoreType.DMA((LOADS + 1,)),
        ],
        compiler_params=params,
        name="prep",
    )(modes, weight_ids)

    both = ("space", "modes")
    x_pairs = [(s, s ^ 1) for s in range(n)]
    z_pairs = [(s, (s + (2 if s % 2 else -2)) % n) for s in range(n)]
    same = lambda pairs: [(2 * a + m, 2 * b + m) for a, b in pairs for m in range(2)]
    cross = lambda pairs: [(2 * a + m, 2 * b + 1 - m) for a, b in pairs for m in range(2)]
    xs = lax.ppermute(xs, both, same(x_pairs))
    xc = lax.ppermute(xc, both, cross(x_pairs))
    zs = lax.ppermute(zs, both, same(z_pairs))
    zc = lax.ppermute(zc, both, cross(z_pairs))
    other = lax.ppermute(to_core, "modes", [(0, 1), (1, 0)])

    acc = pl.pallas_call(
        local_kernel,
        out_shape=jax.ShapeDtypeStruct((JB, 2 * nk, 2 * nk), f32),
        in_specs=[vmem, vmem, vmem, smem, smem],
        out_specs=vmem,
        scratch_shapes=[
            pltpu.VMEM((JB, 2 * nk, nx // 2 * comps * nz), bf16),
            pltpu.VMEM((2 * nk, nx // 2 * comps * nz), bf16),
            pltpu.VMEM((nx, nz), f32),
        ],
        compiler_params=params,
        cost_estimate=pl.CostEstimate(flops=900_000_000, bytes_accessed=2_400_000, transcendentals=0),
        name="local",
    )(own, other, weight_ids, weight_table, j_block)

    per_target = 2 * nk // n
    chunk = max(16, per_target)
    pieces = 2 * nk // chunk
    keep, send = pl.pallas_call(
        functools.partial(cross_kernel, chunk, n),
        out_shape=[
            jax.ShapeDtypeStruct((pieces, JB, chunk, nk), f32),
            jax.ShapeDtypeStruct((pieces, JB, chunk, nk), bf16),
        ],
        in_specs=[vmem] * 7 + [smem, smem, vmem],
        out_specs=[vmem] * 2,
        scratch_shapes=[
            pltpu.VMEM((JB, 2 * nk, 3 * nx // 4 * comps * nz), bf16),
            pltpu.VMEM((2 * nk, 3 * nx // 4 * comps * nz), bf16),
            pltpu.VMEM((nx, nz), f32),
        ],
        compiler_params=params,
        cost_estimate=pl.CostEstimate(flops=1_300_000_000, bytes_accessed=4_000_000, transcendentals=0),
        name="cross",
    )(own, other, xs, xc, zs, zc, weight_ids, weight_table, j_block, acc)

    got = lax.ppermute(send, "modes", [(0, 1), (1, 0)])
    if n == 2 * NEAR:
        piece = (JB, chunk, nk)
        mine, *shares = pl.pallas_call(
            near_kernel,
            out_shape=[jax.ShapeDtypeStruct((2, *piece), f32)]
            + [jax.ShapeDtypeStruct((2, *piece), bf16)] * (NEAR - 1),
            in_specs=[vmem] * 2,
            out_specs=[vmem] * NEAR,
            compiler_params=params,
            name="near",
        )(keep, got)
        parts = [
            lax.ppermute(part, "space", [(s, s ^ step) for s in range(n)])
            for step, part in enumerate(shares, 1)
        ]
        keep, send = pl.pallas_call(
            far_kernel,
            out_shape=[jax.ShapeDtypeStruct(piece, f32), jax.ShapeDtypeStruct(piece, bf16)],
            in_specs=[vmem] * NEAR,
            out_specs=[vmem] * 2,
            compiler_params=params,
            name="far",
        )(mine, *parts)
        got = lax.ppermute(send, "space", [(s, s ^ NEAR) for s in range(n)])
        return pl.pallas_call(
            total_kernel,
            out_shape=jax.ShapeDtypeStruct((chunk, JB, nk), f32),
            in_specs=[vmem] * 2,
            out_specs=vmem,
            compiler_params=params,
            name="total",
        )(keep, got)
    share = (keep + got).astype(bf16)
    if chunk != per_target:
        share = share.reshape(pieces, JB, chunk // per_target, per_target, nk)
        share = share.transpose(0, 2, 1, 3, 4).reshape(n, JB, per_target, nk)
    parts = lax.all_to_all(share, "space", 0, 0, tiled=True)
    return jnp.sum(parts.astype(f32), axis=0).transpose(1, 0, 2)


def solution(mesh):
    return jax.shard_map(
        functools.partial(on_device, mesh.shape["space"]),
        mesh=mesh,
        in_specs=(
            P("modes", None, ("groups", "space"), None, None),
            P(("groups", "space"), None, None),
            P(),
            P("groups"),
        ),
        out_specs=P(("groups", "space"), None, "modes"),
        check_vma=False,
    )
```

```python
import functools

import jax
import jax.numpy as jnp
from jax import lax
from jax.experimental import pallas as pl
from jax.experimental.pallas import tpu as pltpu
from jax.sharding import PartitionSpec as P

JB = 4
NW = 16
IDROWS = 16
PADROWS = 16
LOADS = 4
NEAR = 4
VMEM_LIMIT = 48 * 1024 * 1024
PREP_LIMIT = 53_100 * 1024


def prep_kernel(modes_hbm, own_ref, core_ref, zs_ref, xs_ref, zc_ref, xc_ref, modes_ref, tr, sems):
    m = lax.axis_index("modes")
    q = lax.rem(lax.axis_index("space"), 2)
    nk, comps, _, nx, nz = modes_hbm.shape
    step = nk // LOADS
    copies = [
        pltpu.make_async_copy(
            modes_hbm.at[pl.ds(p * step, step)], modes_ref.at[pl.ds(p * step, step)], sems.at[p]
        )
        for p in range(LOADS)
    ]
    for copy in copies:
        copy.start()
    for p in range(LOADS):
        copies[p].wait()
        block = pl.ds(p * step, step)
        for c in range(comps):
            value = modes_ref[block, c, 0].astype(jnp.float32)
            tr[:, c, block] = jnp.swapaxes(value, 0, 1).astype(jnp.bfloat16)
    quarter = nx // 4
    for r in range(nx // 2 + 2):
        own_ref[r] = tr[lax.rem(nx // 2 * m + nx - 1 + r, nx)]
        core_ref[r] = tr[lax.rem(nx // 2 * (1 - m) + nx - 1 + r, nx)]
    for ref, at in (
        (xs_ref, 2 * m + 1 - q),
        (xc_ref, 2 * (1 - m) + 1 - q),
        (zs_ref, 2 * m + q),
        (zc_ref, 2 * (1 - m) + q),
    ):
        for row in range(quarter):
            for c in range(comps):
                ref[pl.ds((row * comps + c) * nk, nk), :] = tr[at * quarter + row, c]
    for ref in (zs_ref, xs_ref):
        pad = ref.shape[0] - quarter * comps * nk
        ref[pl.ds(quarter * comps * nk, pad), :] = jnp.zeros((pad, nz), jnp.bfloat16)


def ids_kernel(ids_ref, zc_ref, xc_ref, _, zc_out, xc_out):
    m = lax.axis_index("modes")
    q = lax.rem(lax.axis_index("space"), 2)
    body, nz = xc_ref.shape
    quarter = ids_ref.shape[1] // 4
    for ref, out, at in ((zc_ref, zc_out, 2 * (1 - m) + q), (xc_ref, xc_out, 2 * (1 - m) + 1 - q)):
        out[pl.ds(0, body), :] = ref[...]
        ids = [
            jnp.broadcast_to(ids_ref[0, pl.ds(at * quarter + row, 1), :], (IDROWS // quarter, nz))
            for row in range(quarter)
        ]
        out[pl.ds(body, IDROWS), :] = (
            jnp.concatenate(ids, axis=0).astype(jnp.float32).astype(jnp.bfloat16)
        )


def picks(jb_ref, m, nk):
    first = jb_ref[0] * JB
    row = lax.broadcasted_iota(jnp.int32, (16, nk), 0)
    col = lax.broadcasted_iota(jnp.int32, (16, nk), 1)
    want = jnp.where(row < JB, first + row, -1)
    own = (want == col + m * nk).astype(jnp.float32).astype(jnp.bfloat16)
    other = (want == col + (1 - m) * nk).astype(jnp.float32).astype(jnp.bfloat16)
    return own, other


def picked(pick, own, other):
    return jnp.dot(pick[0], own, preferred_element_type=jnp.float32) + jnp.dot(
        pick[1], other, preferred_element_type=jnp.float32
    )


def weights_of(ids, table_ref):
    weight = jnp.zeros(ids.shape, jnp.float32)
    for entry in range(NW):
        weight = jnp.where(ids == entry, table_ref[entry], weight)
    return weight


def dot_nt(a, b):
    return lax.dot_general(a, b, (((1,), (1,)), ((), ())), preferred_element_type=jnp.float32)


def local_kernel(own_ref, other_ref, ids_ref, table_ref, jb_ref, acc_ref, adv, wts, wscr):
    m = lax.axis_index("modes")
    rows, comps, nk, nz = own_ref.shape
    rows -= 2
    pick = picks(jb_ref, m, nk)
    wscr[...] = weights_of(ids_ref[0], table_ref)
    for r in range(rows):
        phi = [picked(pick, own_ref[r + 1, d], other_ref[r + 1, d]) for d in range(comps)]
        weight = wscr[pl.ds(rows * m + r, 1), :]
        for c in range(comps):
            at = pl.ds((r * comps + c) * nz, nz)
            for half, ref in enumerate((own_ref, other_ref)):
                block = pl.ds(half * nk, nk)
                here = ref[r + 1, c].astype(jnp.float32)
                gx = 0.5 * (ref[r + 2, c].astype(jnp.float32) - ref[r, c].astype(jnp.float32))
                gz = 0.5 * (pltpu.roll(here, nz - 1, 1) - pltpu.roll(here, 1, 1))
                gx = gx.astype(jnp.bfloat16).astype(jnp.float32)
                gz = gz.astype(jnp.bfloat16).astype(jnp.float32)
                wts[block, at] = (weight * here).astype(jnp.bfloat16)
                for j in range(JB):
                    total = phi[0][j : j + 1] * gx + phi[2][j : j + 1] * gz
                    adv[j, block, at] = total.astype(jnp.bfloat16)
    for j in range(JB):
        acc_ref[j] = dot_nt(adv[j], wts[...])


def cross_kernel(
    chunk, planes, own_ref, other_ref, zs_ref, xs_ref, zc_ref, xc_ref, ids_ref, table_ref, jb_ref, acc_ref,
    keep_ref, send_ref, adv, wts, wscr,
):
    m = lax.axis_index("modes")
    plane = lax.axis_index("space")
    q = lax.rem(plane, 2)
    inside = jnp.where(jnp.logical_or(plane == 1, plane == planes - 2), 0.0, 1.0)
    inside = inside.astype(jnp.bfloat16)
    sigma = jnp.where(q == 0, 0.5, -0.5)
    rows, comps, nk, nz = own_ref.shape
    rows -= 2
    quarter = rows // 2
    span = quarter * comps * nz
    pick = picks(jb_ref, m, nk)
    wscr[...] = weights_of(ids_ref[0], table_ref)
    w1 = weights_of(xc_ref[pl.ds(span, IDROWS), :].astype(jnp.float32), table_ref)
    w2 = weights_of(zc_ref[pl.ds(span, IDROWS), :].astype(jnp.float32), table_ref)
    for r in range(quarter):
        row0 = 1 + quarter * q + r
        weight0 = wscr[pl.ds(rows * m + quarter * q + r, 1), :]
        idrow = IDROWS // quarter * r
        weight1, weight2 = w1[idrow : idrow + 1], w2[idrow : idrow + 1]
        along = pl.ds((r * comps + 1) * nk, nk)
        phi0 = (sigma * picked(pick, own_ref[row0, 1], other_ref[row0, 1])).astype(jnp.bfloat16)
        phi1 = (sigma * picked(pick, xs_ref[along, :], xc_ref[along, :])).astype(jnp.bfloat16)
        phi2 = (-sigma * picked(pick, zs_ref[along, :], zc_ref[along, :])).astype(jnp.bfloat16)
        for c in range(comps):
            lane = (r * comps + c) * nz
            src = pl.ds((r * comps + c) * nk, nk)
            for half, (p0, p1, p2) in enumerate(
                ((own_ref, xs_ref, zs_ref), (other_ref, xc_ref, zc_ref))
            ):
                block = pl.ds(half * nk, nk)
                f0 = p0[row0, c]
                f1 = p1[src, :]
                f2 = inside * p2[src, :]
                gy = f2 - f0
                for part, (field, weight) in enumerate(((f0, weight0), (f1, weight1), (f2, weight2))):
                    wts[block, pl.ds(part * span + lane, nz)] = (
                        weight * field.astype(jnp.float32)
                    ).astype(jnp.bfloat16)
                for j in range(JB):
                    for part, (phi, field) in enumerate(((phi0, f1), (phi1, gy), (phi2, f1))):
                        adv[j, block, pl.ds(part * span + lane, nz)] = phi[j : j + 1] * field
    per_half = nk // chunk
    for j in range(JB):
        total = acc_ref[j] + dot_nt(adv[j], wts[...])
        for half in range(2):
            first = per_half * (m if half == 0 else 1 - m)
            for part in range(per_half):
                piece = total[half * nk + part * chunk : half * nk + (part + 1) * chunk]
                keep_ref[first + part, j] = piece[:, :nk]
                send_ref[first + part, j] = piece[:, nk:].astype(jnp.bfloat16)


def near_kernel(keep_ref, got_ref, mine_ref, *out_refs):
    s = lax.axis_index("space")
    low = lax.rem(s, NEAR)
    for step, ref in enumerate((mine_ref,) + out_refs):
        for level in range(mine_ref.shape[0]):
            to = NEAR * level + jnp.bitwise_xor(low, step)
            ref[level] = (keep_ref[to] + got_ref[to].astype(jnp.float32)).astype(ref.dtype)


def far_kernel(mine_ref, *refs):
    *parts, keep_ref, send_ref = refs
    level = lax.div(lax.axis_index("space"), NEAR)
    for ref, at in ((keep_ref, level), (send_ref, 1 - level)):
        total = mine_ref[at]
        for part in parts:
            total = total + part[at].astype(jnp.float32)
        ref[...] = total.astype(ref.dtype)


def total_kernel(keep_ref, got_ref, out_ref):
    total = keep_ref[...] + got_ref[...].astype(jnp.float32)
    for j in range(JB):
        out_ref[:, j, :] = total[j]


def on_device(n, modes, weight_ids, weight_table, j_block):
    nk, comps, _, nx, nz = modes.shape
    bf16, f32 = jnp.bfloat16, jnp.float32
    vmem = pl.BlockSpec(memory_space=pltpu.VMEM)
    smem = pl.BlockSpec(memory_space=pltpu.SMEM)
    params = pltpu.CompilerParams(vmem_limit_bytes=VMEM_LIMIT)
    six = nx // 2 + 2
    body = nx // 4 * comps * nk
    own, to_core, zs, xs, zc, xc = pl.pallas_call(
        prep_kernel,
        out_shape=[jax.ShapeDtypeStruct((six, comps, nk, nz), bf16)] * 2
        + [jax.ShapeDtypeStruct((body + PADROWS, nz), bf16)] * 2
        + [jax.ShapeDtypeStruct((body, nz), bf16)] * 2,
        in_specs=[pl.BlockSpec(memory_space=pltpu.HBM)],
        out_specs=[vmem] * 6,
        scratch_shapes=[
            pltpu.VMEM(modes.shape, bf16),
            pltpu.VMEM((nx, comps, nk, nz), bf16),
            pltpu.SemaphoreType.DMA((LOADS,)),
        ],
        compiler_params=pltpu.CompilerParams(vmem_limit_bytes=PREP_LIMIT),
        name="prep",
    )(modes)

    both = ("space", "modes")
    x_pairs = [(s, s ^ 1) for s in range(n)]
    z_pairs = [(s, (s + (2 if s % 2 else -2)) % n) for s in range(n)]
    same = lambda pairs: [(2 * a + m, 2 * b + m) for a, b in pairs for m in range(2)]
    cross = lambda pairs: [(2 * a + m, 2 * b + 1 - m) for a, b in pairs for m in range(2)]
    other = lax.ppermute(to_core, "modes", [(0, 1), (1, 0)])
    zs = lax.ppermute(zs, both, same(z_pairs))
    xs = lax.ppermute(xs, both, same(x_pairs))
    zc, xc = pl.pallas_call(
        ids_kernel,
        out_shape=[jax.ShapeDtypeStruct((body + IDROWS, nz), bf16)] * 2,
        in_specs=[vmem] * 3 + [pl.BlockSpec(memory_space=pl.ANY)],
        out_specs=[vmem] * 2,
        compiler_params=params,
        name="ids",
    )(weight_ids, zc, xc, other)
    zc = lax.ppermute(zc, both, cross(z_pairs))
    xc = lax.ppermute(xc, both, cross(x_pairs))

    acc = pl.pallas_call(
        local_kernel,
        out_shape=jax.ShapeDtypeStruct((JB, 2 * nk, 2 * nk), f32),
        in_specs=[vmem, vmem, vmem, smem, smem],
        out_specs=vmem,
        scratch_shapes=[
            pltpu.VMEM((JB, 2 * nk, nx // 2 * comps * nz), bf16),
            pltpu.VMEM((2 * nk, nx // 2 * comps * nz), bf16),
            pltpu.VMEM((nx, nz), f32),
        ],
        compiler_params=params,
        cost_estimate=pl.CostEstimate(flops=900_000_000, bytes_accessed=2_400_000, transcendentals=0),
        name="local",
    )(own, other, weight_ids, weight_table, j_block)

    per_target = 2 * nk // n
    chunk = max(16, per_target)
    pieces = 2 * nk // chunk
    keep, send = pl.pallas_call(
        functools.partial(cross_kernel, chunk, n),
        out_shape=[
            jax.ShapeDtypeStruct((pieces, JB, chunk, nk), f32),
            jax.ShapeDtypeStruct((pieces, JB, chunk, nk), bf16),
        ],
        in_specs=[vmem] * 7 + [smem, smem, vmem],
        out_specs=[vmem] * 2,
        scratch_shapes=[
            pltpu.VMEM((JB, 2 * nk, 3 * nx // 4 * comps * nz), bf16),
            pltpu.VMEM((2 * nk, 3 * nx // 4 * comps * nz), bf16),
            pltpu.VMEM((nx, nz), f32),
        ],
        compiler_params=params,
        cost_estimate=pl.CostEstimate(flops=1_300_000_000, bytes_accessed=4_000_000, transcendentals=0),
        name="cross",
    )(own, other, zs, xs, zc, xc, weight_ids, weight_table, j_block, acc)

    got = lax.ppermute(send, "modes", [(0, 1), (1, 0)])
    if n == 2 * NEAR:
        piece = (JB, chunk, nk)
        mine, *shares = pl.pallas_call(
            near_kernel,
            out_shape=[jax.ShapeDtypeStruct((2, *piece), f32)]
            + [jax.ShapeDtypeStruct((2, *piece), bf16)] * (NEAR - 1),
            in_specs=[vmem] * 2,
            out_specs=[vmem] * NEAR,
            compiler_params=params,
            name="near",
        )(keep, got)
        parts = [
            lax.ppermute(shares[step - 1], "space", [(s, s ^ step) for s in range(n)])
            for step in (3, 1, 2)
        ]
        keep, send = pl.pallas_call(
            far_kernel,
            out_shape=[jax.ShapeDtypeStruct(piece, f32), jax.ShapeDtypeStruct(piece, bf16)],
            in_specs=[vmem] * NEAR,
            out_specs=[vmem] * 2,
            compiler_params=params,
            name="far",
        )(mine, *parts)
        got = lax.ppermute(send, "space", [(s, s ^ NEAR) for s in range(n)])
        return pl.pallas_call(
            total_kernel,
            out_shape=jax.ShapeDtypeStruct((chunk, JB, nk), f32),
            in_specs=[vmem] * 2,
            out_specs=vmem,
            compiler_params=params,
            name="total",
        )(keep, got)
    share = (keep + got).astype(bf16)
    if chunk != per_target:
        share = share.reshape(pieces, JB, chunk // per_target, per_target, nk)
        share = share.transpose(0, 2, 1, 3, 4).reshape(n, JB, per_target, nk)
    parts = lax.all_to_all(share, "space", 0, 0, tiled=True)
    return jnp.sum(parts.astype(f32), axis=0).transpose(1, 0, 2)


def solution(mesh):
    return jax.shard_map(
        functools.partial(on_device, mesh.shape["space"]),
        mesh=mesh,
        in_specs=(
            P("modes", None, ("groups", "space"), None, None),
            P(("groups", "space"), None, None),
            P(),
            P("groups"),
        ),
        out_specs=P(("groups", "space"), None, "modes"),
        check_vma=False,
    )
```

```python
import functools

import jax
import jax.numpy as jnp
from jax import lax
from jax.experimental import pallas as pl
from jax.experimental.pallas import tpu as pltpu
from jax.sharding import PartitionSpec as P

JB = 4
NW = 16
IDROWS = 16
PADROWS = 16
LOADS = 4
ORDER = ((0, 1, 2), (1, 2, 0))
VMEM_LIMIT = 48 * 1024 * 1024
PREP_LIMIT = 53_100 * 1024


def prep_kernel(modes_hbm, own_ref, core_ref, zs_ref, xs_ref, zc_ref, xc_ref, modes_ref, tr, sems):
    m = lax.axis_index("modes")
    q = lax.rem(lax.axis_index("space"), 2)
    nk, comps, _, nx, nz = modes_hbm.shape
    step = nk // LOADS
    copies = [
        pltpu.make_async_copy(
            modes_hbm.at[pl.ds(p * step, step)], modes_ref.at[pl.ds(p * step, step)], sems.at[p]
        )
        for p in range(LOADS)
    ]
    for copy in copies:
        copy.start()
    for p in range(LOADS):
        copies[p].wait()
        block = pl.ds(p * step, step)
        for c in range(comps):
            value = modes_ref[block, c, 0].astype(jnp.float32)
            tr[:, c, block] = jnp.swapaxes(value, 0, 1).astype(jnp.bfloat16)
    quarter = nx // 4
    for r in range(nx // 2 + 2):
        own_ref[r] = tr[lax.rem(nx // 2 * m + nx - 1 + r, nx)]
        core_ref[r] = tr[lax.rem(nx // 2 * (1 - m) + nx - 1 + r, nx)]
    for ref, at in (
        (xs_ref, 2 * m + 1 - q),
        (xc_ref, 2 * (1 - m) + 1 - q),
        (zs_ref, 2 * m + q),
        (zc_ref, 2 * (1 - m) + q),
    ):
        for row in range(quarter):
            for c in range(comps):
                ref[pl.ds((row * comps + c) * nk, nk), :] = tr[at * quarter + row, c]
    for ref in (zs_ref, xs_ref):
        pad = ref.shape[0] - quarter * comps * nk
        ref[pl.ds(quarter * comps * nk, pad), :] = jnp.zeros((pad, nz), jnp.bfloat16)


def ids_kernel(ids_ref, zc_ref, xc_ref, _, zc_out, xc_out):
    m = lax.axis_index("modes")
    q = lax.rem(lax.axis_index("space"), 2)
    body, nz = xc_ref.shape
    quarter = ids_ref.shape[1] // 4
    for ref, out, at in ((zc_ref, zc_out, 2 * (1 - m) + q), (xc_ref, xc_out, 2 * (1 - m) + 1 - q)):
        out[pl.ds(0, body), :] = ref[...]
        ids = [
            jnp.broadcast_to(ids_ref[0, pl.ds(at * quarter + row, 1), :], (IDROWS // quarter, nz))
            for row in range(quarter)
        ]
        out[pl.ds(body, IDROWS), :] = (
            jnp.concatenate(ids, axis=0).astype(jnp.float32).astype(jnp.bfloat16)
        )


def picks(jb_ref, m, nk):
    first = jb_ref[0] * JB
    row = lax.broadcasted_iota(jnp.int32, (16, nk), 0)
    col = lax.broadcasted_iota(jnp.int32, (16, nk), 1)
    want = jnp.where(row < JB, first + row, -1)
    own = (want == col + m * nk).astype(jnp.float32).astype(jnp.bfloat16)
    other = (want == col + (1 - m) * nk).astype(jnp.float32).astype(jnp.bfloat16)
    return own, other


def picked(pick, own, other):
    return jnp.dot(pick[0], own, preferred_element_type=jnp.float32) + jnp.dot(
        pick[1], other, preferred_element_type=jnp.float32
    )


def weights_of(ids, table_ref):
    weight = jnp.zeros(ids.shape, jnp.float32)
    for entry in range(NW):
        weight = jnp.where(ids == entry, table_ref[entry], weight)
    return weight


def dot_nt(a, b):
    return lax.dot_general(a, b, (((1,), (1,)), ((), ())), preferred_element_type=jnp.float32)


def local_kernel(own_ref, other_ref, ids_ref, table_ref, jb_ref, acc_ref, adv, wts, wscr):
    m = lax.axis_index("modes")
    rows, comps, nk, nz = own_ref.shape
    rows -= 2
    pick = picks(jb_ref, m, nk)
    wscr[...] = weights_of(ids_ref[0], table_ref)
    for r in range(rows):
        phi = [picked(pick, own_ref[r + 1, d], other_ref[r + 1, d]) for d in range(comps)]
        weight = wscr[pl.ds(rows * m + r, 1), :]
        for c in range(comps):
            at = pl.ds((r * comps + c) * nz, nz)
            for half, ref in enumerate((own_ref, other_ref)):
                block = pl.ds(half * nk, nk)
                here = ref[r + 1, c].astype(jnp.float32)
                gx = 0.5 * (ref[r + 2, c].astype(jnp.float32) - ref[r, c].astype(jnp.float32))
                gz = 0.5 * (pltpu.roll(here, nz - 1, 1) - pltpu.roll(here, 1, 1))
                gx = gx.astype(jnp.bfloat16).astype(jnp.float32)
                gz = gz.astype(jnp.bfloat16).astype(jnp.float32)
                wts[block, at] = (weight * here).astype(jnp.bfloat16)
                for j in range(JB):
                    total = phi[0][j : j + 1] * gx + phi[2][j : j + 1] * gz
                    adv[pl.ds((2 * j + half) * nk, nk), at] = total.astype(jnp.bfloat16)
    acc_ref[...] = dot_nt(adv[...], wts[...])


def cross_kernel(
    chunk, planes, own_ref, other_ref, zs_ref, xs_ref, zc_ref, xc_ref, ids_ref, table_ref, jb_ref, acc_ref,
    keep_ref, send_ref, adv, wts, wscr,
):
    m = lax.axis_index("modes")
    plane = lax.axis_index("space")
    q = lax.rem(plane, 2)
    inside = jnp.where(jnp.logical_or(plane == 1, plane == planes - 2), 0.0, 1.0)
    inside = inside.astype(jnp.bfloat16)
    sigma = jnp.where(q == 0, 0.5, -0.5)
    rows, comps, nk, nz = own_ref.shape
    rows -= 2
    quarter = rows // 2
    span = quarter * comps * nz
    pick = picks(jb_ref, m, nk)
    wscr[...] = weights_of(ids_ref[0], table_ref)
    w1 = weights_of(xc_ref[pl.ds(span, IDROWS), :].astype(jnp.float32), table_ref)
    w2 = weights_of(zc_ref[pl.ds(span, IDROWS), :].astype(jnp.float32), table_ref)
    for r in range(quarter):
        row0 = 1 + quarter * q + r
        weight0 = wscr[pl.ds(rows * m + quarter * q + r, 1), :]
        idrow = IDROWS // quarter * r
        weight1, weight2 = w1[idrow : idrow + 1], w2[idrow : idrow + 1]
        along = pl.ds((r * comps + 1) * nk, nk)
        phi0 = (sigma * picked(pick, own_ref[row0, 1], other_ref[row0, 1])).astype(jnp.bfloat16)
        phi1 = (sigma * picked(pick, xs_ref[along, :], xc_ref[along, :])).astype(jnp.bfloat16)
        phi2 = (-sigma * picked(pick, zs_ref[along, :], zc_ref[along, :])).astype(jnp.bfloat16)
        for c in range(comps):
            lane = (r * comps + c) * nz
            src = pl.ds((r * comps + c) * nk, nk)
            for half, (p0, p1, p2) in enumerate(
                ((own_ref, xs_ref, zs_ref), (other_ref, xc_ref, zc_ref))
            ):
                block = pl.ds(half * nk, nk)
                f0 = p0[row0, c]
                f1 = p1[src, :]
                f2 = inside * p2[src, :]
                gy = f2 - f0
                for part, (field, weight) in enumerate(((f0, weight0), (f1, weight1), (f2, weight2))):
                    wts[block, pl.ds(part * span + lane, nz)] = (
                        weight * field.astype(jnp.float32)
                    ).astype(jnp.bfloat16)
                for j in range(JB):
                    for part, (phi, field) in enumerate(((phi0, f1), (phi1, gy), (phi2, f1))):
                        adv[pl.ds((2 * j + half) * nk, nk), pl.ds(part * span + lane, nz)] = (
                            phi[j : j + 1] * field
                        )
    per_half = nk // chunk
    total = acc_ref[...] + dot_nt(adv[...], wts[...])
    for j in range(JB):
        for half in range(2):
            first = per_half * (m if half == 0 else 1 - m)
            for part in range(per_half):
                at = (2 * j + half) * nk + part * chunk
                piece = total[at : at + chunk]
                keep_ref[first + part, j] = piece[:, :nk]
                send_ref[first + part, j] = piece[:, nk:].astype(jnp.bfloat16)


def first_kernel(keep_ref, got_ref, keep_out, send_out):
    m = lax.axis_index("modes")
    s = lax.axis_index("space")
    at = [jnp.where(m == 0, *stage) for stage in zip(*ORDER)]
    own = lax.rem(lax.shift_right_logical(s, at[0]), 2)
    for second in range(2):
        for third in range(2):
            rest = lax.shift_left(second, at[1]) + lax.shift_left(third, at[2])
            for ref, bit in ((keep_out, own), (send_out, 1 - own)):
                to = lax.shift_left(bit, at[0]) + rest
                total = keep_ref[to] + got_ref[to].astype(jnp.float32)
                ref[second, third] = total.astype(ref.dtype)


def stage_kernel(stage, keep_ref, got_ref, keep_out, send_out):
    m = lax.axis_index("modes")
    bit = jnp.where(m == 0, ORDER[0][stage], ORDER[1][stage])
    own = lax.rem(lax.shift_right_logical(lax.axis_index("space"), bit), 2)
    for ref, at in ((keep_out, own), (send_out, 1 - own)):
        ref[...] = (keep_ref[at] + got_ref[at].astype(jnp.float32)).astype(ref.dtype)


def total_kernel(keep_ref, got_ref, out_ref):
    total = keep_ref[...] + got_ref[...].astype(jnp.float32)
    for j in range(JB):
        out_ref[:, j, :] = total[j]


def on_device(n, modes, weight_ids, weight_table, j_block):
    nk, comps, _, nx, nz = modes.shape
    bf16, f32 = jnp.bfloat16, jnp.float32
    vmem = pl.BlockSpec(memory_space=pltpu.VMEM)
    smem = pl.BlockSpec(memory_space=pltpu.SMEM)
    params = pltpu.CompilerParams(vmem_limit_bytes=VMEM_LIMIT)
    six = nx // 2 + 2
    body = nx // 4 * comps * nk
    own, to_core, zs, xs, zc, xc = pl.pallas_call(
        prep_kernel,
        out_shape=[jax.ShapeDtypeStruct((six, comps, nk, nz), bf16)] * 2
        + [jax.ShapeDtypeStruct((body + PADROWS, nz), bf16)] * 2
        + [jax.ShapeDtypeStruct((body, nz), bf16)] * 2,
        in_specs=[pl.BlockSpec(memory_space=pltpu.HBM)],
        out_specs=[vmem] * 6,
        scratch_shapes=[
            pltpu.VMEM(modes.shape, bf16),
            pltpu.VMEM((nx, comps, nk, nz), bf16),
            pltpu.SemaphoreType.DMA((LOADS,)),
        ],
        compiler_params=pltpu.CompilerParams(vmem_limit_bytes=PREP_LIMIT),
        name="prep",
    )(modes)

    both = ("space", "modes")
    x_pairs = [(s, s ^ 1) for s in range(n)]
    z_pairs = [(s, (s + (2 if s % 2 else -2)) % n) for s in range(n)]
    same = lambda pairs: [(2 * a + m, 2 * b + m) for a, b in pairs for m in range(2)]
    cross = lambda pairs: [(2 * a + m, 2 * b + 1 - m) for a, b in pairs for m in range(2)]
    other = lax.ppermute(to_core, "modes", [(0, 1), (1, 0)])
    zs = lax.ppermute(zs, both, same(z_pairs))
    xs = lax.ppermute(xs, both, same(x_pairs))
    zc, xc = pl.pallas_call(
        ids_kernel,
        out_shape=[jax.ShapeDtypeStruct((body + IDROWS, nz), bf16)] * 2,
        in_specs=[vmem] * 3 + [pl.BlockSpec(memory_space=pl.ANY)],
        out_specs=[vmem] * 2,
        compiler_params=params,
        name="ids",
    )(weight_ids, zc, xc, other)
    zc = lax.ppermute(zc, both, cross(z_pairs))
    xc = lax.ppermute(xc, both, cross(x_pairs))

    acc = pl.pallas_call(
        local_kernel,
        out_shape=jax.ShapeDtypeStruct((JB * 2 * nk, 2 * nk), f32),
        in_specs=[vmem, vmem, vmem, smem, smem],
        out_specs=vmem,
        scratch_shapes=[
            pltpu.VMEM((JB * 2 * nk, nx // 2 * comps * nz), bf16),
            pltpu.VMEM((2 * nk, nx // 2 * comps * nz), bf16),
            pltpu.VMEM((nx, nz), f32),
        ],
        compiler_params=params,
        cost_estimate=pl.CostEstimate(flops=900_000_000, bytes_accessed=2_400_000, transcendentals=0),
        name="local",
    )(own, other, weight_ids, weight_table, j_block)

    per_target = 2 * nk // n
    chunk = max(16, per_target)
    pieces = 2 * nk // chunk
    keep, send = pl.pallas_call(
        functools.partial(cross_kernel, chunk, n),
        out_shape=[
            jax.ShapeDtypeStruct((pieces, JB, chunk, nk), f32),
            jax.ShapeDtypeStruct((pieces, JB, chunk, nk), bf16),
        ],
        in_specs=[vmem] * 7 + [smem, smem, vmem],
        out_specs=[vmem] * 2,
        scratch_shapes=[
            pltpu.VMEM((JB * 2 * nk, 3 * nx // 4 * comps * nz), bf16),
            pltpu.VMEM((2 * nk, 3 * nx // 4 * comps * nz), bf16),
            pltpu.VMEM((nx, nz), f32),
        ],
        compiler_params=params,
        cost_estimate=pl.CostEstimate(flops=1_300_000_000, bytes_accessed=4_000_000, transcendentals=0),
        name="cross",
    )(own, other, zs, xs, zc, xc, weight_ids, weight_table, j_block, acc)

    got = lax.ppermute(send, "modes", [(0, 1), (1, 0)])
    if n == 8:
        left = (2, 2, JB, chunk, nk)
        for stage in range(3):
            if stage == 0:
                body_of, dims = first_kernel, left
            else:
                body_of, dims = functools.partial(stage_kernel, stage), left[stage:]
            keep, send = pl.pallas_call(
                body_of,
                out_shape=[jax.ShapeDtypeStruct(dims, f32), jax.ShapeDtypeStruct(dims, bf16)],
                in_specs=[vmem] * 2,
                out_specs=[vmem] * 2,
                compiler_params=params,
                name=f"stage{stage}",
            )(keep, got)
            pairs = [
                (2 * s + m, 2 * (s ^ (1 << ORDER[m][stage])) + m) for s in range(n) for m in range(2)
            ]
            got = lax.ppermute(send, both, pairs)
        return pl.pallas_call(
            total_kernel,
            out_shape=jax.ShapeDtypeStruct((chunk, JB, nk), f32),
            in_specs=[vmem] * 2,
            out_specs=vmem,
            compiler_params=params,
            name="total",
        )(keep, got)
    share = (keep + got).astype(bf16)
    if chunk != per_target:
        share = share.reshape(pieces, JB, chunk // per_target, per_target, nk)
        share = share.transpose(0, 2, 1, 3, 4).reshape(n, JB, per_target, nk)
    parts = lax.all_to_all(share, "space", 0, 0, tiled=True)
    return jnp.sum(parts.astype(f32), axis=0).transpose(1, 0, 2)


def solution(mesh):
    return jax.shard_map(
        functools.partial(on_device, mesh.shape["space"]),
        mesh=mesh,
        in_specs=(
            P("modes", None, ("groups", "space"), None, None),
            P(("groups", "space"), None, None),
            P(),
            P("groups"),
        ),
        out_specs=P(("groups", "space"), None, "modes"),
        check_vma=False,
    )
```

```python
import functools

import jax
import jax.numpy as jnp
from jax import lax
from jax.experimental import pallas as pl
from jax.experimental.pallas import tpu as pltpu
from jax.sharding import PartitionSpec as P

JB = 4
NW = 16
IDROWS = 16
PADROWS = 16
LOADS = 4
NEAR = 4
VMEM_LIMIT = 48 * 1024 * 1024
PREP_LIMIT = 53_100 * 1024


def prep_kernel(modes_hbm, own_ref, core_ref, zs_ref, xs_ref, zc_ref, xc_ref, modes_ref, tr, sems):
    m = lax.axis_index("modes")
    q = lax.rem(lax.axis_index("space"), 2)
    nk, comps, _, nx, nz = modes_hbm.shape
    step = nk // LOADS
    copies = [
        pltpu.make_async_copy(
            modes_hbm.at[pl.ds(p * step, step)], modes_ref.at[pl.ds(p * step, step)], sems.at[p]
        )
        for p in range(LOADS)
    ]
    for copy in copies:
        copy.start()
    for p in range(LOADS):
        copies[p].wait()
        block = pl.ds(p * step, step)
        for c in range(comps):
            value = modes_ref[block, c, 0].astype(jnp.float32)
            tr[:, c, block] = jnp.swapaxes(value, 0, 1).astype(jnp.bfloat16)
    quarter = nx // 4
    for r in range(nx // 2 + 2):
        own_ref[r] = tr[lax.rem(nx // 2 * m + nx - 1 + r, nx)]
        core_ref[r] = tr[lax.rem(nx // 2 * (1 - m) + nx - 1 + r, nx)]
    for ref, at in (
        (xs_ref, 2 * m + 1 - q),
        (xc_ref, 2 * (1 - m) + 1 - q),
        (zs_ref, 2 * m + q),
        (zc_ref, 2 * (1 - m) + q),
    ):
        for row in range(quarter):
            for c in range(comps):
                ref[pl.ds((row * comps + c) * nk, nk), :] = tr[at * quarter + row, c]
    for ref in (zs_ref, xs_ref):
        pad = ref.shape[0] - quarter * comps * nk
        ref[pl.ds(quarter * comps * nk, pad), :] = jnp.zeros((pad, nz), jnp.bfloat16)


def ids_kernel(ids_ref, zc_ref, xc_ref, _, zc_out, xc_out):
    m = lax.axis_index("modes")
    q = lax.rem(lax.axis_index("space"), 2)
    body, nz = xc_ref.shape
    quarter = ids_ref.shape[1] // 4
    for ref, out, at in ((zc_ref, zc_out, 2 * (1 - m) + q), (xc_ref, xc_out, 2 * (1 - m) + 1 - q)):
        out[pl.ds(0, body), :] = ref[...]
        ids = [
            jnp.broadcast_to(ids_ref[0, pl.ds(at * quarter + row, 1), :], (IDROWS // quarter, nz))
            for row in range(quarter)
        ]
        out[pl.ds(body, IDROWS), :] = (
            jnp.concatenate(ids, axis=0).astype(jnp.float32).astype(jnp.bfloat16)
        )


def picks(jb_ref, m, nk):
    first = jb_ref[0] * JB
    row = lax.broadcasted_iota(jnp.int32, (16, nk), 0)
    col = lax.broadcasted_iota(jnp.int32, (16, nk), 1)
    want = jnp.where(row < JB, first + row, -1)
    own = (want == col + m * nk).astype(jnp.float32).astype(jnp.bfloat16)
    other = (want == col + (1 - m) * nk).astype(jnp.float32).astype(jnp.bfloat16)
    return own, other


def picked(pick, own, other):
    return jnp.dot(pick[0], own, preferred_element_type=jnp.float32) + jnp.dot(
        pick[1], other, preferred_element_type=jnp.float32
    )


def weights_of(ids, table_ref):
    weight = jnp.zeros(ids.shape, jnp.float32)
    for entry in range(NW):
        weight = jnp.where(ids == entry, table_ref[entry], weight)
    return weight


def dot_nt(a, b):
    return lax.dot_general(a, b, (((1,), (1,)), ((), ())), preferred_element_type=jnp.float32)


def local_kernel(own_ref, other_ref, ids_ref, table_ref, jb_ref, acc_ref, adv, wts, wscr):
    m = lax.axis_index("modes")
    rows, comps, nk, nz = own_ref.shape
    rows -= 2
    pick = picks(jb_ref, m, nk)
    wscr[...] = weights_of(ids_ref[0], table_ref)
    for r in range(rows):
        phi = [picked(pick, own_ref[r + 1, d], other_ref[r + 1, d]) for d in range(comps)]
        weight = wscr[pl.ds(rows * m + r, 1), :]
        for c in range(comps):
            at = pl.ds((r * comps + c) * nz, nz)
            for half, ref in enumerate((own_ref, other_ref)):
                block = pl.ds(half * nk, nk)
                here = ref[r + 1, c].astype(jnp.float32)
                gx = 0.5 * (ref[r + 2, c].astype(jnp.float32) - ref[r, c].astype(jnp.float32))
                gz = 0.5 * (pltpu.roll(here, nz - 1, 1) - pltpu.roll(here, 1, 1))
                gx = gx.astype(jnp.bfloat16).astype(jnp.float32)
                gz = gz.astype(jnp.bfloat16).astype(jnp.float32)
                wts[block, at] = (weight * here).astype(jnp.bfloat16)
                for j in range(JB):
                    total = phi[0][j : j + 1] * gx + phi[2][j : j + 1] * gz
                    adv[pl.ds((2 * j + half) * nk, nk), at] = total.astype(jnp.bfloat16)
    acc_ref[...] = dot_nt(adv[...], wts[...])


def sign_of_plane():
    return jnp.where(lax.rem(lax.axis_index("space"), 2) == 0, 0.5, -0.5)


def early_kernel(
    own_ref, other_ref, _, xs_ref, xc_ref, ids_ref, table_ref, jb_ref, acc_ref, out_ref, w1_ref, adv, wts, wscr
):
    m = lax.axis_index("modes")
    q = lax.rem(lax.axis_index("space"), 2)
    rows, comps, nk, nz = own_ref.shape
    rows -= 2
    quarter = rows // 2
    pick = picks(jb_ref, m, nk)
    wscr[...] = weights_of(ids_ref[0], table_ref)
    w1 = weights_of(xc_ref[pl.ds(quarter * comps * nk, IDROWS), :].astype(jnp.float32), table_ref)
    for r in range(quarter):
        row0 = 1 + quarter * q + r
        weight0 = wscr[pl.ds(rows * m + quarter * q + r, 1), :]
        weight1 = w1[IDROWS // quarter * r : IDROWS // quarter * r + 1]
        phi0 = sign_of_plane() * picked(pick, own_ref[row0, 1], other_ref[row0, 1])
        phi0 = phi0.astype(jnp.bfloat16)
        for c in range(comps):
            at = pl.ds((r * comps + c) * nz, nz)
            src = pl.ds((r * comps + c) * nk, nk)
            for half, (p0, p1) in enumerate(((own_ref, xs_ref), (other_ref, xc_ref))):
                block = pl.ds(half * nk, nk)
                f0, f1 = p0[row0, c], p1[src, :]
                wts[block, at] = (weight0 * f0.astype(jnp.float32)).astype(jnp.bfloat16)
                w1_ref[block, at] = (weight1 * f1.astype(jnp.float32)).astype(jnp.bfloat16)
                for j in range(JB):
                    adv[pl.ds((2 * j + half) * nk, nk), at] = phi0[j : j + 1] * f1
    out_ref[...] = acc_ref[...] + dot_nt(adv[...], wts[...])


def cross_kernel(classes_of, chunk, planes, has_w2, own_ref, other_ref, *refs):
    zs_ref, xs_ref, zc_ref, xc_ref, w1_ref, table_ref, jb_ref, acc_ref, *refs = refs
    if has_w2:
        w2_ref, keep_ref, send_ref, adv = refs
    else:
        keep_ref, send_ref, w2_ref, adv = refs
    m = lax.axis_index("modes")
    plane = lax.axis_index("space")
    q = lax.rem(plane, 2)
    inside = jnp.where(jnp.logical_or(plane == 1, plane == planes - 2), 0.0, 1.0)
    inside = inside.astype(jnp.bfloat16)
    rows, comps, nk, nz = own_ref.shape
    quarter = (rows - 2) // 2
    span = quarter * comps * nz
    pick = picks(jb_ref, m, nk)
    classes = [pl.multiple_of(chunk * cls, chunk) for cls in classes_of(plane)]
    w2 = weights_of(zc_ref[pl.ds(quarter * comps * nk, IDROWS), :].astype(jnp.float32), table_ref)
    for r in range(quarter):
        row0 = 1 + quarter * q + r
        along = pl.ds((r * comps + 1) * nk, nk)
        phi1 = sign_of_plane() * picked(pick, xs_ref[along, :], xc_ref[along, :])
        phi2 = -sign_of_plane() * picked(pick, zs_ref[along, :], zc_ref[along, :])
        phi1, phi2 = phi1.astype(jnp.bfloat16), phi2.astype(jnp.bfloat16)
        weight2 = w2[IDROWS // quarter * r : IDROWS // quarter * r + 1]
        for c in range(comps):
            lane = (r * comps + c) * nz
            src = (r * comps + c) * nk
            for half, (p0, p1, p2) in enumerate(
                ((own_ref, xs_ref, zs_ref), (other_ref, xc_ref, zc_ref))
            ):
                if not has_w2:
                    f2 = inside * p2[pl.ds(src, nk), :]
                    w2_ref[pl.ds(half * nk, nk), pl.ds(lane, nz)] = (
                        weight2 * f2.astype(jnp.float32)
                    ).astype(jnp.bfloat16)
                for at, cls in enumerate(classes):
                    f0 = p0[row0, c, pl.ds(cls, chunk), :]
                    f1 = p1[pl.ds(src + cls, chunk), :]
                    gy = inside * p2[pl.ds(src + cls, chunk), :] - f0
                    for j in range(JB):
                        block = pl.ds(((2 * at + half) * JB + j) * chunk, chunk)
                        adv[block, pl.ds(lane, nz)] = phi1[j : j + 1] * gy
                        adv[block, pl.ds(span + lane, nz)] = phi2[j : j + 1] * f1
    total = dot_nt(adv[:, pl.ds(0, span)], w1_ref[...])
    total = total + dot_nt(adv[:, pl.ds(span, span)], w2_ref[...])
    for at, cls in enumerate(classes):
        for half in range(2):
            level = m if half == 0 else 1 - m
            for j in range(JB):
                first = ((2 * at + half) * JB + j) * chunk
                piece = total[first : first + chunk] + acc_ref[pl.ds((2 * j + half) * nk + cls, chunk), :]
                keep_ref[at, level, j] = piece[:, :nk]
                send_ref[at, level, j] = piece[:, nk:].astype(jnp.bfloat16)


def near_kernel(keep_ref, got_ref, *out_refs):
    for at, ref in enumerate(out_refs):
        ref[...] = (keep_ref[at] + got_ref[at].astype(jnp.float32)).astype(ref.dtype)


def far_kernel(mine_ref, *refs):
    *parts, keep_ref, send_ref = refs
    level = lax.div(lax.axis_index("space"), NEAR)
    for ref, at in ((keep_ref, level), (send_ref, 1 - level)):
        total = mine_ref[at]
        for part in parts:
            total = total + part[at].astype(jnp.float32)
        ref[...] = total.astype(ref.dtype)


def total_kernel(keep_ref, got_ref, out_ref):
    total = keep_ref[...] + got_ref[...].astype(jnp.float32)
    for j in range(JB):
        out_ref[:, j, :] = total[j]


def on_device(n, modes, weight_ids, weight_table, j_block):
    nk, comps, _, nx, nz = modes.shape
    bf16, f32 = jnp.bfloat16, jnp.float32
    vmem = pl.BlockSpec(memory_space=pltpu.VMEM)
    smem = pl.BlockSpec(memory_space=pltpu.SMEM)
    params = pltpu.CompilerParams(vmem_limit_bytes=VMEM_LIMIT)
    six = nx // 2 + 2
    body = nx // 4 * comps * nk
    own, to_core, zs, xs, zc, xc = pl.pallas_call(
        prep_kernel,
        out_shape=[jax.ShapeDtypeStruct((six, comps, nk, nz), bf16)] * 2
        + [jax.ShapeDtypeStruct((body + PADROWS, nz), bf16)] * 2
        + [jax.ShapeDtypeStruct((body, nz), bf16)] * 2,
        in_specs=[pl.BlockSpec(memory_space=pltpu.HBM)],
        out_specs=[vmem] * 6,
        scratch_shapes=[
            pltpu.VMEM(modes.shape, bf16),
            pltpu.VMEM((nx, comps, nk, nz), bf16),
            pltpu.SemaphoreType.DMA((LOADS,)),
        ],
        compiler_params=pltpu.CompilerParams(vmem_limit_bytes=PREP_LIMIT),
        name="prep",
    )(modes)

    both = ("space", "modes")
    x_pairs = [(s, s ^ 1) for s in range(n)]
    z_pairs = [(s, (s + (2 if s % 2 else -2)) % n) for s in range(n)]
    same = lambda pairs: [(2 * a + m, 2 * b + m) for a, b in pairs for m in range(2)]
    cross = lambda pairs: [(2 * a + m, 2 * b + 1 - m) for a, b in pairs for m in range(2)]
    other = lax.ppermute(to_core, "modes", [(0, 1), (1, 0)])
    zs = lax.ppermute(zs, both, same(z_pairs))
    xs = lax.ppermute(xs, both, same(x_pairs))
    zc, xc = pl.pallas_call(
        ids_kernel,
        out_shape=[jax.ShapeDtypeStruct((body + IDROWS, nz), bf16)] * 2,
        in_specs=[vmem] * 3 + [pl.BlockSpec(memory_space=pl.ANY)],
        out_specs=[vmem] * 2,
        compiler_params=params,
        name="ids",
    )(weight_ids, zc, xc, other)
    xc = lax.ppermute(xc, both, cross(x_pairs))
    zc = lax.ppermute(zc, both, cross(z_pairs))

    def estimate(depth, size):
        return pl.CostEstimate(
            flops=2 * JB * (2 * nk) ** 2 * depth, bytes_accessed=size, transcendentals=0
        )

    depth = nx // 4 * comps * nz
    acc = pl.pallas_call(
        local_kernel,
        out_shape=jax.ShapeDtypeStruct((JB * 2 * nk, 2 * nk), f32),
        in_specs=[vmem, vmem, vmem, smem, smem],
        out_specs=vmem,
        scratch_shapes=[
            pltpu.VMEM((JB * 2 * nk, 2 * depth), bf16),
            pltpu.VMEM((2 * nk, 2 * depth), bf16),
            pltpu.VMEM((nx, nz), f32),
        ],
        compiler_params=params,
        cost_estimate=estimate(2 * depth, 2_400_000),
        name="local",
    )(own, other, weight_ids, weight_table, j_block)
    acc, w1 = pl.pallas_call(
        early_kernel,
        out_shape=[
            jax.ShapeDtypeStruct((JB * 2 * nk, 2 * nk), f32),
            jax.ShapeDtypeStruct((2 * nk, depth), bf16),
        ],
        in_specs=[vmem, vmem, pl.BlockSpec(memory_space=pl.ANY)] + [vmem] * 3 + [smem, smem, vmem],
        out_specs=[vmem] * 2,
        scratch_shapes=[
            pltpu.VMEM((JB * 2 * nk, depth), bf16),
            pltpu.VMEM((2 * nk, depth), bf16),
            pltpu.VMEM((nx, nz), f32),
        ],
        compiler_params=params,
        cost_estimate=estimate(depth, 2_400_000),
        name="early",
    )(own, other, zs, xs, xc, weight_ids, weight_table, j_block, acc)

    per_target = 2 * nk // n
    chunk = max(16, per_target)

    def crossed(count, classes_of, w2):
        piece = (count, 2, JB, chunk, nk)
        out_shape = [jax.ShapeDtypeStruct(piece, f32), jax.ShapeDtypeStruct(piece, bf16)]
        if not w2:
            out_shape.append(jax.ShapeDtypeStruct((2 * nk, depth), bf16))
        return pl.pallas_call(
            functools.partial(cross_kernel, classes_of, chunk, n, bool(w2)),
            out_shape=out_shape,
            in_specs=[vmem] * 7 + [smem, smem] + [vmem] * (1 + len(w2)),
            out_specs=[vmem] * len(out_shape),
            scratch_shapes=[pltpu.VMEM((count * 2 * JB * chunk, 2 * depth), bf16)],
            compiler_params=params,
            cost_estimate=estimate(depth, 4_000_000),
            name="cross",
        )(own, other, zs, xs, zc, xc, w1, weight_table, j_block, acc, *w2)

    swap = [(0, 1), (1, 0)]
    if n == 2 * NEAR:
        def partners(*steps):
            return lambda s: [jnp.bitwise_xor(lax.rem(s, NEAR), step) for step in steps]

        keep_a, send_a, w2 = crossed(2, partners(3, 1), ())
        got_a = lax.ppermute(send_a, "modes", swap)
        keep_b, send_b = crossed(2, partners(0, 2), (w2,))
        got_b = lax.ppermute(send_b, "modes", swap)
        piece = (JB, chunk, nk)

        def summed(kinds, keep, got):
            return pl.pallas_call(
                near_kernel,
                out_shape=[jax.ShapeDtypeStruct((2, *piece), kind) for kind in kinds],
                in_specs=[vmem] * 2,
                out_specs=[vmem] * 2,
                compiler_params=params,
                name="near",
            )(keep, got)

        part_3, part_1 = summed((bf16, bf16), keep_a, got_a)
        mine, part_2 = summed((f32, bf16), keep_b, got_b)
        parts = [
            lax.ppermute(part, "space", [(s, s ^ step) for s in range(n)])
            for part, step in ((part_3, 3), (part_1, 1), (part_2, 2))
        ]
        keep, send = pl.pallas_call(
            far_kernel,
            out_shape=[jax.ShapeDtypeStruct(piece, f32), jax.ShapeDtypeStruct(piece, bf16)],
            in_specs=[vmem] * NEAR,
            out_specs=[vmem] * 2,
            compiler_params=params,
            name="far",
        )(mine, *parts)
        got = lax.ppermute(send, "space", [(s, s ^ NEAR) for s in range(n)])
        return pl.pallas_call(
            total_kernel,
            out_shape=jax.ShapeDtypeStruct((chunk, JB, nk), f32),
            in_specs=[vmem] * 2,
            out_specs=vmem,
            compiler_params=params,
            name="total",
        )(keep, got)

    count = nk // chunk
    keep, send, _ = crossed(count, lambda s: list(range(count)), ())
    share = (keep + lax.ppermute(send, "modes", swap)).astype(bf16)
    share = share.reshape(count, 2, JB, chunk // per_target, per_target, nk)
    share = share.transpose(1, 0, 3, 2, 4, 5).reshape(n, JB, per_target, nk)
    parts = lax.all_to_all(share, "space", 0, 0, tiled=True)
    return jnp.sum(parts.astype(f32), axis=0).transpose(1, 0, 2)


def solution(mesh):
    return jax.shard_map(
        functools.partial(on_device, mesh.shape["space"]),
        mesh=mesh,
        in_specs=(
            P("modes", None, ("groups", "space"), None, None),
            P(("groups", "space"), None, None),
            P(),
            P("groups"),
        ),
        out_specs=P(("groups", "space"), None, "modes"),
        check_vma=False,
    )
```

```python
import functools

import jax
import jax.numpy as jnp
from jax import lax
from jax.experimental import pallas as pl
from jax.experimental.pallas import tpu as pltpu
from jax.sharding import PartitionSpec as P

JB = 4
NW = 16
IDROWS = 16
PADROWS = 16
LOADS = 4
NEAR = 4
VMEM_LIMIT = 48 * 1024 * 1024
PREP_LIMIT = 53_100 * 1024


def prep_kernel(modes_hbm, own_ref, core_ref, zs_ref, xs_ref, zc_ref, xc_ref, modes_ref, tr, sems):
    m = lax.axis_index("modes")
    q = lax.rem(lax.axis_index("space"), 2)
    nk, comps, _, nx, nz = modes_hbm.shape
    step = nk // LOADS
    copies = [
        pltpu.make_async_copy(
            modes_hbm.at[pl.ds(p * step, step)], modes_ref.at[pl.ds(p * step, step)], sems.at[p]
        )
        for p in range(LOADS)
    ]
    for copy in copies:
        copy.start()
    for p in range(LOADS):
        copies[p].wait()
        block = pl.ds(p * step, step)
        for c in range(comps):
            value = modes_ref[block, c, 0].astype(jnp.float32)
            tr[:, c, block] = jnp.swapaxes(value, 0, 1).astype(jnp.bfloat16)
    quarter = nx // 4
    for r in range(nx // 2 + 2):
        own_ref[r] = tr[lax.rem(nx // 2 * m + nx - 1 + r, nx)]
        core_ref[r] = tr[lax.rem(nx // 2 * (1 - m) + nx - 1 + r, nx)]
    for ref, at in (
        (xs_ref, 2 * m + 1 - q),
        (xc_ref, 2 * (1 - m) + 1 - q),
        (zs_ref, 2 * m + q),
        (zc_ref, 2 * (1 - m) + q),
    ):
        for row in range(quarter):
            for c in range(comps):
                ref[pl.ds((row * comps + c) * nk, nk), :] = tr[at * quarter + row, c]
    for ref in (zs_ref, xs_ref):
        pad = ref.shape[0] - quarter * comps * nk
        ref[pl.ds(quarter * comps * nk, pad), :] = jnp.zeros((pad, nz), jnp.bfloat16)


def ids_kernel(ids_ref, zc_ref, xc_ref, _, zc_out, xc_out):
    m = lax.axis_index("modes")
    q = lax.rem(lax.axis_index("space"), 2)
    body, nz = xc_ref.shape
    quarter = ids_ref.shape[1] // 4
    for ref, out, at in ((zc_ref, zc_out, 2 * (1 - m) + q), (xc_ref, xc_out, 2 * (1 - m) + 1 - q)):
        out[pl.ds(0, body), :] = ref[...]
        ids = [
            jnp.broadcast_to(ids_ref[0, pl.ds(at * quarter + row, 1), :], (IDROWS // quarter, nz))
            for row in range(quarter)
        ]
        out[pl.ds(body, IDROWS), :] = (
            jnp.concatenate(ids, axis=0).astype(jnp.float32).astype(jnp.bfloat16)
        )


def picks(jb_ref, m, nk):
    first = jb_ref[0] * JB
    owner = (first >= nk).astype(jnp.int32)
    row = first - owner * nk
    within = lax.rem(row, 16)
    return owner == m, pl.multiple_of(row - within, 16), within


def picked(pick, own, other):
    mine, block, within = pick
    rows = jnp.where(
        mine, own[pl.ds(block, 16), :].astype(jnp.float32), other[pl.ds(block, 16), :].astype(jnp.float32)
    )
    result = rows[0:JB]
    for start in range(JB, 16, JB):
        result = jnp.where(within == start, rows[start : start + JB], result)
    return result


def spread(row):
    return jnp.broadcast_to(row, (16, row.shape[1])).astype(jnp.bfloat16)[None]


def scaled(tile, field):
    rows, lanes = field.shape
    return (tile * field.reshape(rows // 16, 16, lanes)).reshape(rows, lanes)


def weights_of(ids, table_ref):
    weight = jnp.zeros(ids.shape, jnp.float32)
    for entry in range(NW):
        weight = jnp.where(ids == entry, table_ref[entry], weight)
    return weight


def dot_nt(a, b):
    return lax.dot_general(a, b, (((1,), (1,)), ((), ())), preferred_element_type=jnp.float32)


def local_kernel(own_ref, other_ref, ids_ref, table_ref, jb_ref, acc_ref, adv, wts, wscr):
    m = lax.axis_index("modes")
    rows, comps, nk, nz = own_ref.shape
    rows -= 2
    pick = picks(jb_ref, m, nk)
    wscr[...] = weights_of(ids_ref[0], table_ref)
    for r in range(rows):
        phi = [picked(pick, own_ref.at[r + 1, d], other_ref.at[r + 1, d]) for d in range(comps)]
        weight = wscr[pl.ds(rows * m + r, 1), :]
        for c in range(comps):
            at = pl.ds((r * comps + c) * nz, nz)
            for half, ref in enumerate((own_ref, other_ref)):
                block = pl.ds(half * nk, nk)
                here = ref[r + 1, c].astype(jnp.float32)
                gx = 0.5 * (ref[r + 2, c].astype(jnp.float32) - ref[r, c].astype(jnp.float32))
                gz = 0.5 * (pltpu.roll(here, nz - 1, 1) - pltpu.roll(here, 1, 1))
                gx = gx.astype(jnp.bfloat16).astype(jnp.float32)
                gz = gz.astype(jnp.bfloat16).astype(jnp.float32)
                wts[block, at] = (weight * here).astype(jnp.bfloat16)
                for j in range(JB):
                    total = phi[0][j : j + 1] * gx + phi[2][j : j + 1] * gz
                    adv[pl.ds((2 * j + half) * nk, nk), at] = total.astype(jnp.bfloat16)
    acc_ref[...] = dot_nt(adv[...], wts[...])


def sign_of_plane():
    return jnp.where(lax.rem(lax.axis_index("space"), 2) == 0, 0.5, -0.5)


def early_kernel(
    own_ref, other_ref, _, xs_ref, xc_ref, ids_ref, table_ref, jb_ref, acc_ref, out_ref, w1_ref, adv, wts, wscr
):
    m = lax.axis_index("modes")
    q = lax.rem(lax.axis_index("space"), 2)
    rows, comps, nk, nz = own_ref.shape
    rows -= 2
    quarter = rows // 2
    pick = picks(jb_ref, m, nk)
    wscr[...] = weights_of(ids_ref[0], table_ref)
    w1 = weights_of(xc_ref[pl.ds(quarter * comps * nk, IDROWS), :].astype(jnp.float32), table_ref)
    for r in range(quarter):
        row0 = 1 + quarter * q + r
        weight0 = wscr[pl.ds(rows * m + quarter * q + r, 1), :]
        weight1 = w1[IDROWS // quarter * r : IDROWS // quarter * r + 1]
        phi0 = sign_of_plane() * picked(pick, own_ref.at[row0, 1], other_ref.at[row0, 1])
        phi0 = [spread(phi0[j : j + 1]) for j in range(JB)]
        for c in range(comps):
            at = pl.ds((r * comps + c) * nz, nz)
            src = pl.ds((r * comps + c) * nk, nk)
            for half, (p0, p1) in enumerate(((own_ref, xs_ref), (other_ref, xc_ref))):
                block = pl.ds(half * nk, nk)
                f0, f1 = p0[row0, c], p1[src, :]
                wts[block, at] = (weight0 * f0.astype(jnp.float32)).astype(jnp.bfloat16)
                w1_ref[block, at] = (weight1 * f1.astype(jnp.float32)).astype(jnp.bfloat16)
                for j in range(JB):
                    adv[pl.ds((2 * j + half) * nk, nk), at] = scaled(phi0[j], f1)
    out_ref[...] = acc_ref[...] + dot_nt(adv[...], wts[...])


def cross_kernel(classes_of, chunk, planes, has_w2, own_ref, other_ref, *refs):
    zs_ref, xs_ref, zc_ref, xc_ref, w1_ref, table_ref, jb_ref, acc_ref, *refs = refs
    if has_w2:
        w2_ref, keep_ref, send_ref, adv = refs
    else:
        keep_ref, send_ref, w2_ref, adv = refs
    m = lax.axis_index("modes")
    plane = lax.axis_index("space")
    q = lax.rem(plane, 2)
    inside = jnp.where(jnp.logical_or(plane == 1, plane == planes - 2), 0.0, 1.0)
    inside = inside.astype(jnp.bfloat16)
    rows, comps, nk, nz = own_ref.shape
    quarter = (rows - 2) // 2
    span = quarter * comps * nz
    pick = picks(jb_ref, m, nk)
    classes = [pl.multiple_of(chunk * cls, chunk) for cls in classes_of(plane)]
    w2 = weights_of(zc_ref[pl.ds(quarter * comps * nk, IDROWS), :].astype(jnp.float32), table_ref)
    for r in range(quarter):
        row0 = 1 + quarter * q + r
        along = pl.ds((r * comps + 1) * nk, nk)
        phi1 = sign_of_plane() * picked(pick, xs_ref.at[along], xc_ref.at[along])
        phi2 = -sign_of_plane() * picked(pick, zs_ref.at[along], zc_ref.at[along])
        phi1 = [spread(phi1[j : j + 1]) for j in range(JB)]
        phi2 = [spread(phi2[j : j + 1]) for j in range(JB)]
        weight2 = w2[IDROWS // quarter * r : IDROWS // quarter * r + 1]
        for c in range(comps):
            lane = (r * comps + c) * nz
            src = (r * comps + c) * nk
            for half, (p0, p1, p2) in enumerate(
                ((own_ref, xs_ref, zs_ref), (other_ref, xc_ref, zc_ref))
            ):
                if not has_w2:
                    f2 = inside * p2[pl.ds(src, nk), :]
                    w2_ref[pl.ds(half * nk, nk), pl.ds(lane, nz)] = (
                        weight2 * f2.astype(jnp.float32)
                    ).astype(jnp.bfloat16)
                for at, cls in enumerate(classes):
                    f0 = p0[row0, c, pl.ds(cls, chunk), :]
                    f1 = p1[pl.ds(src + cls, chunk), :]
                    gy = inside * p2[pl.ds(src + cls, chunk), :] - f0
                    for j in range(JB):
                        block = pl.ds(((2 * at + half) * JB + j) * chunk, chunk)
                        adv[block, pl.ds(lane, nz)] = scaled(phi1[j], gy)
                        adv[block, pl.ds(span + lane, nz)] = scaled(phi2[j], f1)
    total = dot_nt(adv[:, pl.ds(0, span)], w1_ref[...])
    total = total + dot_nt(adv[:, pl.ds(span, span)], w2_ref[...])
    for at, cls in enumerate(classes):
        for half in range(2):
            level = m if half == 0 else 1 - m
            for j in range(JB):
                first = ((2 * at + half) * JB + j) * chunk
                piece = total[first : first + chunk] + acc_ref[pl.ds((2 * j + half) * nk + cls, chunk), :]
                keep_ref[at, level, j] = piece[:, :nk]
                send_ref[at, level, j] = piece[:, nk:].astype(jnp.bfloat16)


def near_kernel(keep_ref, got_ref, *out_refs):
    for at, ref in enumerate(out_refs):
        ref[...] = (keep_ref[at] + got_ref[at].astype(jnp.float32)).astype(ref.dtype)


def far_kernel(mine_ref, *refs):
    *parts, keep_ref, send_ref = refs
    level = lax.div(lax.axis_index("space"), NEAR)
    for ref, at in ((keep_ref, level), (send_ref, 1 - level)):
        total = mine_ref[at]
        for part in parts:
            total = total + part[at].astype(jnp.float32)
        ref[...] = total.astype(ref.dtype)


def total_kernel(keep_ref, got_ref, out_ref):
    total = keep_ref[...] + got_ref[...].astype(jnp.float32)
    for j in range(JB):
        out_ref[:, j, :] = total[j]


def on_device(n, modes, weight_ids, weight_table, j_block):
    nk, comps, _, nx, nz = modes.shape
    bf16, f32 = jnp.bfloat16, jnp.float32
    vmem = pl.BlockSpec(memory_space=pltpu.VMEM)
    smem = pl.BlockSpec(memory_space=pltpu.SMEM)
    params = pltpu.CompilerParams(vmem_limit_bytes=VMEM_LIMIT)
    six = nx // 2 + 2
    body = nx // 4 * comps * nk
    own, to_core, zs, xs, zc, xc = pl.pallas_call(
        prep_kernel,
        out_shape=[jax.ShapeDtypeStruct((six, comps, nk, nz), bf16)] * 2
        + [jax.ShapeDtypeStruct((body + PADROWS, nz), bf16)] * 2
        + [jax.ShapeDtypeStruct((body, nz), bf16)] * 2,
        in_specs=[pl.BlockSpec(memory_space=pltpu.HBM)],
        out_specs=[vmem] * 6,
        scratch_shapes=[
            pltpu.VMEM(modes.shape, bf16),
            pltpu.VMEM((nx, comps, nk, nz), bf16),
            pltpu.SemaphoreType.DMA((LOADS,)),
        ],
        compiler_params=pltpu.CompilerParams(vmem_limit_bytes=PREP_LIMIT),
        name="prep",
    )(modes)

    both = ("space", "modes")
    x_pairs = [(s, s ^ 1) for s in range(n)]
    z_pairs = [(s, (s + (2 if s % 2 else -2)) % n) for s in range(n)]
    same = lambda pairs: [(2 * a + m, 2 * b + m) for a, b in pairs for m in range(2)]
    cross = lambda pairs: [(2 * a + m, 2 * b + 1 - m) for a, b in pairs for m in range(2)]
    other = lax.ppermute(to_core, "modes", [(0, 1), (1, 0)])
    zs = lax.ppermute(zs, both, same(z_pairs))
    xs = lax.ppermute(xs, both, same(x_pairs))
    zc, xc = pl.pallas_call(
        ids_kernel,
        out_shape=[jax.ShapeDtypeStruct((body + IDROWS, nz), bf16)] * 2,
        in_specs=[vmem] * 3 + [pl.BlockSpec(memory_space=pl.ANY)],
        out_specs=[vmem] * 2,
        compiler_params=params,
        name="ids",
    )(weight_ids, zc, xc, other)
    xc = lax.ppermute(xc, both, cross(x_pairs))
    zc = lax.ppermute(zc, both, cross(z_pairs))

    def estimate(depth, size):
        return pl.CostEstimate(
            flops=2 * JB * (2 * nk) ** 2 * depth, bytes_accessed=size, transcendentals=0
        )

    depth = nx // 4 * comps * nz
    acc = pl.pallas_call(
        local_kernel,
        out_shape=jax.ShapeDtypeStruct((JB * 2 * nk, 2 * nk), f32),
        in_specs=[vmem, vmem, vmem, smem, smem],
        out_specs=vmem,
        scratch_shapes=[
            pltpu.VMEM((JB * 2 * nk, 2 * depth), bf16),
            pltpu.VMEM((2 * nk, 2 * depth), bf16),
            pltpu.VMEM((nx, nz), f32),
        ],
        compiler_params=params,
        cost_estimate=estimate(2 * depth, 2_400_000),
        name="local",
    )(own, other, weight_ids, weight_table, j_block)
    acc, w1 = pl.pallas_call(
        early_kernel,
        out_shape=[
            jax.ShapeDtypeStruct((JB * 2 * nk, 2 * nk), f32),
            jax.ShapeDtypeStruct((2 * nk, depth), bf16),
        ],
        in_specs=[vmem, vmem, pl.BlockSpec(memory_space=pl.ANY)] + [vmem] * 3 + [smem, smem, vmem],
        out_specs=[vmem] * 2,
        scratch_shapes=[
            pltpu.VMEM((JB * 2 * nk, depth), bf16),
            pltpu.VMEM((2 * nk, depth), bf16),
            pltpu.VMEM((nx, nz), f32),
        ],
        compiler_params=params,
        cost_estimate=estimate(depth, 2_400_000),
        name="early",
    )(own, other, zs, xs, xc, weight_ids, weight_table, j_block, acc)

    per_target = 2 * nk // n
    chunk = max(16, per_target)

    def crossed(count, classes_of, w2):
        piece = (count, 2, JB, chunk, nk)
        out_shape = [jax.ShapeDtypeStruct(piece, f32), jax.ShapeDtypeStruct(piece, bf16)]
        if not w2:
            out_shape.append(jax.ShapeDtypeStruct((2 * nk, depth), bf16))
        return pl.pallas_call(
            functools.partial(cross_kernel, classes_of, chunk, n, bool(w2)),
            out_shape=out_shape,
            in_specs=[vmem] * 7 + [smem, smem] + [vmem] * (1 + len(w2)),
            out_specs=[vmem] * len(out_shape),
            scratch_shapes=[pltpu.VMEM((count * 2 * JB * chunk, 2 * depth), bf16)],
            compiler_params=params,
            cost_estimate=estimate(depth, 4_000_000),
            name="cross",
        )(own, other, zs, xs, zc, xc, w1, weight_table, j_block, acc, *w2)

    swap = [(0, 1), (1, 0)]
    if n == 2 * NEAR:
        def partners(*steps):
            return lambda s: [jnp.bitwise_xor(lax.rem(s, NEAR), step) for step in steps]

        keep_a, send_a, w2 = crossed(2, partners(3, 1), ())
        got_a = lax.ppermute(send_a, "modes", swap)
        keep_b, send_b = crossed(2, partners(0, 2), (w2,))
        got_b = lax.ppermute(send_b, "modes", swap)
        piece = (JB, chunk, nk)

        def summed(kinds, keep, got):
            return pl.pallas_call(
                near_kernel,
                out_shape=[jax.ShapeDtypeStruct((2, *piece), kind) for kind in kinds],
                in_specs=[vmem] * 2,
                out_specs=[vmem] * 2,
                compiler_params=params,
                name="near",
            )(keep, got)

        part_3, part_1 = summed((bf16, bf16), keep_a, got_a)
        mine, part_2 = summed((f32, bf16), keep_b, got_b)
        parts = [
            lax.ppermute(part, "space", [(s, s ^ step) for s in range(n)])
            for part, step in ((part_3, 3), (part_1, 1), (part_2, 2))
        ]
        keep, send = pl.pallas_call(
            far_kernel,
            out_shape=[jax.ShapeDtypeStruct(piece, f32), jax.ShapeDtypeStruct(piece, bf16)],
            in_specs=[vmem] * NEAR,
            out_specs=[vmem] * 2,
            compiler_params=params,
            name="far",
        )(mine, *parts)
        got = lax.ppermute(send, "space", [(s, s ^ NEAR) for s in range(n)])
        return pl.pallas_call(
            total_kernel,
            out_shape=jax.ShapeDtypeStruct((chunk, JB, nk), f32),
            in_specs=[vmem] * 2,
            out_specs=vmem,
            compiler_params=params,
            name="total",
        )(keep, got)

    count = nk // chunk
    keep, send, _ = crossed(count, lambda s: list(range(count)), ())
    share = (keep + lax.ppermute(send, "modes", swap)).astype(bf16)
    share = share.reshape(count, 2, JB, chunk // per_target, per_target, nk)
    share = share.transpose(1, 0, 3, 2, 4, 5).reshape(n, JB, per_target, nk)
    parts = lax.all_to_all(share, "space", 0, 0, tiled=True)
    return jnp.sum(parts.astype(f32), axis=0).transpose(1, 0, 2)


def solution(mesh):
    return jax.shard_map(
        functools.partial(on_device, mesh.shape["space"]),
        mesh=mesh,
        in_specs=(
            P("modes", None, ("groups", "space"), None, None),
            P(("groups", "space"), None, None),
            P(),
            P("groups"),
        ),
        out_specs=P(("groups", "space"), None, "modes"),
        check_vma=False,
    )
```

```python
import functools

import jax
import jax.numpy as jnp
from jax import lax
from jax.experimental import pallas as pl
from jax.experimental.pallas import tpu as pltpu
from jax.sharding import PartitionSpec as P

JB = 4
NW = 16
IDROWS = 16
PADROWS = 16
LOADS = 4
NEAR = 4
VMEM_LIMIT = 48 * 1024 * 1024
PREP_LIMIT = 53_100 * 1024


def prep_kernel(modes_hbm, own_ref, core_ref, zs_ref, xs_ref, zc_ref, xc_ref, modes_ref, tr, sems):
    m = lax.axis_index("modes")
    q = lax.rem(lax.axis_index("space"), 2)
    nk, comps, _, nx, nz = modes_hbm.shape
    step = nk // LOADS
    copies = [
        pltpu.make_async_copy(
            modes_hbm.at[pl.ds(p * step, step)], modes_ref.at[pl.ds(p * step, step)], sems.at[p]
        )
        for p in range(LOADS)
    ]
    for copy in copies:
        copy.start()
    for p in range(LOADS):
        copies[p].wait()
        block = pl.ds(p * step, step)
        for c in range(comps):
            value = modes_ref[block, c, 0].astype(jnp.float32)
            tr[:, c, block] = jnp.swapaxes(value, 0, 1).astype(jnp.bfloat16)
    quarter = nx // 4
    for r in range(nx // 2 + 2):
        own_ref[r] = tr[lax.rem(nx // 2 * m + nx - 1 + r, nx)]
        core_ref[r] = tr[lax.rem(nx // 2 * (1 - m) + nx - 1 + r, nx)]
    for ref, at in (
        (xs_ref, 2 * m + 1 - q),
        (xc_ref, 2 * (1 - m) + 1 - q),
        (zs_ref, 2 * m + q),
        (zc_ref, 2 * (1 - m) + q),
    ):
        for row in range(quarter):
            for c in range(comps):
                ref[pl.ds((row * comps + c) * nk, nk), :] = tr[at * quarter + row, c]
    for ref in (zs_ref, xs_ref):
        pad = ref.shape[0] - quarter * comps * nk
        ref[pl.ds(quarter * comps * nk, pad), :] = jnp.zeros((pad, nz), jnp.bfloat16)


def weights_of(ids, table_ref):
    weight = jnp.zeros(ids.shape, jnp.float32)
    for entry in range(NW):
        weight = jnp.where(ids == entry, table_ref[entry], weight)
    return weight


def ids_kernel(ids_ref, table_ref, zc_ref, xc_ref, _, weight_out, zc_out, xc_out):
    m = lax.axis_index("modes")
    q = lax.rem(lax.axis_index("space"), 2)
    body, nz = xc_ref.shape
    quarter = ids_ref.shape[1] // 4
    weight_out[...] = weights_of(ids_ref[0], table_ref)
    for ref, out, at in ((zc_ref, zc_out, 2 * (1 - m) + q), (xc_ref, xc_out, 2 * (1 - m) + 1 - q)):
        out[pl.ds(0, body), :] = ref[...]
        ids = [
            jnp.broadcast_to(ids_ref[0, pl.ds(at * quarter + row, 1), :], (IDROWS // quarter, nz))
            for row in range(quarter)
        ]
        out[pl.ds(body, IDROWS), :] = (
            jnp.concatenate(ids, axis=0).astype(jnp.float32).astype(jnp.bfloat16)
        )


def picks(jb_ref, m, nk):
    first = jb_ref[0] * JB
    owner = (first >= nk).astype(jnp.int32)
    row = first - owner * nk
    within = lax.rem(row, 16)
    return owner == m, pl.multiple_of(row - within, 16), within


def picked(pick, own, other):
    mine, block, within = pick
    rows = jnp.where(
        mine, own[pl.ds(block, 16), :].astype(jnp.float32), other[pl.ds(block, 16), :].astype(jnp.float32)
    )
    result = rows[0:JB]
    for start in range(JB, 16, JB):
        result = jnp.where(within == start, rows[start : start + JB], result)
    return result


def spread(row):
    return jnp.broadcast_to(row, (16, row.shape[1])).astype(jnp.bfloat16)[None]


def scaled(tile, field):
    rows, lanes = field.shape
    return (tile * field.reshape(rows // 16, 16, lanes)).reshape(rows, lanes)


def dot_nt(a, b):
    return lax.dot_general(a, b, (((1,), (1,)), ((), ())), preferred_element_type=jnp.float32)


def local_kernel(own_ref, other_ref, weight_ref, jb_ref, acc_ref, w0_ref, adv, wts):
    m = lax.axis_index("modes")
    q = lax.rem(lax.axis_index("space"), 2)
    rows, comps, nk, nz = own_ref.shape
    rows -= 2
    pick = picks(jb_ref, m, nk)
    for r in range(rows):
        phi = [picked(pick, own_ref.at[r + 1, d], other_ref.at[r + 1, d]) for d in range(comps)]
        weight = weight_ref[pl.ds(rows * m + r, 1), :]
        for c in range(comps):
            for half, ref in enumerate((own_ref, other_ref)):
                block = pl.ds(half * nk, nk)
                here = ref[r + 1, c].astype(jnp.float32)
                gx = 0.5 * (ref[r + 2, c].astype(jnp.float32) - ref[r, c].astype(jnp.float32))
                gz = 0.5 * (pltpu.roll(here, nz - 1, 1) - pltpu.roll(here, 1, 1))
                gx = gx.astype(jnp.bfloat16).astype(jnp.float32)
                gz = gz.astype(jnp.bfloat16).astype(jnp.float32)
                wts[r, block, pl.ds(c * nz, nz)] = (weight * here).astype(jnp.bfloat16)
                for j in range(JB):
                    total = phi[0][j : j + 1] * gx + phi[2][j : j + 1] * gz
                    adv[r, pl.ds((2 * j + half) * nk, nk), pl.ds(c * nz, nz)] = total.astype(jnp.bfloat16)
    total = dot_nt(adv[0], wts[0])
    for r in range(1, rows):
        total = total + dot_nt(adv[r], wts[r])
    acc_ref[...] = total
    quarter = rows // 2
    for r in range(quarter):
        w0_ref[r] = wts[quarter * q + r]


def cross_kernel(classes_of, chunk, planes, has_weighted, own_ref, other_ref, *refs):
    zs_ref, xs_ref, zc_ref, xc_ref, w0_ref, table_ref, jb_ref, acc_ref, *refs = refs
    if has_weighted:
        wts, keep_ref, send_ref, adv = refs
    else:
        keep_ref, send_ref, wts, adv = refs
    m = lax.axis_index("modes")
    plane = lax.axis_index("space")
    q = lax.rem(plane, 2)
    sigma = jnp.where(q == 0, 0.5, -0.5)
    inside = jnp.where(jnp.logical_or(plane == 1, plane == planes - 2), 0.0, 1.0)
    rows, comps, nk, nz = own_ref.shape
    quarter = (rows - 2) // 2
    span = quarter * comps * nz
    pick = picks(jb_ref, m, nk)
    classes = [pl.multiple_of(chunk * cls, chunk) for cls in classes_of(plane)]
    if not has_weighted:
        ids = pl.ds(quarter * comps * nk, IDROWS)
        w1 = weights_of(xc_ref[ids, :].astype(jnp.float32), table_ref)
        w2 = inside * weights_of(zc_ref[ids, :].astype(jnp.float32), table_ref)
        for r in range(quarter):
            wts[:, pl.ds(r * comps * nz, comps * nz)] = w0_ref[r]
            row = IDROWS // quarter * r
            for c in range(comps):
                lane = (r * comps + c) * nz
                src = pl.ds((r * comps + c) * nk, nk)
                for half, (p1, p2) in enumerate(((xs_ref, zs_ref), (xc_ref, zc_ref))):
                    block = pl.ds(half * nk, nk)
                    for part, (field, weight) in enumerate(((p1, w1), (p2, w2)), 1):
                        wts[block, pl.ds(part * span + lane, nz)] = (
                            weight[row : row + 1] * field[src, :].astype(jnp.float32)
                        ).astype(jnp.bfloat16)
    phis = []
    for r in range(quarter):
        row0 = 1 + quarter * q + r
        along = pl.ds((r * comps + 1) * nk, nk)
        phi0 = sigma * picked(pick, own_ref.at[row0, 1], other_ref.at[row0, 1])
        phi1 = sigma * picked(pick, xs_ref.at[along], xc_ref.at[along])
        phi2 = -sigma * picked(pick, zs_ref.at[along], zc_ref.at[along])
        phis.append([[spread(phi[j : j + 1]) for j in range(JB)] for phi in (phi0, phi1, phi2)])
    inside = inside.astype(jnp.bfloat16)
    for at, cls in enumerate(classes):
        for r in range(quarter):
            row0 = 1 + quarter * q + r
            phi0, phi1, phi2 = phis[r]
            for c in range(comps):
                lane = (r * comps + c) * nz
                src = (r * comps + c) * nk
                for half, (p0, p1, p2) in enumerate(
                    ((own_ref, xs_ref, zs_ref), (other_ref, xc_ref, zc_ref))
                ):
                    f0 = p0[row0, c, pl.ds(cls, chunk), :]
                    f1 = p1[pl.ds(src + cls, chunk), :]
                    gy = inside * p2[pl.ds(src + cls, chunk), :] - f0
                    for j in range(JB):
                        here = pl.ds((half * JB + j) * chunk, chunk)
                        adv[at, here, pl.ds(lane, nz)] = scaled(phi0[j], f1)
                        adv[at, here, pl.ds(span + lane, nz)] = scaled(phi1[j], gy)
                        adv[at, here, pl.ds(2 * span + lane, nz)] = scaled(phi2[j], f1)
        total = dot_nt(adv[at], wts[...])
        for half in range(2):
            level = m if half == 0 else 1 - m
            for j in range(JB):
                first = (half * JB + j) * chunk
                piece = total[first : first + chunk] + acc_ref[pl.ds((2 * j + half) * nk + cls, chunk), :]
                keep_ref[at, level, j] = piece[:, :nk]
                send_ref[at, level, j] = piece[:, nk:].astype(jnp.bfloat16)


def near_kernel(keep_ref, got_ref, *out_refs):
    for at, ref in enumerate(out_refs):
        ref[...] = (keep_ref[at] + got_ref[at].astype(jnp.float32)).astype(ref.dtype)


def far_kernel(mine_ref, *refs):
    *parts, keep_ref, send_ref = refs
    level = lax.div(lax.axis_index("space"), NEAR)
    for ref, at in ((keep_ref, level), (send_ref, 1 - level)):
        total = mine_ref[at]
        for part in parts:
            total = total + part[at].astype(jnp.float32)
        ref[...] = total.astype(ref.dtype)


def total_kernel(keep_ref, got_ref, out_ref):
    total = keep_ref[...] + got_ref[...].astype(jnp.float32)
    for j in range(JB):
        out_ref[:, j, :] = total[j]


def on_device(n, modes, weight_ids, weight_table, j_block):
    nk, comps, _, nx, nz = modes.shape
    bf16, f32 = jnp.bfloat16, jnp.float32
    vmem = pl.BlockSpec(memory_space=pltpu.VMEM)
    smem = pl.BlockSpec(memory_space=pltpu.SMEM)
    params = pltpu.CompilerParams(vmem_limit_bytes=VMEM_LIMIT)
    six = nx // 2 + 2
    body = nx // 4 * comps * nk
    own, to_core, zs, xs, zc, xc = pl.pallas_call(
        prep_kernel,
        out_shape=[jax.ShapeDtypeStruct((six, comps, nk, nz), bf16)] * 2
        + [jax.ShapeDtypeStruct((body + PADROWS, nz), bf16)] * 2
        + [jax.ShapeDtypeStruct((body, nz), bf16)] * 2,
        in_specs=[pl.BlockSpec(memory_space=pltpu.HBM)],
        out_specs=[vmem] * 6,
        scratch_shapes=[
            pltpu.VMEM(modes.shape, bf16),
            pltpu.VMEM((nx, comps, nk, nz), bf16),
            pltpu.SemaphoreType.DMA((LOADS,)),
        ],
        compiler_params=pltpu.CompilerParams(vmem_limit_bytes=PREP_LIMIT),
        cost_estimate=pl.CostEstimate(flops=1_500_000_000, bytes_accessed=2_800_000, transcendentals=0),
        name="prep",
    )(modes)

    both = ("space", "modes")
    x_pairs = [(s, s ^ 1) for s in range(n)]
    z_pairs = [(s, (s + (2 if s % 2 else -2)) % n) for s in range(n)]
    same = lambda pairs: [(2 * a + m, 2 * b + m) for a, b in pairs for m in range(2)]
    cross = lambda pairs: [(2 * a + m, 2 * b + 1 - m) for a, b in pairs for m in range(2)]
    other = lax.ppermute(to_core, "modes", [(0, 1), (1, 0)])
    zs = lax.ppermute(zs, both, same(z_pairs))
    xs = lax.ppermute(xs, both, same(x_pairs))
    weight, zc, xc = pl.pallas_call(
        ids_kernel,
        out_shape=[jax.ShapeDtypeStruct((nx, nz), f32)]
        + [jax.ShapeDtypeStruct((body + IDROWS, nz), bf16)] * 2,
        in_specs=[vmem, smem, vmem, vmem, pl.BlockSpec(memory_space=pl.ANY)],
        out_specs=[vmem] * 3,
        compiler_params=params,
        name="ids",
    )(weight_ids, weight_table, zc, xc, other)
    xc = lax.ppermute(xc, both, cross(x_pairs))
    zc = lax.ppermute(zc, both, cross(z_pairs))

    def estimate(depth, size):
        return pl.CostEstimate(
            flops=2 * JB * (2 * nk) ** 2 * depth, bytes_accessed=size, transcendentals=0
        )

    depth = nx // 4 * comps * nz
    quarter = nx // 4
    depth = quarter * comps * nz
    acc, w0 = pl.pallas_call(
        local_kernel,
        out_shape=[
            jax.ShapeDtypeStruct((JB * 2 * nk, 2 * nk), f32),
            jax.ShapeDtypeStruct((quarter, 2 * nk, comps * nz), bf16),
        ],
        in_specs=[vmem, vmem, vmem, smem],
        out_specs=[vmem] * 2,
        scratch_shapes=[
            pltpu.VMEM((2 * quarter, JB * 2 * nk, comps * nz), bf16),
            pltpu.VMEM((2 * quarter, 2 * nk, comps * nz), bf16),
        ],
        compiler_params=params,
        cost_estimate=pl.CostEstimate(flops=900_000_000, bytes_accessed=2_400_000, transcendentals=0),
        name="local",
    )(own, other, weight, j_block)

    per_target = 2 * nk // n
    chunk = max(16, per_target)

    def crossed(count, classes_of, weighted):
        piece = (count, 2, JB, chunk, nk)
        out_shape = [jax.ShapeDtypeStruct(piece, f32), jax.ShapeDtypeStruct(piece, bf16)]
        if not weighted:
            out_shape.append(jax.ShapeDtypeStruct((2 * nk, 3 * depth), bf16))
        return pl.pallas_call(
            functools.partial(cross_kernel, classes_of, chunk, n, bool(weighted)),
            out_shape=out_shape,
            in_specs=[vmem] * 7 + [smem, smem] + [vmem] * (1 + len(weighted)),
            out_specs=[vmem] * len(out_shape),
            scratch_shapes=[pltpu.VMEM((count, 2 * JB * chunk, 3 * depth), bf16)],
            compiler_params=params,
            cost_estimate=pl.CostEstimate(
                flops=900_000_000, bytes_accessed=4_000_000, transcendentals=0
            ),
            name="cross",
        )(own, other, zs, xs, zc, xc, w0, weight_table, j_block, acc, *weighted)

    swap = [(0, 1), (1, 0)]
    if n == 2 * NEAR:
        def partners(*steps):
            return lambda s: [jnp.bitwise_xor(lax.rem(s, NEAR), step) for step in steps]

        keep_a, send_a, w2 = crossed(2, partners(3, 1), ())
        got_a = lax.ppermute(send_a, "modes", swap)
        keep_b, send_b = crossed(2, partners(0, 2), (w2,))
        got_b = lax.ppermute(send_b, "modes", swap)
        piece = (JB, chunk, nk)

        def summed(kinds, keep, got):
            return pl.pallas_call(
                near_kernel,
                out_shape=[jax.ShapeDtypeStruct((2, *piece), kind) for kind in kinds],
                in_specs=[vmem] * 2,
                out_specs=[vmem] * 2,
                compiler_params=params,
                name="near",
            )(keep, got)

        part_3, part_1 = summed((bf16, bf16), keep_a, got_a)
        mine, part_2 = summed((f32, bf16), keep_b, got_b)
        parts = [
            lax.ppermute(part, "space", [(s, s ^ step) for s in range(n)])
            for part, step in ((part_3, 3), (part_1, 1), (part_2, 2))
        ]
        keep, send = pl.pallas_call(
            far_kernel,
            out_shape=[jax.ShapeDtypeStruct(piece, f32), jax.ShapeDtypeStruct(piece, bf16)],
            in_specs=[vmem] * NEAR,
            out_specs=[vmem] * 2,
            compiler_params=params,
            name="far",
        )(mine, *parts)
        got = lax.ppermute(send, "space", [(s, s ^ NEAR) for s in range(n)])
        return pl.pallas_call(
            total_kernel,
            out_shape=jax.ShapeDtypeStruct((chunk, JB, nk), f32),
            in_specs=[vmem] * 2,
            out_specs=vmem,
            compiler_params=params,
            name="total",
        )(keep, got)

    count = nk // chunk
    keep, send, _ = crossed(count, lambda s: list(range(count)), ())
    share = (keep + lax.ppermute(send, "modes", swap)).astype(bf16)
    share = share.reshape(count, 2, JB, chunk // per_target, per_target, nk)
    share = share.transpose(1, 0, 3, 2, 4, 5).reshape(n, JB, per_target, nk)
    parts = lax.all_to_all(share, "space", 0, 0, tiled=True)
    return jnp.sum(parts.astype(f32), axis=0).transpose(1, 0, 2)


def solution(mesh):
    return jax.shard_map(
        functools.partial(on_device, mesh.shape["space"]),
        mesh=mesh,
        in_specs=(
            P("modes", None, ("groups", "space"), None, None),
            P(("groups", "space"), None, None),
            P(),
            P("groups"),
        ),
        out_specs=P(("groups", "space"), None, "modes"),
        check_vma=False,
    )
```

```python
import functools

import jax
import jax.numpy as jnp
from jax import lax
from jax.experimental import pallas as pl
from jax.experimental.pallas import tpu as pltpu
from jax.sharding import PartitionSpec as P

JB = 4
NW = 16
PADROWS = 16
LOADS = 4
NEAR = 4
VMEM_LIMIT = 48 * 1024 * 1024
PREP_LIMIT = 53_100 * 1024


def prep_kernel(modes_hbm, own_ref, core_ref, zs_ref, xs_ref, zc_ref, xc_ref, modes_ref, tr, sems):
    m = lax.axis_index("modes")
    q = lax.rem(lax.axis_index("space"), 2)
    nk, comps, _, nx, nz = modes_hbm.shape
    step = nk // LOADS
    copies = [
        pltpu.make_async_copy(
            modes_hbm.at[pl.ds(p * step, step)], modes_ref.at[pl.ds(p * step, step)], sems.at[p]
        )
        for p in range(LOADS)
    ]
    for copy in copies:
        copy.start()
    for p in range(LOADS):
        copies[p].wait()
        block = pl.ds(p * step, step)
        for c in range(comps):
            value = modes_ref[block, c, 0].astype(jnp.float32)
            tr[:, c, block] = jnp.swapaxes(value, 0, 1).astype(jnp.bfloat16)
    quarter = nx // 4
    for r in range(nx // 2 + 2):
        own_ref[r] = tr[lax.rem(nx // 2 * m + nx - 1 + r, nx)]
        core_ref[r] = tr[lax.rem(nx // 2 * (1 - m) + nx - 1 + r, nx)]
    for ref, at in (
        (xs_ref, 2 * m + 1 - q),
        (xc_ref, 2 * (1 - m) + 1 - q),
        (zs_ref, 2 * m + q),
        (zc_ref, 2 * (1 - m) + q),
    ):
        for row in range(quarter):
            for c in range(comps):
                ref[pl.ds((row * comps + c) * nk, nk), :] = tr[at * quarter + row, c]
    for ref in (zs_ref, xs_ref):
        pad = ref.shape[0] - quarter * comps * nk
        ref[pl.ds(quarter * comps * nk, pad), :] = jnp.zeros((pad, nz), jnp.bfloat16)


def weights_kernel(ids_ref, table_ref, zc_ref, xc_ref, _, weight_ref, zc_out, xc_out):
    m = lax.axis_index("modes")
    q = lax.rem(lax.axis_index("space"), 2)
    body, nz = xc_ref.shape
    nx = ids_ref.shape[1]
    quarter = nx // 4
    table = table_ref[...]
    weight = jnp.zeros((nx, nz), jnp.float32)
    for entry in range(NW):
        weight = jnp.where(ids_ref[0] == entry, table[:, entry : entry + 1], weight)
    weight_ref[...] = weight
    for ref, out, at in ((zc_ref, zc_out, 2 * (1 - m) + q), (xc_ref, xc_out, 2 * (1 - m) + 1 - q)):
        out[pl.ds(0, body), :] = ref[...]
        rest = jnp.concatenate(
            [
                jnp.broadcast_to(weight_ref[pl.ds(at * quarter + row, 1), :], (8, nz))
                for row in range(quarter)
            ],
            axis=0,
        )
        piece_of = lax.rem(lax.broadcasted_iota(jnp.int32, rest.shape, 0), 8)
        pieces = jnp.zeros(rest.shape, jnp.float32)
        for piece in range(3):
            rounded = rest.astype(jnp.bfloat16).astype(jnp.float32)
            pieces = jnp.where(piece_of == piece, rounded, pieces)
            rest = rest - rounded
        out[pl.ds(body, 8 * quarter), :] = pieces.astype(jnp.bfloat16)


def received_weights(ref, first, quarter):
    pieces = ref[pl.ds(first, 8 * quarter), :].astype(jnp.float32)
    return [
        pieces[8 * r : 8 * r + 1] + pieces[8 * r + 1 : 8 * r + 2] + pieces[8 * r + 2 : 8 * r + 3]
        for r in range(quarter)
    ]


def picks(jb_ref, m, nk):
    first = jb_ref[0] * JB
    owner = (first >= nk).astype(jnp.int32)
    row = first - owner * nk
    within = lax.rem(row, 16)
    return owner == m, pl.multiple_of(row - within, 16), within


def picked(pick, own, other):
    mine, block, within = pick
    rows = jnp.where(
        mine, own[pl.ds(block, 16), :].astype(jnp.float32), other[pl.ds(block, 16), :].astype(jnp.float32)
    )
    result = rows[0:JB]
    for start in range(JB, 16, JB):
        result = jnp.where(within == start, rows[start : start + JB], result)
    return result


def spread(row):
    return jnp.broadcast_to(row, (16, row.shape[1])).astype(jnp.bfloat16)[None]


def scaled(tile, field):
    rows, lanes = field.shape
    return (tile * field.reshape(rows // 16, 16, lanes)).reshape(rows, lanes)


def dot_nt(a, b):
    return lax.dot_general(a, b, (((1,), (1,)), ((), ())), preferred_element_type=jnp.float32)


def local_kernel(own_ref, other_ref, weight_ref, jb_ref, acc_ref, w0_ref, adv, wts):
    m = lax.axis_index("modes")
    q = lax.rem(lax.axis_index("space"), 2)
    rows, comps, nk, nz = own_ref.shape
    rows -= 2
    pick = picks(jb_ref, m, nk)
    for r in range(rows):
        phi = [picked(pick, own_ref.at[r + 1, d], other_ref.at[r + 1, d]) for d in range(comps)]
        weight = weight_ref[pl.ds(rows * m + r, 1), :]
        for c in range(comps):
            for half, ref in enumerate((own_ref, other_ref)):
                block = pl.ds(half * nk, nk)
                here = ref[r + 1, c].astype(jnp.float32)
                gx = 0.5 * (ref[r + 2, c].astype(jnp.float32) - ref[r, c].astype(jnp.float32))
                gz = 0.5 * (pltpu.roll(here, nz - 1, 1) - pltpu.roll(here, 1, 1))
                gx = gx.astype(jnp.bfloat16).astype(jnp.float32)
                gz = gz.astype(jnp.bfloat16).astype(jnp.float32)
                wts[r, block, pl.ds(c * nz, nz)] = (weight * here).astype(jnp.bfloat16)
                for j in range(JB):
                    total = phi[0][j : j + 1] * gx + phi[2][j : j + 1] * gz
                    adv[r, pl.ds((2 * j + half) * nk, nk), pl.ds(c * nz, nz)] = total.astype(jnp.bfloat16)
    total = dot_nt(adv[0], wts[0])
    for r in range(1, rows):
        total = total + dot_nt(adv[r], wts[r])
    acc_ref[...] = total
    quarter = rows // 2
    for r in range(quarter):
        w0_ref[r] = wts[quarter * q + r]


def cross_kernel(classes_of, chunk, planes, has_weighted, own_ref, other_ref, *refs):
    zs_ref, xs_ref, zc_ref, xc_ref, w0_ref, jb_ref, acc_ref, *refs = refs
    if has_weighted:
        wts, keep_ref, send_ref, adv = refs
    else:
        keep_ref, send_ref, wts, adv = refs
    m = lax.axis_index("modes")
    plane = lax.axis_index("space")
    q = lax.rem(plane, 2)
    sigma = jnp.where(q == 0, 0.5, -0.5)
    inside = jnp.where(jnp.logical_or(plane == 1, plane == planes - 2), 0.0, 1.0)
    rows, comps, nk, nz = own_ref.shape
    quarter = (rows - 2) // 2
    span = quarter * comps * nz
    pick = picks(jb_ref, m, nk)
    classes = [pl.multiple_of(chunk * cls, chunk) for cls in classes_of(plane)]
    if not has_weighted:
        w1 = received_weights(xc_ref, quarter * comps * nk, quarter)
        w2 = [inside * weight for weight in received_weights(zc_ref, quarter * comps * nk, quarter)]
        for r in range(quarter):
            wts[:, pl.ds(r * comps * nz, comps * nz)] = w0_ref[r]
            for c in range(comps):
                lane = (r * comps + c) * nz
                src = pl.ds((r * comps + c) * nk, nk)
                for half, (p1, p2) in enumerate(((xs_ref, zs_ref), (xc_ref, zc_ref))):
                    block = pl.ds(half * nk, nk)
                    for part, (field, weight) in enumerate(((p1, w1[r]), (p2, w2[r])), 1):
                        wts[block, pl.ds(part * span + lane, nz)] = (
                            weight * field[src, :].astype(jnp.float32)
                        ).astype(jnp.bfloat16)
    phis = []
    for r in range(quarter):
        row0 = 1 + quarter * q + r
        along = pl.ds((r * comps + 1) * nk, nk)
        phi0 = sigma * picked(pick, own_ref.at[row0, 1], other_ref.at[row0, 1])
        phi1 = sigma * picked(pick, xs_ref.at[along], xc_ref.at[along])
        phi2 = -sigma * picked(pick, zs_ref.at[along], zc_ref.at[along])
        phis.append([[spread(phi[j : j + 1]) for j in range(JB)] for phi in (phi0, phi1, phi2)])
    inside = inside.astype(jnp.bfloat16)
    for at, cls in enumerate(classes):
        for r in range(quarter):
            row0 = 1 + quarter * q + r
            phi0, phi1, phi2 = phis[r]
            for c in range(comps):
                lane = (r * comps + c) * nz
                src = (r * comps + c) * nk
                for half, (p0, p1, p2) in enumerate(
                    ((own_ref, xs_ref, zs_ref), (other_ref, xc_ref, zc_ref))
                ):
                    f0 = p0[row0, c, pl.ds(cls, chunk), :]
                    f1 = p1[pl.ds(src + cls, chunk), :]
                    gy = inside * p2[pl.ds(src + cls, chunk), :] - f0
                    for j in range(JB):
                        here = pl.ds((half * JB + j) * chunk, chunk)
                        adv[at, here, pl.ds(lane, nz)] = scaled(phi0[j], f1)
                        adv[at, here, pl.ds(span + lane, nz)] = scaled(phi1[j], gy)
                        adv[at, here, pl.ds(2 * span + lane, nz)] = scaled(phi2[j], f1)
        total = dot_nt(adv[at], wts[...])
        for half in range(2):
            level = m if half == 0 else 1 - m
            for j in range(JB):
                first = (half * JB + j) * chunk
                piece = total[first : first + chunk] + acc_ref[pl.ds((2 * j + half) * nk + cls, chunk), :]
                keep_ref[at, level, j] = piece[:, :nk]
                send_ref[at, level, j] = piece[:, nk:].astype(jnp.bfloat16)


def near_kernel(keep_ref, got_ref, *out_refs):
    for at, ref in enumerate(out_refs):
        ref[...] = (keep_ref[at] + got_ref[at].astype(jnp.float32)).astype(ref.dtype)


def far_kernel(mine_ref, *refs):
    *parts, keep_ref, send_ref = refs
    level = lax.div(lax.axis_index("space"), NEAR)
    for ref, at in ((keep_ref, level), (send_ref, 1 - level)):
        total = mine_ref[at]
        for part in parts:
            total = total + part[at].astype(jnp.float32)
        ref[...] = total.astype(ref.dtype)


def total_kernel(keep_ref, got_ref, out_ref):
    total = keep_ref[...] + got_ref[...].astype(jnp.float32)
    for j in range(JB):
        out_ref[:, j, :] = total[j]


def on_device(n, modes, weight_ids, weight_table, j_block):
    nk, comps, _, nx, nz = modes.shape
    bf16, f32 = jnp.bfloat16, jnp.float32
    vmem = pl.BlockSpec(memory_space=pltpu.VMEM)
    smem = pl.BlockSpec(memory_space=pltpu.SMEM)
    params = pltpu.CompilerParams(vmem_limit_bytes=VMEM_LIMIT)
    six = nx // 2 + 2
    quarter = nx // 4
    body = quarter * comps * nk
    own, to_core, zs, xs, zc, xc = pl.pallas_call(
        prep_kernel,
        out_shape=[jax.ShapeDtypeStruct((six, comps, nk, nz), bf16)] * 2
        + [jax.ShapeDtypeStruct((body + PADROWS, nz), bf16)] * 2
        + [jax.ShapeDtypeStruct((body, nz), bf16)] * 2,
        in_specs=[pl.BlockSpec(memory_space=pltpu.HBM)],
        out_specs=[vmem] * 6,
        scratch_shapes=[
            pltpu.VMEM(modes.shape, bf16),
            pltpu.VMEM((nx, comps, nk, nz), bf16),
            pltpu.SemaphoreType.DMA((LOADS,)),
        ],
        compiler_params=pltpu.CompilerParams(vmem_limit_bytes=PREP_LIMIT),
        cost_estimate=pl.CostEstimate(flops=1_500_000_000, bytes_accessed=2_800_000, transcendentals=0),
        name="prep",
    )(modes)

    both = ("space", "modes")
    x_pairs = [(s, s ^ 1) for s in range(n)]
    z_pairs = [(s, (s + (2 if s % 2 else -2)) % n) for s in range(n)]
    same = lambda pairs: [(2 * a + m, 2 * b + m) for a, b in pairs for m in range(2)]
    cross = lambda pairs: [(2 * a + m, 2 * b + 1 - m) for a, b in pairs for m in range(2)]
    other = lax.ppermute(to_core, "modes", [(0, 1), (1, 0)])
    zs = lax.ppermute(zs, both, same(z_pairs))
    xs = lax.ppermute(xs, both, same(x_pairs))
    weight, zc, xc = pl.pallas_call(
        weights_kernel,
        out_shape=[jax.ShapeDtypeStruct((nx, nz), f32)]
        + [jax.ShapeDtypeStruct((body + 8 * quarter, nz), bf16)] * 2,
        in_specs=[vmem] * 4 + [pl.BlockSpec(memory_space=pl.ANY)],
        out_specs=[vmem] * 3,
        compiler_params=params,
        name="weights",
    )(weight_ids, weight_table.reshape(1, NW), zc, xc, other)
    xc = lax.ppermute(xc, both, cross(x_pairs))
    zc = lax.ppermute(zc, both, cross(z_pairs))

    def estimate(depth, size):
        return pl.CostEstimate(
            flops=2 * JB * (2 * nk) ** 2 * depth, bytes_accessed=size, transcendentals=0
        )

    depth = nx // 4 * comps * nz
    depth = quarter * comps * nz
    acc, w0 = pl.pallas_call(
        local_kernel,
        out_shape=[
            jax.ShapeDtypeStruct((JB * 2 * nk, 2 * nk), f32),
            jax.ShapeDtypeStruct((quarter, 2 * nk, comps * nz), bf16),
        ],
        in_specs=[vmem, vmem, vmem, smem],
        out_specs=[vmem] * 2,
        scratch_shapes=[
            pltpu.VMEM((2 * quarter, JB * 2 * nk, comps * nz), bf16),
            pltpu.VMEM((2 * quarter, 2 * nk, comps * nz), bf16),
        ],
        compiler_params=params,
        cost_estimate=pl.CostEstimate(flops=900_000_000, bytes_accessed=2_400_000, transcendentals=0),
        name="local",
    )(own, other, weight, j_block)

    per_target = 2 * nk // n
    chunk = max(16, per_target)

    def crossed(count, classes_of, weighted):
        piece = (count, 2, JB, chunk, nk)
        out_shape = [jax.ShapeDtypeStruct(piece, f32), jax.ShapeDtypeStruct(piece, bf16)]
        if not weighted:
            out_shape.append(jax.ShapeDtypeStruct((2 * nk, 3 * depth), bf16))
        return pl.pallas_call(
            functools.partial(cross_kernel, classes_of, chunk, n, bool(weighted)),
            out_shape=out_shape,
            in_specs=[vmem] * 7 + [smem] + [vmem] * (1 + len(weighted)),
            out_specs=[vmem] * len(out_shape),
            scratch_shapes=[pltpu.VMEM((count, 2 * JB * chunk, 3 * depth), bf16)],
            compiler_params=params,
            cost_estimate=pl.CostEstimate(
                flops=900_000_000, bytes_accessed=4_000_000, transcendentals=0
            ),
            name="cross",
        )(own, other, zs, xs, zc, xc, w0, j_block, acc, *weighted)

    swap = [(0, 1), (1, 0)]
    if n == 2 * NEAR:
        def partners(*steps):
            return lambda s: [jnp.bitwise_xor(lax.rem(s, NEAR), step) for step in steps]

        keep_a, send_a, w2 = crossed(2, partners(3, 1), ())
        got_a = lax.ppermute(send_a, "modes", swap)
        keep_b, send_b = crossed(2, partners(0, 2), (w2,))
        got_b = lax.ppermute(send_b, "modes", swap)
        piece = (JB, chunk, nk)

        def summed(kinds, keep, got):
            return pl.pallas_call(
                near_kernel,
                out_shape=[jax.ShapeDtypeStruct((2, *piece), kind) for kind in kinds],
                in_specs=[vmem] * 2,
                out_specs=[vmem] * 2,
                compiler_params=params,
                name="near",
            )(keep, got)

        part_3, part_1 = summed((bf16, bf16), keep_a, got_a)
        mine, part_2 = summed((f32, bf16), keep_b, got_b)
        parts = [
            lax.ppermute(part, "space", [(s, s ^ step) for s in range(n)])
            for part, step in ((part_3, 3), (part_1, 1), (part_2, 2))
        ]
        keep, send = pl.pallas_call(
            far_kernel,
            out_shape=[jax.ShapeDtypeStruct(piece, f32), jax.ShapeDtypeStruct(piece, bf16)],
            in_specs=[vmem] * NEAR,
            out_specs=[vmem] * 2,
            compiler_params=params,
            name="far",
        )(mine, *parts)
        got = lax.ppermute(send, "space", [(s, s ^ NEAR) for s in range(n)])
        return pl.pallas_call(
            total_kernel,
            out_shape=jax.ShapeDtypeStruct((chunk, JB, nk), f32),
            in_specs=[vmem] * 2,
            out_specs=vmem,
            compiler_params=params,
            name="total",
        )(keep, got)

    count = nk // chunk
    keep, send, _ = crossed(count, lambda s: list(range(count)), ())
    share = (keep + lax.ppermute(send, "modes", swap)).astype(bf16)
    share = share.reshape(count, 2, JB, chunk // per_target, per_target, nk)
    share = share.transpose(1, 0, 3, 2, 4, 5).reshape(n, JB, per_target, nk)
    parts = lax.all_to_all(share, "space", 0, 0, tiled=True)
    return jnp.sum(parts.astype(f32), axis=0).transpose(1, 0, 2)


def solution(mesh):
    return jax.shard_map(
        functools.partial(on_device, mesh.shape["space"]),
        mesh=mesh,
        in_specs=(
            P("modes", None, ("groups", "space"), None, None),
            P(("groups", "space"), None, None),
            P(),
            P("groups"),
        ),
        out_specs=P(("groups", "space"), None, "modes"),
        check_vma=False,
    )
```

```python
import functools

import jax
import jax.numpy as jnp
from jax import lax
from jax.experimental import pallas as pl
from jax.experimental.pallas import tpu as pltpu
from jax.sharding import PartitionSpec as P

JB = 4
NW = 16
PADROWS = 16
LOADS = 8
NEAR = 4
VMEM_LIMIT = 48 * 1024 * 1024
PREP_LIMIT = 53_100 * 1024


def prep_kernel(modes_hbm, own_ref, core_ref, zs_ref, xs_ref, zc_ref, xc_ref, modes_ref, tr, sems):
    m = lax.axis_index("modes")
    q = lax.rem(lax.axis_index("space"), 2)
    nk, comps, _, nx, nz = modes_hbm.shape
    step = nk // LOADS
    copies = [
        pltpu.make_async_copy(
            modes_hbm.at[pl.ds(p * step, step)], modes_ref.at[pl.ds(p * step, step)], sems.at[p]
        )
        for p in range(LOADS)
    ]
    for copy in copies:
        copy.start()
    quarter = nx // 4
    for p in range(LOADS):
        copies[p].wait()
        block = pl.ds(p * step, step)
        for c in range(comps):
            value = modes_ref[block, c, 0].astype(jnp.float32)
            tr[:, c, block] = jnp.swapaxes(value, 0, 1).astype(jnp.bfloat16)
        for ref, at in (
            (zs_ref, 2 * m + q),
            (xs_ref, 2 * m + 1 - q),
            (zc_ref, 2 * (1 - m) + q),
            (xc_ref, 2 * (1 - m) + 1 - q),
        ):
            for row in range(quarter):
                for c in range(comps):
                    first = (row * comps + c) * nk + p * step
                    ref[pl.ds(first, step), :] = tr[at * quarter + row, c, block]
        for r in range(nx // 2 + 2):
            core_ref[r, :, block] = tr[lax.rem(nx // 2 * (1 - m) + nx - 1 + r, nx), :, block]
            own_ref[r, :, block] = tr[lax.rem(nx // 2 * m + nx - 1 + r, nx), :, block]
    for ref in (zs_ref, xs_ref):
        pad = ref.shape[0] - quarter * comps * nk
        ref[pl.ds(quarter * comps * nk, pad), :] = jnp.zeros((pad, nz), jnp.bfloat16)


def weights_kernel(ids_ref, table_ref, zc_ref, xc_ref, _, weight_ref, xc_out, ze_out, zo_out):
    m = lax.axis_index("modes")
    q = lax.rem(lax.axis_index("space"), 2)
    body, nz = xc_ref.shape
    nx = ids_ref.shape[1]
    quarter = nx // 4
    table = table_ref[...]
    weight = jnp.zeros((nx, nz), jnp.float32)
    for entry in range(NW):
        weight = jnp.where(ids_ref[0] == entry, table[:, entry : entry + 1], weight)
    weight_ref[...] = weight
    for ref, outs, at in (
        (xc_ref, (xc_out,), 2 * (1 - m) + 1 - q),
        (zc_ref, (ze_out, zo_out), 2 * (1 - m) + q),
    ):
        rest = jnp.concatenate(
            [
                jnp.broadcast_to(weight_ref[pl.ds(at * quarter + row, 1), :], (8, nz))
                for row in range(quarter)
            ],
            axis=0,
        )
        piece_of = lax.rem(lax.broadcasted_iota(jnp.int32, rest.shape, 0), 8)
        pieces = jnp.zeros(rest.shape, jnp.float32)
        for piece in range(3):
            rounded = rest.astype(jnp.bfloat16).astype(jnp.float32)
            pieces = jnp.where(piece_of == piece, rounded, pieces)
            rest = rest - rounded
        for out in outs:
            out[pl.ds(0, body), :] = ref[...]
            out[pl.ds(body, 8 * quarter), :] = pieces.astype(jnp.bfloat16)


def received_weights(sent, quarter):
    pieces = sent.astype(jnp.float32)
    return [
        pieces[8 * r : 8 * r + 1] + pieces[8 * r + 1 : 8 * r + 2] + pieces[8 * r + 2 : 8 * r + 3]
        for r in range(quarter)
    ]


def picks(jb_ref, m, nk):
    first = jb_ref[0] * JB
    owner = (first >= nk).astype(jnp.int32)
    row = first - owner * nk
    within = lax.rem(row, 16)
    return owner == m, pl.multiple_of(row - within, 16), within


def picked(pick, own, other):
    mine, block, within = pick
    rows = pl.ds(block, 16)
    rows = jnp.where(mine, own(rows).astype(jnp.float32), other(rows).astype(jnp.float32))
    result = rows[0:JB]
    for start in range(JB, 16, JB):
        result = jnp.where(within == start, rows[start : start + JB], result)
    return result


def spread(row):
    return jnp.broadcast_to(row, (16, row.shape[1])).astype(jnp.bfloat16)[None]


def scaled(tile, field):
    rows, lanes = field.shape
    return (tile * field.reshape(rows // 16, 16, lanes)).reshape(rows, lanes)


def dot_nt(a, b):
    return lax.dot_general(a, b, (((1,), (1,)), ((), ())), preferred_element_type=jnp.float32)


def local_kernel(own_ref, other_ref, weight_ref, jb_ref, acc_ref, w0_ref, adv, wts):
    m = lax.axis_index("modes")
    q = lax.rem(lax.axis_index("space"), 2)
    rows, comps, nk, nz = own_ref.shape
    rows -= 2
    pick = picks(jb_ref, m, nk)
    for r in range(rows):
        phi = [picked(pick, lambda at: own_ref[r + 1, d, at, :], lambda at: other_ref[r + 1, d, at, :]) for d in range(comps)]
        weight = weight_ref[pl.ds(rows * m + r, 1), :]
        for c in range(comps):
            for half, ref in enumerate((own_ref, other_ref)):
                block = pl.ds(half * nk, nk)
                here = ref[r + 1, c].astype(jnp.float32)
                gx = 0.5 * (ref[r + 2, c].astype(jnp.float32) - ref[r, c].astype(jnp.float32))
                gz = 0.5 * (pltpu.roll(here, nz - 1, 1) - pltpu.roll(here, 1, 1))
                gx = gx.astype(jnp.bfloat16).astype(jnp.float32)
                gz = gz.astype(jnp.bfloat16).astype(jnp.float32)
                wts[r, block, pl.ds(c * nz, nz)] = (weight * here).astype(jnp.bfloat16)
                for j in range(JB):
                    total = phi[0][j : j + 1] * gx + phi[2][j : j + 1] * gz
                    adv[r, pl.ds((2 * j + half) * nk, nk), pl.ds(c * nz, nz)] = total.astype(jnp.bfloat16)
    total = dot_nt(adv[0], wts[0])
    for r in range(1, rows):
        total = total + dot_nt(adv[r], wts[r])
    acc_ref[...] = total
    quarter = rows // 2
    for r in range(quarter):
        w0_ref[r] = wts[quarter * q + r]


def cross_kernel(classes_of, chunk, planes, has_weighted, own_ref, other_ref, *refs):
    xs_ref, zs_ref, xc_ref, ze_ref, zo_ref, w0_ref, jb_ref, acc_ref, *refs = refs
    if has_weighted:
        wts, keep_ref, send_ref, adv = refs
    else:
        keep_ref, send_ref, wts, adv = refs
    m = lax.axis_index("modes")
    plane = lax.axis_index("space")
    q = lax.rem(plane, 2)
    sigma = jnp.where(q == 0, 0.5, -0.5)
    inside = jnp.where(jnp.logical_or(plane == 1, plane == planes - 2), 0.0, 1.0)
    by_even = lax.rem(lax.div(plane, 2), 2) == q

    def zc_rows(rows):
        return jnp.where(by_even, ze_ref[rows, :], zo_ref[rows, :])

    rows, comps, nk, nz = own_ref.shape
    quarter = (rows - 2) // 2
    span = quarter * comps * nz
    pick = picks(jb_ref, m, nk)
    classes = [pl.multiple_of(chunk * cls, chunk) for cls in classes_of(plane)]
    if not has_weighted:
        sent = pl.ds(quarter * comps * nk, 8 * quarter)
        w1 = received_weights(xc_ref[sent, :], quarter)
        w2 = [inside * weight for weight in received_weights(zc_rows(sent), quarter)]
        for r in range(quarter):
            wts[:, pl.ds(r * comps * nz, comps * nz)] = w0_ref[r]
            for c in range(comps):
                lane = (r * comps + c) * nz
                src = pl.ds((r * comps + c) * nk, nk)
                for half, (f1, f2) in enumerate(
                    ((xs_ref[src, :], zs_ref[src, :]), (xc_ref[src, :], zc_rows(src)))
                ):
                    block = pl.ds(half * nk, nk)
                    for part, (field, weight) in enumerate(((f1, w1[r]), (f2, w2[r])), 1):
                        wts[block, pl.ds(part * span + lane, nz)] = (
                            weight * field.astype(jnp.float32)
                        ).astype(jnp.bfloat16)
    phis = []
    for r in range(quarter):
        row0 = 1 + quarter * q + r
        along = (r * comps + 1) * nk

        def moved(at):
            return pl.ds(pl.multiple_of(along + at.start, 16), at.size)

        phi0 = sigma * picked(
            pick, lambda at: own_ref[row0, 1, at, :], lambda at: other_ref[row0, 1, at, :]
        )
        phi1 = sigma * picked(pick, lambda at: xs_ref[moved(at), :], lambda at: xc_ref[moved(at), :])
        phi2 = -sigma * picked(pick, lambda at: zs_ref[moved(at), :], lambda at: zc_rows(moved(at)))
        phis.append([[spread(phi[j : j + 1]) for j in range(JB)] for phi in (phi0, phi1, phi2)])
    inside = inside.astype(jnp.bfloat16)
    for at, cls in enumerate(classes):
        for r in range(quarter):
            row0 = 1 + quarter * q + r
            phi0, phi1, phi2 = phis[r]
            for c in range(comps):
                lane = (r * comps + c) * nz
                src = (r * comps + c) * nk
                rows_at = pl.ds(pl.multiple_of(src + cls, 16), chunk)
                for half, (p0, p1) in enumerate(((own_ref, xs_ref), (other_ref, xc_ref))):
                    f0 = p0[row0, c, pl.ds(cls, chunk), :]
                    f1 = p1[rows_at, :]
                    gy = inside * (zc_rows(rows_at) if half else zs_ref[rows_at, :]) - f0
                    for j in range(JB):
                        here = pl.ds((half * JB + j) * chunk, chunk)
                        adv[at, here, pl.ds(lane, nz)] = scaled(phi0[j], f1)
                        adv[at, here, pl.ds(span + lane, nz)] = scaled(phi1[j], gy)
                        adv[at, here, pl.ds(2 * span + lane, nz)] = scaled(phi2[j], f1)
        total = dot_nt(adv[at], wts[...])
        for half in range(2):
            level = m if half == 0 else 1 - m
            for j in range(JB):
                first = (half * JB + j) * chunk
                piece = total[first : first + chunk] + acc_ref[pl.ds((2 * j + half) * nk + cls, chunk), :]
                keep_ref[at, level, j] = piece[:, :nk]
                send_ref[at, level, j] = piece[:, nk:].astype(jnp.bfloat16)


def near_kernel(keep_ref, got_ref, *out_refs):
    for at, ref in enumerate(out_refs):
        ref[...] = (keep_ref[at] + got_ref[at].astype(jnp.float32)).astype(ref.dtype)


def far_kernel(mine_ref, *refs):
    *parts, keep_ref, send_ref = refs
    level = lax.div(lax.axis_index("space"), NEAR)
    for ref, at in ((keep_ref, level), (send_ref, 1 - level)):
        total = mine_ref[at]
        for part in parts:
            total = total + part[at].astype(jnp.float32)
        ref[...] = total.astype(ref.dtype)


def total_kernel(keep_ref, got_ref, out_ref):
    total = keep_ref[...] + got_ref[...].astype(jnp.float32)
    for j in range(JB):
        out_ref[:, j, :] = total[j]


def level_swaps(n, odd):
    pairs = []
    for s in range(n):
        to = s // 2 + (1 if s // 2 % 2 == odd else -1)
        pairs.append((s, 2 * to + s % 2 if 0 <= to < n // 2 else s))
    return pairs


def on_device(n, modes, weight_ids, weight_table, j_block):
    nk, comps, _, nx, nz = modes.shape
    bf16, f32 = jnp.bfloat16, jnp.float32
    vmem = pl.BlockSpec(memory_space=pltpu.VMEM)
    smem = pl.BlockSpec(memory_space=pltpu.SMEM)
    params = pltpu.CompilerParams(vmem_limit_bytes=VMEM_LIMIT)
    six = nx // 2 + 2
    quarter = nx // 4
    body = quarter * comps * nk
    own, to_core, zs, xs, zc, xc = pl.pallas_call(
        prep_kernel,
        out_shape=[jax.ShapeDtypeStruct((six, comps, nk, nz), bf16)] * 2
        + [jax.ShapeDtypeStruct((body + PADROWS, nz), bf16)] * 2
        + [jax.ShapeDtypeStruct((body, nz), bf16)] * 2,
        in_specs=[pl.BlockSpec(memory_space=pltpu.HBM)],
        out_specs=[vmem] * 6,
        scratch_shapes=[
            pltpu.VMEM(modes.shape, bf16),
            pltpu.VMEM((nx, comps, nk, nz), bf16),
            pltpu.SemaphoreType.DMA((LOADS,)),
        ],
        compiler_params=pltpu.CompilerParams(vmem_limit_bytes=PREP_LIMIT),
        cost_estimate=pl.CostEstimate(flops=1_500_000_000, bytes_accessed=2_800_000, transcendentals=0),
        name="prep",
    )(modes)

    both = ("space", "modes")
    x_pairs = [(s, s ^ 1) for s in range(n)]
    z_pairs = [(s, (s + (2 if s % 2 else -2)) % n) for s in range(n)]
    same = lambda pairs: [(2 * a + m, 2 * b + m) for a, b in pairs for m in range(2)]
    cross = lambda pairs: [(2 * a + m, 2 * b + 1 - m) for a, b in pairs for m in range(2)]
    other = lax.ppermute(to_core, "modes", [(0, 1), (1, 0)])
    zs = lax.ppermute(zs, both, same(z_pairs))
    xs = lax.ppermute(xs, both, same(x_pairs))
    weight, xc, *zc = pl.pallas_call(
        weights_kernel,
        out_shape=[jax.ShapeDtypeStruct((nx, nz), f32)]
        + [jax.ShapeDtypeStruct((body + 8 * quarter, nz), bf16)] * 3,
        in_specs=[vmem] * 4 + [pl.BlockSpec(memory_space=pl.ANY)],
        out_specs=[vmem] * 4,
        compiler_params=params,
        name="weights",
    )(weight_ids, weight_table.reshape(1, NW), zc, xc, other)
    xc = lax.ppermute(xc, both, cross(x_pairs))
    zc = [
        lax.ppermute(
            zc[odd],
            both,
            [(2 * a + m, 2 * b + (m if a == b else 1 - m)) for a, b in level_swaps(n, odd) for m in range(2)],
        )
        for odd in range(2)
    ]

    depth = quarter * comps * nz
    acc, w0 = pl.pallas_call(
        local_kernel,
        out_shape=[
            jax.ShapeDtypeStruct((JB * 2 * nk, 2 * nk), f32),
            jax.ShapeDtypeStruct((quarter, 2 * nk, comps * nz), bf16),
        ],
        in_specs=[vmem, vmem, vmem, smem],
        out_specs=[vmem] * 2,
        scratch_shapes=[
            pltpu.VMEM((2 * quarter, JB * 2 * nk, comps * nz), bf16),
            pltpu.VMEM((2 * quarter, 2 * nk, comps * nz), bf16),
        ],
        compiler_params=params,
        cost_estimate=pl.CostEstimate(flops=900_000_000, bytes_accessed=2_400_000, transcendentals=0),
        name="local",
    )(own, other, weight, j_block)

    per_target = 2 * nk // n
    chunk = max(16, per_target)

    def crossed(count, classes_of, weighted):
        piece = (count, 2, JB, chunk, nk)
        out_shape = [jax.ShapeDtypeStruct(piece, f32), jax.ShapeDtypeStruct(piece, bf16)]
        if not weighted:
            out_shape.append(jax.ShapeDtypeStruct((2 * nk, 3 * depth), bf16))
        return pl.pallas_call(
            functools.partial(cross_kernel, classes_of, chunk, n, bool(weighted)),
            out_shape=out_shape,
            in_specs=[vmem] * 8 + [smem] + [vmem] * (1 + len(weighted)),
            out_specs=[vmem] * len(out_shape),
            scratch_shapes=[pltpu.VMEM((count, 2 * JB * chunk, 3 * depth), bf16)],
            compiler_params=params,
            cost_estimate=pl.CostEstimate(
                flops=900_000_000, bytes_accessed=4_000_000, transcendentals=0
            ),
            name="cross",
        )(own, other, xs, zs, xc, *zc, w0, j_block, acc, *weighted)

    swap = [(0, 1), (1, 0)]
    if n == 2 * NEAR:
        def partners(*steps):
            return lambda s: [jnp.bitwise_xor(lax.rem(s, NEAR), step) for step in steps]

        keep_a, send_a, w2 = crossed(2, partners(3, 1), ())
        got_a = lax.ppermute(send_a, "modes", swap)
        keep_b, send_b = crossed(2, partners(0, 2), (w2,))
        got_b = lax.ppermute(send_b, "modes", swap)
        piece = (JB, chunk, nk)

        def summed(kinds, keep, got):
            return pl.pallas_call(
                near_kernel,
                out_shape=[jax.ShapeDtypeStruct((2, *piece), kind) for kind in kinds],
                in_specs=[vmem] * 2,
                out_specs=[vmem] * 2,
                compiler_params=params,
                name="near",
            )(keep, got)

        part_3, part_1 = summed((bf16, bf16), keep_a, got_a)
        mine, part_2 = summed((f32, bf16), keep_b, got_b)
        parts = [
            lax.ppermute(part, "space", [(s, s ^ step) for s in range(n)])
            for part, step in ((part_3, 3), (part_1, 1), (part_2, 2))
        ]
        keep, send = pl.pallas_call(
            far_kernel,
            out_shape=[jax.ShapeDtypeStruct(piece, f32), jax.ShapeDtypeStruct(piece, bf16)],
            in_specs=[vmem] * NEAR,
            out_specs=[vmem] * 2,
            compiler_params=params,
            name="far",
        )(mine, *parts)
        got = lax.ppermute(send, "space", [(s, s ^ NEAR) for s in range(n)])
        return pl.pallas_call(
            total_kernel,
            out_shape=jax.ShapeDtypeStruct((chunk, JB, nk), f32),
            in_specs=[vmem] * 2,
            out_specs=vmem,
            compiler_params=params,
            name="total",
        )(keep, got)

    count = nk // chunk
    keep, send, _ = crossed(count, lambda s: list(range(count)), ())
    share = (keep + lax.ppermute(send, "modes", swap)).astype(bf16)
    share = share.reshape(count, 2, JB, chunk // per_target, per_target, nk)
    share = share.transpose(1, 0, 3, 2, 4, 5).reshape(n, JB, per_target, nk)
    parts = lax.all_to_all(share, "space", 0, 0, tiled=True)
    return jnp.sum(parts.astype(f32), axis=0).transpose(1, 0, 2)


def solution(mesh):
    return jax.shard_map(
        functools.partial(on_device, mesh.shape["space"]),
        mesh=mesh,
        in_specs=(
            P("modes", None, ("groups", "space"), None, None),
            P(("groups", "space"), None, None),
            P(),
            P("groups"),
        ),
        out_specs=P(("groups", "space"), None, "modes"),
        check_vma=False,
    )
```

```python
import functools

import jax
import jax.numpy as jnp
from jax import lax
from jax.experimental import pallas as pl
from jax.experimental.pallas import tpu as pltpu
from jax.sharding import PartitionSpec as P

JB = 4
NW = 16
PADROWS = 16
LOADS = 4
X_FIRST = 0b10011111
NEAR = 4
VMEM_LIMIT = 48 * 1024 * 1024
PREP_LIMIT = 53_100 * 1024


def x_first(s, planes):
    if planes != 8:
        return s >= 0
    return lax.rem(lax.shift_right_logical(X_FIRST, s), 2) == 1


def prep_kernel(
    planes, modes_hbm, own_ref, core_ref, first_ref, second_ref, xc_ref, zc_ref, modes_ref, tr, sems
):
    m = lax.axis_index("modes")
    s = lax.axis_index("space")
    q = lax.rem(s, 2)
    to_x, to_z = 2 * m + 1 - q, 2 * m + q
    x_now = x_first(s, planes)
    nk, comps, _, nx, nz = modes_hbm.shape
    step = nk // LOADS
    copies = [
        pltpu.make_async_copy(
            modes_hbm.at[pl.ds(p * step, step)], modes_ref.at[pl.ds(p * step, step)], sems.at[p]
        )
        for p in range(LOADS)
    ]
    for copy in copies:
        copy.start()
    for p in range(LOADS):
        copies[p].wait()
        block = pl.ds(p * step, step)
        for c in range(comps):
            value = modes_ref[block, c, 0].astype(jnp.float32)
            tr[:, c, block] = jnp.swapaxes(value, 0, 1).astype(jnp.bfloat16)
    quarter = nx // 4
    for r in range(nx // 2 + 2):
        own_ref[r] = tr[lax.rem(nx // 2 * m + nx - 1 + r, nx)]
        core_ref[r] = tr[lax.rem(nx // 2 * (1 - m) + nx - 1 + r, nx)]
    for ref, at in (
        (first_ref, jnp.where(x_now, to_x, to_z)),
        (second_ref, jnp.where(x_now, to_z, to_x)),
        (xc_ref, 2 * (1 - m) + 1 - q),
        (zc_ref, 2 * (1 - m) + q),
    ):
        for row in range(quarter):
            for c in range(comps):
                ref[pl.ds((row * comps + c) * nk, nk), :] = tr[at * quarter + row, c]
    for ref in (first_ref, second_ref):
        pad = ref.shape[0] - quarter * comps * nk
        ref[pl.ds(quarter * comps * nk, pad), :] = jnp.zeros((pad, nz), jnp.bfloat16)


def weights_kernel(ids_ref, table_ref, xc_ref, zc_ref, _, weight_ref, xc_out, zc_out):
    m = lax.axis_index("modes")
    q = lax.rem(lax.axis_index("space"), 2)
    body, nz = xc_ref.shape
    nx = ids_ref.shape[1]
    quarter = nx // 4
    table = table_ref[...]
    weight = jnp.zeros((nx, nz), jnp.float32)
    for entry in range(NW):
        weight = jnp.where(ids_ref[0] == entry, table[:, entry : entry + 1], weight)
    weight_ref[...] = weight
    for ref, out, at in ((zc_ref, zc_out, 2 * (1 - m) + q), (xc_ref, xc_out, 2 * (1 - m) + 1 - q)):
        out[pl.ds(0, body), :] = ref[...]
        rest = jnp.concatenate(
            [
                jnp.broadcast_to(weight_ref[pl.ds(at * quarter + row, 1), :], (8, nz))
                for row in range(quarter)
            ],
            axis=0,
        )
        piece_of = lax.rem(lax.broadcasted_iota(jnp.int32, rest.shape, 0), 8)
        pieces = jnp.zeros(rest.shape, jnp.float32)
        for piece in range(3):
            rounded = rest.astype(jnp.bfloat16).astype(jnp.float32)
            pieces = jnp.where(piece_of == piece, rounded, pieces)
            rest = rest - rounded
        out[pl.ds(body, 8 * quarter), :] = pieces.astype(jnp.bfloat16)


def received_weights(ref, first, quarter):
    pieces = ref[pl.ds(first, 8 * quarter), :].astype(jnp.float32)
    return [
        pieces[8 * r : 8 * r + 1] + pieces[8 * r + 1 : 8 * r + 2] + pieces[8 * r + 2 : 8 * r + 3]
        for r in range(quarter)
    ]


def picks(jb_ref, m, nk):
    first = jb_ref[0] * JB
    owner = (first >= nk).astype(jnp.int32)
    row = first - owner * nk
    within = lax.rem(row, 16)
    return owner == m, pl.multiple_of(row - within, 16), within


def picked(pick, own, other):
    mine, block, within = pick
    rows = pl.ds(block, 16)
    rows = jnp.where(mine, own(rows).astype(jnp.float32), other(rows).astype(jnp.float32))
    result = rows[0:JB]
    for start in range(JB, 16, JB):
        result = jnp.where(within == start, rows[start : start + JB], result)
    return result


def spread(row):
    return jnp.broadcast_to(row, (16, row.shape[1])).astype(jnp.bfloat16)[None]


def scaled(tile, field):
    rows, lanes = field.shape
    return (tile * field.reshape(rows // 16, 16, lanes)).reshape(rows, lanes)


def dot_nt(a, b):
    return lax.dot_general(a, b, (((1,), (1,)), ((), ())), preferred_element_type=jnp.float32)


def local_kernel(own_ref, other_ref, weight_ref, jb_ref, acc_ref, w0_ref, adv, wts):
    m = lax.axis_index("modes")
    q = lax.rem(lax.axis_index("space"), 2)
    rows, comps, nk, nz = own_ref.shape
    rows -= 2
    pick = picks(jb_ref, m, nk)
    for r in range(rows):
        phi = [picked(pick, lambda at: own_ref[r + 1, d, at, :], lambda at: other_ref[r + 1, d, at, :]) for d in range(comps)]
        weight = weight_ref[pl.ds(rows * m + r, 1), :]
        for c in range(comps):
            for half, ref in enumerate((own_ref, other_ref)):
                block = pl.ds(half * nk, nk)
                here = ref[r + 1, c].astype(jnp.float32)
                gx = 0.5 * (ref[r + 2, c].astype(jnp.float32) - ref[r, c].astype(jnp.float32))
                gz = 0.5 * (pltpu.roll(here, nz - 1, 1) - pltpu.roll(here, 1, 1))
                gx = gx.astype(jnp.bfloat16).astype(jnp.float32)
                gz = gz.astype(jnp.bfloat16).astype(jnp.float32)
                wts[r, block, pl.ds(c * nz, nz)] = (weight * here).astype(jnp.bfloat16)
                for j in range(JB):
                    total = phi[0][j : j + 1] * gx + phi[2][j : j + 1] * gz
                    adv[r, pl.ds((2 * j + half) * nk, nk), pl.ds(c * nz, nz)] = total.astype(jnp.bfloat16)
    total = dot_nt(adv[0], wts[0])
    for r in range(1, rows):
        total = total + dot_nt(adv[r], wts[r])
    acc_ref[...] = total
    quarter = rows // 2
    for r in range(quarter):
        w0_ref[r] = wts[quarter * q + r]


def cross_kernel(classes_of, chunk, planes, has_weighted, own_ref, other_ref, *refs):
    first_ref, second_ref, xc_ref, zc_ref, w0_ref, jb_ref, acc_ref, *refs = refs
    if has_weighted:
        wts, keep_ref, send_ref, adv = refs
    else:
        keep_ref, send_ref, wts, adv = refs
    m = lax.axis_index("modes")
    plane = lax.axis_index("space")
    q = lax.rem(plane, 2)
    sigma = jnp.where(q == 0, 0.5, -0.5)
    inside = jnp.where(jnp.logical_or(plane == 1, plane == planes - 2), 0.0, 1.0)
    x_came = x_first(jnp.bitwise_xor(plane, 1), planes)

    def xs_rows(rows):
        return jnp.where(x_came, first_ref[rows, :], second_ref[rows, :])

    def zs_rows(rows):
        return jnp.where(x_came, second_ref[rows, :], first_ref[rows, :])

    rows, comps, nk, nz = own_ref.shape
    quarter = (rows - 2) // 2
    span = quarter * comps * nz
    pick = picks(jb_ref, m, nk)
    classes = [pl.multiple_of(chunk * cls, chunk) for cls in classes_of(plane)]
    if not has_weighted:
        w1 = received_weights(xc_ref, quarter * comps * nk, quarter)
        w2 = [inside * weight for weight in received_weights(zc_ref, quarter * comps * nk, quarter)]
        for r in range(quarter):
            wts[:, pl.ds(r * comps * nz, comps * nz)] = w0_ref[r]
            for c in range(comps):
                lane = (r * comps + c) * nz
                src = pl.ds((r * comps + c) * nk, nk)
                for half, (f1, f2) in enumerate(
                    ((xs_rows(src), zs_rows(src)), (xc_ref[src, :], zc_ref[src, :]))
                ):
                    block = pl.ds(half * nk, nk)
                    for part, (field, weight) in enumerate(((f1, w1[r]), (f2, w2[r])), 1):
                        wts[block, pl.ds(part * span + lane, nz)] = (
                            weight * field.astype(jnp.float32)
                        ).astype(jnp.bfloat16)
    phis = []
    for r in range(quarter):
        row0 = 1 + quarter * q + r
        along = (r * comps + 1) * nk

        def moved(at):
            return pl.ds(pl.multiple_of(along + at.start, 16), at.size)

        phi0 = sigma * picked(
            pick, lambda at: own_ref[row0, 1, at, :], lambda at: other_ref[row0, 1, at, :]
        )
        phi1 = sigma * picked(pick, lambda at: xs_rows(moved(at)), lambda at: xc_ref[moved(at), :])
        phi2 = -sigma * picked(pick, lambda at: zs_rows(moved(at)), lambda at: zc_ref[moved(at), :])
        phis.append([[spread(phi[j : j + 1]) for j in range(JB)] for phi in (phi0, phi1, phi2)])
    inside = inside.astype(jnp.bfloat16)
    for at, cls in enumerate(classes):
        for r in range(quarter):
            row0 = 1 + quarter * q + r
            phi0, phi1, phi2 = phis[r]
            for c in range(comps):
                lane = (r * comps + c) * nz
                src = (r * comps + c) * nk
                rows_at = pl.ds(pl.multiple_of(src + cls, 16), chunk)
                for half, (p0, f1, f2) in enumerate(
                    (
                        (own_ref, xs_rows(rows_at), zs_rows(rows_at)),
                        (other_ref, xc_ref[rows_at, :], zc_ref[rows_at, :]),
                    )
                ):
                    f0 = p0[row0, c, pl.ds(cls, chunk), :]
                    gy = inside * f2 - f0
                    for j in range(JB):
                        here = pl.ds((half * JB + j) * chunk, chunk)
                        adv[at, here, pl.ds(lane, nz)] = scaled(phi0[j], f1)
                        adv[at, here, pl.ds(span + lane, nz)] = scaled(phi1[j], gy)
                        adv[at, here, pl.ds(2 * span + lane, nz)] = scaled(phi2[j], f1)
        total = dot_nt(adv[at], wts[...])
        for half in range(2):
            level = m if half == 0 else 1 - m
            for j in range(JB):
                first = (half * JB + j) * chunk
                piece = total[first : first + chunk] + acc_ref[pl.ds((2 * j + half) * nk + cls, chunk), :]
                keep_ref[at, level, j] = piece[:, :nk]
                send_ref[at, level, j] = piece[:, nk:].astype(jnp.bfloat16)


def near_kernel(keep_ref, got_ref, *out_refs):
    for at, ref in enumerate(out_refs):
        ref[...] = (keep_ref[at] + got_ref[at].astype(jnp.float32)).astype(ref.dtype)


def far_kernel(mine_ref, *refs):
    *parts, keep_ref, send_ref = refs
    level = lax.div(lax.axis_index("space"), NEAR)
    for ref, at in ((keep_ref, level), (send_ref, 1 - level)):
        total = mine_ref[at]
        for part in parts:
            total = total + part[at].astype(jnp.float32)
        ref[...] = total.astype(ref.dtype)


def total_kernel(keep_ref, got_ref, out_ref):
    total = keep_ref[...] + got_ref[...].astype(jnp.float32)
    for j in range(JB):
        out_ref[:, j, :] = total[j]


def on_device(n, modes, weight_ids, weight_table, j_block):
    nk, comps, _, nx, nz = modes.shape
    bf16, f32 = jnp.bfloat16, jnp.float32
    vmem = pl.BlockSpec(memory_space=pltpu.VMEM)
    smem = pl.BlockSpec(memory_space=pltpu.SMEM)
    params = pltpu.CompilerParams(vmem_limit_bytes=VMEM_LIMIT)
    six = nx // 2 + 2
    quarter = nx // 4
    body = quarter * comps * nk
    own, to_core, first, second, xc, zc = pl.pallas_call(
        functools.partial(prep_kernel, n),
        out_shape=[jax.ShapeDtypeStruct((six, comps, nk, nz), bf16)] * 2
        + [jax.ShapeDtypeStruct((body + PADROWS, nz), bf16)] * 2
        + [jax.ShapeDtypeStruct((body, nz), bf16)] * 2,
        in_specs=[pl.BlockSpec(memory_space=pltpu.HBM)],
        out_specs=[vmem] * 6,
        scratch_shapes=[
            pltpu.VMEM(modes.shape, bf16),
            pltpu.VMEM((nx, comps, nk, nz), bf16),
            pltpu.SemaphoreType.DMA((LOADS,)),
        ],
        compiler_params=pltpu.CompilerParams(vmem_limit_bytes=PREP_LIMIT),
        cost_estimate=pl.CostEstimate(flops=1_500_000_000, bytes_accessed=2_800_000, transcendentals=0),
        name="prep",
    )(modes)

    both = ("space", "modes")
    x_to = lambda s: s ^ 1
    z_to = lambda s: s + 2 if s % 2 else s - 2
    x_now = [n != 8 or X_FIRST >> s & 1 for s in range(n)]
    firsts = [(s, x_to(s) if x_now[s] else z_to(s)) for s in range(n)]
    seconds = [(s, z_to(s) % n if x_now[s] else x_to(s)) for s in range(n)]
    same = lambda pairs: [(2 * a + m, 2 * b + m) for a, b in pairs for m in range(2)]
    cross = lambda pairs: [(2 * a + m, 2 * b + 1 - m) for a, b in pairs for m in range(2)]
    other = lax.ppermute(to_core, "modes", [(0, 1), (1, 0)])
    first = lax.ppermute(first, both, same(firsts))
    second = lax.ppermute(second, both, same(seconds))
    weight, xc, zc = pl.pallas_call(
        weights_kernel,
        out_shape=[jax.ShapeDtypeStruct((nx, nz), f32)]
        + [jax.ShapeDtypeStruct((body + 8 * quarter, nz), bf16)] * 2,
        in_specs=[vmem] * 4 + [pl.BlockSpec(memory_space=pl.ANY)],
        out_specs=[vmem] * 3,
        compiler_params=params,
        name="weights",
    )(weight_ids, weight_table.reshape(1, NW), xc, zc, other)
    xc = lax.ppermute(xc, both, cross([(s, x_to(s)) for s in range(n)]))
    zc = lax.ppermute(zc, both, cross([(s, z_to(s)) for s in range(n) if 0 <= z_to(s) < n]))

    depth = quarter * comps * nz
    acc, w0 = pl.pallas_call(
        local_kernel,
        out_shape=[
            jax.ShapeDtypeStruct((JB * 2 * nk, 2 * nk), f32),
            jax.ShapeDtypeStruct((quarter, 2 * nk, comps * nz), bf16),
        ],
        in_specs=[vmem, vmem, vmem, smem],
        out_specs=[vmem] * 2,
        scratch_shapes=[
            pltpu.VMEM((2 * quarter, JB * 2 * nk, comps * nz), bf16),
            pltpu.VMEM((2 * quarter, 2 * nk, comps * nz), bf16),
        ],
        compiler_params=params,
        cost_estimate=pl.CostEstimate(flops=900_000_000, bytes_accessed=2_400_000, transcendentals=0),
        name="local",
    )(own, other, weight, j_block)

    per_target = 2 * nk // n
    chunk = max(16, per_target)

    def crossed(count, classes_of, weighted):
        piece = (count, 2, JB, chunk, nk)
        out_shape = [jax.ShapeDtypeStruct(piece, f32), jax.ShapeDtypeStruct(piece, bf16)]
        if not weighted:
            out_shape.append(jax.ShapeDtypeStruct((2 * nk, 3 * depth), bf16))
        return pl.pallas_call(
            functools.partial(cross_kernel, classes_of, chunk, n, bool(weighted)),
            out_shape=out_shape,
            in_specs=[vmem] * 7 + [smem] + [vmem] * (1 + len(weighted)),
            out_specs=[vmem] * len(out_shape),
            scratch_shapes=[pltpu.VMEM((count, 2 * JB * chunk, 3 * depth), bf16)],
            compiler_params=params,
            cost_estimate=pl.CostEstimate(
                flops=900_000_000, bytes_accessed=4_000_000, transcendentals=0
            ),
            name="cross",
        )(own, other, first, second, xc, zc, w0, j_block, acc, *weighted)

    swap = [(0, 1), (1, 0)]
    if n == 2 * NEAR:
        def partners(*steps):
            return lambda s: [jnp.bitwise_xor(lax.rem(s, NEAR), step) for step in steps]

        keep_a, send_a, w2 = crossed(2, partners(3, 1), ())
        got_a = lax.ppermute(send_a, "modes", swap)
        keep_b, send_b = crossed(2, partners(0, 2), (w2,))
        got_b = lax.ppermute(send_b, "modes", swap)
        piece = (JB, chunk, nk)

        def summed(kinds, keep, got):
            return pl.pallas_call(
                near_kernel,
                out_shape=[jax.ShapeDtypeStruct((2, *piece), kind) for kind in kinds],
                in_specs=[vmem] * 2,
                out_specs=[vmem] * 2,
                compiler_params=params,
                name="near",
            )(keep, got)

        part_3, part_1 = summed((bf16, bf16), keep_a, got_a)
        mine, part_2 = summed((f32, bf16), keep_b, got_b)
        parts = [
            lax.ppermute(part, "space", [(s, s ^ step) for s in range(n)])
            for part, step in ((part_3, 3), (part_1, 1), (part_2, 2))
        ]
        keep, send = pl.pallas_call(
            far_kernel,
            out_shape=[jax.ShapeDtypeStruct(piece, f32), jax.ShapeDtypeStruct(piece, bf16)],
            in_specs=[vmem] * NEAR,
            out_specs=[vmem] * 2,
            compiler_params=params,
            name="far",
        )(mine, *parts)
        got = lax.ppermute(send, "space", [(s, s ^ NEAR) for s in range(n)])
        return pl.pallas_call(
            total_kernel,
            out_shape=jax.ShapeDtypeStruct((chunk, JB, nk), f32),
            in_specs=[vmem] * 2,
            out_specs=vmem,
            compiler_params=params,
            name="total",
        )(keep, got)

    count = nk // chunk
    keep, send, _ = crossed(count, lambda s: list(range(count)), ())
    share = (keep + lax.ppermute(send, "modes", swap)).astype(bf16)
    share = share.reshape(count, 2, JB, chunk // per_target, per_target, nk)
    share = share.transpose(1, 0, 3, 2, 4, 5).reshape(n, JB, per_target, nk)
    parts = lax.all_to_all(share, "space", 0, 0, tiled=True)
    return jnp.sum(parts.astype(f32), axis=0).transpose(1, 0, 2)


def solution(mesh):
    return jax.shard_map(
        functools.partial(on_device, mesh.shape["space"]),
        mesh=mesh,
        in_specs=(
            P("modes", None, ("groups", "space"), None, None),
            P(("groups", "space"), None, None),
            P(),
            P("groups"),
        ),
        out_specs=P(("groups", "space"), None, "modes"),
        check_vma=False,
    )
```

```python
import functools

import jax
import jax.numpy as jnp
from jax import lax
from jax.experimental import pallas as pl
from jax.experimental.pallas import tpu as pltpu
from jax.sharding import PartitionSpec as P

JB = 4
NW = 16
PADROWS = 16
LOADS = 4
X_FIRST = 0b10011111
NEAR = 4
VMEM_LIMIT = 48 * 1024 * 1024
PREP_LIMIT = 53_100 * 1024


def x_first(s, planes):
    if planes != 8:
        return s >= 0
    return lax.rem(lax.shift_right_logical(X_FIRST, s), 2) == 1


def prep_kernel(
    planes, modes_hbm, own_ref, core_ref, first_ref, second_ref, xc_ref, zc_ref, modes_ref, tr, sems
):
    m = lax.axis_index("modes")
    s = lax.axis_index("space")
    q = lax.rem(s, 2)
    to_x, to_z = 2 * m + 1 - q, 2 * m + q
    x_now = x_first(s, planes)
    nk, comps, _, nx, nz = modes_hbm.shape
    step = nk // LOADS
    copies = [
        pltpu.make_async_copy(
            modes_hbm.at[pl.ds(p * step, step)], modes_ref.at[pl.ds(p * step, step)], sems.at[p]
        )
        for p in range(LOADS)
    ]
    for copy in copies:
        copy.start()
    for p in range(LOADS):
        copies[p].wait()
        block = pl.ds(p * step, step)
        for c in range(comps):
            value = modes_ref[block, c, 0].astype(jnp.float32)
            tr[:, c, block] = jnp.swapaxes(value, 0, 1).astype(jnp.bfloat16)
    quarter = nx // 4
    for r in range(nx // 2 + 2):
        own_ref[r] = tr[lax.rem(nx // 2 * m + nx - 1 + r, nx)]
        core_ref[r] = tr[lax.rem(nx // 2 * (1 - m) + nx - 1 + r, nx)]
    for ref, at in (
        (first_ref, jnp.where(x_now, to_x, to_z)),
        (second_ref, jnp.where(x_now, to_z, to_x)),
        (xc_ref, 2 * (1 - m) + 1 - q),
        (zc_ref, 2 * (1 - m) + q),
    ):
        for row in range(quarter):
            for c in range(comps):
                ref[pl.ds((row * comps + c) * nk, nk), :] = tr[at * quarter + row, c]
    for ref in (first_ref, second_ref):
        pad = ref.shape[0] - quarter * comps * nk
        ref[pl.ds(quarter * comps * nk, pad), :] = jnp.zeros((pad, nz), jnp.bfloat16)


def weights_kernel(ids_ref, table_ref, xc_ref, zc_ref, _, weight_ref, xc_out, zc_out):
    m = lax.axis_index("modes")
    q = lax.rem(lax.axis_index("space"), 2)
    body, nz = xc_ref.shape
    nx = ids_ref.shape[1]
    quarter = nx // 4
    table = table_ref[...]
    weight = jnp.zeros((nx, nz), jnp.float32)
    for entry in range(NW):
        weight = jnp.where(ids_ref[0] == entry, table[:, entry : entry + 1], weight)
    weight_ref[...] = weight
    for ref, out, at in ((zc_ref, zc_out, 2 * (1 - m) + q), (xc_ref, xc_out, 2 * (1 - m) + 1 - q)):
        out[pl.ds(0, body), :] = ref[...]
        rest = jnp.concatenate(
            [
                jnp.broadcast_to(weight_ref[pl.ds(at * quarter + row, 1), :], (8, nz))
                for row in range(quarter)
            ],
            axis=0,
        )
        piece_of = lax.rem(lax.broadcasted_iota(jnp.int32, rest.shape, 0), 8)
        pieces = jnp.zeros(rest.shape, jnp.float32)
        for piece in range(3):
            rounded = rest.astype(jnp.bfloat16).astype(jnp.float32)
            pieces = jnp.where(piece_of == piece, rounded, pieces)
            rest = rest - rounded
        out[pl.ds(body, 8 * quarter), :] = pieces.astype(jnp.bfloat16)


def received_weights(ref, first, quarter):
    pieces = ref[pl.ds(first, 8 * quarter), :].astype(jnp.float32)
    return [
        pieces[8 * r : 8 * r + 1] + pieces[8 * r + 1 : 8 * r + 2] + pieces[8 * r + 2 : 8 * r + 3]
        for r in range(quarter)
    ]


def picks(jb_ref, m, nk):
    first = jb_ref[0] * JB
    owner = (first >= nk).astype(jnp.int32)
    row = first - owner * nk
    within = lax.rem(row, 16)
    return owner == m, pl.multiple_of(row - within, 16), within


def picked(pick, own, other):
    mine, block, within = pick
    rows = pl.ds(block, 16)
    rows = jnp.where(mine, own(rows).astype(jnp.float32), other(rows).astype(jnp.float32))
    result = rows[0:JB]
    for start in range(JB, 16, JB):
        result = jnp.where(within == start, rows[start : start + JB], result)
    return result


def spread(row):
    return jnp.broadcast_to(row, (16, row.shape[1])).astype(jnp.bfloat16)[None]


def scaled(tile, field):
    rows, lanes = field.shape
    return (tile * field.reshape(rows // 16, 16, lanes)).reshape(rows, lanes)


def dot_nt(a, b):
    return lax.dot_general(a, b, (((1,), (1,)), ((), ())), preferred_element_type=jnp.float32)


def local_kernel(own_ref, other_ref, weight_ref, jb_ref, acc_ref, w0_ref, adv, wts):
    m = lax.axis_index("modes")
    q = lax.rem(lax.axis_index("space"), 2)
    rows, comps, nk, nz = own_ref.shape
    rows -= 2
    pick = picks(jb_ref, m, nk)
    for r in range(rows):
        phi = [picked(pick, lambda at: own_ref[r + 1, d, at, :], lambda at: other_ref[r + 1, d, at, :]) for d in range(comps)]
        weight = weight_ref[pl.ds(rows * m + r, 1), :]
        for c in range(comps):
            for half, ref in enumerate((own_ref, other_ref)):
                block = pl.ds(half * nk, nk)
                here = ref[r + 1, c].astype(jnp.float32)
                gx = 0.5 * (ref[r + 2, c].astype(jnp.float32) - ref[r, c].astype(jnp.float32))
                gz = 0.5 * (pltpu.roll(here, nz - 1, 1) - pltpu.roll(here, 1, 1))
                gx = gx.astype(jnp.bfloat16).astype(jnp.float32)
                gz = gz.astype(jnp.bfloat16).astype(jnp.float32)
                wts[r, block, pl.ds(c * nz, nz)] = (weight * here).astype(jnp.bfloat16)
                for j in range(JB):
                    total = phi[0][j : j + 1] * gx + phi[2][j : j + 1] * gz
                    adv[r, pl.ds((2 * j + half) * nk, nk), pl.ds(c * nz, nz)] = total.astype(jnp.bfloat16)
    total = dot_nt(adv[0], wts[0])
    for r in range(1, rows):
        total = total + dot_nt(adv[r], wts[r])
    acc_ref[...] = total
    quarter = rows // 2
    for r in range(quarter):
        w0_ref[r] = wts[quarter * q + r]


def cross_kernel(classes_of, chunk, planes, has_weighted, own_ref, other_ref, *refs):
    first_ref, second_ref, xc_ref, zc_ref, w0_ref, jb_ref, acc_ref, *refs = refs
    if has_weighted:
        wts, keep_ref, send_ref, adv = refs
    else:
        keep_ref, send_ref, wts, adv = refs
    m = lax.axis_index("modes")
    plane = lax.axis_index("space")
    q = lax.rem(plane, 2)
    sigma = jnp.where(q == 0, 0.5, -0.5)
    inside = jnp.where(jnp.logical_or(plane == 1, plane == planes - 2), 0.0, 1.0)
    x_came = x_first(jnp.bitwise_xor(plane, 1), planes)

    def xs_rows(rows):
        return jnp.where(x_came, first_ref[rows, :], second_ref[rows, :])

    def zs_rows(rows):
        return jnp.where(x_came, second_ref[rows, :], first_ref[rows, :])

    rows, comps, nk, nz = own_ref.shape
    quarter = (rows - 2) // 2
    span = quarter * comps * nz
    pick = picks(jb_ref, m, nk)
    classes = [pl.multiple_of(chunk * cls, chunk) for cls in classes_of(plane)]
    if not has_weighted:
        w1 = received_weights(xc_ref, quarter * comps * nk, quarter)
        w2 = [inside * weight for weight in received_weights(zc_ref, quarter * comps * nk, quarter)]
        for r in range(quarter):
            wts[:, pl.ds(r * comps * nz, comps * nz)] = w0_ref[r]
            for c in range(comps):
                lane = (r * comps + c) * nz
                src = pl.ds((r * comps + c) * nk, nk)
                for half, (f1, f2) in enumerate(
                    ((xs_rows(src), zs_rows(src)), (xc_ref[src, :], zc_ref[src, :]))
                ):
                    block = pl.ds(half * nk, nk)
                    for part, (field, weight) in enumerate(((f1, w1[r]), (f2, w2[r])), 1):
                        wts[block, pl.ds(part * span + lane, nz)] = (
                            weight * field.astype(jnp.float32)
                        ).astype(jnp.bfloat16)
    phis = []
    for r in range(quarter):
        row0 = 1 + quarter * q + r
        along = (r * comps + 1) * nk

        def moved(at):
            return pl.ds(pl.multiple_of(along + at.start, 16), at.size)

        phi0 = sigma * picked(
            pick, lambda at: own_ref[row0, 1, at, :], lambda at: other_ref[row0, 1, at, :]
        )
        phi1 = sigma * picked(pick, lambda at: xs_rows(moved(at)), lambda at: xc_ref[moved(at), :])
        phi2 = -sigma * picked(pick, lambda at: zs_rows(moved(at)), lambda at: zc_ref[moved(at), :])
        phis.append([[spread(phi[j : j + 1]) for j in range(JB)] for phi in (phi0, phi1, phi2)])
    inside = inside.astype(jnp.bfloat16)
    for at, cls in enumerate(classes):
        for r in range(quarter):
            row0 = 1 + quarter * q + r
            phi0, phi1, phi2 = phis[r]
            for c in range(comps):
                lane = (r * comps + c) * nz
                src = (r * comps + c) * nk
                rows_at = pl.ds(pl.multiple_of(src + cls, 16), chunk)
                for half, (p0, f1, f2) in enumerate(
                    (
                        (own_ref, xs_rows(rows_at), zs_rows(rows_at)),
                        (other_ref, xc_ref[rows_at, :], zc_ref[rows_at, :]),
                    )
                ):
                    f0 = p0[row0, c, pl.ds(cls, chunk), :]
                    gy = inside * f2 - f0
                    for j in range(JB):
                        here = pl.ds((half * JB + j) * chunk, chunk)
                        adv[at, here, pl.ds(lane, nz)] = scaled(phi0[j], f1)
                        adv[at, here, pl.ds(span + lane, nz)] = scaled(phi1[j], gy)
                        adv[at, here, pl.ds(2 * span + lane, nz)] = scaled(phi2[j], f1)
        total = dot_nt(adv[at], wts[...])
        for half in range(2):
            level = m if half == 0 else 1 - m
            for j in range(JB):
                first = (half * JB + j) * chunk
                piece = total[first : first + chunk] + acc_ref[pl.ds((2 * j + half) * nk + cls, chunk), :]
                keep_ref[at, level, j] = piece[:, :nk]
                send_ref[at, level, j] = piece[:, nk:].astype(jnp.bfloat16)


def near_kernel(by_core, keep_ref, got_ref, *out_refs):
    first_core = lax.axis_index("modes") == 0
    totals = [keep_ref[at] + got_ref[at].astype(jnp.float32) for at in range(2)]
    for at, ref in enumerate(out_refs):
        total = jnp.where(first_core, totals[at], totals[1 - at]) if by_core else totals[at]
        ref[...] = total.astype(ref.dtype)


def far_kernel(mine_ref, *refs):
    *parts, keep_ref, send_ref = refs
    level = lax.div(lax.axis_index("space"), NEAR)
    for ref, at in ((keep_ref, level), (send_ref, 1 - level)):
        total = mine_ref[at]
        for part in parts:
            total = total + part[at].astype(jnp.float32)
        ref[...] = total.astype(ref.dtype)


def total_kernel(keep_ref, got_ref, out_ref):
    total = keep_ref[...] + got_ref[...].astype(jnp.float32)
    for j in range(JB):
        out_ref[:, j, :] = total[j]


def on_device(n, modes, weight_ids, weight_table, j_block):
    nk, comps, _, nx, nz = modes.shape
    bf16, f32 = jnp.bfloat16, jnp.float32
    vmem = pl.BlockSpec(memory_space=pltpu.VMEM)
    smem = pl.BlockSpec(memory_space=pltpu.SMEM)
    params = pltpu.CompilerParams(vmem_limit_bytes=VMEM_LIMIT)
    six = nx // 2 + 2
    quarter = nx // 4
    body = quarter * comps * nk
    own, to_core, first, second, xc, zc = pl.pallas_call(
        functools.partial(prep_kernel, n),
        out_shape=[jax.ShapeDtypeStruct((six, comps, nk, nz), bf16)] * 2
        + [jax.ShapeDtypeStruct((body + PADROWS, nz), bf16)] * 2
        + [jax.ShapeDtypeStruct((body, nz), bf16)] * 2,
        in_specs=[pl.BlockSpec(memory_space=pltpu.HBM)],
        out_specs=[vmem] * 6,
        scratch_shapes=[
            pltpu.VMEM(modes.shape, bf16),
            pltpu.VMEM((nx, comps, nk, nz), bf16),
            pltpu.SemaphoreType.DMA((LOADS,)),
        ],
        compiler_params=pltpu.CompilerParams(vmem_limit_bytes=PREP_LIMIT),
        cost_estimate=pl.CostEstimate(flops=1_500_000_000, bytes_accessed=2_800_000, transcendentals=0),
        name="prep",
    )(modes)

    both = ("space", "modes")
    x_to = lambda s: s ^ 1
    z_to = lambda s: s + 2 if s % 2 else s - 2
    x_now = [n != 8 or X_FIRST >> s & 1 for s in range(n)]
    firsts = [(s, x_to(s) if x_now[s] else z_to(s)) for s in range(n)]
    seconds = [(s, z_to(s) % n if x_now[s] else x_to(s)) for s in range(n)]
    same = lambda pairs: [(2 * a + m, 2 * b + m) for a, b in pairs for m in range(2)]
    cross = lambda pairs: [(2 * a + m, 2 * b + 1 - m) for a, b in pairs for m in range(2)]
    other = lax.ppermute(to_core, "modes", [(0, 1), (1, 0)])
    first = lax.ppermute(first, both, same(firsts))
    second = lax.ppermute(second, both, same(seconds))
    weight, xc, zc = pl.pallas_call(
        weights_kernel,
        out_shape=[jax.ShapeDtypeStruct((nx, nz), f32)]
        + [jax.ShapeDtypeStruct((body + 8 * quarter, nz), bf16)] * 2,
        in_specs=[vmem] * 4 + [pl.BlockSpec(memory_space=pl.ANY)],
        out_specs=[vmem] * 3,
        compiler_params=params,
        name="weights",
    )(weight_ids, weight_table.reshape(1, NW), xc, zc, other)
    xc = lax.ppermute(xc, both, cross([(s, x_to(s)) for s in range(n)]))
    zc = lax.ppermute(zc, both, cross([(s, z_to(s)) for s in range(n) if 0 <= z_to(s) < n]))

    depth = quarter * comps * nz
    acc, w0 = pl.pallas_call(
        local_kernel,
        out_shape=[
            jax.ShapeDtypeStruct((JB * 2 * nk, 2 * nk), f32),
            jax.ShapeDtypeStruct((quarter, 2 * nk, comps * nz), bf16),
        ],
        in_specs=[vmem, vmem, vmem, smem],
        out_specs=[vmem] * 2,
        scratch_shapes=[
            pltpu.VMEM((2 * quarter, JB * 2 * nk, comps * nz), bf16),
            pltpu.VMEM((2 * quarter, 2 * nk, comps * nz), bf16),
        ],
        compiler_params=params,
        cost_estimate=pl.CostEstimate(flops=900_000_000, bytes_accessed=2_400_000, transcendentals=0),
        name="local",
    )(own, other, weight, j_block)

    per_target = 2 * nk // n
    chunk = max(16, per_target)

    def crossed(count, classes_of, weighted):
        piece = (count, 2, JB, chunk, nk)
        out_shape = [jax.ShapeDtypeStruct(piece, f32), jax.ShapeDtypeStruct(piece, bf16)]
        if not weighted:
            out_shape.append(jax.ShapeDtypeStruct((2 * nk, 3 * depth), bf16))
        return pl.pallas_call(
            functools.partial(cross_kernel, classes_of, chunk, n, bool(weighted)),
            out_shape=out_shape,
            in_specs=[vmem] * 7 + [smem] + [vmem] * (1 + len(weighted)),
            out_specs=[vmem] * len(out_shape),
            scratch_shapes=[pltpu.VMEM((count, 2 * JB * chunk, 3 * depth), bf16)],
            compiler_params=params,
            cost_estimate=pl.CostEstimate(
                flops=900_000_000, bytes_accessed=4_000_000, transcendentals=0
            ),
            name="cross",
        )(own, other, first, second, xc, zc, w0, j_block, acc, *weighted)

    swap = [(0, 1), (1, 0)]
    if n == 2 * NEAR:
        def partners(*steps):
            return lambda s: [jnp.bitwise_xor(lax.rem(s, NEAR), step) for step in steps]

        keep_a, send_a, w2 = crossed(2, partners(3, 1), ())
        got_a = lax.ppermute(send_a, "modes", swap)
        keep_b, send_b = crossed(2, partners(0, 2), (w2,))
        got_b = lax.ppermute(send_b, "modes", swap)
        piece = (JB, chunk, nk)

        def summed(by_core, kinds, keep, got):
            return pl.pallas_call(
                functools.partial(near_kernel, by_core),
                out_shape=[jax.ShapeDtypeStruct((2, *piece), kind) for kind in kinds],
                in_specs=[vmem] * 2,
                out_specs=[vmem] * 2,
                compiler_params=params,
                name="near",
            )(keep, got)

        out_0, out_1 = summed(True, (bf16, bf16), keep_a, got_a)
        mine, out_2 = summed(False, (f32, bf16), keep_b, got_b)
        parts = [
            lax.ppermute(
                part, both, [(2 * s + m, 2 * (s ^ steps[m]) + m) for s in range(n) for m in range(2)]
            )
            for part, steps in ((out_0, (3, 1)), (out_1, (1, 3)), (out_2, (2, 2)))
        ]
        keep, send = pl.pallas_call(
            far_kernel,
            out_shape=[jax.ShapeDtypeStruct(piece, f32), jax.ShapeDtypeStruct(piece, bf16)],
            in_specs=[vmem] * NEAR,
            out_specs=[vmem] * 2,
            compiler_params=params,
            name="far",
        )(mine, *parts)
        got = lax.ppermute(send, "space", [(s, s ^ NEAR) for s in range(n)])
        return pl.pallas_call(
            total_kernel,
            out_shape=jax.ShapeDtypeStruct((chunk, JB, nk), f32),
            in_specs=[vmem] * 2,
            out_specs=vmem,
            compiler_params=params,
            name="total",
        )(keep, got)

    count = nk // chunk
    keep, send, _ = crossed(count, lambda s: list(range(count)), ())
    share = (keep + lax.ppermute(send, "modes", swap)).astype(bf16)
    share = share.reshape(count, 2, JB, chunk // per_target, per_target, nk)
    share = share.transpose(1, 0, 3, 2, 4, 5).reshape(n, JB, per_target, nk)
    parts = lax.all_to_all(share, "space", 0, 0, tiled=True)
    return jnp.sum(parts.astype(f32), axis=0).transpose(1, 0, 2)


def solution(mesh):
    return jax.shard_map(
        functools.partial(on_device, mesh.shape["space"]),
        mesh=mesh,
        in_specs=(
            P("modes", None, ("groups", "space"), None, None),
            P(("groups", "space"), None, None),
            P(),
            P("groups"),
        ),
        out_specs=P(("groups", "space"), None, "modes"),
        check_vma=False,
    )
```

```python
import functools

import jax
import jax.numpy as jnp
from jax import lax
from jax.experimental import pallas as pl
from jax.experimental.pallas import tpu as pltpu
from jax.sharding import PartitionSpec as P

JB = 4
NW = 16
PADROWS = 16
LOADS = 4
NEAR = 4
VMEM_LIMIT = 48 * 1024 * 1024
PREP_LIMIT = 53_100 * 1024


def prep_kernel(modes_hbm, own_ref, core_ref, xs_ref, zs_ref, xc_ref, zc_ref, modes_ref, tr, sems):
    m = lax.axis_index("modes")
    q = lax.rem(lax.axis_index("space"), 2)
    nk, comps, _, nx, nz = modes_hbm.shape
    step = nk // LOADS
    copies = [
        pltpu.make_async_copy(
            modes_hbm.at[pl.ds(p * step, step)], modes_ref.at[pl.ds(p * step, step)], sems.at[p]
        )
        for p in range(LOADS)
    ]
    for copy in copies:
        copy.start()
    for p in range(LOADS):
        copies[p].wait()
        block = pl.ds(p * step, step)
        for c in range(comps):
            value = modes_ref[block, c, 0].astype(jnp.float32)
            tr[:, c, block] = jnp.swapaxes(value, 0, 1).astype(jnp.bfloat16)
    quarter = nx // 4
    for r in range(nx // 2 + 2):
        own_ref[r] = tr[lax.rem(nx // 2 * m + nx - 1 + r, nx)]
        core_ref[r] = tr[lax.rem(nx // 2 * (1 - m) + nx - 1 + r, nx)]
    for ref, at in (
        (xs_ref, 2 * m + 1 - q),
        (xc_ref, 2 * (1 - m) + 1 - q),
        (zs_ref, 2 * m + q),
        (zc_ref, 2 * (1 - m) + q),
    ):
        for row in range(quarter):
            for c in range(comps):
                ref[pl.ds((row * comps + c) * nk, nk), :] = tr[at * quarter + row, c]
    for ref in (zs_ref, xs_ref):
        pad = ref.shape[0] - quarter * comps * nk
        ref[pl.ds(quarter * comps * nk, pad), :] = jnp.zeros((pad, nz), jnp.bfloat16)


def weights_kernel(ids_ref, table_ref, xc_ref, zc_ref, _, weight_ref, xc_out, zc_out):
    m = lax.axis_index("modes")
    q = lax.rem(lax.axis_index("space"), 2)
    body, nz = xc_ref.shape
    nx = ids_ref.shape[1]
    quarter = nx // 4
    table = table_ref[...]
    weight = jnp.zeros((nx, nz), jnp.float32)
    for entry in range(NW):
        weight = jnp.where(ids_ref[0] == entry, table[0:1, entry : entry + 1], weight)
    weight_ref[...] = weight
    for ref, out, at in ((zc_ref, zc_out, 2 * (1 - m) + q), (xc_ref, xc_out, 2 * (1 - m) + 1 - q)):
        out[pl.ds(0, body), :] = ref[...]
        rest = jnp.concatenate(
            [
                jnp.broadcast_to(weight_ref[pl.ds(at * quarter + row, 1), :], (8, nz))
                for row in range(quarter)
            ],
            axis=0,
        )
        piece_of = lax.rem(lax.broadcasted_iota(jnp.int32, rest.shape, 0), 8)
        pieces = jnp.zeros(rest.shape, jnp.float32)
        for piece in range(3):
            rounded = rest.astype(jnp.bfloat16).astype(jnp.float32)
            pieces = jnp.where(piece_of == piece, rounded, pieces)
            rest = rest - rounded
        out[pl.ds(body, 8 * quarter), :] = pieces.astype(jnp.bfloat16)


def received_weights(ref, first, quarter):
    pieces = ref[pl.ds(first, 8 * quarter), :].astype(jnp.float32)
    return [
        pieces[8 * r : 8 * r + 1] + pieces[8 * r + 1 : 8 * r + 2] + pieces[8 * r + 2 : 8 * r + 3]
        for r in range(quarter)
    ]


def picks(jb_ref, m, nk):
    first = jb_ref[0] * JB
    owner = (first >= nk).astype(jnp.int32)
    row = first - owner * nk
    within = lax.rem(row, 16)
    return owner == m, pl.multiple_of(row - within, 16), within


def picked(pick, own, other):
    mine, block, within = pick
    rows = jnp.where(
        mine, own[pl.ds(block, 16), :].astype(jnp.float32), other[pl.ds(block, 16), :].astype(jnp.float32)
    )
    result = rows[0:JB]
    for start in range(JB, 16, JB):
        result = jnp.where(within == start, rows[start : start + JB], result)
    return result


def spread(row):
    return jnp.broadcast_to(row, (16, row.shape[1])).astype(jnp.bfloat16)[None]


def scaled(tile, field):
    rows, lanes = field.shape
    return (tile * field.reshape(rows // 16, 16, lanes)).reshape(rows, lanes)


def dot_nt(a, b):
    return lax.dot_general(a, b, (((1,), (1,)), ((), ())), preferred_element_type=jnp.float32)


def local_kernel(own_ref, other_ref, weight_ref, jb_ref, acc_ref, w0_ref, adv, wts):
    m = lax.axis_index("modes")
    q = lax.rem(lax.axis_index("space"), 2)
    rows, comps, nk, nz = own_ref.shape
    rows -= 2
    pick = picks(jb_ref, m, nk)
    for r in range(rows):
        phi = [picked(pick, own_ref.at[r + 1, d], other_ref.at[r + 1, d]) for d in range(comps)]
        weight = weight_ref[pl.ds(rows * m + r, 1), :]
        for c in range(comps):
            for half, ref in enumerate((own_ref, other_ref)):
                block = pl.ds(half * nk, nk)
                here = ref[r + 1, c].astype(jnp.float32)
                gx = 0.5 * (ref[r + 2, c].astype(jnp.float32) - ref[r, c].astype(jnp.float32))
                gz = 0.5 * (pltpu.roll(here, nz - 1, 1) - pltpu.roll(here, 1, 1))
                gx = gx.astype(jnp.bfloat16).astype(jnp.float32)
                gz = gz.astype(jnp.bfloat16).astype(jnp.float32)
                wts[r, block, pl.ds(c * nz, nz)] = (weight * here).astype(jnp.bfloat16)
                for j in range(JB):
                    total = phi[0][j : j + 1] * gx + phi[2][j : j + 1] * gz
                    adv[r, pl.ds((2 * j + half) * nk, nk), pl.ds(c * nz, nz)] = total.astype(jnp.bfloat16)
    total = dot_nt(adv[0], wts[0])
    for r in range(1, rows):
        total = total + dot_nt(adv[r], wts[r])
    acc_ref[...] = total
    quarter = rows // 2
    for r in range(quarter):
        w0_ref[r] = wts[quarter * q + r]


def sign_of_plane():
    return jnp.where(lax.rem(lax.axis_index("space"), 2) == 0, 0.5, -0.5)


def early_kernel(own_ref, other_ref, xs_ref, _, xc_ref, w0_ref, jb_ref, acc_ref, out_ref, w1_ref, adv):
    m = lax.axis_index("modes")
    q = lax.rem(lax.axis_index("space"), 2)
    rows, comps, nk, nz = own_ref.shape
    quarter = (rows - 2) // 2
    pick = picks(jb_ref, m, nk)
    weights = received_weights(xc_ref, quarter * comps * nk, quarter)
    for r in range(quarter):
        row0 = 1 + quarter * q + r
        phi0 = sign_of_plane() * picked(pick, own_ref.at[row0, 1], other_ref.at[row0, 1])
        phi0 = [spread(phi0[j : j + 1]) for j in range(JB)]
        for c in range(comps):
            at = pl.ds((r * comps + c) * nz, nz)
            src = pl.ds((r * comps + c) * nk, nk)
            for half, p1 in enumerate((xs_ref, xc_ref)):
                f1 = p1[src, :]
                w1_ref[pl.ds(half * nk, nk), at] = (weights[r] * f1.astype(jnp.float32)).astype(
                    jnp.bfloat16
                )
                for j in range(JB):
                    adv[r, pl.ds((2 * j + half) * nk, nk), pl.ds(c * nz, nz)] = scaled(phi0[j], f1)
    total = acc_ref[...]
    for r in range(quarter):
        total = total + dot_nt(adv[r], w0_ref[r])
    out_ref[...] = total


def cross_kernel(classes_of, chunk, planes, has_weighted, own_ref, other_ref, *refs):
    xs_ref, zs_ref, xc_ref, zc_ref, w1_ref, jb_ref, acc_ref, *refs = refs
    if has_weighted:
        wts, keep_ref, send_ref, adv = refs
    else:
        keep_ref, send_ref, wts, adv = refs
    m = lax.axis_index("modes")
    plane = lax.axis_index("space")
    q = lax.rem(plane, 2)
    inside = jnp.where(jnp.logical_or(plane == 1, plane == planes - 2), 0.0, 1.0)
    rows, comps, nk, nz = own_ref.shape
    quarter = (rows - 2) // 2
    span = quarter * comps * nz
    pick = picks(jb_ref, m, nk)
    classes = [pl.multiple_of(chunk * cls, chunk) for cls in classes_of(plane)]
    if not has_weighted:
        weights = received_weights(zc_ref, quarter * comps * nk, quarter)
        wts[:, pl.ds(0, span)] = w1_ref[...]
        for r in range(quarter):
            weight = inside * weights[r]
            for c in range(comps):
                src = pl.ds((r * comps + c) * nk, nk)
                for half, p2 in enumerate((zs_ref, zc_ref)):
                    wts[pl.ds(half * nk, nk), pl.ds(span + (r * comps + c) * nz, nz)] = (
                        weight * p2[src, :].astype(jnp.float32)
                    ).astype(jnp.bfloat16)
    phis = []
    for r in range(quarter):
        along = pl.ds((r * comps + 1) * nk, nk)
        phi1 = sign_of_plane() * picked(pick, xs_ref.at[along], xc_ref.at[along])
        phi2 = -sign_of_plane() * picked(pick, zs_ref.at[along], zc_ref.at[along])
        phis.append([[spread(phi[j : j + 1]) for j in range(JB)] for phi in (phi1, phi2)])
    inside = inside.astype(jnp.bfloat16)
    for at, cls in enumerate(classes):
        for r in range(quarter):
            row0 = 1 + quarter * q + r
            phi1, phi2 = phis[r]
            for c in range(comps):
                lane = (r * comps + c) * nz
                src = (r * comps + c) * nk
                for half, (p0, p1, p2) in enumerate(
                    ((own_ref, xs_ref, zs_ref), (other_ref, xc_ref, zc_ref))
                ):
                    f0 = p0[row0, c, pl.ds(cls, chunk), :]
                    f1 = p1[pl.ds(src + cls, chunk), :]
                    gy = inside * p2[pl.ds(src + cls, chunk), :] - f0
                    for j in range(JB):
                        here = pl.ds((half * JB + j) * chunk, chunk)
                        adv[at, here, pl.ds(lane, nz)] = scaled(phi1[j], gy)
                        adv[at, here, pl.ds(span + lane, nz)] = scaled(phi2[j], f1)
        total = dot_nt(adv[at], wts[...])
        for half in range(2):
            level = m if half == 0 else 1 - m
            for j in range(JB):
                first = (half * JB + j) * chunk
                piece = total[first : first + chunk] + acc_ref[pl.ds((2 * j + half) * nk + cls, chunk), :]
                keep_ref[at, level, j] = piece[:, :nk]
                send_ref[at, level, j] = piece[:, nk:].astype(jnp.bfloat16)


def near_kernel(keep_ref, got_ref, *out_refs):
    for at, ref in enumerate(out_refs):
        ref[...] = (keep_ref[at] + got_ref[at].astype(jnp.float32)).astype(ref.dtype)


def far_kernel(mine_ref, *refs):
    *parts, keep_ref, send_ref = refs
    level = lax.div(lax.axis_index("space"), NEAR)
    for ref, at in ((keep_ref, level), (send_ref, 1 - level)):
        total = mine_ref[at]
        for part in parts:
            total = total + part[at].astype(jnp.float32)
        ref[...] = total.astype(ref.dtype)


def total_kernel(keep_ref, got_ref, out_ref):
    total = keep_ref[...] + got_ref[...].astype(jnp.float32)
    for j in range(JB):
        out_ref[:, j, :] = total[j]


def on_device(n, modes, weight_ids, weight_table, j_block):
    nk, comps, _, nx, nz = modes.shape
    bf16, f32 = jnp.bfloat16, jnp.float32
    vmem = pl.BlockSpec(memory_space=pltpu.VMEM)
    smem = pl.BlockSpec(memory_space=pltpu.SMEM)
    params = pltpu.CompilerParams(vmem_limit_bytes=VMEM_LIMIT)
    six = nx // 2 + 2
    quarter = nx // 4
    body = quarter * comps * nk
    own, to_core, xs, zs, xc, zc = pl.pallas_call(
        prep_kernel,
        out_shape=[jax.ShapeDtypeStruct((six, comps, nk, nz), bf16)] * 2
        + [jax.ShapeDtypeStruct((body + PADROWS, nz), bf16)] * 2
        + [jax.ShapeDtypeStruct((body, nz), bf16)] * 2,
        in_specs=[pl.BlockSpec(memory_space=pltpu.HBM)],
        out_specs=[vmem] * 6,
        scratch_shapes=[
            pltpu.VMEM(modes.shape, bf16),
            pltpu.VMEM((nx, comps, nk, nz), bf16),
            pltpu.SemaphoreType.DMA((LOADS,)),
        ],
        compiler_params=pltpu.CompilerParams(vmem_limit_bytes=PREP_LIMIT),
        cost_estimate=pl.CostEstimate(flops=1_500_000_000, bytes_accessed=2_800_000, transcendentals=0),
        name="prep",
    )(modes)

    both = ("space", "modes")
    x_pairs = [(s, s ^ 1) for s in range(n)]
    z_pairs = [(s, (s + (2 if s % 2 else -2)) % n) for s in range(n)]
    same = lambda pairs: [(2 * a + m, 2 * b + m) for a, b in pairs for m in range(2)]
    cross = lambda pairs: [(2 * a + m, 2 * b + 1 - m) for a, b in pairs for m in range(2)]
    other = lax.ppermute(to_core, "modes", [(0, 1), (1, 0)])
    xs = lax.ppermute(xs, both, same(x_pairs))
    zs = lax.ppermute(zs, both, same(z_pairs))
    weight, xc, zc = pl.pallas_call(
        weights_kernel,
        out_shape=[jax.ShapeDtypeStruct((nx, nz), f32)]
        + [jax.ShapeDtypeStruct((body + 8 * quarter, nz), bf16)] * 2,
        in_specs=[vmem] * 4 + [pl.BlockSpec(memory_space=pl.ANY)],
        out_specs=[vmem] * 3,
        compiler_params=params,
        name="weights",
    )(weight_ids, jnp.broadcast_to(weight_table[None], (8, NW)), xc, zc, other)
    xc = lax.ppermute(xc, both, cross(x_pairs))
    zc = lax.ppermute(zc, both, cross([(s, to) for s, to in z_pairs if abs(s - to) == 2]))

    depth = nx // 4 * comps * nz
    depth = quarter * comps * nz
    acc, w0 = pl.pallas_call(
        local_kernel,
        out_shape=[
            jax.ShapeDtypeStruct((JB * 2 * nk, 2 * nk), f32),
            jax.ShapeDtypeStruct((quarter, 2 * nk, comps * nz), bf16),
        ],
        in_specs=[vmem, vmem, vmem, smem],
        out_specs=[vmem] * 2,
        scratch_shapes=[
            pltpu.VMEM((2 * quarter, JB * 2 * nk, comps * nz), bf16),
            pltpu.VMEM((2 * quarter, 2 * nk, comps * nz), bf16),
        ],
        compiler_params=params,
        cost_estimate=pl.CostEstimate(flops=900_000_000, bytes_accessed=2_400_000, transcendentals=0),
        name="local",
    )(own, other, weight, j_block)

    acc, w1 = pl.pallas_call(
        early_kernel,
        out_shape=[
            jax.ShapeDtypeStruct((JB * 2 * nk, 2 * nk), f32),
            jax.ShapeDtypeStruct((2 * nk, depth), bf16),
        ],
        in_specs=[vmem] * 3 + [pl.BlockSpec(memory_space=pl.ANY), vmem, vmem, smem, vmem],
        out_specs=[vmem] * 2,
        scratch_shapes=[pltpu.VMEM((quarter, JB * 2 * nk, comps * nz), bf16)],
        compiler_params=params,
        cost_estimate=pl.CostEstimate(flops=600_000_000, bytes_accessed=2_400_000, transcendentals=0),
        name="early",
    )(own, other, xs, zs, xc, w0, j_block, acc)

    per_target = 2 * nk // n
    chunk = max(16, per_target)

    def crossed(count, classes_of, weighted):
        piece = (count, 2, JB, chunk, nk)
        out_shape = [jax.ShapeDtypeStruct(piece, f32), jax.ShapeDtypeStruct(piece, bf16)]
        if not weighted:
            out_shape.append(jax.ShapeDtypeStruct((2 * nk, 2 * depth), bf16))
        return pl.pallas_call(
            functools.partial(cross_kernel, classes_of, chunk, n, bool(weighted)),
            out_shape=out_shape,
            in_specs=[vmem] * 7 + [smem] + [vmem] * (1 + len(weighted)),
            out_specs=[vmem] * len(out_shape),
            scratch_shapes=[pltpu.VMEM((count, 2 * JB * chunk, 2 * depth), bf16)],
            compiler_params=params,
            cost_estimate=pl.CostEstimate(
                flops=900_000_000, bytes_accessed=4_000_000, transcendentals=0
            ),
            name="cross",
        )(own, other, xs, zs, xc, zc, w1, j_block, acc, *weighted)

    swap = [(0, 1), (1, 0)]
    if n == 2 * NEAR:
        def partners(*steps):
            return lambda s: [jnp.bitwise_xor(lax.rem(s, NEAR), step) for step in steps]

        keep_a, send_a, w2 = crossed(2, partners(3, 1), ())
        got_a = lax.ppermute(send_a, "modes", swap)
        keep_b, send_b = crossed(2, partners(0, 2), (w2,))
        got_b = lax.ppermute(send_b, "modes", swap)
        piece = (JB, chunk, nk)

        def summed(kinds, keep, got):
            return pl.pallas_call(
                near_kernel,
                out_shape=[jax.ShapeDtypeStruct((2, *piece), kind) for kind in kinds],
                in_specs=[vmem] * 2,
                out_specs=[vmem] * 2,
                compiler_params=params,
                name="near",
            )(keep, got)

        part_3, part_1 = summed((bf16, bf16), keep_a, got_a)
        mine, part_2 = summed((f32, bf16), keep_b, got_b)
        parts = [
            lax.ppermute(part, "space", [(s, s ^ step) for s in range(n)])
            for part, step in ((part_3, 3), (part_1, 1), (part_2, 2))
        ]
        keep, send = pl.pallas_call(
            far_kernel,
            out_shape=[jax.ShapeDtypeStruct(piece, f32), jax.ShapeDtypeStruct(piece, bf16)],
            in_specs=[vmem] * NEAR,
            out_specs=[vmem] * 2,
            compiler_params=params,
            name="far",
        )(mine, *parts)
        got = lax.ppermute(send, "space", [(s, s ^ NEAR) for s in range(n)])
        return pl.pallas_call(
            total_kernel,
            out_shape=jax.ShapeDtypeStruct((chunk, JB, nk), f32),
            in_specs=[vmem] * 2,
            out_specs=vmem,
            compiler_params=params,
            name="total",
        )(keep, got)

    count = nk // chunk
    keep, send, _ = crossed(count, lambda s: list(range(count)), ())
    share = (keep + lax.ppermute(send, "modes", swap)).astype(bf16)
    share = share.reshape(count, 2, JB, chunk // per_target, per_target, nk)
    share = share.transpose(1, 0, 3, 2, 4, 5).reshape(n, JB, per_target, nk)
    parts = lax.all_to_all(share, "space", 0, 0, tiled=True)
    return jnp.sum(parts.astype(f32), axis=0).transpose(1, 0, 2)


def solution(mesh):
    return jax.shard_map(
        functools.partial(on_device, mesh.shape["space"]),
        mesh=mesh,
        in_specs=(
            P("modes", None, ("groups", "space"), None, None),
            P(("groups", "space"), None, None),
            P(),
            P("groups"),
        ),
        out_specs=P(("groups", "space"), None, "modes"),
        check_vma=False,
    )
```

```python
import functools

import jax
import jax.numpy as jnp
from jax import lax
from jax.experimental import pallas as pl
from jax.experimental.pallas import tpu as pltpu
from jax.sharding import PartitionSpec as P

JB = 4
NW = 16
PADROWS = 16
LOADS = 4
NEAR = 4
VMEM_LIMIT = 48 * 1024 * 1024
PREP_LIMIT = 53_100 * 1024


def prep_kernel(modes_hbm, own_ref, core_ref, xs_ref, zs_ref, xc_ref, zc_ref, modes_ref, tr, sems):
    m = lax.axis_index("modes")
    q = lax.rem(lax.axis_index("space"), 2)
    nk, comps, _, nx, nz = modes_hbm.shape
    step = nk // LOADS
    copies = [
        pltpu.make_async_copy(
            modes_hbm.at[pl.ds(p * step, step)], modes_ref.at[pl.ds(p * step, step)], sems.at[p]
        )
        for p in range(LOADS)
    ]
    for copy in copies:
        copy.start()
    for p in range(LOADS):
        copies[p].wait()
        block = pl.ds(p * step, step)
        for c in range(comps):
            value = modes_ref[block, c, 0].astype(jnp.float32)
            tr[:, c, block] = jnp.swapaxes(value, 0, 1).astype(jnp.bfloat16)
    quarter = nx // 4
    for r in range(nx // 2 + 2):
        own_ref[r] = tr[lax.rem(nx // 2 * m + nx - 1 + r, nx)]
        core_ref[r] = tr[lax.rem(nx // 2 * (1 - m) + nx - 1 + r, nx)]
    for ref, at in (
        (xs_ref, 2 * m + 1 - q),
        (xc_ref, 2 * (1 - m) + 1 - q),
        (zs_ref, 2 * m + q),
        (zc_ref, 2 * (1 - m) + q),
    ):
        for row in range(quarter):
            for c in range(comps):
                ref[pl.ds((row * comps + c) * nk, nk), :] = tr[at * quarter + row, c]
    for ref in (zs_ref, xs_ref):
        pad = ref.shape[0] - quarter * comps * nk
        ref[pl.ds(quarter * comps * nk, pad), :] = jnp.zeros((pad, nz), jnp.bfloat16)


def weights_kernel(ids_ref, table_ref, xc_ref, zc_ref, _, weight_ref, xc_out, zc_out):
    m = lax.axis_index("modes")
    q = lax.rem(lax.axis_index("space"), 2)
    body, nz = xc_ref.shape
    nx = ids_ref.shape[1]
    quarter = nx // 4
    table = table_ref[...]
    weight = jnp.zeros((nx, nz), jnp.float32)
    for entry in range(NW):
        weight = jnp.where(ids_ref[0] == entry, table[0:1, entry : entry + 1], weight)
    weight_ref[...] = weight
    for ref, out, at in ((zc_ref, zc_out, 2 * (1 - m) + q), (xc_ref, xc_out, 2 * (1 - m) + 1 - q)):
        out[pl.ds(0, body), :] = ref[...]
        rest = jnp.concatenate(
            [
                jnp.broadcast_to(weight_ref[pl.ds(at * quarter + row, 1), :], (8, nz))
                for row in range(quarter)
            ],
            axis=0,
        )
        piece_of = lax.rem(lax.broadcasted_iota(jnp.int32, rest.shape, 0), 8)
        pieces = jnp.zeros(rest.shape, jnp.float32)
        for piece in range(3):
            rounded = rest.astype(jnp.bfloat16).astype(jnp.float32)
            pieces = jnp.where(piece_of == piece, rounded, pieces)
            rest = rest - rounded
        out[pl.ds(body, 8 * quarter), :] = pieces.astype(jnp.bfloat16)


def received_weights(ref, first, quarter):
    pieces = ref[pl.ds(first, 8 * quarter), :].astype(jnp.float32)
    return [
        pieces[8 * r : 8 * r + 1] + pieces[8 * r + 1 : 8 * r + 2] + pieces[8 * r + 2 : 8 * r + 3]
        for r in range(quarter)
    ]


def picks(jb_ref, m, nk):
    first = jb_ref[0] * JB
    owner = (first >= nk).astype(jnp.int32)
    row = first - owner * nk
    within = lax.rem(row, 16)
    return owner == m, pl.multiple_of(row - within, 16), within


def picked(pick, own, other):
    mine, block, within = pick
    rows = jnp.where(
        mine, own[pl.ds(block, 16), :].astype(jnp.float32), other[pl.ds(block, 16), :].astype(jnp.float32)
    )
    result = rows[0:JB]
    for start in range(JB, 16, JB):
        result = jnp.where(within == start, rows[start : start + JB], result)
    return result


def spread(row):
    return jnp.broadcast_to(row, (16, row.shape[1])).astype(jnp.bfloat16)[None]


def scaled(tile, field):
    rows, lanes = field.shape
    return (tile * field.reshape(rows // 16, 16, lanes)).reshape(rows, lanes)


def dot_nt(a, b):
    return lax.dot_general(a, b, (((1,), (1,)), ((), ())), preferred_element_type=jnp.float32)


def local_kernel(own_ref, other_ref, weight_ref, jb_ref, acc_ref, w0_ref, adv, wts):
    m = lax.axis_index("modes")
    q = lax.rem(lax.axis_index("space"), 2)
    rows, comps, nk, nz = own_ref.shape
    rows -= 2
    pick = picks(jb_ref, m, nk)
    for r in range(rows):
        phi = [picked(pick, own_ref.at[r + 1, d], other_ref.at[r + 1, d]) for d in range(comps)]
        weight = weight_ref[pl.ds(rows * m + r, 1), :]
        for c in range(comps):
            for half, ref in enumerate((own_ref, other_ref)):
                block = pl.ds(half * nk, nk)
                here = ref[r + 1, c].astype(jnp.float32)
                gx = 0.5 * (ref[r + 2, c].astype(jnp.float32) - ref[r, c].astype(jnp.float32))
                gz = 0.5 * (pltpu.roll(here, nz - 1, 1) - pltpu.roll(here, 1, 1))
                gx = gx.astype(jnp.bfloat16).astype(jnp.float32)
                gz = gz.astype(jnp.bfloat16).astype(jnp.float32)
                wts[r, block, pl.ds(c * nz, nz)] = (weight * here).astype(jnp.bfloat16)
                for j in range(JB):
                    total = phi[0][j : j + 1] * gx + phi[2][j : j + 1] * gz
                    adv[r, pl.ds((2 * j + half) * nk, nk), pl.ds(c * nz, nz)] = total.astype(jnp.bfloat16)
    total = dot_nt(adv[0], wts[0])
    for r in range(1, rows):
        total = total + dot_nt(adv[r], wts[r])
    acc_ref[...] = total
    quarter = rows // 2
    for r in range(quarter):
        w0_ref[r] = wts[quarter * q + r]


def sign_of_plane():
    return jnp.where(lax.rem(lax.axis_index("space"), 2) == 0, 0.5, -0.5)


def early_kernel(own_ref, other_ref, xs_ref, _, xc_ref, w0_ref, jb_ref, acc_ref, out_ref, w1_ref, adv):
    m = lax.axis_index("modes")
    q = lax.rem(lax.axis_index("space"), 2)
    rows, comps, nk, nz = own_ref.shape
    quarter = (rows - 2) // 2
    pick = picks(jb_ref, m, nk)
    weights = received_weights(xc_ref, quarter * comps * nk, quarter)
    for r in range(quarter):
        row0 = 1 + quarter * q + r
        phi0 = sign_of_plane() * picked(pick, own_ref.at[row0, 1], other_ref.at[row0, 1])
        phi0 = [spread(phi0[j : j + 1]) for j in range(JB)]
        for c in range(comps):
            at = pl.ds((r * comps + c) * nz, nz)
            src = pl.ds((r * comps + c) * nk, nk)
            for half, p1 in enumerate((xs_ref, xc_ref)):
                f1 = p1[src, :]
                w1_ref[pl.ds(half * nk, nk), at] = (weights[r] * f1.astype(jnp.float32)).astype(
                    jnp.bfloat16
                )
                for j in range(JB):
                    adv[r, pl.ds((2 * j + half) * nk, nk), pl.ds(c * nz, nz)] = scaled(phi0[j], f1)
    total = acc_ref[...]
    for r in range(quarter):
        total = total + dot_nt(adv[r], w0_ref[r])
    out_ref[...] = total


def cross_kernel(classes_of, chunk, planes, has_weighted, own_ref, other_ref, *refs):
    xs_ref, zs_ref, xc_ref, zc_ref, w1_ref, jb_ref, acc_ref, *refs = refs
    if has_weighted:
        wts, keep_ref, send_ref, adv = refs
    else:
        keep_ref, send_ref, wts, adv = refs
    m = lax.axis_index("modes")
    plane = lax.axis_index("space")
    q = lax.rem(plane, 2)
    inside = jnp.where(jnp.logical_or(plane == 1, plane == planes - 2), 0.0, 1.0)
    rows, comps, nk, nz = own_ref.shape
    quarter = (rows - 2) // 2
    span = quarter * comps * nz
    pick = picks(jb_ref, m, nk)
    classes = [pl.multiple_of(chunk * cls, chunk) for cls in classes_of(plane)]
    if not has_weighted:
        weights = received_weights(zc_ref, quarter * comps * nk, quarter)
        wts[:, pl.ds(0, span)] = w1_ref[...]
        for r in range(quarter):
            weight = inside * weights[r]
            for c in range(comps):
                src = pl.ds((r * comps + c) * nk, nk)
                for half, p2 in enumerate((zs_ref, zc_ref)):
                    wts[pl.ds(half * nk, nk), pl.ds(span + (r * comps + c) * nz, nz)] = (
                        weight * p2[src, :].astype(jnp.float32)
                    ).astype(jnp.bfloat16)
    phis = []
    for r in range(quarter):
        along = pl.ds((r * comps + 1) * nk, nk)
        phi1 = sign_of_plane() * picked(pick, xs_ref.at[along], xc_ref.at[along])
        phi2 = -sign_of_plane() * picked(pick, zs_ref.at[along], zc_ref.at[along])
        phis.append([[spread(phi[j : j + 1]) for j in range(JB)] for phi in (phi1, phi2)])
    inside = inside.astype(jnp.bfloat16)
    for at, cls in enumerate(classes):
        for r in range(quarter):
            row0 = 1 + quarter * q + r
            phi1, phi2 = phis[r]
            for c in range(comps):
                lane = (r * comps + c) * nz
                src = (r * comps + c) * nk
                for half, (p0, p1, p2) in enumerate(
                    ((own_ref, xs_ref, zs_ref), (other_ref, xc_ref, zc_ref))
                ):
                    f0 = p0[row0, c, pl.ds(cls, chunk), :]
                    f1 = p1[pl.ds(src + cls, chunk), :]
                    gy = inside * p2[pl.ds(src + cls, chunk), :] - f0
                    for j in range(JB):
                        here = pl.ds((half * JB + j) * chunk, chunk)
                        adv[at, here, pl.ds(lane, nz)] = scaled(phi1[j], gy)
                        adv[at, here, pl.ds(span + lane, nz)] = scaled(phi2[j], f1)
        total = dot_nt(adv[at], wts[...])
        for half in range(2):
            level = m if half == 0 else 1 - m
            for j in range(JB):
                first = (half * JB + j) * chunk
                piece = total[first : first + chunk] + acc_ref[pl.ds((2 * j + half) * nk + cls, chunk), :]
                keep_ref[at, level, j] = piece[:, :nk]
                send_ref[at, level, j] = piece[:, nk:].astype(jnp.bfloat16)


def near_kernel(keep_ref, got_ref, *out_refs):
    for at, ref in enumerate(out_refs):
        ref[...] = (keep_ref[at] + got_ref[at].astype(jnp.float32)).astype(ref.dtype)


def far_kernel(mine_ref, *refs):
    *parts, keep_ref, send_ref = refs
    level = lax.div(lax.axis_index("space"), NEAR)
    for ref, at in ((keep_ref, level), (send_ref, 1 - level)):
        total = mine_ref[at]
        for part in parts:
            total = total + part[at].astype(jnp.float32)
        ref[...] = total.astype(ref.dtype)


def total_kernel(keep_ref, got_ref, out_ref):
    total = keep_ref[...] + got_ref[...].astype(jnp.float32)
    for j in range(JB):
        out_ref[:, j, :] = total[j]


def on_device(n, modes, weight_ids, weight_table, j_block):
    nk, comps, _, nx, nz = modes.shape
    bf16, f32 = jnp.bfloat16, jnp.float32
    vmem = pl.BlockSpec(memory_space=pltpu.VMEM)
    smem = pl.BlockSpec(memory_space=pltpu.SMEM)
    params = pltpu.CompilerParams(vmem_limit_bytes=VMEM_LIMIT)
    six = nx // 2 + 2
    quarter = nx // 4
    body = quarter * comps * nk
    own, to_core, xs, zs, xc, zc = pl.pallas_call(
        prep_kernel,
        out_shape=[jax.ShapeDtypeStruct((six, comps, nk, nz), bf16)] * 2
        + [jax.ShapeDtypeStruct((body + PADROWS, nz), bf16)] * 2
        + [jax.ShapeDtypeStruct((body, nz), bf16)] * 2,
        in_specs=[pl.BlockSpec(memory_space=pltpu.HBM)],
        out_specs=[vmem] * 6,
        scratch_shapes=[
            pltpu.VMEM(modes.shape, bf16),
            pltpu.VMEM((nx, comps, nk, nz), bf16),
            pltpu.SemaphoreType.DMA((LOADS,)),
        ],
        compiler_params=pltpu.CompilerParams(vmem_limit_bytes=PREP_LIMIT),
        cost_estimate=pl.CostEstimate(flops=1_500_000_000, bytes_accessed=2_800_000, transcendentals=0),
        name="prep",
    )(modes)

    both = ("space", "modes")
    x_pairs = [(s, s ^ 1) for s in range(n)]
    z_pairs = [(s, (s + (2 if s % 2 else -2)) % n) for s in range(n)]
    same = lambda pairs: [(2 * a + m, 2 * b + m) for a, b in pairs for m in range(2)]
    cross = lambda pairs: [(2 * a + m, 2 * b + 1 - m) for a, b in pairs for m in range(2)]
    other = lax.ppermute(to_core, "modes", [(0, 1), (1, 0)])
    xs = lax.ppermute(xs, both, same(x_pairs))
    zs = lax.ppermute(zs, both, same(z_pairs))
    weight, xc, zc = pl.pallas_call(
        weights_kernel,
        out_shape=[jax.ShapeDtypeStruct((nx, nz), f32)]
        + [jax.ShapeDtypeStruct((body + 8 * quarter, nz), bf16)] * 2,
        in_specs=[vmem] * 4 + [pl.BlockSpec(memory_space=pl.ANY)],
        out_specs=[vmem] * 3,
        compiler_params=params,
        name="weights",
    )(weight_ids, jnp.broadcast_to(weight_table[None], (8, NW)), xc, zc, other)
    xc = lax.ppermute(xc, both, cross(x_pairs))
    zc = lax.ppermute(zc, both, cross([(s, to) for s, to in z_pairs if abs(s - to) == 2]))

    depth = nx // 4 * comps * nz
    depth = quarter * comps * nz
    acc, w0 = pl.pallas_call(
        local_kernel,
        out_shape=[
            jax.ShapeDtypeStruct((JB * 2 * nk, 2 * nk), f32),
            jax.ShapeDtypeStruct((quarter, 2 * nk, comps * nz), bf16),
        ],
        in_specs=[vmem, vmem, vmem, smem],
        out_specs=[vmem] * 2,
        scratch_shapes=[
            pltpu.VMEM((2 * quarter, JB * 2 * nk, comps * nz), bf16),
            pltpu.VMEM((2 * quarter, 2 * nk, comps * nz), bf16),
        ],
        compiler_params=params,
        cost_estimate=pl.CostEstimate(flops=900_000_000, bytes_accessed=2_400_000, transcendentals=0),
        name="local",
    )(own, other, weight, j_block)

    acc, w1 = pl.pallas_call(
        early_kernel,
        out_shape=[
            jax.ShapeDtypeStruct((JB * 2 * nk, 2 * nk), f32),
            jax.ShapeDtypeStruct((2 * nk, depth), bf16),
        ],
        in_specs=[vmem] * 3 + [pl.BlockSpec(memory_space=pl.ANY), vmem, vmem, smem, vmem],
        out_specs=[vmem] * 2,
        scratch_shapes=[pltpu.VMEM((quarter, JB * 2 * nk, comps * nz), bf16)],
        compiler_params=params,
        cost_estimate=pl.CostEstimate(flops=600_000_000, bytes_accessed=2_400_000, transcendentals=0),
        name="early",
    )(own, other, xs, zs, xc, w0, j_block, acc)

    per_target = 2 * nk // n
    chunk = max(16, per_target)

    def crossed(count, classes_of, weighted):
        piece = (count, 2, JB, chunk, nk)
        out_shape = [jax.ShapeDtypeStruct(piece, f32), jax.ShapeDtypeStruct(piece, bf16)]
        if not weighted:
            out_shape.append(jax.ShapeDtypeStruct((2 * nk, 2 * depth), bf16))
        return pl.pallas_call(
            functools.partial(cross_kernel, classes_of, chunk, n, bool(weighted)),
            out_shape=out_shape,
            in_specs=[vmem] * 7 + [smem] + [vmem] * (1 + len(weighted)),
            out_specs=[vmem] * len(out_shape),
            scratch_shapes=[pltpu.VMEM((count, 2 * JB * chunk, 2 * depth), bf16)],
            compiler_params=params,
            cost_estimate=pl.CostEstimate(
                flops=900_000_000, bytes_accessed=4_000_000, transcendentals=0
            ),
            name="cross",
        )(own, other, xs, zs, xc, zc, w1, j_block, acc, *weighted)

    swap = [(0, 1), (1, 0)]
    if n == 2 * NEAR:
        def partners(*steps):
            return lambda s: [jnp.bitwise_xor(lax.rem(s, NEAR), step) for step in steps]

        keep_a, send_a, w2 = crossed(2, partners(3, 2), ())
        got_a = lax.ppermute(send_a, "modes", swap)
        keep_b, send_b = crossed(2, partners(0, 1), (w2,))
        got_b = lax.ppermute(send_b, "modes", swap)
        piece = (JB, chunk, nk)

        def summed(kinds, keep, got):
            return pl.pallas_call(
                near_kernel,
                out_shape=[jax.ShapeDtypeStruct((2, *piece), kind) for kind in kinds],
                in_specs=[vmem] * 2,
                out_specs=[vmem] * 2,
                compiler_params=params,
                name="near",
            )(keep, got)

        part_3, part_2 = summed((bf16, bf16), keep_a, got_a)
        mine, part_1 = summed((f32, bf16), keep_b, got_b)
        parts = [
            lax.ppermute(part, "space", [(s, s ^ step) for s in range(n)])
            for part, step in ((part_3, 3), (part_2, 2), (part_1, 1))
        ]
        keep, send = pl.pallas_call(
            far_kernel,
            out_shape=[jax.ShapeDtypeStruct(piece, f32), jax.ShapeDtypeStruct(piece, bf16)],
            in_specs=[vmem] * NEAR,
            out_specs=[vmem] * 2,
            compiler_params=params,
            name="far",
        )(mine, *parts)
        got = lax.ppermute(send, "space", [(s, s ^ NEAR) for s in range(n)])
        return pl.pallas_call(
            total_kernel,
            out_shape=jax.ShapeDtypeStruct((chunk, JB, nk), f32),
            in_specs=[vmem] * 2,
            out_specs=vmem,
            compiler_params=params,
            name="total",
        )(keep, got)

    count = nk // chunk
    keep, send, _ = crossed(count, lambda s: list(range(count)), ())
    share = (keep + lax.ppermute(send, "modes", swap)).astype(bf16)
    share = share.reshape(count, 2, JB, chunk // per_target, per_target, nk)
    share = share.transpose(1, 0, 3, 2, 4, 5).reshape(n, JB, per_target, nk)
    parts = lax.all_to_all(share, "space", 0, 0, tiled=True)
    return jnp.sum(parts.astype(f32), axis=0).transpose(1, 0, 2)


def solution(mesh):
    return jax.shard_map(
        functools.partial(on_device, mesh.shape["space"]),
        mesh=mesh,
        in_specs=(
            P("modes", None, ("groups", "space"), None, None),
            P(("groups", "space"), None, None),
            P(),
            P("groups"),
        ),
        out_specs=P(("groups", "space"), None, "modes"),
        check_vma=False,
    )
```

```python
import functools

import jax
import jax.numpy as jnp
from jax import lax
from jax.experimental import pallas as pl
from jax.experimental.pallas import tpu as pltpu
from jax.sharding import PartitionSpec as P

JB = 4
NW = 16
PADROWS = 16
LOADS = 4
NEAR = 4
VMEM_LIMIT = 48 * 1024 * 1024
PREP_LIMIT = 53_600 * 1024


def copy_rows(ref, tr, at):
    nx, comps, nk, _ = tr.shape
    for row in range(nx // 4):
        for c in range(comps):
            ref[pl.ds((row * comps + c) * nk, nk), :] = tr[at * (nx // 4) + row, c]


def prep_kernel(modes_hbm, tr, xs_ref, zs_ref, modes_ref, sems):
    m = lax.axis_index("modes")
    q = lax.rem(lax.axis_index("space"), 2)
    nk, comps, _, nx, nz = modes_hbm.shape
    step = nk // LOADS
    copies = [
        pltpu.make_async_copy(
            modes_hbm.at[pl.ds(p * step, step)], modes_ref.at[pl.ds(p * step, step)], sems.at[p]
        )
        for p in range(LOADS)
    ]
    for copy in copies:
        copy.start()
    for p in range(LOADS):
        copies[p].wait()
        block = pl.ds(p * step, step)
        for c in range(comps):
            value = modes_ref[block, c, 0].astype(jnp.float32)
            tr[:, c, block] = jnp.swapaxes(value, 0, 1).astype(jnp.bfloat16)
    body = nx // 4 * comps * nk
    for ref, at in ((xs_ref, 2 * m + 1 - q), (zs_ref, 2 * m + q)):
        copy_rows(ref, tr, at)
        ref[pl.ds(body, PADROWS), :] = jnp.zeros((PADROWS, nz), jnp.bfloat16)


def weights_kernel(ids_ref, table_ref, tr, _, weight_ref, xc_ref, zc_ref):
    m = lax.axis_index("modes")
    q = lax.rem(lax.axis_index("space"), 2)
    nx, comps, nk, nz = tr.shape
    quarter = nx // 4
    table = table_ref[...]
    weight = jnp.zeros((nx, nz), jnp.float32)
    for entry in range(NW):
        weight = jnp.where(ids_ref[0] == entry, table[0:1, entry : entry + 1], weight)
    weight_ref[...] = weight
    for ref, at in ((xc_ref, 2 * (1 - m) + 1 - q), (zc_ref, 2 * (1 - m) + q)):
        copy_rows(ref, tr, at)
        rest = jnp.concatenate(
            [
                jnp.broadcast_to(weight_ref[pl.ds(at * quarter + row, 1), :], (8, nz))
                for row in range(quarter)
            ],
            axis=0,
        )
        piece_of = lax.rem(lax.broadcasted_iota(jnp.int32, rest.shape, 0), 8)
        pieces = jnp.zeros(rest.shape, jnp.float32)
        for piece in range(3):
            rounded = rest.astype(jnp.bfloat16).astype(jnp.float32)
            pieces = jnp.where(piece_of == piece, rounded, pieces)
            rest = rest - rounded
        ref[pl.ds(quarter * comps * nk, 8 * quarter), :] = pieces.astype(jnp.bfloat16)


def received_weights(ref, first, quarter):
    pieces = ref[pl.ds(first, 8 * quarter), :].astype(jnp.float32)
    return [
        pieces[8 * r : 8 * r + 1] + pieces[8 * r + 1 : 8 * r + 2] + pieces[8 * r + 2 : 8 * r + 3]
        for r in range(quarter)
    ]


def picks(jb_ref, m, nk):
    first = jb_ref[0] * JB
    owner = (first >= nk).astype(jnp.int32)
    row = first - owner * nk
    within = lax.rem(row, 16)
    return owner == m, pl.multiple_of(row - within, 16), within


def picked(pick, own, other):
    mine, block, within = pick
    rows = jnp.where(
        mine, own[pl.ds(block, 16), :].astype(jnp.float32), other[pl.ds(block, 16), :].astype(jnp.float32)
    )
    result = rows[0:JB]
    for start in range(JB, 16, JB):
        result = jnp.where(within == start, rows[start : start + JB], result)
    return result


def spread(row):
    return jnp.broadcast_to(row, (16, row.shape[1])).astype(jnp.bfloat16)[None]


def scaled(tile, field):
    rows, lanes = field.shape
    return (tile * field.reshape(rows // 16, 16, lanes)).reshape(rows, lanes)


def dot_nt(a, b):
    return lax.dot_general(a, b, (((1,), (1,)), ((), ())), preferred_element_type=jnp.float32)


def local_kernel(own_ref, other_ref, weight_ref, jb_ref, acc_ref, w0_ref, adv, wts):
    m = lax.axis_index("modes")
    q = lax.rem(lax.axis_index("space"), 2)
    nx, comps, nk, nz = own_ref.shape
    rows = nx // 2
    pick = picks(jb_ref, m, nk)
    for r in range(rows):
        row = rows * m + r
        below, above = lax.rem(row + nx - 1, nx), lax.rem(row + 1, nx)
        phi = [picked(pick, own_ref.at[row, d], other_ref.at[row, d]) for d in range(comps)]
        weight = weight_ref[pl.ds(row, 1), :]
        for c in range(comps):
            for half, ref in enumerate((own_ref, other_ref)):
                block = pl.ds(half * nk, nk)
                here = ref[row, c].astype(jnp.float32)
                gx = 0.5 * (ref[above, c].astype(jnp.float32) - ref[below, c].astype(jnp.float32))
                gz = 0.5 * (pltpu.roll(here, nz - 1, 1) - pltpu.roll(here, 1, 1))
                gx = gx.astype(jnp.bfloat16).astype(jnp.float32)
                gz = gz.astype(jnp.bfloat16).astype(jnp.float32)
                wts[r, block, pl.ds(c * nz, nz)] = (weight * here).astype(jnp.bfloat16)
                for j in range(JB):
                    total = phi[0][j : j + 1] * gx + phi[2][j : j + 1] * gz
                    adv[r, pl.ds((2 * j + half) * nk, nk), pl.ds(c * nz, nz)] = total.astype(jnp.bfloat16)
    total = dot_nt(adv[0], wts[0])
    for r in range(1, rows):
        total = total + dot_nt(adv[r], wts[r])
    acc_ref[...] = total
    quarter = rows // 2
    for r in range(quarter):
        w0_ref[r] = wts[quarter * q + r]


def sign_of_plane():
    return jnp.where(lax.rem(lax.axis_index("space"), 2) == 0, 0.5, -0.5)


def early_kernel(own_ref, other_ref, xs_ref, _, xc_ref, w0_ref, jb_ref, acc_ref, out_ref, w1_ref, adv):
    m = lax.axis_index("modes")
    q = lax.rem(lax.axis_index("space"), 2)
    nx, comps, nk, nz = own_ref.shape
    quarter = nx // 4
    pick = picks(jb_ref, m, nk)
    weights = received_weights(xc_ref, quarter * comps * nk, quarter)
    for r in range(quarter):
        row0 = quarter * (2 * m + q) + r
        phi0 = sign_of_plane() * picked(pick, own_ref.at[row0, 1], other_ref.at[row0, 1])
        phi0 = [spread(phi0[j : j + 1]) for j in range(JB)]
        for c in range(comps):
            at = pl.ds((r * comps + c) * nz, nz)
            src = pl.ds((r * comps + c) * nk, nk)
            for half, p1 in enumerate((xs_ref, xc_ref)):
                f1 = p1[src, :]
                w1_ref[pl.ds(half * nk, nk), at] = (weights[r] * f1.astype(jnp.float32)).astype(
                    jnp.bfloat16
                )
                for j in range(JB):
                    adv[r, pl.ds((2 * j + half) * nk, nk), pl.ds(c * nz, nz)] = scaled(phi0[j], f1)
    total = acc_ref[...]
    for r in range(quarter):
        total = total + dot_nt(adv[r], w0_ref[r])
    out_ref[...] = total


def cross_kernel(classes_of, chunk, planes, has_weighted, own_ref, other_ref, *refs):
    xs_ref, zs_ref, xc_ref, zc_ref, w1_ref, jb_ref, acc_ref, *refs = refs
    if has_weighted:
        wts, keep_ref, send_ref, adv = refs
    else:
        keep_ref, send_ref, wts, adv = refs
    m = lax.axis_index("modes")
    plane = lax.axis_index("space")
    q = lax.rem(plane, 2)
    inside = jnp.where(jnp.logical_or(plane == 1, plane == planes - 2), 0.0, 1.0)
    nx, comps, nk, nz = own_ref.shape
    quarter = nx // 4
    span = quarter * comps * nz
    pick = picks(jb_ref, m, nk)
    classes = [pl.multiple_of(chunk * cls, chunk) for cls in classes_of(plane)]
    if not has_weighted:
        weights = received_weights(zc_ref, quarter * comps * nk, quarter)
        wts[:, pl.ds(0, span)] = w1_ref[...]
        for r in range(quarter):
            weight = inside * weights[r]
            for c in range(comps):
                src = pl.ds((r * comps + c) * nk, nk)
                for half, p2 in enumerate((zs_ref, zc_ref)):
                    wts[pl.ds(half * nk, nk), pl.ds(span + (r * comps + c) * nz, nz)] = (
                        weight * p2[src, :].astype(jnp.float32)
                    ).astype(jnp.bfloat16)
    phis = []
    for r in range(quarter):
        along = pl.ds((r * comps + 1) * nk, nk)
        phi1 = sign_of_plane() * picked(pick, xs_ref.at[along], xc_ref.at[along])
        phi2 = -sign_of_plane() * picked(pick, zs_ref.at[along], zc_ref.at[along])
        phis.append([[spread(phi[j : j + 1]) for j in range(JB)] for phi in (phi1, phi2)])
    inside = inside.astype(jnp.bfloat16)
    for at, cls in enumerate(classes):
        for r in range(quarter):
            row0 = quarter * (2 * m + q) + r
            phi1, phi2 = phis[r]
            for c in range(comps):
                lane = (r * comps + c) * nz
                src = (r * comps + c) * nk
                for half, (p0, p1, p2) in enumerate(
                    ((own_ref, xs_ref, zs_ref), (other_ref, xc_ref, zc_ref))
                ):
                    f0 = p0[row0, c, pl.ds(cls, chunk), :]
                    f1 = p1[pl.ds(src + cls, chunk), :]
                    gy = inside * p2[pl.ds(src + cls, chunk), :] - f0
                    for j in range(JB):
                        here = pl.ds((half * JB + j) * chunk, chunk)
                        adv[at, here, pl.ds(lane, nz)] = scaled(phi1[j], gy)
                        adv[at, here, pl.ds(span + lane, nz)] = scaled(phi2[j], f1)
        total = dot_nt(adv[at], wts[...])
        for half in range(2):
            level = m if half == 0 else 1 - m
            for j in range(JB):
                first = (half * JB + j) * chunk
                piece = total[first : first + chunk] + acc_ref[pl.ds((2 * j + half) * nk + cls, chunk), :]
                keep_ref[at, level, j] = piece[:, :nk]
                send_ref[at, level, j] = piece[:, nk:].astype(jnp.bfloat16)


def near_kernel(keep_ref, got_ref, *out_refs):
    for at, ref in enumerate(out_refs):
        ref[...] = (keep_ref[at] + got_ref[at].astype(jnp.float32)).astype(ref.dtype)


def far_kernel(mine_ref, *refs):
    *parts, keep_ref, send_ref = refs
    level = lax.div(lax.axis_index("space"), NEAR)
    for ref, at in ((keep_ref, level), (send_ref, 1 - level)):
        total = mine_ref[at]
        for part in parts:
            total = total + part[at].astype(jnp.float32)
        ref[...] = total.astype(ref.dtype)


def total_kernel(keep_ref, got_ref, out_ref):
    total = keep_ref[...] + got_ref[...].astype(jnp.float32)
    for j in range(JB):
        out_ref[:, j, :] = total[j]


def on_device(n, modes, weight_ids, weight_table, j_block):
    nk, comps, _, nx, nz = modes.shape
    bf16, f32 = jnp.bfloat16, jnp.float32
    vmem = pl.BlockSpec(memory_space=pltpu.VMEM)
    smem = pl.BlockSpec(memory_space=pltpu.SMEM)
    params = pltpu.CompilerParams(vmem_limit_bytes=VMEM_LIMIT)
    quarter = nx // 4
    body = quarter * comps * nk
    own, xs, zs = pl.pallas_call(
        prep_kernel,
        out_shape=[jax.ShapeDtypeStruct((nx, comps, nk, nz), bf16)]
        + [jax.ShapeDtypeStruct((body + PADROWS, nz), bf16)] * 2,
        in_specs=[pl.BlockSpec(memory_space=pltpu.HBM)],
        out_specs=[vmem] * 3,
        scratch_shapes=[pltpu.VMEM(modes.shape, bf16), pltpu.SemaphoreType.DMA((LOADS,))],
        compiler_params=pltpu.CompilerParams(vmem_limit_bytes=PREP_LIMIT),
        cost_estimate=pl.CostEstimate(flops=1_500_000_000, bytes_accessed=2_800_000, transcendentals=0),
        name="prep",
    )(modes)

    both = ("space", "modes")
    x_pairs = [(s, s ^ 1) for s in range(n)]
    z_pairs = [(s, (s + (2 if s % 2 else -2)) % n) for s in range(n)]
    same = lambda pairs: [(2 * a + m, 2 * b + m) for a, b in pairs for m in range(2)]
    cross = lambda pairs: [(2 * a + m, 2 * b + 1 - m) for a, b in pairs for m in range(2)]
    other = lax.ppermute(own, "modes", [(0, 1), (1, 0)])
    xs = lax.ppermute(xs, both, same(x_pairs))
    zs = lax.ppermute(zs, both, same(z_pairs))
    weight, xc, zc = pl.pallas_call(
        weights_kernel,
        out_shape=[jax.ShapeDtypeStruct((nx, nz), f32)]
        + [jax.ShapeDtypeStruct((body + 8 * quarter, nz), bf16)] * 2,
        in_specs=[vmem] * 3 + [pl.BlockSpec(memory_space=pl.ANY)],
        out_specs=[vmem] * 3,
        compiler_params=params,
        name="weights",
    )(weight_ids, jnp.broadcast_to(weight_table[None], (8, NW)), own, other)
    xc = lax.ppermute(xc, both, cross(x_pairs))
    zc = lax.ppermute(zc, both, cross([(s, to) for s, to in z_pairs if abs(s - to) == 2]))

    depth = nx // 4 * comps * nz
    depth = quarter * comps * nz
    acc, w0 = pl.pallas_call(
        local_kernel,
        out_shape=[
            jax.ShapeDtypeStruct((JB * 2 * nk, 2 * nk), f32),
            jax.ShapeDtypeStruct((quarter, 2 * nk, comps * nz), bf16),
        ],
        in_specs=[vmem, vmem, vmem, smem],
        out_specs=[vmem] * 2,
        scratch_shapes=[
            pltpu.VMEM((2 * quarter, JB * 2 * nk, comps * nz), bf16),
            pltpu.VMEM((2 * quarter, 2 * nk, comps * nz), bf16),
        ],
        compiler_params=params,
        cost_estimate=pl.CostEstimate(flops=900_000_000, bytes_accessed=2_400_000, transcendentals=0),
        name="local",
    )(own, other, weight, j_block)

    acc, w1 = pl.pallas_call(
        early_kernel,
        out_shape=[
            jax.ShapeDtypeStruct((JB * 2 * nk, 2 * nk), f32),
            jax.ShapeDtypeStruct((2 * nk, depth), bf16),
        ],
        in_specs=[vmem] * 3 + [pl.BlockSpec(memory_space=pl.ANY), vmem, vmem, smem, vmem],
        out_specs=[vmem] * 2,
        scratch_shapes=[pltpu.VMEM((quarter, JB * 2 * nk, comps * nz), bf16)],
        compiler_params=params,
        cost_estimate=pl.CostEstimate(flops=600_000_000, bytes_accessed=2_400_000, transcendentals=0),
        name="early",
    )(own, other, xs, zs, xc, w0, j_block, acc)

    per_target = 2 * nk // n
    chunk = max(16, per_target)

    def crossed(count, classes_of, weighted):
        piece = (count, 2, JB, chunk, nk)
        out_shape = [jax.ShapeDtypeStruct(piece, f32), jax.ShapeDtypeStruct(piece, bf16)]
        if not weighted:
            out_shape.append(jax.ShapeDtypeStruct((2 * nk, 2 * depth), bf16))
        return pl.pallas_call(
            functools.partial(cross_kernel, classes_of, chunk, n, bool(weighted)),
            out_shape=out_shape,
            in_specs=[vmem] * 7 + [smem] + [vmem] * (1 + len(weighted)),
            out_specs=[vmem] * len(out_shape),
            scratch_shapes=[pltpu.VMEM((count, 2 * JB * chunk, 2 * depth), bf16)],
            compiler_params=params,
            cost_estimate=pl.CostEstimate(
                flops=900_000_000, bytes_accessed=4_000_000, transcendentals=0
            ),
            name="cross",
        )(own, other, xs, zs, xc, zc, w1, j_block, acc, *weighted)

    swap = [(0, 1), (1, 0)]
    if n == 2 * NEAR:
        def partners(*steps):
            return lambda s: [jnp.bitwise_xor(lax.rem(s, NEAR), step) for step in steps]

        keep_a, send_a, w2 = crossed(2, partners(3, 1), ())
        got_a = lax.ppermute(send_a, "modes", swap)
        keep_b, send_b = crossed(2, partners(0, 2), (w2,))
        got_b = lax.ppermute(send_b, "modes", swap)
        piece = (JB, chunk, nk)

        def summed(kinds, keep, got):
            return pl.pallas_call(
                near_kernel,
                out_shape=[jax.ShapeDtypeStruct((2, *piece), kind) for kind in kinds],
                in_specs=[vmem] * 2,
                out_specs=[vmem] * 2,
                compiler_params=params,
                name="near",
            )(keep, got)

        part_3, part_1 = summed((bf16, bf16), keep_a, got_a)
        mine, part_2 = summed((f32, bf16), keep_b, got_b)
        parts = [
            lax.ppermute(part, "space", [(s, s ^ step) for s in range(n)])
            for part, step in ((part_3, 3), (part_1, 1), (part_2, 2))
        ]
        keep, send = pl.pallas_call(
            far_kernel,
            out_shape=[jax.ShapeDtypeStruct(piece, f32), jax.ShapeDtypeStruct(piece, bf16)],
            in_specs=[vmem] * NEAR,
            out_specs=[vmem] * 2,
            compiler_params=params,
            name="far",
        )(mine, *parts)
        got = lax.ppermute(send, "space", [(s, s ^ NEAR) for s in range(n)])
        return pl.pallas_call(
            total_kernel,
            out_shape=jax.ShapeDtypeStruct((chunk, JB, nk), f32),
            in_specs=[vmem] * 2,
            out_specs=vmem,
            compiler_params=params,
            name="total",
        )(keep, got)

    count = nk // chunk
    keep, send, _ = crossed(count, lambda s: list(range(count)), ())
    share = (keep + lax.ppermute(send, "modes", swap)).astype(bf16)
    share = share.reshape(count, 2, JB, chunk // per_target, per_target, nk)
    share = share.transpose(1, 0, 3, 2, 4, 5).reshape(n, JB, per_target, nk)
    parts = lax.all_to_all(share, "space", 0, 0, tiled=True)
    return jnp.sum(parts.astype(f32), axis=0).transpose(1, 0, 2)


def solution(mesh):
    return jax.shard_map(
        functools.partial(on_device, mesh.shape["space"]),
        mesh=mesh,
        in_specs=(
            P("modes", None, ("groups", "space"), None, None),
            P(("groups", "space"), None, None),
            P(),
            P("groups"),
        ),
        out_specs=P(("groups", "space"), None, "modes"),
        check_vma=False,
    )
```

```python
import functools

import jax
import jax.numpy as jnp
from jax import lax
from jax.experimental import pallas as pl
from jax.experimental.pallas import tpu as pltpu
from jax.sharding import PartitionSpec as P

JB = 4
NW = 16
PADROWS = 16
LOADS = 4
NEAR = 4
VMEM_LIMIT = 48 * 1024 * 1024
PREP_LIMIT = 53_600 * 1024


def copy_rows(ref, tr, at):
    nx, comps, nk, _ = tr.shape
    for row in range(nx // 4):
        for c in range(comps):
            ref[pl.ds((row * comps + c) * nk, nk), :] = tr[at * (nx // 4) + row, c]


def prep_kernel(modes_hbm, tr, xs_ref, zs_ref, modes_ref, sems):
    m = lax.axis_index("modes")
    q = lax.rem(lax.axis_index("space"), 2)
    nk, comps, _, nx, nz = modes_hbm.shape
    step = nk // LOADS
    copies = [
        pltpu.make_async_copy(
            modes_hbm.at[pl.ds(p * step, step)], modes_ref.at[pl.ds(p * step, step)], sems.at[p]
        )
        for p in range(LOADS)
    ]
    for copy in copies:
        copy.start()
    for p in range(LOADS):
        copies[p].wait()
        block = pl.ds(p * step, step)
        for c in range(comps):
            value = modes_ref[block, c, 0].astype(jnp.float32)
            tr[:, c, block] = jnp.swapaxes(value, 0, 1).astype(jnp.bfloat16)
    body = nx // 4 * comps * nk
    for ref, at in ((xs_ref, 2 * m + 1 - q), (zs_ref, 2 * m + q)):
        copy_rows(ref, tr, at)
        ref[pl.ds(body, PADROWS), :] = jnp.zeros((PADROWS, nz), jnp.bfloat16)


def weights_kernel(ids_ref, table_ref, tr, _, weight_ref, xc_ref, zc_ref):
    m = lax.axis_index("modes")
    q = lax.rem(lax.axis_index("space"), 2)
    nx, comps, nk, nz = tr.shape
    quarter = nx // 4
    table = table_ref[...]
    weight = jnp.zeros((nx, nz), jnp.float32)
    for entry in range(NW):
        weight = jnp.where(ids_ref[0] == entry, table[0:1, entry : entry + 1], weight)
    weight_ref[...] = weight
    for ref, at in ((xc_ref, 2 * (1 - m) + 1 - q), (zc_ref, 2 * (1 - m) + q)):
        copy_rows(ref, tr, at)
        rest = jnp.concatenate(
            [
                jnp.broadcast_to(weight_ref[pl.ds(at * quarter + row, 1), :], (8, nz))
                for row in range(quarter)
            ],
            axis=0,
        )
        piece_of = lax.rem(lax.broadcasted_iota(jnp.int32, rest.shape, 0), 8)
        pieces = jnp.zeros(rest.shape, jnp.float32)
        for piece in range(3):
            rounded = rest.astype(jnp.bfloat16).astype(jnp.float32)
            pieces = jnp.where(piece_of == piece, rounded, pieces)
            rest = rest - rounded
        ref[pl.ds(quarter * comps * nk, 8 * quarter), :] = pieces.astype(jnp.bfloat16)


def received_weights(ref, first, quarter):
    pieces = ref[pl.ds(first, 8 * quarter), :].astype(jnp.float32)
    return [
        pieces[8 * r : 8 * r + 1] + pieces[8 * r + 1 : 8 * r + 2] + pieces[8 * r + 2 : 8 * r + 3]
        for r in range(quarter)
    ]


def picks(jb_ref, m, nk):
    first = jb_ref[0] * JB
    owner = (first >= nk).astype(jnp.int32)
    row = first - owner * nk
    within = lax.rem(row, 16)
    return owner == m, pl.multiple_of(row - within, 16), within


def picked(pick, own, other):
    mine, block, within = pick
    rows = jnp.where(
        mine, own[pl.ds(block, 16), :].astype(jnp.float32), other[pl.ds(block, 16), :].astype(jnp.float32)
    )
    result = rows[0:JB]
    for start in range(JB, 16, JB):
        result = jnp.where(within == start, rows[start : start + JB], result)
    return result


def spread(row):
    return jnp.broadcast_to(row, (16, row.shape[1])).astype(jnp.bfloat16)[None]


def scaled(tile, field):
    rows, lanes = field.shape
    return (tile * field.reshape(rows // 16, 16, lanes)).reshape(rows, lanes)


def dot_nt(a, b):
    return lax.dot_general(a, b, (((1,), (1,)), ((), ())), preferred_element_type=jnp.float32)


def local_kernel(own_ref, other_ref, weight_ref, jb_ref, acc_ref, w0_ref, adv, wts):
    m = lax.axis_index("modes")
    q = lax.rem(lax.axis_index("space"), 2)
    nx, comps, nk, nz = own_ref.shape
    rows = nx // 2
    pick = picks(jb_ref, m, nk)
    for r in range(rows):
        row = rows * m + r
        below, above = lax.rem(row + nx - 1, nx), lax.rem(row + 1, nx)
        phi = [picked(pick, own_ref.at[row, d], other_ref.at[row, d]) for d in range(comps)]
        weight = weight_ref[pl.ds(row, 1), :]
        for c in range(comps):
            for half, ref in enumerate((own_ref, other_ref)):
                block = pl.ds(half * nk, nk)
                here = ref[row, c].astype(jnp.float32)
                gx = 0.5 * (ref[above, c].astype(jnp.float32) - ref[below, c].astype(jnp.float32))
                gz = 0.5 * (pltpu.roll(here, nz - 1, 1) - pltpu.roll(here, 1, 1))
                gx = gx.astype(jnp.bfloat16).astype(jnp.float32)
                gz = gz.astype(jnp.bfloat16).astype(jnp.float32)
                wts[r, block, pl.ds(c * nz, nz)] = (weight * here).astype(jnp.bfloat16)
                for j in range(JB):
                    total = phi[0][j : j + 1] * gx + phi[2][j : j + 1] * gz
                    adv[r, pl.ds((2 * j + half) * nk, nk), pl.ds(c * nz, nz)] = total.astype(jnp.bfloat16)
    total = dot_nt(adv[0], wts[0])
    for r in range(1, rows):
        total = total + dot_nt(adv[r], wts[r])
    acc_ref[...] = total
    quarter = rows // 2
    for r in range(quarter):
        w0_ref[r] = wts[quarter * q + r]


def sign_of_plane():
    return jnp.where(lax.rem(lax.axis_index("space"), 2) == 0, 0.5, -0.5)


def early_kernel(own_ref, other_ref, xs_ref, _, xc_ref, w0_ref, jb_ref, acc_ref, out_ref, w1_ref, adv):
    m = lax.axis_index("modes")
    q = lax.rem(lax.axis_index("space"), 2)
    nx, comps, nk, nz = own_ref.shape
    quarter = nx // 4
    pick = picks(jb_ref, m, nk)
    weights = received_weights(xc_ref, quarter * comps * nk, quarter)
    for r in range(quarter):
        row0 = quarter * (2 * m + q) + r
        phi0 = sign_of_plane() * picked(pick, own_ref.at[row0, 1], other_ref.at[row0, 1])
        phi0 = [spread(phi0[j : j + 1]) for j in range(JB)]
        for c in range(comps):
            at = pl.ds((r * comps + c) * nz, nz)
            src = pl.ds((r * comps + c) * nk, nk)
            for half, p1 in enumerate((xs_ref, xc_ref)):
                f1 = p1[src, :]
                w1_ref[pl.ds(half * nk, nk), at] = (weights[r] * f1.astype(jnp.float32)).astype(
                    jnp.bfloat16
                )
                for j in range(JB):
                    adv[r, pl.ds((2 * j + half) * nk, nk), pl.ds(c * nz, nz)] = scaled(phi0[j], f1)
    total = acc_ref[...]
    for r in range(quarter):
        total = total + dot_nt(adv[r], w0_ref[r])
    out_ref[...] = total


def cross_kernel(classes_of, chunk, planes, has_weighted, own_ref, other_ref, *refs):
    xs_ref, zs_ref, xc_ref, zc_ref, w1_ref, jb_ref, acc_ref, *refs = refs
    if has_weighted:
        wts, keep_ref, send_ref, adv = refs
    else:
        keep_ref, send_ref, wts, adv = refs
    m = lax.axis_index("modes")
    plane = lax.axis_index("space")
    q = lax.rem(plane, 2)
    inside = jnp.where(jnp.logical_or(plane == 1, plane == planes - 2), 0.0, 1.0)
    nx, comps, nk, nz = own_ref.shape
    quarter = nx // 4
    span = quarter * comps * nz
    pick = picks(jb_ref, m, nk)
    classes = [pl.multiple_of(chunk * cls, chunk) for cls in classes_of(plane)]
    if not has_weighted:
        weights = received_weights(zc_ref, quarter * comps * nk, quarter)
        wts[:, pl.ds(0, span)] = w1_ref[...]
        for r in range(quarter):
            weight = inside * weights[r]
            for c in range(comps):
                src = pl.ds((r * comps + c) * nk, nk)
                for half, p2 in enumerate((zs_ref, zc_ref)):
                    wts[pl.ds(half * nk, nk), pl.ds(span + (r * comps + c) * nz, nz)] = (
                        weight * p2[src, :].astype(jnp.float32)
                    ).astype(jnp.bfloat16)
    phis = []
    for r in range(quarter):
        along = pl.ds((r * comps + 1) * nk, nk)
        phi1 = sign_of_plane() * picked(pick, xs_ref.at[along], xc_ref.at[along])
        phi2 = -sign_of_plane() * picked(pick, zs_ref.at[along], zc_ref.at[along])
        phis.append([[spread(phi[j : j + 1]) for j in range(JB)] for phi in (phi1, phi2)])
    inside = inside.astype(jnp.bfloat16)
    for at, cls in enumerate(classes):
        for r in range(quarter):
            row0 = quarter * (2 * m + q) + r
            phi1, phi2 = phis[r]
            for c in range(comps):
                lane = (r * comps + c) * nz
                src = (r * comps + c) * nk
                for half, (p0, p1, p2) in enumerate(
                    ((own_ref, xs_ref, zs_ref), (other_ref, xc_ref, zc_ref))
                ):
                    f0 = p0[row0, c, pl.ds(cls, chunk), :]
                    f1 = p1[pl.ds(src + cls, chunk), :]
                    gy = inside * p2[pl.ds(src + cls, chunk), :] - f0
                    for j in range(JB):
                        here = pl.ds((half * JB + j) * chunk, chunk)
                        adv[at, here, pl.ds(lane, nz)] = scaled(phi1[j], gy)
                        adv[at, here, pl.ds(span + lane, nz)] = scaled(phi2[j], f1)
        total = dot_nt(adv[at], wts[...])
        for half in range(2):
            level = m if half == 0 else 1 - m
            for j in range(JB):
                first = (half * JB + j) * chunk
                piece = total[first : first + chunk] + acc_ref[pl.ds((2 * j + half) * nk + cls, chunk), :]
                keep_ref[at, level, j] = piece[:, :nk]
                send_ref[at, level, j] = piece[:, nk:].astype(jnp.bfloat16)


def near_kernel(keep_ref, got_ref, *out_refs):
    for at, ref in enumerate(out_refs):
        ref[...] = (keep_ref[at] + got_ref[at].astype(jnp.float32)).astype(ref.dtype)


def far_kernel(mine_ref, *refs):
    *parts, keep_ref, send_ref = refs
    level = lax.div(lax.axis_index("space"), NEAR)
    for ref, at in ((keep_ref, level), (send_ref, 1 - level)):
        total = mine_ref[at]
        for part in parts:
            total = total + part[at].astype(jnp.float32)
        ref[...] = total.astype(ref.dtype)


def total_kernel(keep_ref, got_ref, out_ref):
    total = keep_ref[...] + got_ref[...].astype(jnp.float32)
    for j in range(JB):
        out_ref[:, j, :] = total[j]


def on_device(n, modes, weight_ids, weight_table, j_block):
    nk, comps, _, nx, nz = modes.shape
    bf16, f32 = jnp.bfloat16, jnp.float32
    vmem = pl.BlockSpec(memory_space=pltpu.VMEM)
    smem = pl.BlockSpec(memory_space=pltpu.SMEM)
    params = pltpu.CompilerParams(vmem_limit_bytes=VMEM_LIMIT)
    quarter = nx // 4
    body = quarter * comps * nk
    own, xs, zs = pl.pallas_call(
        prep_kernel,
        out_shape=[jax.ShapeDtypeStruct((nx, comps, nk, nz), bf16)]
        + [jax.ShapeDtypeStruct((body + PADROWS, nz), bf16)] * 2,
        in_specs=[pl.BlockSpec(memory_space=pltpu.HBM)],
        out_specs=[vmem] * 3,
        scratch_shapes=[pltpu.VMEM(modes.shape, bf16), pltpu.SemaphoreType.DMA((LOADS,))],
        compiler_params=pltpu.CompilerParams(vmem_limit_bytes=PREP_LIMIT),
        cost_estimate=pl.CostEstimate(flops=1_500_000_000, bytes_accessed=2_800_000, transcendentals=0),
        name="prep",
    )(modes)

    both = ("space", "modes")
    x_pairs = [(s, s ^ 1) for s in range(n)]
    z_pairs = [(s, (s + (2 if s % 2 else -2)) % n) for s in range(n)]
    same = lambda pairs: [(2 * a + m, 2 * b + m) for a, b in pairs for m in range(2)]
    cross = lambda pairs: [(2 * a + m, 2 * b + 1 - m) for a, b in pairs for m in range(2)]
    other = lax.ppermute(own, "modes", [(0, 1), (1, 0)])
    xs = lax.ppermute(xs, both, same(x_pairs))
    zs = lax.ppermute(zs, both, same(z_pairs))
    weight, xc, zc = pl.pallas_call(
        weights_kernel,
        out_shape=[jax.ShapeDtypeStruct((nx, nz), f32)]
        + [jax.ShapeDtypeStruct((body + 8 * quarter, nz), bf16)] * 2,
        in_specs=[vmem] * 3 + [pl.BlockSpec(memory_space=pl.ANY)],
        out_specs=[vmem] * 3,
        compiler_params=params,
        name="weights",
    )(weight_ids, jnp.broadcast_to(weight_table[None], (8, NW)), own, other)
    xc = lax.ppermute(xc, both, cross(x_pairs))
    zc = lax.ppermute(zc, both, cross([(s, to) for s, to in z_pairs if abs(s - to) == 2]))

    depth = nx // 4 * comps * nz
    depth = quarter * comps * nz
    acc, w0 = pl.pallas_call(
        local_kernel,
        out_shape=[
            jax.ShapeDtypeStruct((JB * 2 * nk, 2 * nk), f32),
            jax.ShapeDtypeStruct((quarter, 2 * nk, comps * nz), bf16),
        ],
        in_specs=[vmem, vmem, vmem, smem],
        out_specs=[vmem] * 2,
        scratch_shapes=[
            pltpu.VMEM((2 * quarter, JB * 2 * nk, comps * nz), bf16),
            pltpu.VMEM((2 * quarter, 2 * nk, comps * nz), bf16),
        ],
        compiler_params=params,
        cost_estimate=pl.CostEstimate(flops=900_000_000, bytes_accessed=2_400_000, transcendentals=0),
        name="local",
    )(own, other, weight, j_block)

    acc, w1 = pl.pallas_call(
        early_kernel,
        out_shape=[
            jax.ShapeDtypeStruct((JB * 2 * nk, 2 * nk), f32),
            jax.ShapeDtypeStruct((2 * nk, depth), bf16),
        ],
        in_specs=[vmem] * 3 + [pl.BlockSpec(memory_space=pl.ANY), vmem, vmem, smem, vmem],
        out_specs=[vmem] * 2,
        scratch_shapes=[pltpu.VMEM((quarter, JB * 2 * nk, comps * nz), bf16)],
        compiler_params=params,
        cost_estimate=pl.CostEstimate(flops=600_000_000, bytes_accessed=2_400_000, transcendentals=0),
        name="early",
    )(own, other, xs, zs, xc, w0, j_block, acc)

    per_target = 2 * nk // n
    chunk = max(16, per_target)

    def crossed(count, classes_of, weighted):
        piece = (count, 2, JB, chunk, nk)
        out_shape = [jax.ShapeDtypeStruct(piece, f32), jax.ShapeDtypeStruct(piece, bf16)]
        if not weighted:
            out_shape.append(jax.ShapeDtypeStruct((2 * nk, 2 * depth), bf16))
        return pl.pallas_call(
            functools.partial(cross_kernel, classes_of, chunk, n, bool(weighted)),
            out_shape=out_shape,
            in_specs=[vmem] * 7 + [smem] + [vmem] * (1 + len(weighted)),
            out_specs=[vmem] * len(out_shape),
            scratch_shapes=[pltpu.VMEM((count, 2 * JB * chunk, 2 * depth), bf16)],
            compiler_params=params,
            cost_estimate=pl.CostEstimate(
                flops=900_000_000, bytes_accessed=4_000_000, transcendentals=0
            ),
            name="cross",
        )(own, other, xs, zs, xc, zc, w1, j_block, acc, *weighted)

    swap = [(0, 1), (1, 0)]
    if n == 2 * NEAR:
        def partners(*steps):
            return lambda s: [jnp.bitwise_xor(lax.rem(s, NEAR), step) for step in steps]

        keep_a, send_a, w2 = crossed(2, partners(1, 3), ())
        got_a = lax.ppermute(send_a, "modes", swap)
        keep_b, send_b = crossed(2, partners(0, 2), (w2,))
        got_b = lax.ppermute(send_b, "modes", swap)
        piece = (JB, chunk, nk)

        def summed(kinds, keep, got):
            return pl.pallas_call(
                near_kernel,
                out_shape=[jax.ShapeDtypeStruct((2, *piece), kind) for kind in kinds],
                in_specs=[vmem] * 2,
                out_specs=[vmem] * 2,
                compiler_params=params,
                name="near",
            )(keep, got)

        part_1, part_3 = summed((bf16, bf16), keep_a, got_a)
        mine, part_2 = summed((f32, bf16), keep_b, got_b)
        parts = [
            lax.ppermute(part, "space", [(s, s ^ step) for s in range(n)])
            for part, step in ((part_1, 1), (part_3, 3), (part_2, 2))
        ]
        keep, send = pl.pallas_call(
            far_kernel,
            out_shape=[jax.ShapeDtypeStruct(piece, f32), jax.ShapeDtypeStruct(piece, bf16)],
            in_specs=[vmem] * NEAR,
            out_specs=[vmem] * 2,
            compiler_params=params,
            name="far",
        )(mine, *parts)
        got = lax.ppermute(send, "space", [(s, s ^ NEAR) for s in range(n)])
        return pl.pallas_call(
            total_kernel,
            out_shape=jax.ShapeDtypeStruct((chunk, JB, nk), f32),
            in_specs=[vmem] * 2,
            out_specs=vmem,
            compiler_params=params,
            name="total",
        )(keep, got)

    count = nk // chunk
    keep, send, _ = crossed(count, lambda s: list(range(count)), ())
    share = (keep + lax.ppermute(send, "modes", swap)).astype(bf16)
    share = share.reshape(count, 2, JB, chunk // per_target, per_target, nk)
    share = share.transpose(1, 0, 3, 2, 4, 5).reshape(n, JB, per_target, nk)
    parts = lax.all_to_all(share, "space", 0, 0, tiled=True)
    return jnp.sum(parts.astype(f32), axis=0).transpose(1, 0, 2)


def solution(mesh):
    return jax.shard_map(
        functools.partial(on_device, mesh.shape["space"]),
        mesh=mesh,
        in_specs=(
            P("modes", None, ("groups", "space"), None, None),
            P(("groups", "space"), None, None),
            P(),
            P("groups"),
        ),
        out_specs=P(("groups", "space"), None, "modes"),
        check_vma=False,
    )
```

```python
import functools

import jax
import jax.numpy as jnp
from jax import lax
from jax.experimental import pallas as pl
from jax.experimental.pallas import tpu as pltpu
from jax.sharding import PartitionSpec as P

JB = 4
NW = 16
PADROWS = 16
LOADS = 4
NEAR = 4
VMEM_LIMIT = 48 * 1024 * 1024
PREP_LIMIT = 53_600 * 1024


def copy_rows(ref, tr, at):
    nx, comps, nk, _ = tr.shape
    for row in range(nx // 4):
        for c in range(comps):
            ref[pl.ds((row * comps + c) * nk, nk), :] = tr[at * (nx // 4) + row, c]


def prep_kernel(modes_hbm, tr, xs_ref, zs_ref, modes_ref, sems):
    m = lax.axis_index("modes")
    q = lax.rem(lax.axis_index("space"), 2)
    nk, comps, _, nx, nz = modes_hbm.shape
    step = nk // LOADS
    copies = [
        pltpu.make_async_copy(
            modes_hbm.at[pl.ds(p * step, step)], modes_ref.at[pl.ds(p * step, step)], sems.at[p]
        )
        for p in range(LOADS)
    ]
    for copy in copies:
        copy.start()
    for p in range(LOADS):
        copies[p].wait()
        block = pl.ds(p * step, step)
        for c in range(comps):
            value = modes_ref[block, c, 0].astype(jnp.float32)
            tr[:, c, block] = jnp.swapaxes(value, 0, 1).astype(jnp.bfloat16)
    body = nx // 4 * comps * nk
    for ref, at in ((xs_ref, 2 * m + 1 - q), (zs_ref, 2 * m + q)):
        copy_rows(ref, tr, at)
        ref[pl.ds(body, PADROWS), :] = jnp.zeros((PADROWS, nz), jnp.bfloat16)


def weights_kernel(ids_ref, table_ref, tr, _, weight_ref, xc_ref, zc_ref):
    m = lax.axis_index("modes")
    q = lax.rem(lax.axis_index("space"), 2)
    nx, comps, nk, nz = tr.shape
    quarter = nx // 4
    table = table_ref[...]
    weight = jnp.zeros((nx, nz), jnp.float32)
    for entry in range(NW):
        weight = jnp.where(ids_ref[0] == entry, table[0:1, entry : entry + 1], weight)
    weight_ref[...] = weight
    for ref, at in ((xc_ref, 2 * (1 - m) + 1 - q), (zc_ref, 2 * (1 - m) + q)):
        copy_rows(ref, tr, at)
        rest = jnp.concatenate(
            [
                jnp.broadcast_to(weight_ref[pl.ds(at * quarter + row, 1), :], (8, nz))
                for row in range(quarter)
            ],
            axis=0,
        )
        piece_of = lax.rem(lax.broadcasted_iota(jnp.int32, rest.shape, 0), 8)
        pieces = jnp.zeros(rest.shape, jnp.float32)
        for piece in range(3):
            rounded = rest.astype(jnp.bfloat16).astype(jnp.float32)
            pieces = jnp.where(piece_of == piece, rounded, pieces)
            rest = rest - rounded
        ref[pl.ds(quarter * comps * nk, 8 * quarter), :] = pieces.astype(jnp.bfloat16)


def received_weights(ref, first, quarter):
    pieces = ref[pl.ds(first, 8 * quarter), :].astype(jnp.float32)
    return [
        pieces[8 * r : 8 * r + 1] + pieces[8 * r + 1 : 8 * r + 2] + pieces[8 * r + 2 : 8 * r + 3]
        for r in range(quarter)
    ]


def picks(jb_ref, m, nk):
    first = jb_ref[0] * JB
    owner = (first >= nk).astype(jnp.int32)
    row = first - owner * nk
    within = lax.rem(row, 16)
    return owner == m, pl.multiple_of(row - within, 16), within


def picked(pick, own, other):
    mine, block, within = pick
    rows = jnp.where(
        mine, own[pl.ds(block, 16), :].astype(jnp.float32), other[pl.ds(block, 16), :].astype(jnp.float32)
    )
    result = rows[0:JB]
    for start in range(JB, 16, JB):
        result = jnp.where(within == start, rows[start : start + JB], result)
    return result


def spread(row):
    return jnp.broadcast_to(row, (16, row.shape[1])).astype(jnp.bfloat16)[None]


def scaled(tile, field):
    rows, lanes = field.shape
    return (tile * field.reshape(rows // 16, 16, lanes)).reshape(rows, lanes)


def dot_nt(a, b):
    return lax.dot_general(a, b, (((1,), (1,)), ((), ())), preferred_element_type=jnp.float32)


def local_kernel(own_ref, other_ref, weight_ref, jb_ref, acc_ref, w0_ref, adv, wts):
    m = lax.axis_index("modes")
    q = lax.rem(lax.axis_index("space"), 2)
    nx, comps, nk, nz = own_ref.shape
    rows = nx // 2
    pick = picks(jb_ref, m, nk)
    for r in range(rows):
        row = rows * m + r
        below, above = lax.rem(row + nx - 1, nx), lax.rem(row + 1, nx)
        phi = [picked(pick, own_ref.at[row, d], other_ref.at[row, d]) for d in range(comps)]
        weight = weight_ref[pl.ds(row, 1), :]
        for c in range(comps):
            for half, ref in enumerate((own_ref, other_ref)):
                block = pl.ds(half * nk, nk)
                here = ref[row, c].astype(jnp.float32)
                gx = 0.5 * (ref[above, c].astype(jnp.float32) - ref[below, c].astype(jnp.float32))
                gz = 0.5 * (pltpu.roll(here, nz - 1, 1) - pltpu.roll(here, 1, 1))
                gx = gx.astype(jnp.bfloat16).astype(jnp.float32)
                gz = gz.astype(jnp.bfloat16).astype(jnp.float32)
                wts[r, block, pl.ds(c * nz, nz)] = (weight * here).astype(jnp.bfloat16)
                for j in range(JB):
                    total = phi[0][j : j + 1] * gx + phi[2][j : j + 1] * gz
                    adv[r, pl.ds((2 * j + half) * nk, nk), pl.ds(c * nz, nz)] = total.astype(jnp.bfloat16)
    total = dot_nt(adv[0], wts[0])
    for r in range(1, rows):
        total = total + dot_nt(adv[r], wts[r])
    acc_ref[...] = total
    quarter = rows // 2
    for r in range(quarter):
        w0_ref[r] = wts[quarter * q + r]


def sign_of_plane():
    return jnp.where(lax.rem(lax.axis_index("space"), 2) == 0, 0.5, -0.5)


def early_kernel(own_ref, other_ref, xs_ref, _, xc_ref, w0_ref, jb_ref, acc_ref, out_ref, w1_ref, adv):
    m = lax.axis_index("modes")
    q = lax.rem(lax.axis_index("space"), 2)
    nx, comps, nk, nz = own_ref.shape
    quarter = nx // 4
    pick = picks(jb_ref, m, nk)
    weights = received_weights(xc_ref, quarter * comps * nk, quarter)
    for r in range(quarter):
        row0 = quarter * (2 * m + q) + r
        phi0 = sign_of_plane() * picked(pick, own_ref.at[row0, 1], other_ref.at[row0, 1])
        phi0 = [spread(phi0[j : j + 1]) for j in range(JB)]
        for c in range(comps):
            at = pl.ds((r * comps + c) * nz, nz)
            src = pl.ds((r * comps + c) * nk, nk)
            for half, p1 in enumerate((xs_ref, xc_ref)):
                f1 = p1[src, :]
                w1_ref[pl.ds(half * nk, nk), at] = (weights[r] * f1.astype(jnp.float32)).astype(
                    jnp.bfloat16
                )
                for j in range(JB):
                    adv[r, pl.ds((2 * j + half) * nk, nk), pl.ds(c * nz, nz)] = scaled(phi0[j], f1)
    total = acc_ref[...]
    for r in range(quarter):
        total = total + dot_nt(adv[r], w0_ref[r])
    out_ref[...] = total


def cross_kernel(classes_of, chunk, planes, has_weighted, own_ref, other_ref, *refs):
    xs_ref, zs_ref, xc_ref, zc_ref, w1_ref, jb_ref, acc_ref, *refs = refs
    if has_weighted:
        wts, keep_ref, send_ref, adv = refs
    else:
        keep_ref, send_ref, wts, adv = refs
    m = lax.axis_index("modes")
    plane = lax.axis_index("space")
    q = lax.rem(plane, 2)
    inside = jnp.where(jnp.logical_or(plane == 1, plane == planes - 2), 0.0, 1.0)
    nx, comps, nk, nz = own_ref.shape
    quarter = nx // 4
    span = quarter * comps * nz
    pick = picks(jb_ref, m, nk)
    classes = [pl.multiple_of(chunk * cls, chunk) for cls in classes_of(plane)]
    if not has_weighted:
        weights = received_weights(zc_ref, quarter * comps * nk, quarter)
        wts[:, pl.ds(0, span)] = w1_ref[...]
        for r in range(quarter):
            weight = inside * weights[r]
            for c in range(comps):
                src = pl.ds((r * comps + c) * nk, nk)
                for half, p2 in enumerate((zs_ref, zc_ref)):
                    wts[pl.ds(half * nk, nk), pl.ds(span + (r * comps + c) * nz, nz)] = (
                        weight * p2[src, :].astype(jnp.float32)
                    ).astype(jnp.bfloat16)
    phis = []
    for r in range(quarter):
        along = pl.ds((r * comps + 1) * nk, nk)
        phi1 = sign_of_plane() * picked(pick, xs_ref.at[along], xc_ref.at[along])
        phi2 = -sign_of_plane() * picked(pick, zs_ref.at[along], zc_ref.at[along])
        phis.append([[spread(phi[j : j + 1]) for j in range(JB)] for phi in (phi1, phi2)])
    inside = inside.astype(jnp.bfloat16)
    for at, cls in enumerate(classes):
        for r in range(quarter):
            row0 = quarter * (2 * m + q) + r
            phi1, phi2 = phis[r]
            for c in range(comps):
                lane = (r * comps + c) * nz
                src = (r * comps + c) * nk
                for half, (p0, p1, p2) in enumerate(
                    ((own_ref, xs_ref, zs_ref), (other_ref, xc_ref, zc_ref))
                ):
                    f0 = p0[row0, c, pl.ds(cls, chunk), :]
                    f1 = p1[pl.ds(src + cls, chunk), :]
                    gy = inside * p2[pl.ds(src + cls, chunk), :] - f0
                    for j in range(JB):
                        here = pl.ds((half * JB + j) * chunk, chunk)
                        adv[at, here, pl.ds(lane, nz)] = scaled(phi1[j], gy)
                        adv[at, here, pl.ds(span + lane, nz)] = scaled(phi2[j], f1)
        total = dot_nt(adv[at], wts[...])
        for half in range(2):
            level = m if half == 0 else 1 - m
            for j in range(JB):
                first = (half * JB + j) * chunk
                piece = total[first : first + chunk] + acc_ref[pl.ds((2 * j + half) * nk + cls, chunk), :]
                keep_ref[at, level, j] = piece[:, :nk]
                send_ref[at, level, j] = piece[:, nk:].astype(jnp.bfloat16)


def near_kernel(keep_ref, got_ref, *out_refs):
    for at, ref in enumerate(out_refs):
        ref[...] = (keep_ref[at] + got_ref[at].astype(jnp.float32)).astype(ref.dtype)


def far_kernel(mine_ref, *refs):
    *parts, keep_ref, send_ref = refs
    level = lax.div(lax.axis_index("space"), NEAR)
    for ref, at in ((keep_ref, level), (send_ref, 1 - level)):
        total = mine_ref[at]
        for part in parts:
            total = total + part[at].astype(jnp.float32)
        ref[...] = total.astype(ref.dtype)


def total_kernel(keep_ref, got_ref, out_ref):
    total = keep_ref[...] + got_ref[...].astype(jnp.float32)
    for j in range(JB):
        out_ref[:, j, :] = total[j]


def on_device(n, modes, weight_ids, weight_table, j_block):
    nk, comps, _, nx, nz = modes.shape
    bf16, f32 = jnp.bfloat16, jnp.float32
    vmem = pl.BlockSpec(memory_space=pltpu.VMEM)
    smem = pl.BlockSpec(memory_space=pltpu.SMEM)
    params = pltpu.CompilerParams(vmem_limit_bytes=VMEM_LIMIT)
    quarter = nx // 4
    body = quarter * comps * nk
    own, xs, zs = pl.pallas_call(
        prep_kernel,
        out_shape=[jax.ShapeDtypeStruct((nx, comps, nk, nz), bf16)]
        + [jax.ShapeDtypeStruct((body + PADROWS, nz), bf16)] * 2,
        in_specs=[pl.BlockSpec(memory_space=pltpu.HBM)],
        out_specs=[vmem] * 3,
        scratch_shapes=[pltpu.VMEM(modes.shape, bf16), pltpu.SemaphoreType.DMA((LOADS,))],
        compiler_params=pltpu.CompilerParams(vmem_limit_bytes=PREP_LIMIT),
        cost_estimate=pl.CostEstimate(flops=1_500_000_000, bytes_accessed=2_800_000, transcendentals=0),
        name="prep",
    )(modes)

    both = ("space", "modes")
    x_pairs = [(s, s ^ 1) for s in range(n)]
    z_pairs = [(s, (s + (2 if s % 2 else -2)) % n) for s in range(n)]
    same = lambda pairs: [(2 * a + m, 2 * b + m) for a, b in pairs for m in range(2)]
    cross = lambda pairs: [(2 * a + m, 2 * b + 1 - m) for a, b in pairs for m in range(2)]
    other = lax.ppermute(own, "modes", [(0, 1), (1, 0)])
    xs = lax.ppermute(xs, both, same(x_pairs))
    zs = lax.ppermute(zs, both, same(z_pairs))
    weight, xc, zc = pl.pallas_call(
        weights_kernel,
        out_shape=[jax.ShapeDtypeStruct((nx, nz), f32)]
        + [jax.ShapeDtypeStruct((body + 8 * quarter, nz), bf16)] * 2,
        in_specs=[vmem] * 3 + [pl.BlockSpec(memory_space=pl.ANY)],
        out_specs=[vmem] * 3,
        compiler_params=params,
        name="weights",
    )(weight_ids, jnp.broadcast_to(weight_table[None], (8, NW)), own, other)
    xc = lax.ppermute(xc, both, cross(x_pairs))
    zc = lax.ppermute(zc, both, cross([(s, to) for s, to in z_pairs if abs(s - to) == 2]))

    depth = nx // 4 * comps * nz
    depth = quarter * comps * nz
    acc, w0 = pl.pallas_call(
        local_kernel,
        out_shape=[
            jax.ShapeDtypeStruct((JB * 2 * nk, 2 * nk), f32),
            jax.ShapeDtypeStruct((quarter, 2 * nk, comps * nz), bf16),
        ],
        in_specs=[vmem, vmem, vmem, smem],
        out_specs=[vmem] * 2,
        scratch_shapes=[
            pltpu.VMEM((2 * quarter, JB * 2 * nk, comps * nz), bf16),
            pltpu.VMEM((2 * quarter, 2 * nk, comps * nz), bf16),
        ],
        compiler_params=params,
        cost_estimate=pl.CostEstimate(flops=900_000_000, bytes_accessed=2_400_000, transcendentals=0),
        name="local",
    )(own, other, weight, j_block)

    acc, w1 = pl.pallas_call(
        early_kernel,
        out_shape=[
            jax.ShapeDtypeStruct((JB * 2 * nk, 2 * nk), f32),
            jax.ShapeDtypeStruct((2 * nk, depth), bf16),
        ],
        in_specs=[vmem] * 3 + [pl.BlockSpec(memory_space=pl.ANY), vmem, vmem, smem, vmem],
        out_specs=[vmem] * 2,
        scratch_shapes=[pltpu.VMEM((quarter, JB * 2 * nk, comps * nz), bf16)],
        compiler_params=params,
        cost_estimate=pl.CostEstimate(flops=600_000_000, bytes_accessed=2_400_000, transcendentals=0),
        name="early",
    )(own, other, xs, zs, xc, w0, j_block, acc)

    per_target = 2 * nk // n
    chunk = max(16, per_target)

    def crossed(count, classes_of, weighted):
        piece = (count, 2, JB, chunk, nk)
        out_shape = [jax.ShapeDtypeStruct(piece, f32), jax.ShapeDtypeStruct(piece, bf16)]
        if not weighted:
            out_shape.append(jax.ShapeDtypeStruct((2 * nk, 2 * depth), bf16))
        return pl.pallas_call(
            functools.partial(cross_kernel, classes_of, chunk, n, bool(weighted)),
            out_shape=out_shape,
            in_specs=[vmem] * 7 + [smem] + [vmem] * (1 + len(weighted)),
            out_specs=[vmem] * len(out_shape),
            scratch_shapes=[pltpu.VMEM((count, 2 * JB * chunk, 2 * depth), bf16)],
            compiler_params=params,
            cost_estimate=pl.CostEstimate(
                flops=900_000_000, bytes_accessed=4_000_000, transcendentals=0
            ),
            name="cross",
        )(own, other, xs, zs, xc, zc, w1, j_block, acc, *weighted)

    swap = [(0, 1), (1, 0)]
    if n == 2 * NEAR:
        def partners(*steps):
            return lambda s: [jnp.bitwise_xor(lax.rem(s, NEAR), step) for step in steps]

        keep_a, send_a, w2 = crossed(2, partners(1, 2), ())
        got_a = lax.ppermute(send_a, "modes", swap)
        keep_b, send_b = crossed(2, partners(0, 3), (w2,))
        got_b = lax.ppermute(send_b, "modes", swap)
        piece = (JB, chunk, nk)

        def summed(kinds, keep, got):
            return pl.pallas_call(
                near_kernel,
                out_shape=[jax.ShapeDtypeStruct((2, *piece), kind) for kind in kinds],
                in_specs=[vmem] * 2,
                out_specs=[vmem] * 2,
                compiler_params=params,
                name="near",
            )(keep, got)

        part_1, part_2 = summed((bf16, bf16), keep_a, got_a)
        mine, part_3 = summed((f32, bf16), keep_b, got_b)
        parts = [
            lax.ppermute(part, "space", [(s, s ^ step) for s in range(n)])
            for part, step in ((part_1, 1), (part_2, 2), (part_3, 3))
        ]
        keep, send = pl.pallas_call(
            far_kernel,
            out_shape=[jax.ShapeDtypeStruct(piece, f32), jax.ShapeDtypeStruct(piece, bf16)],
            in_specs=[vmem] * NEAR,
            out_specs=[vmem] * 2,
            compiler_params=params,
            name="far",
        )(mine, *parts)
        got = lax.ppermute(send, "space", [(s, s ^ NEAR) for s in range(n)])
        return pl.pallas_call(
            total_kernel,
            out_shape=jax.ShapeDtypeStruct((chunk, JB, nk), f32),
            in_specs=[vmem] * 2,
            out_specs=vmem,
            compiler_params=params,
            name="total",
        )(keep, got)

    count = nk // chunk
    keep, send, _ = crossed(count, lambda s: list(range(count)), ())
    share = (keep + lax.ppermute(send, "modes", swap)).astype(bf16)
    share = share.reshape(count, 2, JB, chunk // per_target, per_target, nk)
    share = share.transpose(1, 0, 3, 2, 4, 5).reshape(n, JB, per_target, nk)
    parts = lax.all_to_all(share, "space", 0, 0, tiled=True)
    return jnp.sum(parts.astype(f32), axis=0).transpose(1, 0, 2)


def solution(mesh):
    return jax.shard_map(
        functools.partial(on_device, mesh.shape["space"]),
        mesh=mesh,
        in_specs=(
            P("modes", None, ("groups", "space"), None, None),
            P(("groups", "space"), None, None),
            P(),
            P("groups"),
        ),
        out_specs=P(("groups", "space"), None, "modes"),
        check_vma=False,
    )
```

```python
import functools

import jax
import jax.numpy as jnp
from jax import lax
from jax.experimental import pallas as pl
from jax.experimental.pallas import tpu as pltpu
from jax.sharding import PartitionSpec as P

JB = 4
NW = 16
PADROWS = 16
LOADS = 4
X_FIRST = 0b10011111
NEAR = 4
VMEM_LIMIT = 48 * 1024 * 1024
PREP_LIMIT = 53_600 * 1024


def x_first(s, planes):
    if planes != 8:
        return s >= 0
    return lax.rem(lax.shift_right_logical(X_FIRST, s), 2) == 1


def copy_rows(ref, tr, at):
    nx, comps, nk, _ = tr.shape
    for row in range(nx // 4):
        for c in range(comps):
            ref[pl.ds((row * comps + c) * nk, nk), :] = tr[at * (nx // 4) + row, c]


def prep_kernel(planes, modes_hbm, tr, first_ref, second_ref, modes_ref, sems):
    m = lax.axis_index("modes")
    s = lax.axis_index("space")
    q = lax.rem(s, 2)
    nk, comps, _, nx, nz = modes_hbm.shape
    step = nk // LOADS
    copies = [
        pltpu.make_async_copy(
            modes_hbm.at[pl.ds(p * step, step)], modes_ref.at[pl.ds(p * step, step)], sems.at[p]
        )
        for p in range(LOADS)
    ]
    for copy in copies:
        copy.start()
    for p in range(LOADS):
        copies[p].wait()
        block = pl.ds(p * step, step)
        for c in range(comps):
            value = modes_ref[block, c, 0].astype(jnp.float32)
            tr[:, c, block] = jnp.swapaxes(value, 0, 1).astype(jnp.bfloat16)
    body = nx // 4 * comps * nk
    to_x, to_z = 2 * m + 1 - q, 2 * m + q
    x_now = x_first(s, planes)
    for ref, at in (
        (first_ref, jnp.where(x_now, to_x, to_z)),
        (second_ref, jnp.where(x_now, to_z, to_x)),
    ):
        copy_rows(ref, tr, at)
        ref[pl.ds(body, PADROWS), :] = jnp.zeros((PADROWS, nz), jnp.bfloat16)


def weights_kernel(ids_ref, table_ref, tr, _, weight_ref, xc_ref, zc_ref):
    m = lax.axis_index("modes")
    q = lax.rem(lax.axis_index("space"), 2)
    nx, comps, nk, nz = tr.shape
    quarter = nx // 4
    table = table_ref[...]
    weight = jnp.zeros((nx, nz), jnp.float32)
    for entry in range(NW):
        weight = jnp.where(ids_ref[0] == entry, table[0:1, entry : entry + 1], weight)
    weight_ref[...] = weight
    for ref, at in ((xc_ref, 2 * (1 - m) + 1 - q), (zc_ref, 2 * (1 - m) + q)):
        copy_rows(ref, tr, at)
        rest = jnp.concatenate(
            [
                jnp.broadcast_to(weight_ref[pl.ds(at * quarter + row, 1), :], (8, nz))
                for row in range(quarter)
            ],
            axis=0,
        )
        piece_of = lax.rem(lax.broadcasted_iota(jnp.int32, rest.shape, 0), 8)
        pieces = jnp.zeros(rest.shape, jnp.float32)
        for piece in range(3):
            rounded = rest.astype(jnp.bfloat16).astype(jnp.float32)
            pieces = jnp.where(piece_of == piece, rounded, pieces)
            rest = rest - rounded
        ref[pl.ds(quarter * comps * nk, 8 * quarter), :] = pieces.astype(jnp.bfloat16)


def received_weights(ref, first, quarter):
    pieces = ref[pl.ds(first, 8 * quarter), :].astype(jnp.float32)
    return [
        pieces[8 * r : 8 * r + 1] + pieces[8 * r + 1 : 8 * r + 2] + pieces[8 * r + 2 : 8 * r + 3]
        for r in range(quarter)
    ]


def picks(jb_ref, m, nk):
    first = jb_ref[0] * JB
    owner = (first >= nk).astype(jnp.int32)
    row = first - owner * nk
    within = lax.rem(row, 16)
    return owner == m, pl.multiple_of(row - within, 16), within


def picked(pick, own, other):
    mine, block, within = pick
    rows = pl.ds(block, 16)
    rows = jnp.where(mine, own(rows).astype(jnp.float32), other(rows).astype(jnp.float32))
    result = rows[0:JB]
    for start in range(JB, 16, JB):
        result = jnp.where(within == start, rows[start : start + JB], result)
    return result


def spread(row):
    return jnp.broadcast_to(row, (16, row.shape[1])).astype(jnp.bfloat16)[None]


def scaled(tile, field):
    rows, lanes = field.shape
    return (tile * field.reshape(rows // 16, 16, lanes)).reshape(rows, lanes)


def dot_nt(a, b):
    return lax.dot_general(a, b, (((1,), (1,)), ((), ())), preferred_element_type=jnp.float32)


def local_kernel(own_ref, other_ref, weight_ref, jb_ref, acc_ref, w0_ref, adv, wts):
    m = lax.axis_index("modes")
    q = lax.rem(lax.axis_index("space"), 2)
    nx, comps, nk, nz = own_ref.shape
    rows = nx // 2
    pick = picks(jb_ref, m, nk)
    for r in range(rows):
        row = rows * m + r
        below, above = lax.rem(row + nx - 1, nx), lax.rem(row + 1, nx)
        phi = [picked(pick, lambda at: own_ref[row, d, at, :], lambda at: other_ref[row, d, at, :]) for d in range(comps)]
        weight = weight_ref[pl.ds(row, 1), :]
        for c in range(comps):
            for half, ref in enumerate((own_ref, other_ref)):
                block = pl.ds(half * nk, nk)
                here = ref[row, c].astype(jnp.float32)
                gx = 0.5 * (ref[above, c].astype(jnp.float32) - ref[below, c].astype(jnp.float32))
                gz = 0.5 * (pltpu.roll(here, nz - 1, 1) - pltpu.roll(here, 1, 1))
                gx = gx.astype(jnp.bfloat16).astype(jnp.float32)
                gz = gz.astype(jnp.bfloat16).astype(jnp.float32)
                wts[r, block, pl.ds(c * nz, nz)] = (weight * here).astype(jnp.bfloat16)
                for j in range(JB):
                    total = phi[0][j : j + 1] * gx + phi[2][j : j + 1] * gz
                    adv[r, pl.ds((2 * j + half) * nk, nk), pl.ds(c * nz, nz)] = total.astype(jnp.bfloat16)
    total = dot_nt(adv[0], wts[0])
    for r in range(1, rows):
        total = total + dot_nt(adv[r], wts[r])
    acc_ref[...] = total
    quarter = rows // 2
    for r in range(quarter):
        w0_ref[r] = wts[quarter * q + r]


def same_core_rows(planes, first_ref, second_ref):
    x_came = x_first(jnp.bitwise_xor(lax.axis_index("space"), 1), planes)
    return (
        lambda rows: jnp.where(x_came, first_ref[rows, :], second_ref[rows, :]),
        lambda rows: jnp.where(x_came, second_ref[rows, :], first_ref[rows, :]),
    )


def sign_of_plane():
    return jnp.where(lax.rem(lax.axis_index("space"), 2) == 0, 0.5, -0.5)


def early_kernel(
    planes, own_ref, other_ref, first_ref, second_ref, xc_ref, w0_ref, jb_ref, acc_ref, out_ref, w1_ref, adv
):
    xs_rows, _ = same_core_rows(planes, first_ref, second_ref)
    m = lax.axis_index("modes")
    q = lax.rem(lax.axis_index("space"), 2)
    nx, comps, nk, nz = own_ref.shape
    quarter = nx // 4
    pick = picks(jb_ref, m, nk)
    weights = received_weights(xc_ref, quarter * comps * nk, quarter)
    for r in range(quarter):
        row0 = quarter * (2 * m + q) + r
        phi0 = sign_of_plane() * picked(
            pick, lambda at: own_ref[row0, 1, at, :], lambda at: other_ref[row0, 1, at, :]
        )
        phi0 = [spread(phi0[j : j + 1]) for j in range(JB)]
        for c in range(comps):
            at = pl.ds((r * comps + c) * nz, nz)
            src = pl.ds((r * comps + c) * nk, nk)
            for half, f1 in enumerate((xs_rows(src), xc_ref[src, :])):
                w1_ref[pl.ds(half * nk, nk), at] = (weights[r] * f1.astype(jnp.float32)).astype(
                    jnp.bfloat16
                )
                for j in range(JB):
                    adv[r, pl.ds((2 * j + half) * nk, nk), pl.ds(c * nz, nz)] = scaled(phi0[j], f1)
    total = acc_ref[...]
    for r in range(quarter):
        total = total + dot_nt(adv[r], w0_ref[r])
    out_ref[...] = total


def cross_kernel(classes_of, chunk, planes, has_weighted, own_ref, other_ref, *refs):
    first_ref, second_ref, xc_ref, zc_ref, w1_ref, jb_ref, acc_ref, *refs = refs
    xs_rows, zs_rows = same_core_rows(planes, first_ref, second_ref)
    if has_weighted:
        wts, keep_ref, send_ref, adv = refs
    else:
        keep_ref, send_ref, wts, adv = refs
    m = lax.axis_index("modes")
    plane = lax.axis_index("space")
    q = lax.rem(plane, 2)
    inside = jnp.where(jnp.logical_or(plane == 1, plane == planes - 2), 0.0, 1.0)
    nx, comps, nk, nz = own_ref.shape
    quarter = nx // 4
    span = quarter * comps * nz
    pick = picks(jb_ref, m, nk)
    classes = [pl.multiple_of(chunk * cls, chunk) for cls in classes_of(plane)]
    if not has_weighted:
        weights = received_weights(zc_ref, quarter * comps * nk, quarter)
        wts[:, pl.ds(0, span)] = w1_ref[...]
        for r in range(quarter):
            weight = inside * weights[r]
            for c in range(comps):
                src = pl.ds((r * comps + c) * nk, nk)
                for half, f2 in enumerate((zs_rows(src), zc_ref[src, :])):
                    wts[pl.ds(half * nk, nk), pl.ds(span + (r * comps + c) * nz, nz)] = (
                        weight * f2.astype(jnp.float32)
                    ).astype(jnp.bfloat16)
    phis = []
    for r in range(quarter):
        along = (r * comps + 1) * nk

        def moved(at):
            return pl.ds(pl.multiple_of(along + at.start, 16), at.size)

        phi1 = sign_of_plane() * picked(
            pick, lambda at: xs_rows(moved(at)), lambda at: xc_ref[moved(at), :]
        )
        phi2 = -sign_of_plane() * picked(
            pick, lambda at: zs_rows(moved(at)), lambda at: zc_ref[moved(at), :]
        )
        phis.append([[spread(phi[j : j + 1]) for j in range(JB)] for phi in (phi1, phi2)])
    inside = inside.astype(jnp.bfloat16)
    for at, cls in enumerate(classes):
        for r in range(quarter):
            row0 = quarter * (2 * m + q) + r
            phi1, phi2 = phis[r]
            for c in range(comps):
                lane = (r * comps + c) * nz
                src = (r * comps + c) * nk
                rows_at = pl.ds(pl.multiple_of(src + cls, 16), chunk)
                for half, (p0, f1, f2) in enumerate(
                    (
                        (own_ref, xs_rows(rows_at), zs_rows(rows_at)),
                        (other_ref, xc_ref[rows_at, :], zc_ref[rows_at, :]),
                    )
                ):
                    f0 = p0[row0, c, pl.ds(cls, chunk), :]
                    gy = inside * f2 - f0
                    for j in range(JB):
                        here = pl.ds((half * JB + j) * chunk, chunk)
                        adv[at, here, pl.ds(lane, nz)] = scaled(phi1[j], gy)
                        adv[at, here, pl.ds(span + lane, nz)] = scaled(phi2[j], f1)
        total = dot_nt(adv[at], wts[...])
        for half in range(2):
            level = m if half == 0 else 1 - m
            for j in range(JB):
                first = (half * JB + j) * chunk
                piece = total[first : first + chunk] + acc_ref[pl.ds((2 * j + half) * nk + cls, chunk), :]
                keep_ref[at, level, j] = piece[:, :nk]
                send_ref[at, level, j] = piece[:, nk:].astype(jnp.bfloat16)


def near_kernel(keep_ref, got_ref, *out_refs):
    for at, ref in enumerate(out_refs):
        ref[...] = (keep_ref[at] + got_ref[at].astype(jnp.float32)).astype(ref.dtype)


def far_kernel(mine_ref, *refs):
    *parts, keep_ref, send_ref = refs
    level = lax.div(lax.axis_index("space"), NEAR)
    for ref, at in ((keep_ref, level), (send_ref, 1 - level)):
        total = mine_ref[at]
        for part in parts:
            total = total + part[at].astype(jnp.float32)
        ref[...] = total.astype(ref.dtype)


def total_kernel(keep_ref, got_ref, out_ref):
    total = keep_ref[...] + got_ref[...].astype(jnp.float32)
    for j in range(JB):
        out_ref[:, j, :] = total[j]


def on_device(n, modes, weight_ids, weight_table, j_block):
    nk, comps, _, nx, nz = modes.shape
    bf16, f32 = jnp.bfloat16, jnp.float32
    vmem = pl.BlockSpec(memory_space=pltpu.VMEM)
    smem = pl.BlockSpec(memory_space=pltpu.SMEM)
    params = pltpu.CompilerParams(vmem_limit_bytes=VMEM_LIMIT)
    quarter = nx // 4
    body = quarter * comps * nk
    own, first, second = pl.pallas_call(
        functools.partial(prep_kernel, n),
        out_shape=[jax.ShapeDtypeStruct((nx, comps, nk, nz), bf16)]
        + [jax.ShapeDtypeStruct((body + PADROWS, nz), bf16)] * 2,
        in_specs=[pl.BlockSpec(memory_space=pltpu.HBM)],
        out_specs=[vmem] * 3,
        scratch_shapes=[pltpu.VMEM(modes.shape, bf16), pltpu.SemaphoreType.DMA((LOADS,))],
        compiler_params=pltpu.CompilerParams(vmem_limit_bytes=PREP_LIMIT),
        cost_estimate=pl.CostEstimate(flops=1_500_000_000, bytes_accessed=2_800_000, transcendentals=0),
        name="prep",
    )(modes)

    both = ("space", "modes")
    x_to = lambda s: s ^ 1
    z_to = lambda s: s + 2 if s % 2 else s - 2
    x_now = [n != 8 or X_FIRST >> s & 1 for s in range(n)]
    firsts = [(s, x_to(s) if x_now[s] else z_to(s)) for s in range(n)]
    seconds = [(s, z_to(s) % n if x_now[s] else x_to(s)) for s in range(n)]
    same = lambda pairs: [(2 * a + m, 2 * b + m) for a, b in pairs for m in range(2)]
    cross = lambda pairs: [(2 * a + m, 2 * b + 1 - m) for a, b in pairs for m in range(2)]
    other = lax.ppermute(own, "modes", [(0, 1), (1, 0)])
    first = lax.ppermute(first, both, same(firsts))
    second = lax.ppermute(second, both, same(seconds))
    weight, xc, zc = pl.pallas_call(
        weights_kernel,
        out_shape=[jax.ShapeDtypeStruct((nx, nz), f32)]
        + [jax.ShapeDtypeStruct((body + 8 * quarter, nz), bf16)] * 2,
        in_specs=[vmem] * 3 + [pl.BlockSpec(memory_space=pl.ANY)],
        out_specs=[vmem] * 3,
        compiler_params=params,
        name="weights",
    )(weight_ids, jnp.broadcast_to(weight_table[None], (8, NW)), own, other)
    xc = lax.ppermute(xc, both, cross([(s, x_to(s)) for s in range(n)]))
    zc = lax.ppermute(zc, both, cross([(s, z_to(s)) for s in range(n) if 0 <= z_to(s) < n]))

    depth = nx // 4 * comps * nz
    depth = quarter * comps * nz
    acc, w0 = pl.pallas_call(
        local_kernel,
        out_shape=[
            jax.ShapeDtypeStruct((JB * 2 * nk, 2 * nk), f32),
            jax.ShapeDtypeStruct((quarter, 2 * nk, comps * nz), bf16),
        ],
        in_specs=[vmem, vmem, vmem, smem],
        out_specs=[vmem] * 2,
        scratch_shapes=[
            pltpu.VMEM((2 * quarter, JB * 2 * nk, comps * nz), bf16),
            pltpu.VMEM((2 * quarter, 2 * nk, comps * nz), bf16),
        ],
        compiler_params=params,
        cost_estimate=pl.CostEstimate(flops=900_000_000, bytes_accessed=2_400_000, transcendentals=0),
        name="local",
    )(own, other, weight, j_block)

    acc, w1 = pl.pallas_call(
        functools.partial(early_kernel, n),
        out_shape=[
            jax.ShapeDtypeStruct((JB * 2 * nk, 2 * nk), f32),
            jax.ShapeDtypeStruct((2 * nk, depth), bf16),
        ],
        in_specs=[vmem] * 6 + [smem, vmem],
        out_specs=[vmem] * 2,
        scratch_shapes=[pltpu.VMEM((quarter, JB * 2 * nk, comps * nz), bf16)],
        compiler_params=params,
        cost_estimate=pl.CostEstimate(flops=600_000_000, bytes_accessed=2_400_000, transcendentals=0),
        name="early",
    )(own, other, first, second, xc, w0, j_block, acc)

    per_target = 2 * nk // n
    chunk = max(16, per_target)

    def crossed(count, classes_of, weighted):
        piece = (count, 2, JB, chunk, nk)
        out_shape = [jax.ShapeDtypeStruct(piece, f32), jax.ShapeDtypeStruct(piece, bf16)]
        if not weighted:
            out_shape.append(jax.ShapeDtypeStruct((2 * nk, 2 * depth), bf16))
        return pl.pallas_call(
            functools.partial(cross_kernel, classes_of, chunk, n, bool(weighted)),
            out_shape=out_shape,
            in_specs=[vmem] * 7 + [smem] + [vmem] * (1 + len(weighted)),
            out_specs=[vmem] * len(out_shape),
            scratch_shapes=[pltpu.VMEM((count, 2 * JB * chunk, 2 * depth), bf16)],
            compiler_params=params,
            cost_estimate=pl.CostEstimate(
                flops=900_000_000, bytes_accessed=4_000_000, transcendentals=0
            ),
            name="cross",
        )(own, other, first, second, xc, zc, w1, j_block, acc, *weighted)

    swap = [(0, 1), (1, 0)]
    if n == 2 * NEAR:
        def partners(*steps):
            return lambda s: [jnp.bitwise_xor(lax.rem(s, NEAR), step) for step in steps]

        keep_a, send_a, w2 = crossed(2, partners(3, 1), ())
        got_a = lax.ppermute(send_a, "modes", swap)
        keep_b, send_b = crossed(2, partners(0, 2), (w2,))
        got_b = lax.ppermute(send_b, "modes", swap)
        piece = (JB, chunk, nk)

        def summed(kinds, keep, got):
            return pl.pallas_call(
                near_kernel,
                out_shape=[jax.ShapeDtypeStruct((2, *piece), kind) for kind in kinds],
                in_specs=[vmem] * 2,
                out_specs=[vmem] * 2,
                compiler_params=params,
                name="near",
            )(keep, got)

        part_3, part_1 = summed((bf16, bf16), keep_a, got_a)
        mine, part_2 = summed((f32, bf16), keep_b, got_b)
        parts = [
            lax.ppermute(part, "space", [(s, s ^ step) for s in range(n)])
            for part, step in ((part_3, 3), (part_1, 1), (part_2, 2))
        ]
        keep, send = pl.pallas_call(
            far_kernel,
            out_shape=[jax.ShapeDtypeStruct(piece, f32), jax.ShapeDtypeStruct(piece, bf16)],
            in_specs=[vmem] * NEAR,
            out_specs=[vmem] * 2,
            compiler_params=params,
            name="far",
        )(mine, *parts)
        got = lax.ppermute(send, "space", [(s, s ^ NEAR) for s in range(n)])
        return pl.pallas_call(
            total_kernel,
            out_shape=jax.ShapeDtypeStruct((chunk, JB, nk), f32),
            in_specs=[vmem] * 2,
            out_specs=vmem,
            compiler_params=params,
            name="total",
        )(keep, got)

    count = nk // chunk
    keep, send, _ = crossed(count, lambda s: list(range(count)), ())
    share = (keep + lax.ppermute(send, "modes", swap)).astype(bf16)
    share = share.reshape(count, 2, JB, chunk // per_target, per_target, nk)
    share = share.transpose(1, 0, 3, 2, 4, 5).reshape(n, JB, per_target, nk)
    parts = lax.all_to_all(share, "space", 0, 0, tiled=True)
    return jnp.sum(parts.astype(f32), axis=0).transpose(1, 0, 2)


def solution(mesh):
    return jax.shard_map(
        functools.partial(on_device, mesh.shape["space"]),
        mesh=mesh,
        in_specs=(
            P("modes", None, ("groups", "space"), None, None),
            P(("groups", "space"), None, None),
            P(),
            P("groups"),
        ),
        out_specs=P(("groups", "space"), None, "modes"),
        check_vma=False,
    )
```

```python
import functools

import jax
import jax.numpy as jnp
from jax import lax
from jax.experimental import pallas as pl
from jax.experimental.pallas import tpu as pltpu
from jax.sharding import PartitionSpec as P

JB = 4
NW = 16
PADROWS = 16
LOADS = 4
X_FIRST = 0b10011111
NEAR = 4
VMEM_LIMIT = 48 * 1024 * 1024
PREP_LIMIT = 53_600 * 1024


def x_first(s, planes):
    if planes != 8:
        return s >= 0
    return lax.rem(lax.shift_right_logical(X_FIRST, s), 2) == 1


def copy_rows(ref, tr, at):
    nx, comps, nk, _ = tr.shape
    for row in range(nx // 4):
        for c in range(comps):
            ref[pl.ds((row * comps + c) * nk, nk), :] = tr[at * (nx // 4) + row, c]


def prep_kernel(planes, modes_hbm, tr, first_ref, second_ref, modes_ref, sems):
    m = lax.axis_index("modes")
    s = lax.axis_index("space")
    q = lax.rem(s, 2)
    nk, comps, _, nx, nz = modes_hbm.shape
    step = nk // LOADS
    copies = [
        pltpu.make_async_copy(
            modes_hbm.at[pl.ds(p * step, step)], modes_ref.at[pl.ds(p * step, step)], sems.at[p]
        )
        for p in range(LOADS)
    ]
    for copy in copies:
        copy.start()
    for p in range(LOADS):
        copies[p].wait()
        block = pl.ds(p * step, step)
        for c in range(comps):
            value = modes_ref[block, c, 0].astype(jnp.float32)
            tr[:, c, block] = jnp.swapaxes(value, 0, 1).astype(jnp.bfloat16)
    body = nx // 4 * comps * nk
    to_x, to_z = 2 * m + 1 - q, 2 * m + q
    x_now = x_first(s, planes)
    for ref, at in (
        (first_ref, jnp.where(x_now, to_x, to_z)),
        (second_ref, jnp.where(x_now, to_z, to_x)),
    ):
        copy_rows(ref, tr, at)
        ref[pl.ds(body, PADROWS), :] = jnp.zeros((PADROWS, nz), jnp.bfloat16)


def weights_kernel(ids_ref, table_ref, tr, _, weight_ref, xc_ref, zc_ref):
    m = lax.axis_index("modes")
    q = lax.rem(lax.axis_index("space"), 2)
    nx, comps, nk, nz = tr.shape
    quarter = nx // 4
    table = table_ref[...]
    weight = jnp.zeros((nx, nz), jnp.float32)
    for entry in range(NW):
        weight = jnp.where(ids_ref[0] == entry, table[0:1, entry : entry + 1], weight)
    weight_ref[...] = weight
    for ref, at in ((xc_ref, 2 * (1 - m) + 1 - q), (zc_ref, 2 * (1 - m) + q)):
        copy_rows(ref, tr, at)
        rest = jnp.concatenate(
            [
                jnp.broadcast_to(weight_ref[pl.ds(at * quarter + row, 1), :], (8, nz))
                for row in range(quarter)
            ],
            axis=0,
        )
        piece_of = lax.rem(lax.broadcasted_iota(jnp.int32, rest.shape, 0), 8)
        pieces = jnp.zeros(rest.shape, jnp.float32)
        for piece in range(3):
            rounded = rest.astype(jnp.bfloat16).astype(jnp.float32)
            pieces = jnp.where(piece_of == piece, rounded, pieces)
            rest = rest - rounded
        ref[pl.ds(quarter * comps * nk, 8 * quarter), :] = pieces.astype(jnp.bfloat16)


def received_weights(ref, first, quarter):
    pieces = ref[pl.ds(first, 8 * quarter), :].astype(jnp.float32)
    return [
        pieces[8 * r : 8 * r + 1] + pieces[8 * r + 1 : 8 * r + 2] + pieces[8 * r + 2 : 8 * r + 3]
        for r in range(quarter)
    ]


def picks(jb_ref, m, nk):
    first = jb_ref[0] * JB
    owner = (first >= nk).astype(jnp.int32)
    row = first - owner * nk
    within = lax.rem(row, 16)
    return owner == m, pl.multiple_of(row - within, 16), within


def picked(pick, own, other):
    mine, block, within = pick
    rows = pl.ds(block, 16)
    rows = jnp.where(mine, own(rows).astype(jnp.float32), other(rows).astype(jnp.float32))
    result = rows[0:JB]
    for start in range(JB, 16, JB):
        result = jnp.where(within == start, rows[start : start + JB], result)
    return result


def spread(row):
    return jnp.broadcast_to(row, (16, row.shape[1])).astype(jnp.bfloat16)[None]


def scaled(tile, field):
    rows, lanes = field.shape
    return (tile * field.reshape(rows // 16, 16, lanes)).reshape(rows, lanes)


def dot_nt(a, b):
    return lax.dot_general(a, b, (((1,), (1,)), ((), ())), preferred_element_type=jnp.float32)


def local_kernel(own_ref, other_ref, weight_ref, jb_ref, acc_ref, w0_ref, adv, wts):
    m = lax.axis_index("modes")
    q = lax.rem(lax.axis_index("space"), 2)
    nx, comps, nk, nz = own_ref.shape
    rows = nx // 2
    pick = picks(jb_ref, m, nk)
    for r in range(rows):
        row = rows * m + r
        below, above = lax.rem(row + nx - 1, nx), lax.rem(row + 1, nx)
        phi = [picked(pick, lambda at: own_ref[row, d, at, :], lambda at: other_ref[row, d, at, :]) for d in range(comps)]
        weight = weight_ref[pl.ds(row, 1), :]
        for c in range(comps):
            for half, ref in enumerate((own_ref, other_ref)):
                block = pl.ds(half * nk, nk)
                here = ref[row, c].astype(jnp.float32)
                gx = 0.5 * (ref[above, c].astype(jnp.float32) - ref[below, c].astype(jnp.float32))
                gz = 0.5 * (pltpu.roll(here, nz - 1, 1) - pltpu.roll(here, 1, 1))
                gx = gx.astype(jnp.bfloat16).astype(jnp.float32)
                gz = gz.astype(jnp.bfloat16).astype(jnp.float32)
                wts[r, block, pl.ds(c * nz, nz)] = (weight * here).astype(jnp.bfloat16)
                for j in range(JB):
                    total = phi[0][j : j + 1] * gx + phi[2][j : j + 1] * gz
                    adv[r, pl.ds((2 * j + half) * nk, nk), pl.ds(c * nz, nz)] = total.astype(jnp.bfloat16)
    total = dot_nt(adv[0], wts[0])
    for r in range(1, rows):
        total = total + dot_nt(adv[r], wts[r])
    acc_ref[...] = total
    quarter = rows // 2
    for r in range(quarter):
        w0_ref[r] = wts[quarter * q + r]


def same_core_rows(planes, first_ref, second_ref):
    x_came = x_first(jnp.bitwise_xor(lax.axis_index("space"), 1), planes)
    return (
        lambda rows: jnp.where(x_came, first_ref[rows, :], second_ref[rows, :]),
        lambda rows: jnp.where(x_came, second_ref[rows, :], first_ref[rows, :]),
    )


def sign_of_plane():
    return jnp.where(lax.rem(lax.axis_index("space"), 2) == 0, 0.5, -0.5)


def early_kernel(
    planes, own_ref, other_ref, first_ref, second_ref, xc_ref, w0_ref, jb_ref, acc_ref, out_ref, w1_ref, adv
):
    xs_rows, _ = same_core_rows(planes, first_ref, second_ref)
    m = lax.axis_index("modes")
    q = lax.rem(lax.axis_index("space"), 2)
    nx, comps, nk, nz = own_ref.shape
    quarter = nx // 4
    pick = picks(jb_ref, m, nk)
    weights = received_weights(xc_ref, quarter * comps * nk, quarter)
    for r in range(quarter):
        row0 = quarter * (2 * m + q) + r
        phi0 = sign_of_plane() * picked(
            pick, lambda at: own_ref[row0, 1, at, :], lambda at: other_ref[row0, 1, at, :]
        )
        phi0 = [spread(phi0[j : j + 1]) for j in range(JB)]
        for c in range(comps):
            at = pl.ds((r * comps + c) * nz, nz)
            src = pl.ds((r * comps + c) * nk, nk)
            for half, f1 in enumerate((xs_rows(src), xc_ref[src, :])):
                w1_ref[pl.ds(half * nk, nk), at] = (weights[r] * f1.astype(jnp.float32)).astype(
                    jnp.bfloat16
                )
                for j in range(JB):
                    adv[r, pl.ds((2 * j + half) * nk, nk), pl.ds(c * nz, nz)] = scaled(phi0[j], f1)
    total = acc_ref[...]
    for r in range(quarter):
        total = total + dot_nt(adv[r], w0_ref[r])
    out_ref[...] = total


def cross_kernel(classes_of, chunk, planes, has_weighted, own_ref, other_ref, *refs):
    first_ref, second_ref, xc_ref, zc_ref, w1_ref, jb_ref, acc_ref, *refs = refs
    xs_rows, zs_rows = same_core_rows(planes, first_ref, second_ref)
    if has_weighted:
        wts, keep_ref, send_ref, adv = refs
    else:
        keep_ref, send_ref, wts, adv = refs
    m = lax.axis_index("modes")
    plane = lax.axis_index("space")
    q = lax.rem(plane, 2)
    inside = jnp.where(jnp.logical_or(plane == 1, plane == planes - 2), 0.0, 1.0)
    nx, comps, nk, nz = own_ref.shape
    quarter = nx // 4
    span = quarter * comps * nz
    pick = picks(jb_ref, m, nk)
    classes = [pl.multiple_of(chunk * cls, chunk) for cls in classes_of(plane)]
    if not has_weighted:
        weights = received_weights(zc_ref, quarter * comps * nk, quarter)
        wts[:, pl.ds(0, span)] = w1_ref[...]
        for r in range(quarter):
            weight = inside * weights[r]
            for c in range(comps):
                src = pl.ds((r * comps + c) * nk, nk)
                for half, f2 in enumerate((zs_rows(src), zc_ref[src, :])):
                    wts[pl.ds(half * nk, nk), pl.ds(span + (r * comps + c) * nz, nz)] = (
                        weight * f2.astype(jnp.float32)
                    ).astype(jnp.bfloat16)
    phis = []
    for r in range(quarter):
        along = (r * comps + 1) * nk

        def moved(at):
            return pl.ds(pl.multiple_of(along + at.start, 16), at.size)

        phi1 = sign_of_plane() * picked(
            pick, lambda at: xs_rows(moved(at)), lambda at: xc_ref[moved(at), :]
        )
        phi2 = -sign_of_plane() * picked(
            pick, lambda at: zs_rows(moved(at)), lambda at: zc_ref[moved(at), :]
        )
        phis.append([[spread(phi[j : j + 1]) for j in range(JB)] for phi in (phi1, phi2)])
    inside = inside.astype(jnp.bfloat16)
    for at, cls in enumerate(classes):
        for r in range(quarter):
            row0 = quarter * (2 * m + q) + r
            phi1, phi2 = phis[r]
            for c in range(comps):
                lane = (r * comps + c) * nz
                src = (r * comps + c) * nk
                rows_at = pl.ds(pl.multiple_of(src + cls, 16), chunk)
                for half, (p0, f1, f2) in enumerate(
                    (
                        (own_ref, xs_rows(rows_at), zs_rows(rows_at)),
                        (other_ref, xc_ref[rows_at, :], zc_ref[rows_at, :]),
                    )
                ):
                    f0 = p0[row0, c, pl.ds(cls, chunk), :]
                    gy = inside * f2 - f0
                    for j in range(JB):
                        here = pl.ds((half * JB + j) * chunk, chunk)
                        adv[at, here, pl.ds(lane, nz)] = scaled(phi1[j], gy)
                        adv[at, here, pl.ds(span + lane, nz)] = scaled(phi2[j], f1)
        total = dot_nt(adv[at], wts[...])
        for half in range(2):
            level = m if half == 0 else 1 - m
            for j in range(JB):
                first = (half * JB + j) * chunk
                piece = total[first : first + chunk] + acc_ref[pl.ds((2 * j + half) * nk + cls, chunk), :]
                keep_ref[at, level, j] = piece[:, :nk]
                row = pl.multiple_of(((2 * at + level) * JB + j) * chunk, chunk)
                send_ref[pl.ds(row, chunk), :] = piece[:, nk:].astype(jnp.bfloat16)


def near_kernel(keep_ref, got_ref, *out_refs):
    got = got_ref[...].astype(jnp.float32).reshape(keep_ref.shape)
    for at, ref in enumerate(out_refs):
        ref[...] = (keep_ref[at] + got[at]).astype(ref.dtype).reshape(ref.shape)


def far_kernel(mine_ref, *refs):
    *parts, keep_ref, send_ref = refs
    level = lax.div(lax.axis_index("space"), NEAR)
    rows = send_ref.shape[0]
    for ref, at in ((keep_ref, level), (send_ref, 1 - level)):
        total = mine_ref[at]
        for part in parts:
            piece = part[pl.ds(pl.multiple_of(at * rows, rows), rows), :]
            total = total + piece.astype(jnp.float32).reshape(total.shape)
        ref[...] = total.astype(ref.dtype).reshape(ref.shape)


def total_kernel(keep_ref, got_ref, out_ref):
    total = keep_ref[...] + got_ref[...].astype(jnp.float32).reshape(keep_ref.shape)
    for j in range(JB):
        out_ref[:, j, :] = total[j]


def on_device(n, modes, weight_ids, weight_table, j_block):
    nk, comps, _, nx, nz = modes.shape
    bf16, f32 = jnp.bfloat16, jnp.float32
    vmem = pl.BlockSpec(memory_space=pltpu.VMEM)
    smem = pl.BlockSpec(memory_space=pltpu.SMEM)
    params = pltpu.CompilerParams(vmem_limit_bytes=VMEM_LIMIT)
    quarter = nx // 4
    body = quarter * comps * nk
    own, first, second = pl.pallas_call(
        functools.partial(prep_kernel, n),
        out_shape=[jax.ShapeDtypeStruct((nx, comps, nk, nz), bf16)]
        + [jax.ShapeDtypeStruct((body + PADROWS, nz), bf16)] * 2,
        in_specs=[pl.BlockSpec(memory_space=pltpu.HBM)],
        out_specs=[vmem] * 3,
        scratch_shapes=[pltpu.VMEM(modes.shape, bf16), pltpu.SemaphoreType.DMA((LOADS,))],
        compiler_params=pltpu.CompilerParams(vmem_limit_bytes=PREP_LIMIT),
        cost_estimate=pl.CostEstimate(flops=1_500_000_000, bytes_accessed=2_800_000, transcendentals=0),
        name="prep",
    )(modes)

    both = ("space", "modes")
    x_to = lambda s: s ^ 1
    z_to = lambda s: s + 2 if s % 2 else s - 2
    x_now = [n != 8 or X_FIRST >> s & 1 for s in range(n)]
    firsts = [(s, x_to(s) if x_now[s] else z_to(s)) for s in range(n)]
    seconds = [(s, z_to(s) % n if x_now[s] else x_to(s)) for s in range(n)]
    same = lambda pairs: [(2 * a + m, 2 * b + m) for a, b in pairs for m in range(2)]
    cross = lambda pairs: [(2 * a + m, 2 * b + 1 - m) for a, b in pairs for m in range(2)]
    other = lax.ppermute(own, "modes", [(0, 1), (1, 0)])
    first = lax.ppermute(first, both, same(firsts))
    second = lax.ppermute(second, both, same(seconds))
    weight, xc, zc = pl.pallas_call(
        weights_kernel,
        out_shape=[jax.ShapeDtypeStruct((nx, nz), f32)]
        + [jax.ShapeDtypeStruct((body + 8 * quarter, nz), bf16)] * 2,
        in_specs=[vmem] * 3 + [pl.BlockSpec(memory_space=pl.ANY)],
        out_specs=[vmem] * 3,
        compiler_params=params,
        name="weights",
    )(weight_ids, jnp.broadcast_to(weight_table[None], (8, NW)), own, other)
    xc = lax.ppermute(xc, both, cross([(s, x_to(s)) for s in range(n)]))
    zc = lax.ppermute(zc, both, cross([(s, z_to(s)) for s in range(n) if 0 <= z_to(s) < n]))

    depth = nx // 4 * comps * nz
    depth = quarter * comps * nz
    acc, w0 = pl.pallas_call(
        local_kernel,
        out_shape=[
            jax.ShapeDtypeStruct((JB * 2 * nk, 2 * nk), f32),
            jax.ShapeDtypeStruct((quarter, 2 * nk, comps * nz), bf16),
        ],
        in_specs=[vmem, vmem, vmem, smem],
        out_specs=[vmem] * 2,
        scratch_shapes=[
            pltpu.VMEM((2 * quarter, JB * 2 * nk, comps * nz), bf16),
            pltpu.VMEM((2 * quarter, 2 * nk, comps * nz), bf16),
        ],
        compiler_params=params,
        cost_estimate=pl.CostEstimate(flops=900_000_000, bytes_accessed=2_400_000, transcendentals=0),
        name="local",
    )(own, other, weight, j_block)

    acc, w1 = pl.pallas_call(
        functools.partial(early_kernel, n),
        out_shape=[
            jax.ShapeDtypeStruct((JB * 2 * nk, 2 * nk), f32),
            jax.ShapeDtypeStruct((2 * nk, depth), bf16),
        ],
        in_specs=[vmem] * 6 + [smem, vmem],
        out_specs=[vmem] * 2,
        scratch_shapes=[pltpu.VMEM((quarter, JB * 2 * nk, comps * nz), bf16)],
        compiler_params=params,
        cost_estimate=pl.CostEstimate(flops=600_000_000, bytes_accessed=2_400_000, transcendentals=0),
        name="early",
    )(own, other, first, second, xc, w0, j_block, acc)

    per_target = 2 * nk // n
    chunk = max(16, per_target)

    def crossed(count, classes_of, weighted):
        piece = (count, 2, JB, chunk, nk)
        out_shape = [
            jax.ShapeDtypeStruct(piece, f32),
            jax.ShapeDtypeStruct((count * 2 * JB * chunk, nk), bf16),
        ]
        if not weighted:
            out_shape.append(jax.ShapeDtypeStruct((2 * nk, 2 * depth), bf16))
        return pl.pallas_call(
            functools.partial(cross_kernel, classes_of, chunk, n, bool(weighted)),
            out_shape=out_shape,
            in_specs=[vmem] * 7 + [smem] + [vmem] * (1 + len(weighted)),
            out_specs=[vmem] * len(out_shape),
            scratch_shapes=[pltpu.VMEM((count, 2 * JB * chunk, 2 * depth), bf16)],
            compiler_params=params,
            cost_estimate=pl.CostEstimate(
                flops=900_000_000, bytes_accessed=4_000_000, transcendentals=0
            ),
            name="cross",
        )(own, other, first, second, xc, zc, w1, j_block, acc, *weighted)

    swap = [(0, 1), (1, 0)]
    if n == 2 * NEAR:
        def partners(*steps):
            return lambda s: [jnp.bitwise_xor(lax.rem(s, NEAR), step) for step in steps]

        keep_a, send_a, w2 = crossed(2, partners(3, 1), ())
        got_a = lax.ppermute(send_a, "modes", swap)
        keep_b, send_b = crossed(2, partners(0, 2), (w2,))
        got_b = lax.ppermute(send_b, "modes", swap)
        piece = (JB, chunk, nk)

        def summed(out_shape, keep, got):
            return pl.pallas_call(
                near_kernel,
                out_shape=out_shape,
                in_specs=[vmem] * 2,
                out_specs=[vmem] * 2,
                compiler_params=params,
                name="near",
            )(keep, got)

        kept = jax.ShapeDtypeStruct((2, *piece), f32)
        sent = jax.ShapeDtypeStruct((2 * JB * chunk, nk), bf16)
        part_3, part_1 = summed([sent, sent], keep_a, got_a)
        mine, part_2 = summed([kept, sent], keep_b, got_b)
        parts = [
            lax.ppermute(part, "space", [(s, s ^ step) for s in range(n)])
            for part, step in ((part_3, 3), (part_1, 1), (part_2, 2))
        ]
        keep, send = pl.pallas_call(
            far_kernel,
            out_shape=[
                jax.ShapeDtypeStruct(piece, f32),
                jax.ShapeDtypeStruct((JB * chunk, nk), bf16),
            ],
            in_specs=[vmem] * NEAR,
            out_specs=[vmem] * 2,
            compiler_params=params,
            name="far",
        )(mine, *parts)
        got = lax.ppermute(send, "space", [(s, s ^ NEAR) for s in range(n)])
        return pl.pallas_call(
            total_kernel,
            out_shape=jax.ShapeDtypeStruct((chunk, JB, nk), f32),
            in_specs=[vmem] * 2,
            out_specs=vmem,
            compiler_params=params,
            name="total",
        )(keep, got)

    count = nk // chunk
    keep, send, _ = crossed(count, lambda s: list(range(count)), ())
    share = (keep + lax.ppermute(send, "modes", swap).reshape(keep.shape)).astype(bf16)
    share = share.reshape(count, 2, JB, chunk // per_target, per_target, nk)
    share = share.transpose(1, 0, 3, 2, 4, 5).reshape(n, JB, per_target, nk)
    parts = lax.all_to_all(share, "space", 0, 0, tiled=True)
    return jnp.sum(parts.astype(f32), axis=0).transpose(1, 0, 2)


def solution(mesh):
    return jax.shard_map(
        functools.partial(on_device, mesh.shape["space"]),
        mesh=mesh,
        in_specs=(
            P("modes", None, ("groups", "space"), None, None),
            P(("groups", "space"), None, None),
            P(),
            P("groups"),
        ),
        out_specs=P(("groups", "space"), None, "modes"),
        check_vma=False,
    )
```

```python
import functools

import jax
import jax.numpy as jnp
from jax import lax
from jax.experimental import pallas as pl
from jax.experimental.pallas import tpu as pltpu
from jax.sharding import PartitionSpec as P

JB = 4
NW = 16
PADROWS = 16
LOADS = 4
X_FIRST = 0b10011111
NEAR = 4
VMEM_LIMIT = 48 * 1024 * 1024
PREP_LIMIT = 53_600 * 1024


def x_first(s, planes):
    if planes != 8:
        return s >= 0
    return lax.rem(lax.shift_right_logical(X_FIRST, s), 2) == 1


def copy_rows(ref, tr, at):
    nx, comps, nk, _ = tr.shape
    for row in range(nx // 4):
        for c in range(comps):
            ref[pl.ds((row * comps + c) * nk, nk), :] = tr[at * (nx // 4) + row, c]


def prep_kernel(planes, modes_hbm, tr, first_ref, second_ref, modes_ref, sems):
    m = lax.axis_index("modes")
    s = lax.axis_index("space")
    q = lax.rem(s, 2)
    nk, comps, _, nx, nz = modes_hbm.shape
    step = nk // LOADS
    copies = [
        pltpu.make_async_copy(
            modes_hbm.at[pl.ds(p * step, step)], modes_ref.at[pl.ds(p * step, step)], sems.at[p]
        )
        for p in range(LOADS)
    ]
    for copy in copies:
        copy.start()
    for p in range(LOADS):
        copies[p].wait()
        block = pl.ds(p * step, step)
        for c in range(comps):
            value = modes_ref[block, c, 0].astype(jnp.float32)
            tr[:, c, block] = jnp.swapaxes(value, 0, 1).astype(jnp.bfloat16)
    body = nx // 4 * comps * nk
    to_x, to_z = 2 * m + 1 - q, 2 * m + q
    x_now = x_first(s, planes)
    for ref, at in (
        (first_ref, jnp.where(x_now, to_x, to_z)),
        (second_ref, jnp.where(x_now, to_z, to_x)),
    ):
        copy_rows(ref, tr, at)
        ref[pl.ds(body, PADROWS), :] = jnp.zeros((PADROWS, nz), jnp.bfloat16)


def weights_kernel(ids_ref, table_ref, tr, _, weight_ref, xc_ref, zc_ref):
    m = lax.axis_index("modes")
    q = lax.rem(lax.axis_index("space"), 2)
    nx, comps, nk, nz = tr.shape
    quarter = nx // 4
    table = table_ref[...]
    weight = jnp.zeros((nx, nz), jnp.float32)
    for entry in range(NW):
        weight = jnp.where(ids_ref[0] == entry, table[0:1, entry : entry + 1], weight)
    weight_ref[...] = weight
    for ref, at in ((xc_ref, 2 * (1 - m) + 1 - q), (zc_ref, 2 * (1 - m) + q)):
        copy_rows(ref, tr, at)
        rest = jnp.concatenate(
            [
                jnp.broadcast_to(weight_ref[pl.ds(at * quarter + row, 1), :], (8, nz))
                for row in range(quarter)
            ],
            axis=0,
        )
        piece_of = lax.rem(lax.broadcasted_iota(jnp.int32, rest.shape, 0), 8)
        pieces = jnp.zeros(rest.shape, jnp.float32)
        for piece in range(3):
            rounded = rest.astype(jnp.bfloat16).astype(jnp.float32)
            pieces = jnp.where(piece_of == piece, rounded, pieces)
            rest = rest - rounded
        ref[pl.ds(quarter * comps * nk, 8 * quarter), :] = pieces.astype(jnp.bfloat16)


def received_weights(ref, first, quarter):
    pieces = ref[pl.ds(first, 8 * quarter), :].astype(jnp.float32)
    return [
        pieces[8 * r : 8 * r + 1] + pieces[8 * r + 1 : 8 * r + 2] + pieces[8 * r + 2 : 8 * r + 3]
        for r in range(quarter)
    ]


def picks(jb_ref, m, nk):
    first = jb_ref[0] * JB
    owner = (first >= nk).astype(jnp.int32)
    row = first - owner * nk
    within = lax.rem(row, 16)
    return owner == m, pl.multiple_of(row - within, 16), within


def picked(pick, own, other):
    mine, block, within = pick
    rows = pl.ds(block, 16)
    rows = jnp.where(mine, own(rows).astype(jnp.float32), other(rows).astype(jnp.float32))
    result = rows[0:JB]
    for start in range(JB, 16, JB):
        result = jnp.where(within == start, rows[start : start + JB], result)
    return result


def spread(row):
    return jnp.broadcast_to(row, (16, row.shape[1])).astype(jnp.bfloat16)[None]


def scaled(tile, field):
    rows, lanes = field.shape
    return (tile * field.reshape(rows // 16, 16, lanes)).reshape(rows, lanes)


def dot_nt(a, b):
    return lax.dot_general(a, b, (((1,), (1,)), ((), ())), preferred_element_type=jnp.float32)


def local_kernel(own_ref, other_ref, weight_ref, jb_ref, acc_ref, w0_ref, adv, wts):
    m = lax.axis_index("modes")
    q = lax.rem(lax.axis_index("space"), 2)
    nx, comps, nk, nz = own_ref.shape
    rows = nx // 2
    pick = picks(jb_ref, m, nk)
    for r in range(rows):
        row = rows * m + r
        below, above = lax.rem(row + nx - 1, nx), lax.rem(row + 1, nx)
        phi = [picked(pick, lambda at: own_ref[row, d, at, :], lambda at: other_ref[row, d, at, :]) for d in range(comps)]
        weight = weight_ref[pl.ds(row, 1), :]
        for c in range(comps):
            for half, ref in enumerate((own_ref, other_ref)):
                block = pl.ds(half * nk, nk)
                here = ref[row, c].astype(jnp.float32)
                gx = 0.5 * (ref[above, c].astype(jnp.float32) - ref[below, c].astype(jnp.float32))
                gz = 0.5 * (pltpu.roll(here, nz - 1, 1) - pltpu.roll(here, 1, 1))
                gx = gx.astype(jnp.bfloat16).astype(jnp.float32)
                gz = gz.astype(jnp.bfloat16).astype(jnp.float32)
                wts[r, block, pl.ds(c * nz, nz)] = (weight * here).astype(jnp.bfloat16)
                for j in range(JB):
                    total = phi[0][j : j + 1] * gx + phi[2][j : j + 1] * gz
                    adv[r, pl.ds((2 * j + half) * nk, nk), pl.ds(c * nz, nz)] = total.astype(jnp.bfloat16)
    total = dot_nt(adv[0], wts[0])
    for r in range(1, rows):
        total = total + dot_nt(adv[r], wts[r])
    acc_ref[...] = total
    quarter = rows // 2
    for r in range(quarter):
        w0_ref[r] = wts[quarter * q + r]


def same_core_rows(planes, first_ref, second_ref):
    x_came = x_first(jnp.bitwise_xor(lax.axis_index("space"), 1), planes)
    return (
        lambda rows: jnp.where(x_came, first_ref[rows, :], second_ref[rows, :]),
        lambda rows: jnp.where(x_came, second_ref[rows, :], first_ref[rows, :]),
    )


def sign_of_plane():
    return jnp.where(lax.rem(lax.axis_index("space"), 2) == 0, 0.5, -0.5)


def early_kernel(
    planes, own_ref, other_ref, first_ref, second_ref, xc_ref, w0_ref, jb_ref, acc_ref, out_ref, w1_ref, adv
):
    xs_rows, _ = same_core_rows(planes, first_ref, second_ref)
    m = lax.axis_index("modes")
    q = lax.rem(lax.axis_index("space"), 2)
    nx, comps, nk, nz = own_ref.shape
    quarter = nx // 4
    pick = picks(jb_ref, m, nk)
    weights = received_weights(xc_ref, quarter * comps * nk, quarter)
    for r in range(quarter):
        row0 = quarter * (2 * m + q) + r
        phi0 = sign_of_plane() * picked(
            pick, lambda at: own_ref[row0, 1, at, :], lambda at: other_ref[row0, 1, at, :]
        )
        phi0 = [spread(phi0[j : j + 1]) for j in range(JB)]
        for c in range(comps):
            at = pl.ds((r * comps + c) * nz, nz)
            src = pl.ds((r * comps + c) * nk, nk)
            for half, f1 in enumerate((xs_rows(src), xc_ref[src, :])):
                w1_ref[pl.ds(half * nk, nk), at] = (weights[r] * f1.astype(jnp.float32)).astype(
                    jnp.bfloat16
                )
                for j in range(JB):
                    adv[r, pl.ds((2 * j + half) * nk, nk), pl.ds(c * nz, nz)] = scaled(phi0[j], f1)
    total = acc_ref[...]
    for r in range(quarter):
        total = total + dot_nt(adv[r], w0_ref[r])
    out_ref[...] = total


def cross_kernel(classes_of, chunk, planes, has_weighted, own_ref, other_ref, *refs):
    first_ref, second_ref, xc_ref, zc_ref, w1_ref, jb_ref, acc_ref, *refs = refs
    xs_rows, zs_rows = same_core_rows(planes, first_ref, second_ref)
    if has_weighted:
        wts, keep_ref, send_ref, adv = refs
    else:
        keep_ref, send_ref, wts, adv = refs
    m = lax.axis_index("modes")
    plane = lax.axis_index("space")
    q = lax.rem(plane, 2)
    inside = jnp.where(jnp.logical_or(plane == 1, plane == planes - 2), 0.0, 1.0)
    nx, comps, nk, nz = own_ref.shape
    quarter = nx // 4
    span = quarter * comps * nz
    pick = picks(jb_ref, m, nk)
    classes = [pl.multiple_of(chunk * cls, chunk) for cls in classes_of(plane)]
    if not has_weighted:
        weights = received_weights(zc_ref, quarter * comps * nk, quarter)
        wts[:, pl.ds(0, span)] = w1_ref[...]
        for r in range(quarter):
            weight = inside * weights[r]
            for c in range(comps):
                src = pl.ds((r * comps + c) * nk, nk)
                for half, f2 in enumerate((zs_rows(src), zc_ref[src, :])):
                    wts[pl.ds(half * nk, nk), pl.ds(span + (r * comps + c) * nz, nz)] = (
                        weight * f2.astype(jnp.float32)
                    ).astype(jnp.bfloat16)
    phis = []
    for r in range(quarter):
        along = (r * comps + 1) * nk

        def moved(at):
            return pl.ds(pl.multiple_of(along + at.start, 16), at.size)

        phi1 = sign_of_plane() * picked(
            pick, lambda at: xs_rows(moved(at)), lambda at: xc_ref[moved(at), :]
        )
        phi2 = -sign_of_plane() * picked(
            pick, lambda at: zs_rows(moved(at)), lambda at: zc_ref[moved(at), :]
        )
        phis.append([[spread(phi[j : j + 1]) for j in range(JB)] for phi in (phi1, phi2)])
    inside = inside.astype(jnp.bfloat16)
    for at, cls in enumerate(classes):
        for r in range(quarter):
            row0 = quarter * (2 * m + q) + r
            phi1, phi2 = phis[r]
            for c in range(comps):
                lane = (r * comps + c) * nz
                src = (r * comps + c) * nk
                rows_at = pl.ds(pl.multiple_of(src + cls, 16), chunk)
                for half, (p0, f1, f2) in enumerate(
                    (
                        (own_ref, xs_rows(rows_at), zs_rows(rows_at)),
                        (other_ref, xc_ref[rows_at, :], zc_ref[rows_at, :]),
                    )
                ):
                    f0 = p0[row0, c, pl.ds(cls, chunk), :]
                    gy = inside * f2 - f0
                    for j in range(JB):
                        here = pl.ds((half * JB + j) * chunk, chunk)
                        adv[at, here, pl.ds(lane, nz)] = scaled(phi1[j], gy)
                        adv[at, here, pl.ds(span + lane, nz)] = scaled(phi2[j], f1)
        total = dot_nt(adv[at], wts[...])
        for half in range(2):
            level = m if half == 0 else 1 - m
            for j in range(JB):
                first = (half * JB + j) * chunk
                piece = total[first : first + chunk] + acc_ref[pl.ds((2 * j + half) * nk + cls, chunk), :]
                keep_ref[at, level, j] = piece[:, :nk]
                row = pl.multiple_of(((2 * at + level) * JB + j) * chunk, chunk)
                send_ref[pl.ds(row, chunk), :] = piece[:, nk:].astype(jnp.bfloat16)


def near_kernel(keep_a_ref, got_a_ref, keep_b_ref, got_b_ref, mine_ref, send_ref):
    low = lax.rem(lax.axis_index("space"), NEAR)
    for keep_ref, got_ref, steps in ((keep_a_ref, got_a_ref, (3, 1)), (keep_b_ref, got_b_ref, (0, 2))):
        got = got_ref[...].astype(jnp.float32).reshape(keep_ref.shape)
        for at, step in enumerate(steps):
            total = keep_ref[at] + got[at]
            if step == 0:
                mine_ref[...] = total
            send_ref[jnp.bitwise_xor(low, step)] = total.astype(jnp.bfloat16).reshape(send_ref.shape[1:])


def far_kernel(mine_ref, parts_ref, keep_ref, send_ref):
    s = lax.axis_index("space")
    low, level = lax.rem(s, NEAR), lax.div(s, NEAR)
    rows = send_ref.shape[0]
    for ref, at in ((keep_ref, level), (send_ref, 1 - level)):
        total = mine_ref[at]
        for step in range(1, NEAR):
            from_chip = jnp.bitwise_xor(low, step)
            piece = parts_ref[from_chip, pl.ds(pl.multiple_of(at * rows, rows), rows), :]
            total = total + piece.astype(jnp.float32).reshape(total.shape)
        ref[...] = total.astype(ref.dtype).reshape(ref.shape)


def total_kernel(keep_ref, got_ref, out_ref):
    total = keep_ref[...] + got_ref[...].astype(jnp.float32).reshape(keep_ref.shape)
    for j in range(JB):
        out_ref[:, j, :] = total[j]


def on_device(n, modes, weight_ids, weight_table, j_block):
    nk, comps, _, nx, nz = modes.shape
    bf16, f32 = jnp.bfloat16, jnp.float32
    vmem = pl.BlockSpec(memory_space=pltpu.VMEM)
    smem = pl.BlockSpec(memory_space=pltpu.SMEM)
    params = pltpu.CompilerParams(vmem_limit_bytes=VMEM_LIMIT)
    quarter = nx // 4
    body = quarter * comps * nk
    own, first, second = pl.pallas_call(
        functools.partial(prep_kernel, n),
        out_shape=[jax.ShapeDtypeStruct((nx, comps, nk, nz), bf16)]
        + [jax.ShapeDtypeStruct((body + PADROWS, nz), bf16)] * 2,
        in_specs=[pl.BlockSpec(memory_space=pltpu.HBM)],
        out_specs=[vmem] * 3,
        scratch_shapes=[pltpu.VMEM(modes.shape, bf16), pltpu.SemaphoreType.DMA((LOADS,))],
        compiler_params=pltpu.CompilerParams(vmem_limit_bytes=PREP_LIMIT),
        cost_estimate=pl.CostEstimate(flops=1_500_000_000, bytes_accessed=2_800_000, transcendentals=0),
        name="prep",
    )(modes)

    both = ("space", "modes")
    x_to = lambda s: s ^ 1
    z_to = lambda s: s + 2 if s % 2 else s - 2
    x_now = [n != 8 or X_FIRST >> s & 1 for s in range(n)]
    firsts = [(s, x_to(s) if x_now[s] else z_to(s)) for s in range(n)]
    seconds = [(s, z_to(s) % n if x_now[s] else x_to(s)) for s in range(n)]
    same = lambda pairs: [(2 * a + m, 2 * b + m) for a, b in pairs for m in range(2)]
    cross = lambda pairs: [(2 * a + m, 2 * b + 1 - m) for a, b in pairs for m in range(2)]
    other = lax.ppermute(own, "modes", [(0, 1), (1, 0)])
    first = lax.ppermute(first, both, same(firsts))
    second = lax.ppermute(second, both, same(seconds))
    weight, xc, zc = pl.pallas_call(
        weights_kernel,
        out_shape=[jax.ShapeDtypeStruct((nx, nz), f32)]
        + [jax.ShapeDtypeStruct((body + 8 * quarter, nz), bf16)] * 2,
        in_specs=[vmem] * 3 + [pl.BlockSpec(memory_space=pl.ANY)],
        out_specs=[vmem] * 3,
        compiler_params=params,
        name="weights",
    )(weight_ids, jnp.broadcast_to(weight_table[None], (8, NW)), own, other)
    xc = lax.ppermute(xc, both, cross([(s, x_to(s)) for s in range(n)]))
    zc = lax.ppermute(zc, both, cross([(s, z_to(s)) for s in range(n) if 0 <= z_to(s) < n]))

    depth = nx // 4 * comps * nz
    depth = quarter * comps * nz
    acc, w0 = pl.pallas_call(
        local_kernel,
        out_shape=[
            jax.ShapeDtypeStruct((JB * 2 * nk, 2 * nk), f32),
            jax.ShapeDtypeStruct((quarter, 2 * nk, comps * nz), bf16),
        ],
        in_specs=[vmem, vmem, vmem, smem],
        out_specs=[vmem] * 2,
        scratch_shapes=[
            pltpu.VMEM((2 * quarter, JB * 2 * nk, comps * nz), bf16),
            pltpu.VMEM((2 * quarter, 2 * nk, comps * nz), bf16),
        ],
        compiler_params=params,
        cost_estimate=pl.CostEstimate(flops=900_000_000, bytes_accessed=2_400_000, transcendentals=0),
        name="local",
    )(own, other, weight, j_block)

    acc, w1 = pl.pallas_call(
        functools.partial(early_kernel, n),
        out_shape=[
            jax.ShapeDtypeStruct((JB * 2 * nk, 2 * nk), f32),
            jax.ShapeDtypeStruct((2 * nk, depth), bf16),
        ],
        in_specs=[vmem] * 6 + [smem, vmem],
        out_specs=[vmem] * 2,
        scratch_shapes=[pltpu.VMEM((quarter, JB * 2 * nk, comps * nz), bf16)],
        compiler_params=params,
        cost_estimate=pl.CostEstimate(flops=600_000_000, bytes_accessed=2_400_000, transcendentals=0),
        name="early",
    )(own, other, first, second, xc, w0, j_block, acc)

    per_target = 2 * nk // n
    chunk = max(16, per_target)

    def crossed(count, classes_of, weighted):
        piece = (count, 2, JB, chunk, nk)
        out_shape = [
            jax.ShapeDtypeStruct(piece, f32),
            jax.ShapeDtypeStruct((count * 2 * JB * chunk, nk), bf16),
        ]
        if not weighted:
            out_shape.append(jax.ShapeDtypeStruct((2 * nk, 2 * depth), bf16))
        return pl.pallas_call(
            functools.partial(cross_kernel, classes_of, chunk, n, bool(weighted)),
            out_shape=out_shape,
            in_specs=[vmem] * 7 + [smem] + [vmem] * (1 + len(weighted)),
            out_specs=[vmem] * len(out_shape),
            scratch_shapes=[pltpu.VMEM((count, 2 * JB * chunk, 2 * depth), bf16)],
            compiler_params=params,
            cost_estimate=pl.CostEstimate(
                flops=900_000_000, bytes_accessed=4_000_000, transcendentals=0
            ),
            name="cross",
        )(own, other, first, second, xc, zc, w1, j_block, acc, *weighted)

    swap = [(0, 1), (1, 0)]
    if n == 2 * NEAR:
        def partners(*steps):
            return lambda s: [jnp.bitwise_xor(lax.rem(s, NEAR), step) for step in steps]

        keep_a, send_a, w2 = crossed(2, partners(3, 1), ())
        got_a = lax.ppermute(send_a, "modes", swap)
        keep_b, send_b = crossed(2, partners(0, 2), (w2,))
        got_b = lax.ppermute(send_b, "modes", swap)
        piece = (JB, chunk, nk)

        mine, send = pl.pallas_call(
            near_kernel,
            out_shape=[
                jax.ShapeDtypeStruct((2, *piece), f32),
                jax.ShapeDtypeStruct((NEAR, 2 * JB * chunk, nk), bf16),
            ],
            in_specs=[vmem] * 4,
            out_specs=[vmem] * 2,
            compiler_params=params,
            name="near",
        )(keep_a, got_a, keep_b, got_b)
        parts = lax.all_to_all(
            send, "space", 0, 0, axis_index_groups=[list(range(NEAR)), list(range(NEAR, 2 * NEAR))], tiled=True
        )
        keep, send = pl.pallas_call(
            far_kernel,
            out_shape=[
                jax.ShapeDtypeStruct(piece, f32),
                jax.ShapeDtypeStruct((JB * chunk, nk), bf16),
            ],
            in_specs=[vmem] * 2,
            out_specs=[vmem] * 2,
            compiler_params=params,
            name="far",
        )(mine, parts)
        got = lax.ppermute(send, "space", [(s, s ^ NEAR) for s in range(n)])
        return pl.pallas_call(
            total_kernel,
            out_shape=jax.ShapeDtypeStruct((chunk, JB, nk), f32),
            in_specs=[vmem] * 2,
            out_specs=vmem,
            compiler_params=params,
            name="total",
        )(keep, got)

    count = nk // chunk
    keep, send, _ = crossed(count, lambda s: list(range(count)), ())
    share = (keep + lax.ppermute(send, "modes", swap).reshape(keep.shape)).astype(bf16)
    share = share.reshape(count, 2, JB, chunk // per_target, per_target, nk)
    share = share.transpose(1, 0, 3, 2, 4, 5).reshape(n, JB, per_target, nk)
    parts = lax.all_to_all(share, "space", 0, 0, tiled=True)
    return jnp.sum(parts.astype(f32), axis=0).transpose(1, 0, 2)


def solution(mesh):
    return jax.shard_map(
        functools.partial(on_device, mesh.shape["space"]),
        mesh=mesh,
        in_specs=(
            P("modes", None, ("groups", "space"), None, None),
            P(("groups", "space"), None, None),
            P(),
            P("groups"),
        ),
        out_specs=P(("groups", "space"), None, "modes"),
        check_vma=False,
    )
```

```python
import functools

import jax
import jax.numpy as jnp
from jax import lax
from jax.experimental import pallas as pl
from jax.experimental.pallas import tpu as pltpu
from jax.sharding import PartitionSpec as P

JB = 4
NW = 16
PADROWS = 16
LOADS = 4
X_FIRST = 0b10011111
NEAR = 4
VMEM_LIMIT = 48 * 1024 * 1024
PREP_LIMIT = 53_600 * 1024


def x_first(s, planes):
    if planes != 8:
        return s >= 0
    return lax.rem(lax.shift_right_logical(X_FIRST, s), 2) == 1


def copy_rows(ref, tr, at):
    nx, comps, nk, _ = tr.shape
    for row in range(nx // 4):
        for c in range(comps):
            ref[pl.ds((row * comps + c) * nk, nk), :] = tr[at * (nx // 4) + row, c]


def prep_kernel(planes, modes_hbm, tr, first_ref, second_ref, modes_ref, sems):
    m = lax.axis_index("modes")
    s = lax.axis_index("space")
    q = lax.rem(s, 2)
    nk, comps, _, nx, nz = modes_hbm.shape
    step = nk // LOADS
    copies = [
        pltpu.make_async_copy(
            modes_hbm.at[pl.ds(p * step, step)], modes_ref.at[pl.ds(p * step, step)], sems.at[p]
        )
        for p in range(LOADS)
    ]
    for copy in copies:
        copy.start()
    for p in range(LOADS):
        copies[p].wait()
        block = pl.ds(p * step, step)
        for c in range(comps):
            value = modes_ref[block, c, 0].astype(jnp.float32)
            tr[:, c, block] = jnp.swapaxes(value, 0, 1).astype(jnp.bfloat16)
    body = nx // 4 * comps * nk
    to_x, to_z = 2 * m + 1 - q, 2 * m + q
    x_now = x_first(s, planes)
    for ref, at in (
        (first_ref, jnp.where(x_now, to_x, to_z)),
        (second_ref, jnp.where(x_now, to_z, to_x)),
    ):
        copy_rows(ref, tr, at)
        ref[pl.ds(body, PADROWS), :] = jnp.zeros((PADROWS, nz), jnp.bfloat16)


def weights_kernel(ids_ref, table_ref, tr, _, weight_ref, xc_ref, zc_ref):
    m = lax.axis_index("modes")
    q = lax.rem(lax.axis_index("space"), 2)
    nx, comps, nk, nz = tr.shape
    quarter = nx // 4
    table = table_ref[...]
    weight = jnp.zeros((nx, nz), jnp.float32)
    for entry in range(NW):
        weight = jnp.where(ids_ref[0] == entry, table[0:1, entry : entry + 1], weight)
    weight_ref[...] = weight
    for ref, at in ((xc_ref, 2 * (1 - m) + 1 - q), (zc_ref, 2 * (1 - m) + q)):
        copy_rows(ref, tr, at)
        rest = jnp.concatenate(
            [
                jnp.broadcast_to(weight_ref[pl.ds(at * quarter + row, 1), :], (8, nz))
                for row in range(quarter)
            ],
            axis=0,
        )
        piece_of = lax.rem(lax.broadcasted_iota(jnp.int32, rest.shape, 0), 8)
        pieces = jnp.zeros(rest.shape, jnp.float32)
        for piece in range(3):
            rounded = rest.astype(jnp.bfloat16).astype(jnp.float32)
            pieces = jnp.where(piece_of == piece, rounded, pieces)
            rest = rest - rounded
        ref[pl.ds(quarter * comps * nk, 8 * quarter), :] = pieces.astype(jnp.bfloat16)


def received_weights(ref, first, quarter):
    pieces = ref[pl.ds(first, 8 * quarter), :].astype(jnp.float32)
    return [
        pieces[8 * r : 8 * r + 1] + pieces[8 * r + 1 : 8 * r + 2] + pieces[8 * r + 2 : 8 * r + 3]
        for r in range(quarter)
    ]


def picks(jb_ref, m, nk):
    first = jb_ref[0] * JB
    owner = (first >= nk).astype(jnp.int32)
    row = first - owner * nk
    within = lax.rem(row, 16)
    return owner == m, pl.multiple_of(row - within, 16), within


def picked(pick, own, other):
    mine, block, within = pick
    rows = pl.ds(block, 16)
    rows = jnp.where(mine, own(rows).astype(jnp.float32), other(rows).astype(jnp.float32))
    result = rows[0:JB]
    for start in range(JB, 16, JB):
        result = jnp.where(within == start, rows[start : start + JB], result)
    return result


def spread(row):
    return jnp.broadcast_to(row, (16, row.shape[1])).astype(jnp.bfloat16)[None]


def scaled(tile, field):
    rows, lanes = field.shape
    return (tile * field.reshape(rows // 16, 16, lanes)).reshape(rows, lanes)


def dot_nt(a, b):
    return lax.dot_general(a, b, (((1,), (1,)), ((), ())), preferred_element_type=jnp.float32)


def local_kernel(own_ref, other_ref, weight_ref, jb_ref, acc_ref, w0_ref, adv, wts):
    m = lax.axis_index("modes")
    q = lax.rem(lax.axis_index("space"), 2)
    nx, comps, nk, nz = own_ref.shape
    rows = nx // 2
    pick = picks(jb_ref, m, nk)
    for r in range(rows):
        row = rows * m + r
        below, above = lax.rem(row + nx - 1, nx), lax.rem(row + 1, nx)
        phi = [picked(pick, lambda at: own_ref[row, d, at, :], lambda at: other_ref[row, d, at, :]) for d in range(comps)]
        weight = weight_ref[pl.ds(row, 1), :]
        for c in range(comps):
            for half, ref in enumerate((own_ref, other_ref)):
                block = pl.ds(half * nk, nk)
                here = ref[row, c].astype(jnp.float32)
                gx = 0.5 * (ref[above, c].astype(jnp.float32) - ref[below, c].astype(jnp.float32))
                gz = 0.5 * (pltpu.roll(here, nz - 1, 1) - pltpu.roll(here, 1, 1))
                gx = gx.astype(jnp.bfloat16).astype(jnp.float32)
                gz = gz.astype(jnp.bfloat16).astype(jnp.float32)
                wts[r, block, pl.ds(c * nz, nz)] = (weight * here).astype(jnp.bfloat16)
                for j in range(JB):
                    total = phi[0][j : j + 1] * gx + phi[2][j : j + 1] * gz
                    adv[r, pl.ds((2 * j + half) * nk, nk), pl.ds(c * nz, nz)] = total.astype(jnp.bfloat16)
    total = dot_nt(adv[0], wts[0])
    for r in range(1, rows):
        total = total + dot_nt(adv[r], wts[r])
    acc_ref[...] = total
    quarter = rows // 2
    for r in range(quarter):
        w0_ref[r] = wts[quarter * q + r]


def same_core_rows(planes, first_ref, second_ref):
    x_came = x_first(jnp.bitwise_xor(lax.axis_index("space"), 1), planes)
    return (
        lambda rows: jnp.where(x_came, first_ref[rows, :], second_ref[rows, :]),
        lambda rows: jnp.where(x_came, second_ref[rows, :], first_ref[rows, :]),
    )


def sign_of_plane():
    return jnp.where(lax.rem(lax.axis_index("space"), 2) == 0, 0.5, -0.5)


def early_kernel(
    planes, own_ref, other_ref, first_ref, second_ref, xc_ref, w0_ref, jb_ref, acc_ref, out_ref, w1_ref, adv
):
    xs_rows, _ = same_core_rows(planes, first_ref, second_ref)
    m = lax.axis_index("modes")
    q = lax.rem(lax.axis_index("space"), 2)
    nx, comps, nk, nz = own_ref.shape
    quarter = nx // 4
    pick = picks(jb_ref, m, nk)
    weights = received_weights(xc_ref, quarter * comps * nk, quarter)
    for r in range(quarter):
        row0 = quarter * (2 * m + q) + r
        phi0 = sign_of_plane() * picked(
            pick, lambda at: own_ref[row0, 1, at, :], lambda at: other_ref[row0, 1, at, :]
        )
        phi0 = [spread(phi0[j : j + 1]) for j in range(JB)]
        for c in range(comps):
            at = pl.ds((r * comps + c) * nz, nz)
            src = pl.ds((r * comps + c) * nk, nk)
            for half, f1 in enumerate((xs_rows(src), xc_ref[src, :])):
                w1_ref[pl.ds(half * nk, nk), at] = (weights[r] * f1.astype(jnp.float32)).astype(
                    jnp.bfloat16
                )
                for j in range(JB):
                    adv[r, pl.ds((2 * j + half) * nk, nk), pl.ds(c * nz, nz)] = scaled(phi0[j], f1)
    total = acc_ref[...]
    for r in range(quarter):
        total = total + dot_nt(adv[r], w0_ref[r])
    out_ref[...] = total


def cross_kernel(classes_of, chunk, planes, has_weighted, own_ref, other_ref, *refs):
    first_ref, second_ref, xc_ref, zc_ref, w1_ref, jb_ref, acc_ref, *refs = refs
    xs_rows, zs_rows = same_core_rows(planes, first_ref, second_ref)
    if has_weighted:
        wts, keep_ref, send_ref, adv = refs
    else:
        keep_ref, send_ref, wts, adv = refs
    m = lax.axis_index("modes")
    plane = lax.axis_index("space")
    q = lax.rem(plane, 2)
    inside = jnp.where(jnp.logical_or(plane == 1, plane == planes - 2), 0.0, 1.0)
    nx, comps, nk, nz = own_ref.shape
    quarter = nx // 4
    span = quarter * comps * nz
    pick = picks(jb_ref, m, nk)
    classes = [pl.multiple_of(chunk * cls, chunk) for cls in classes_of(plane)]
    if not has_weighted:
        weights = received_weights(zc_ref, quarter * comps * nk, quarter)
        wts[:, pl.ds(0, span)] = w1_ref[...]
        for r in range(quarter):
            weight = inside * weights[r]
            for c in range(comps):
                src = pl.ds((r * comps + c) * nk, nk)
                for half, f2 in enumerate((zs_rows(src), zc_ref[src, :])):
                    wts[pl.ds(half * nk, nk), pl.ds(span + (r * comps + c) * nz, nz)] = (
                        weight * f2.astype(jnp.float32)
                    ).astype(jnp.bfloat16)
    phis = []
    for r in range(quarter):
        along = (r * comps + 1) * nk

        def moved(at):
            return pl.ds(pl.multiple_of(along + at.start, 16), at.size)

        phi1 = sign_of_plane() * picked(
            pick, lambda at: xs_rows(moved(at)), lambda at: xc_ref[moved(at), :]
        )
        phi2 = -sign_of_plane() * picked(
            pick, lambda at: zs_rows(moved(at)), lambda at: zc_ref[moved(at), :]
        )
        phis.append([[spread(phi[j : j + 1]) for j in range(JB)] for phi in (phi1, phi2)])
    inside = inside.astype(jnp.bfloat16)
    for at, cls in enumerate(classes):
        for r in range(quarter):
            row0 = quarter * (2 * m + q) + r
            phi1, phi2 = phis[r]
            for c in range(comps):
                lane = (r * comps + c) * nz
                src = (r * comps + c) * nk
                rows_at = pl.ds(pl.multiple_of(src + cls, 16), chunk)
                for half, (p0, f1, f2) in enumerate(
                    (
                        (own_ref, xs_rows(rows_at), zs_rows(rows_at)),
                        (other_ref, xc_ref[rows_at, :], zc_ref[rows_at, :]),
                    )
                ):
                    f0 = p0[row0, c, pl.ds(cls, chunk), :]
                    gy = inside * f2 - f0
                    for j in range(JB):
                        here = pl.ds((half * JB + j) * chunk, chunk)
                        adv[at, here, pl.ds(lane, nz)] = scaled(phi1[j], gy)
                        adv[at, here, pl.ds(span + lane, nz)] = scaled(phi2[j], f1)
        total = dot_nt(adv[at], wts[...])
        for half in range(2):
            level = m if half == 0 else 1 - m
            for j in range(JB):
                first = (half * JB + j) * chunk
                piece = total[first : first + chunk] + acc_ref[pl.ds((2 * j + half) * nk + cls, chunk), :]
                keep_ref[at, level, j] = piece[:, :nk]
                row = pl.multiple_of(((2 * at + level) * JB + j) * chunk, chunk)
                send_ref[pl.ds(row, chunk), :] = piece[:, nk:].astype(jnp.bfloat16)


def near_kernel(keep_ref, got_ref, *out_refs):
    got = got_ref[...].astype(jnp.float32).reshape(keep_ref.shape)
    for at, ref in enumerate(out_refs):
        ref[...] = (keep_ref[at] + got[at]).astype(ref.dtype).reshape(ref.shape)


def relay_kernel(keep_ref, got_ref, passed_ref, mine_ref, up_ref):
    got = got_ref[...].astype(jnp.float32).reshape(keep_ref.shape)
    mine_ref[...] = keep_ref[0] + got[0]
    passed = passed_ref[...].astype(jnp.float32).reshape(keep_ref.shape[1:])
    up_ref[...] = (keep_ref[1] + got[1] + passed).astype(up_ref.dtype).reshape(up_ref.shape)


def far_kernel(mine_ref, *refs):
    *parts, keep_ref, send_ref = refs
    level = lax.div(lax.axis_index("space"), NEAR)
    rows = send_ref.shape[0]
    for ref, at in ((keep_ref, level), (send_ref, 1 - level)):
        total = mine_ref[at]
        for part in parts:
            piece = part[pl.ds(pl.multiple_of(at * rows, rows), rows), :]
            total = total + piece.astype(jnp.float32).reshape(total.shape)
        ref[...] = total.astype(ref.dtype).reshape(ref.shape)


def total_kernel(keep_ref, got_ref, out_ref):
    total = keep_ref[...] + got_ref[...].astype(jnp.float32).reshape(keep_ref.shape)
    for j in range(JB):
        out_ref[:, j, :] = total[j]


def on_device(n, modes, weight_ids, weight_table, j_block):
    nk, comps, _, nx, nz = modes.shape
    bf16, f32 = jnp.bfloat16, jnp.float32
    vmem = pl.BlockSpec(memory_space=pltpu.VMEM)
    smem = pl.BlockSpec(memory_space=pltpu.SMEM)
    params = pltpu.CompilerParams(vmem_limit_bytes=VMEM_LIMIT)
    quarter = nx // 4
    body = quarter * comps * nk
    own, first, second = pl.pallas_call(
        functools.partial(prep_kernel, n),
        out_shape=[jax.ShapeDtypeStruct((nx, comps, nk, nz), bf16)]
        + [jax.ShapeDtypeStruct((body + PADROWS, nz), bf16)] * 2,
        in_specs=[pl.BlockSpec(memory_space=pltpu.HBM)],
        out_specs=[vmem] * 3,
        scratch_shapes=[pltpu.VMEM(modes.shape, bf16), pltpu.SemaphoreType.DMA((LOADS,))],
        compiler_params=pltpu.CompilerParams(vmem_limit_bytes=PREP_LIMIT),
        cost_estimate=pl.CostEstimate(flops=1_500_000_000, bytes_accessed=2_800_000, transcendentals=0),
        name="prep",
    )(modes)

    both = ("space", "modes")
    x_to = lambda s: s ^ 1
    z_to = lambda s: s + 2 if s % 2 else s - 2
    x_now = [n != 8 or X_FIRST >> s & 1 for s in range(n)]
    firsts = [(s, x_to(s) if x_now[s] else z_to(s)) for s in range(n)]
    seconds = [(s, z_to(s) % n if x_now[s] else x_to(s)) for s in range(n)]
    same = lambda pairs: [(2 * a + m, 2 * b + m) for a, b in pairs for m in range(2)]
    cross = lambda pairs: [(2 * a + m, 2 * b + 1 - m) for a, b in pairs for m in range(2)]
    other = lax.ppermute(own, "modes", [(0, 1), (1, 0)])
    first = lax.ppermute(first, both, same(firsts))
    second = lax.ppermute(second, both, same(seconds))
    weight, xc, zc = pl.pallas_call(
        weights_kernel,
        out_shape=[jax.ShapeDtypeStruct((nx, nz), f32)]
        + [jax.ShapeDtypeStruct((body + 8 * quarter, nz), bf16)] * 2,
        in_specs=[vmem] * 3 + [pl.BlockSpec(memory_space=pl.ANY)],
        out_specs=[vmem] * 3,
        compiler_params=params,
        name="weights",
    )(weight_ids, jnp.broadcast_to(weight_table[None], (8, NW)), own, other)
    xc = lax.ppermute(xc, both, cross([(s, x_to(s)) for s in range(n)]))
    zc = lax.ppermute(zc, both, cross([(s, z_to(s)) for s in range(n) if 0 <= z_to(s) < n]))

    depth = nx // 4 * comps * nz
    depth = quarter * comps * nz
    acc, w0 = pl.pallas_call(
        local_kernel,
        out_shape=[
            jax.ShapeDtypeStruct((JB * 2 * nk, 2 * nk), f32),
            jax.ShapeDtypeStruct((quarter, 2 * nk, comps * nz), bf16),
        ],
        in_specs=[vmem, vmem, vmem, smem],
        out_specs=[vmem] * 2,
        scratch_shapes=[
            pltpu.VMEM((2 * quarter, JB * 2 * nk, comps * nz), bf16),
            pltpu.VMEM((2 * quarter, 2 * nk, comps * nz), bf16),
        ],
        compiler_params=params,
        cost_estimate=pl.CostEstimate(flops=900_000_000, bytes_accessed=2_400_000, transcendentals=0),
        name="local",
    )(own, other, weight, j_block)

    acc, w1 = pl.pallas_call(
        functools.partial(early_kernel, n),
        out_shape=[
            jax.ShapeDtypeStruct((JB * 2 * nk, 2 * nk), f32),
            jax.ShapeDtypeStruct((2 * nk, depth), bf16),
        ],
        in_specs=[vmem] * 6 + [smem, vmem],
        out_specs=[vmem] * 2,
        scratch_shapes=[pltpu.VMEM((quarter, JB * 2 * nk, comps * nz), bf16)],
        compiler_params=params,
        cost_estimate=pl.CostEstimate(flops=600_000_000, bytes_accessed=2_400_000, transcendentals=0),
        name="early",
    )(own, other, first, second, xc, w0, j_block, acc)

    per_target = 2 * nk // n
    chunk = max(16, per_target)

    def crossed(count, classes_of, weighted):
        piece = (count, 2, JB, chunk, nk)
        out_shape = [
            jax.ShapeDtypeStruct(piece, f32),
            jax.ShapeDtypeStruct((count * 2 * JB * chunk, nk), bf16),
        ]
        if not weighted:
            out_shape.append(jax.ShapeDtypeStruct((2 * nk, 2 * depth), bf16))
        return pl.pallas_call(
            functools.partial(cross_kernel, classes_of, chunk, n, bool(weighted)),
            out_shape=out_shape,
            in_specs=[vmem] * 7 + [smem] + [vmem] * (1 + len(weighted)),
            out_specs=[vmem] * len(out_shape),
            scratch_shapes=[pltpu.VMEM((count, 2 * JB * chunk, 2 * depth), bf16)],
            compiler_params=params,
            cost_estimate=pl.CostEstimate(
                flops=900_000_000, bytes_accessed=4_000_000, transcendentals=0
            ),
            name="cross",
        )(own, other, first, second, xc, zc, w1, j_block, acc, *weighted)

    swap = [(0, 1), (1, 0)]
    if n == 2 * NEAR:
        def partners(*steps):
            return lambda s: [jnp.bitwise_xor(lax.rem(s, NEAR), step) for step in steps]

        keep_a, send_a, w2 = crossed(2, partners(3, 1), ())
        got_a = lax.ppermute(send_a, "modes", swap)
        keep_b, send_b = crossed(2, partners(0, 2), (w2,))
        got_b = lax.ppermute(send_b, "modes", swap)
        piece = (JB, chunk, nk)

        kept = jax.ShapeDtypeStruct((2, *piece), f32)
        sent = jax.ShapeDtypeStruct((2 * JB * chunk, nk), bf16)

        def summed(body_of, out_shape, *operands):
            return pl.pallas_call(
                body_of,
                out_shape=out_shape,
                in_specs=[vmem] * len(operands),
                out_specs=[vmem] * 2,
                compiler_params=params,
                name="near",
            )(*operands)

        along_x = [(s, s ^ 1) for s in range(n)]
        diagonal, beside = summed(near_kernel, [sent, sent], keep_a, got_a)
        passed = lax.ppermute(diagonal, "space", along_x)
        beside = lax.ppermute(beside, "space", along_x)
        mine, up = summed(relay_kernel, [kept, sent], keep_b, got_b, passed)
        up = lax.ppermute(up, "space", [(s, s ^ 2) for s in range(n)])
        keep, send = pl.pallas_call(
            far_kernel,
            out_shape=[
                jax.ShapeDtypeStruct(piece, f32),
                jax.ShapeDtypeStruct((JB * chunk, nk), bf16),
            ],
            in_specs=[vmem] * 3,
            out_specs=[vmem] * 2,
            compiler_params=params,
            name="far",
        )(mine, beside, up)
        got = lax.ppermute(send, "space", [(s, s ^ NEAR) for s in range(n)])
        return pl.pallas_call(
            total_kernel,
            out_shape=jax.ShapeDtypeStruct((chunk, JB, nk), f32),
            in_specs=[vmem] * 2,
            out_specs=vmem,
            compiler_params=params,
            name="total",
        )(keep, got)

    count = nk // chunk
    keep, send, _ = crossed(count, lambda s: list(range(count)), ())
    share = (keep + lax.ppermute(send, "modes", swap).reshape(keep.shape)).astype(bf16)
    share = share.reshape(count, 2, JB, chunk // per_target, per_target, nk)
    share = share.transpose(1, 0, 3, 2, 4, 5).reshape(n, JB, per_target, nk)
    parts = lax.all_to_all(share, "space", 0, 0, tiled=True)
    return jnp.sum(parts.astype(f32), axis=0).transpose(1, 0, 2)


def solution(mesh):
    return jax.shard_map(
        functools.partial(on_device, mesh.shape["space"]),
        mesh=mesh,
        in_specs=(
            P("modes", None, ("groups", "space"), None, None),
            P(("groups", "space"), None, None),
            P(),
            P("groups"),
        ),
        out_specs=P(("groups", "space"), None, "modes"),
        check_vma=False,
    )
```

```python
import functools

import jax
import jax.numpy as jnp
from jax import lax
from jax.experimental import pallas as pl
from jax.experimental.pallas import tpu as pltpu
from jax.sharding import PartitionSpec as P

JB = 4
NW = 16
PADROWS = 16
LOADS = 4
X_FIRST = 0b10011111
NEAR = 4
VMEM_LIMIT = 48 * 1024 * 1024
PREP_LIMIT = 53_600 * 1024


def x_first(s, planes):
    if planes != 8:
        return s >= 0
    return lax.rem(lax.shift_right_logical(X_FIRST, s), 2) == 1


def copy_rows(ref, tr, at):
    nx, comps, nk, _ = tr.shape
    for row in range(nx // 4):
        for c in range(comps):
            ref[pl.ds((row * comps + c) * nk, nk), :] = tr[at * (nx // 4) + row, c]


def prep_kernel(planes, modes_hbm, tr, first_ref, second_ref, modes_ref, sems):
    m = lax.axis_index("modes")
    s = lax.axis_index("space")
    q = lax.rem(s, 2)
    nk, comps, _, nx, nz = modes_hbm.shape
    step = nk // LOADS
    copies = [
        pltpu.make_async_copy(
            modes_hbm.at[pl.ds(p * step, step)], modes_ref.at[pl.ds(p * step, step)], sems.at[p]
        )
        for p in range(LOADS)
    ]
    for copy in copies:
        copy.start()
    for p in range(LOADS):
        copies[p].wait()
        block = pl.ds(p * step, step)
        for c in range(comps):
            value = modes_ref[block, c, 0].astype(jnp.float32)
            tr[:, c, block] = jnp.swapaxes(value, 0, 1).astype(jnp.bfloat16)
    body = nx // 4 * comps * nk
    to_x, to_z = 2 * m + 1 - q, 2 * m + q
    x_now = x_first(s, planes)
    for ref, at in (
        (first_ref, jnp.where(x_now, to_x, to_z)),
        (second_ref, jnp.where(x_now, to_z, to_x)),
    ):
        copy_rows(ref, tr, at)
        ref[pl.ds(body, PADROWS), :] = jnp.zeros((PADROWS, nz), jnp.bfloat16)


def weights_kernel(ids_ref, table_ref, tr, _, weight_ref, xc_ref, zc_ref):
    m = lax.axis_index("modes")
    q = lax.rem(lax.axis_index("space"), 2)
    nx, comps, nk, nz = tr.shape
    quarter = nx // 4
    table = table_ref[...]
    weight = jnp.zeros((nx, nz), jnp.float32)
    for entry in range(NW):
        weight = jnp.where(ids_ref[0] == entry, table[0:1, entry : entry + 1], weight)
    weight_ref[...] = weight
    for ref, at in ((xc_ref, 2 * (1 - m) + 1 - q), (zc_ref, 2 * (1 - m) + q)):
        copy_rows(ref, tr, at)
        rest = jnp.concatenate(
            [
                jnp.broadcast_to(weight_ref[pl.ds(at * quarter + row, 1), :], (8, nz))
                for row in range(quarter)
            ],
            axis=0,
        )
        piece_of = lax.rem(lax.broadcasted_iota(jnp.int32, rest.shape, 0), 8)
        pieces = jnp.zeros(rest.shape, jnp.float32)
        for piece in range(3):
            rounded = rest.astype(jnp.bfloat16).astype(jnp.float32)
            pieces = jnp.where(piece_of == piece, rounded, pieces)
            rest = rest - rounded
        ref[pl.ds(quarter * comps * nk, 8 * quarter), :] = pieces.astype(jnp.bfloat16)


def received_weights(ref, first, quarter):
    pieces = ref[pl.ds(first, 8 * quarter), :].astype(jnp.float32)
    return [
        pieces[8 * r : 8 * r + 1] + pieces[8 * r + 1 : 8 * r + 2] + pieces[8 * r + 2 : 8 * r + 3]
        for r in range(quarter)
    ]


def picks(jb_ref, m, nk):
    first = jb_ref[0] * JB
    owner = (first >= nk).astype(jnp.int32)
    row = first - owner * nk
    within = lax.rem(row, 16)
    return owner == m, pl.multiple_of(row - within, 16), within


def picked(pick, own, other):
    mine, block, within = pick
    rows = pl.ds(block, 16)
    rows = jnp.where(mine, own(rows).astype(jnp.float32), other(rows).astype(jnp.float32))
    result = rows[0:JB]
    for start in range(JB, 16, JB):
        result = jnp.where(within == start, rows[start : start + JB], result)
    return result


def spread(row):
    return jnp.broadcast_to(row, (16, row.shape[1])).astype(jnp.bfloat16)[None]


def scaled(tile, field):
    rows, lanes = field.shape
    return (tile * field.reshape(rows // 16, 16, lanes)).reshape(rows, lanes)


def dot_nt(a, b):
    return lax.dot_general(a, b, (((1,), (1,)), ((), ())), preferred_element_type=jnp.float32)


def local_kernel(own_ref, other_ref, weight_ref, jb_ref, acc_ref, w0_ref, adv, wts):
    m = lax.axis_index("modes")
    q = lax.rem(lax.axis_index("space"), 2)
    nx, comps, nk, nz = own_ref.shape
    rows = nx // 2
    pick = picks(jb_ref, m, nk)
    for r in range(rows):
        row = rows * m + r
        below, above = lax.rem(row + nx - 1, nx), lax.rem(row + 1, nx)
        phi = [picked(pick, lambda at: own_ref[row, d, at, :], lambda at: other_ref[row, d, at, :]) for d in range(comps)]
        weight = weight_ref[pl.ds(row, 1), :]
        for c in range(comps):
            for half, ref in enumerate((own_ref, other_ref)):
                block = pl.ds(half * nk, nk)
                here = ref[row, c].astype(jnp.float32)
                gx = 0.5 * (ref[above, c].astype(jnp.float32) - ref[below, c].astype(jnp.float32))
                gz = 0.5 * (pltpu.roll(here, nz - 1, 1) - pltpu.roll(here, 1, 1))
                gx = gx.astype(jnp.bfloat16).astype(jnp.float32)
                gz = gz.astype(jnp.bfloat16).astype(jnp.float32)
                wts[r, block, pl.ds(c * nz, nz)] = (weight * here).astype(jnp.bfloat16)
                for j in range(JB):
                    total = phi[0][j : j + 1] * gx + phi[2][j : j + 1] * gz
                    adv[r, pl.ds((2 * j + half) * nk, nk), pl.ds(c * nz, nz)] = total.astype(jnp.bfloat16)
    total = dot_nt(adv[0], wts[0])
    for r in range(1, rows):
        total = total + dot_nt(adv[r], wts[r])
    acc_ref[...] = total
    quarter = rows // 2
    for r in range(quarter):
        w0_ref[r] = wts[quarter * q + r]


def same_core_rows(planes, first_ref, second_ref):
    x_came = x_first(jnp.bitwise_xor(lax.axis_index("space"), 1), planes)
    return (
        lambda rows: jnp.where(x_came, first_ref[rows, :], second_ref[rows, :]),
        lambda rows: jnp.where(x_came, second_ref[rows, :], first_ref[rows, :]),
    )


def sign_of_plane():
    return jnp.where(lax.rem(lax.axis_index("space"), 2) == 0, 0.5, -0.5)


def early_kernel(
    planes, own_ref, other_ref, first_ref, second_ref, xc_ref, w0_ref, jb_ref, acc_ref, out_ref, w1_ref, adv
):
    xs_rows, _ = same_core_rows(planes, first_ref, second_ref)
    m = lax.axis_index("modes")
    q = lax.rem(lax.axis_index("space"), 2)
    nx, comps, nk, nz = own_ref.shape
    quarter = nx // 4
    pick = picks(jb_ref, m, nk)
    weights = received_weights(xc_ref, quarter * comps * nk, quarter)
    for r in range(quarter):
        row0 = quarter * (2 * m + q) + r
        phi0 = sign_of_plane() * picked(
            pick, lambda at: own_ref[row0, 1, at, :], lambda at: other_ref[row0, 1, at, :]
        )
        phi0 = [spread(phi0[j : j + 1]) for j in range(JB)]
        for c in range(comps):
            at = pl.ds((r * comps + c) * nz, nz)
            src = pl.ds((r * comps + c) * nk, nk)
            for half, f1 in enumerate((xs_rows(src), xc_ref[src, :])):
                w1_ref[pl.ds(half * nk, nk), at] = (weights[r] * f1.astype(jnp.float32)).astype(
                    jnp.bfloat16
                )
                for j in range(JB):
                    adv[r, pl.ds((2 * j + half) * nk, nk), pl.ds(c * nz, nz)] = scaled(phi0[j], f1)
    total = acc_ref[...]
    for r in range(quarter):
        total = total + dot_nt(adv[r], w0_ref[r])
    out_ref[...] = total


def cross_kernel(classes_of, chunk, planes, whole, has_weighted, own_ref, other_ref, *refs):
    first_ref, second_ref, xc_ref, zc_ref, w1_ref, jb_ref, acc_ref, *refs = refs
    xs_rows, zs_rows = same_core_rows(planes, first_ref, second_ref)
    if has_weighted:
        wts, keep_ref, send_ref, adv = refs
    else:
        keep_ref, send_ref, wts, adv = refs
    m = lax.axis_index("modes")
    plane = lax.axis_index("space")
    q = lax.rem(plane, 2)
    inside = jnp.where(jnp.logical_or(plane == 1, plane == planes - 2), 0.0, 1.0)
    nx, comps, nk, nz = own_ref.shape
    quarter = nx // 4
    span = quarter * comps * nz
    pick = picks(jb_ref, m, nk)
    classes = [pl.multiple_of(chunk * cls, chunk) for cls in classes_of(plane)]
    if not has_weighted:
        weights = received_weights(zc_ref, quarter * comps * nk, quarter)
        wts[:, pl.ds(0, span)] = w1_ref[...]
        for r in range(quarter):
            weight = inside * weights[r]
            for c in range(comps):
                src = pl.ds((r * comps + c) * nk, nk)
                for half, f2 in enumerate((zs_rows(src), zc_ref[src, :])):
                    wts[pl.ds(half * nk, nk), pl.ds(span + (r * comps + c) * nz, nz)] = (
                        weight * f2.astype(jnp.float32)
                    ).astype(jnp.bfloat16)
    phis = []
    for r in range(quarter):
        along = (r * comps + 1) * nk

        def moved(at):
            return pl.ds(pl.multiple_of(along + at.start, 16), at.size)

        phi1 = sign_of_plane() * picked(
            pick, lambda at: xs_rows(moved(at)), lambda at: xc_ref[moved(at), :]
        )
        phi2 = -sign_of_plane() * picked(
            pick, lambda at: zs_rows(moved(at)), lambda at: zc_ref[moved(at), :]
        )
        phis.append([[spread(phi[j : j + 1]) for j in range(JB)] for phi in (phi1, phi2)])
    inside = inside.astype(jnp.bfloat16)
    for at, cls in enumerate(classes):
        for r in range(quarter):
            row0 = quarter * (2 * m + q) + r
            phi1, phi2 = phis[r]
            for c in range(comps):
                lane = (r * comps + c) * nz
                src = (r * comps + c) * nk
                rows_at = pl.ds(pl.multiple_of(src + cls, 16), chunk)
                for half, (p0, f1, f2) in enumerate(
                    (
                        (own_ref, xs_rows(rows_at), zs_rows(rows_at)),
                        (other_ref, xc_ref[rows_at, :], zc_ref[rows_at, :]),
                    )
                ):
                    f0 = p0[row0, c, pl.ds(cls, chunk), :]
                    gy = inside * f2 - f0
                    for j in range(JB):
                        here = pl.ds((half * JB + j) * chunk, chunk)
                        adv[at, here, pl.ds(lane, nz)] = scaled(phi1[j], gy)
                        adv[at, here, pl.ds(span + lane, nz)] = scaled(phi2[j], f1)
        total = dot_nt(adv[at], wts[...])
        for half in range(2):
            level = m if half == 0 else 1 - m
            for j in range(JB):
                first = (half * JB + j) * chunk
                piece = total[first : first + chunk] + acc_ref[pl.ds((2 * j + half) * nk + cls, chunk), :]
                row = pl.multiple_of(((2 * at + level) * JB + j) * chunk, chunk)
                if whole:
                    swapped = jnp.concatenate([piece[:, nk:], piece[:, :nk]], axis=1)
                    piece = jnp.where(m == 0, piece, swapped)
                    keep_ref[at, level, j] = piece
                    send_ref[pl.ds(row, chunk), :] = piece.astype(jnp.bfloat16)
                else:
                    keep_ref[at, level, j] = piece[:, :nk]
                    send_ref[pl.ds(row, chunk), :] = piece[:, nk:].astype(jnp.bfloat16)


def near_kernel(keep_ref, got_ref, *out_refs):
    got = got_ref[...].astype(jnp.float32).reshape(keep_ref.shape)
    for at, ref in enumerate(out_refs):
        ref[...] = (keep_ref[at] + got[at]).astype(ref.dtype).reshape(ref.shape)


def far_kernel(mine_ref, *refs):
    *parts, keep_ref, send_ref = refs
    level = lax.div(lax.axis_index("space"), NEAR)
    rows = send_ref.shape[0]
    for ref, at in ((keep_ref, level), (send_ref, 1 - level)):
        total = mine_ref[at]
        for part in parts:
            piece = part[pl.ds(pl.multiple_of(at * rows, rows), rows), :]
            total = total + piece.astype(jnp.float32).reshape(total.shape)
        ref[...] = total.astype(ref.dtype).reshape(ref.shape)


def result_kernel(keep_ref, got_ref, own_ref, send_ref):
    nk = own_ref.shape[2]
    total = keep_ref[...] + got_ref[...].astype(jnp.float32).reshape(keep_ref.shape)
    send_ref[...] = total[:, :, :nk].reshape(send_ref.shape)
    own_ref[...] = total[:, :, nk:]


def total_kernel(own_ref, got_ref, out_ref):
    first_core = lax.axis_index("modes") == 0
    total = jnp.where(first_core, got_ref[...].reshape(own_ref.shape), own_ref[...])
    for j in range(JB):
        out_ref[:, j, :] = total[j]


def on_device(n, modes, weight_ids, weight_table, j_block):
    nk, comps, _, nx, nz = modes.shape
    bf16, f32 = jnp.bfloat16, jnp.float32
    vmem = pl.BlockSpec(memory_space=pltpu.VMEM)
    smem = pl.BlockSpec(memory_space=pltpu.SMEM)
    params = pltpu.CompilerParams(vmem_limit_bytes=VMEM_LIMIT)
    quarter = nx // 4
    body = quarter * comps * nk
    own, first, second = pl.pallas_call(
        functools.partial(prep_kernel, n),
        out_shape=[jax.ShapeDtypeStruct((nx, comps, nk, nz), bf16)]
        + [jax.ShapeDtypeStruct((body + PADROWS, nz), bf16)] * 2,
        in_specs=[pl.BlockSpec(memory_space=pltpu.HBM)],
        out_specs=[vmem] * 3,
        scratch_shapes=[pltpu.VMEM(modes.shape, bf16), pltpu.SemaphoreType.DMA((LOADS,))],
        compiler_params=pltpu.CompilerParams(vmem_limit_bytes=PREP_LIMIT),
        cost_estimate=pl.CostEstimate(flops=1_500_000_000, bytes_accessed=2_800_000, transcendentals=0),
        name="prep",
    )(modes)

    both = ("space", "modes")
    x_to = lambda s: s ^ 1
    z_to = lambda s: s + 2 if s % 2 else s - 2
    x_now = [n != 8 or X_FIRST >> s & 1 for s in range(n)]
    firsts = [(s, x_to(s) if x_now[s] else z_to(s)) for s in range(n)]
    seconds = [(s, z_to(s) % n if x_now[s] else x_to(s)) for s in range(n)]
    same = lambda pairs: [(2 * a + m, 2 * b + m) for a, b in pairs for m in range(2)]
    cross = lambda pairs: [(2 * a + m, 2 * b + 1 - m) for a, b in pairs for m in range(2)]
    other = lax.ppermute(own, "modes", [(0, 1), (1, 0)])
    first = lax.ppermute(first, both, same(firsts))
    second = lax.ppermute(second, both, same(seconds))
    weight, xc, zc = pl.pallas_call(
        weights_kernel,
        out_shape=[jax.ShapeDtypeStruct((nx, nz), f32)]
        + [jax.ShapeDtypeStruct((body + 8 * quarter, nz), bf16)] * 2,
        in_specs=[vmem] * 3 + [pl.BlockSpec(memory_space=pl.ANY)],
        out_specs=[vmem] * 3,
        compiler_params=params,
        name="weights",
    )(weight_ids, jnp.broadcast_to(weight_table[None], (8, NW)), own, other)
    xc = lax.ppermute(xc, both, cross([(s, x_to(s)) for s in range(n)]))
    zc = lax.ppermute(zc, both, cross([(s, z_to(s)) for s in range(n) if 0 <= z_to(s) < n]))

    depth = nx // 4 * comps * nz
    depth = quarter * comps * nz
    acc, w0 = pl.pallas_call(
        local_kernel,
        out_shape=[
            jax.ShapeDtypeStruct((JB * 2 * nk, 2 * nk), f32),
            jax.ShapeDtypeStruct((quarter, 2 * nk, comps * nz), bf16),
        ],
        in_specs=[vmem, vmem, vmem, smem],
        out_specs=[vmem] * 2,
        scratch_shapes=[
            pltpu.VMEM((2 * quarter, JB * 2 * nk, comps * nz), bf16),
            pltpu.VMEM((2 * quarter, 2 * nk, comps * nz), bf16),
        ],
        compiler_params=params,
        cost_estimate=pl.CostEstimate(flops=900_000_000, bytes_accessed=2_400_000, transcendentals=0),
        name="local",
    )(own, other, weight, j_block)

    acc, w1 = pl.pallas_call(
        functools.partial(early_kernel, n),
        out_shape=[
            jax.ShapeDtypeStruct((JB * 2 * nk, 2 * nk), f32),
            jax.ShapeDtypeStruct((2 * nk, depth), bf16),
        ],
        in_specs=[vmem] * 6 + [smem, vmem],
        out_specs=[vmem] * 2,
        scratch_shapes=[pltpu.VMEM((quarter, JB * 2 * nk, comps * nz), bf16)],
        compiler_params=params,
        cost_estimate=pl.CostEstimate(flops=600_000_000, bytes_accessed=2_400_000, transcendentals=0),
        name="early",
    )(own, other, first, second, xc, w0, j_block, acc)

    per_target = 2 * nk // n
    chunk = max(16, per_target)
    whole = n == 2 * NEAR

    def crossed(count, classes_of, weighted):
        lanes = 2 * nk if whole else nk
        out_shape = [
            jax.ShapeDtypeStruct((count, 2, JB, chunk, lanes), f32),
            jax.ShapeDtypeStruct((count * 2 * JB * chunk, lanes), bf16),
        ]
        if not weighted:
            out_shape.append(jax.ShapeDtypeStruct((2 * nk, 2 * depth), bf16))
        return pl.pallas_call(
            functools.partial(cross_kernel, classes_of, chunk, n, whole, bool(weighted)),
            out_shape=out_shape,
            in_specs=[vmem] * 7 + [smem] + [vmem] * (1 + len(weighted)),
            out_specs=[vmem] * len(out_shape),
            scratch_shapes=[pltpu.VMEM((count, 2 * JB * chunk, 2 * depth), bf16)],
            compiler_params=params,
            cost_estimate=pl.CostEstimate(
                flops=900_000_000, bytes_accessed=4_000_000, transcendentals=0
            ),
            name="cross",
        )(own, other, first, second, xc, zc, w1, j_block, acc, *weighted)

    swap = [(0, 1), (1, 0)]
    if whole:
        def partners(*steps):
            return lambda s: [jnp.bitwise_xor(lax.rem(s, NEAR), step) for step in steps]

        def to_chip(value, step):
            pairs = [(2 * s, 2 * s) for s in range(n)] + [(2 * s + 1, 2 * (s ^ step) + 1) for s in range(n)]
            return lax.ppermute(value, both, pairs)

        keep_a, send_a, w2 = crossed(2, partners(3, 1), ())
        got_a = lax.ppermute(send_a, "modes", swap)
        keep_b, send_b = crossed(2, partners(0, 2), (w2,))
        got_b = lax.ppermute(send_b, "modes", swap)
        piece = (JB, chunk, 2 * nk)

        def summed(out_shape, keep, got):
            return pl.pallas_call(
                near_kernel,
                out_shape=out_shape,
                in_specs=[vmem] * 2,
                out_specs=[vmem] * 2,
                compiler_params=params,
                name="near",
            )(keep, got)

        kept = jax.ShapeDtypeStruct((2, *piece), f32)
        sent = jax.ShapeDtypeStruct((2 * JB * chunk, 2 * nk), bf16)
        part_3, part_1 = summed([sent, sent], keep_a, got_a)
        mine, part_2 = summed([kept, sent], keep_b, got_b)
        parts = [to_chip(part, step) for part, step in ((part_3, 3), (part_1, 1), (part_2, 2))]
        keep, send = pl.pallas_call(
            far_kernel,
            out_shape=[
                jax.ShapeDtypeStruct(piece, f32),
                jax.ShapeDtypeStruct((JB * chunk, 2 * nk), bf16),
            ],
            in_specs=[vmem] * NEAR,
            out_specs=[vmem] * 2,
            compiler_params=params,
            name="far",
        )(mine, *parts)
        own_half, other_half = pl.pallas_call(
            result_kernel,
            out_shape=[
                jax.ShapeDtypeStruct((JB, chunk, nk), f32),
                jax.ShapeDtypeStruct((JB * chunk, nk), f32),
            ],
            in_specs=[vmem] * 2,
            out_specs=[vmem] * 2,
            compiler_params=params,
            name="result",
        )(keep, to_chip(send, NEAR))
        return pl.pallas_call(
            total_kernel,
            out_shape=jax.ShapeDtypeStruct((chunk, JB, nk), f32),
            in_specs=[vmem] * 2,
            out_specs=vmem,
            compiler_params=params,
            name="total",
        )(own_half, lax.ppermute(other_half, "modes", swap))

    count = nk // chunk
    keep, send, _ = crossed(count, lambda s: list(range(count)), ())
    share = (keep + lax.ppermute(send, "modes", swap).reshape(keep.shape)).astype(bf16)
    share = share.reshape(count, 2, JB, chunk // per_target, per_target, nk)
    share = share.transpose(1, 0, 3, 2, 4, 5).reshape(n, JB, per_target, nk)
    parts = lax.all_to_all(share, "space", 0, 0, tiled=True)
    return jnp.sum(parts.astype(f32), axis=0).transpose(1, 0, 2)


def solution(mesh):
    return jax.shard_map(
        functools.partial(on_device, mesh.shape["space"]),
        mesh=mesh,
        in_specs=(
            P("modes", None, ("groups", "space"), None, None),
            P(("groups", "space"), None, None),
            P(),
            P("groups"),
        ),
        out_specs=P(("groups", "space"), None, "modes"),
        check_vma=False,
    )
```

```python
import functools

import jax
import jax.numpy as jnp
from jax import lax
from jax.experimental import pallas as pl
from jax.experimental.pallas import tpu as pltpu
from jax.sharding import PartitionSpec as P

JB = 4
NW = 16
PADROWS = 16
LOADS = 4
X_FIRST = 0b10011111
NEAR = 4
VMEM_LIMIT = 48 * 1024 * 1024
PREP_LIMIT = 53_600 * 1024


def x_first(s, planes):
    if planes != 8:
        return s >= 0
    return lax.rem(lax.shift_right_logical(X_FIRST, s), 2) == 1


def copy_rows(ref, tr, at):
    nx, comps, nk, _ = tr.shape
    for row in range(nx // 4):
        for c in range(comps):
            ref[pl.ds((row * comps + c) * nk, nk), :] = tr[at * (nx // 4) + row, c]


def prep_kernel(planes, modes_hbm, tr, first_ref, second_ref, modes_ref, sems):
    m = lax.axis_index("modes")
    s = lax.axis_index("space")
    q = lax.rem(s, 2)
    nk, comps, _, nx, nz = modes_hbm.shape
    step = nk // LOADS
    copies = [
        pltpu.make_async_copy(
            modes_hbm.at[pl.ds(p * step, step)], modes_ref.at[pl.ds(p * step, step)], sems.at[p]
        )
        for p in range(LOADS)
    ]
    for copy in copies:
        copy.start()
    for p in range(LOADS):
        copies[p].wait()
        block = pl.ds(p * step, step)
        for c in range(comps):
            value = modes_ref[block, c, 0].astype(jnp.float32)
            tr[:, c, block] = jnp.swapaxes(value, 0, 1).astype(jnp.bfloat16)
    body = nx // 4 * comps * nk
    to_x, to_z = 2 * m + 1 - q, 2 * m + q
    x_now = x_first(s, planes)
    for ref, at in (
        (first_ref, jnp.where(x_now, to_x, to_z)),
        (second_ref, jnp.where(x_now, to_z, to_x)),
    ):
        copy_rows(ref, tr, at)
        ref[pl.ds(body, PADROWS), :] = jnp.zeros((PADROWS, nz), jnp.bfloat16)


def weights_kernel(ids_ref, table_ref, tr, _, weight_ref, xc_ref, zc_ref):
    m = lax.axis_index("modes")
    q = lax.rem(lax.axis_index("space"), 2)
    nx, comps, nk, nz = tr.shape
    quarter = nx // 4
    table = table_ref[...]
    weight = jnp.zeros((nx, nz), jnp.float32)
    for entry in range(NW):
        weight = jnp.where(ids_ref[0] == entry, table[0:1, entry : entry + 1], weight)
    weight_ref[...] = weight
    for ref, at in ((xc_ref, 2 * (1 - m) + 1 - q), (zc_ref, 2 * (1 - m) + q)):
        copy_rows(ref, tr, at)
        rest = jnp.concatenate(
            [
                jnp.broadcast_to(weight_ref[pl.ds(at * quarter + row, 1), :], (8, nz))
                for row in range(quarter)
            ],
            axis=0,
        )
        piece_of = lax.rem(lax.broadcasted_iota(jnp.int32, rest.shape, 0), 8)
        pieces = jnp.zeros(rest.shape, jnp.float32)
        for piece in range(3):
            rounded = rest.astype(jnp.bfloat16).astype(jnp.float32)
            pieces = jnp.where(piece_of == piece, rounded, pieces)
            rest = rest - rounded
        ref[pl.ds(quarter * comps * nk, 8 * quarter), :] = pieces.astype(jnp.bfloat16)


def received_weights(ref, first, quarter):
    pieces = ref[pl.ds(first, 8 * quarter), :].astype(jnp.float32)
    return [
        pieces[8 * r : 8 * r + 1] + pieces[8 * r + 1 : 8 * r + 2] + pieces[8 * r + 2 : 8 * r + 3]
        for r in range(quarter)
    ]


def picks(jb_ref, m, nk):
    first = jb_ref[0] * JB
    owner = (first >= nk).astype(jnp.int32)
    row = first - owner * nk
    within = lax.rem(row, 16)
    return owner == m, pl.multiple_of(row - within, 16), within


def picked(pick, own, other):
    mine, block, within = pick
    rows = pl.ds(block, 16)
    rows = jnp.where(mine, own(rows).astype(jnp.float32), other(rows).astype(jnp.float32))
    result = rows[0:JB]
    for start in range(JB, 16, JB):
        result = jnp.where(within == start, rows[start : start + JB], result)
    return result


def spread(row):
    return jnp.broadcast_to(row, (16, row.shape[1])).astype(jnp.bfloat16)[None]


def scaled(tile, field):
    rows, lanes = field.shape
    return (tile * field.reshape(rows // 16, 16, lanes)).reshape(rows, lanes)


def dot_nt(a, b):
    return lax.dot_general(a, b, (((1,), (1,)), ((), ())), preferred_element_type=jnp.float32)


def local_kernel(own_ref, other_ref, weight_ref, jb_ref, acc_ref, w0_ref, adv, wts):
    m = lax.axis_index("modes")
    q = lax.rem(lax.axis_index("space"), 2)
    nx, comps, nk, nz = own_ref.shape
    rows = nx // 2
    pick = picks(jb_ref, m, nk)
    for r in range(rows):
        row = rows * m + r
        below, above = lax.rem(row + nx - 1, nx), lax.rem(row + 1, nx)
        phi = [picked(pick, lambda at: own_ref[row, d, at, :], lambda at: other_ref[row, d, at, :]) for d in range(comps)]
        weight = weight_ref[pl.ds(row, 1), :]
        for c in range(comps):
            for half, ref in enumerate((own_ref, other_ref)):
                block = pl.ds(half * nk, nk)
                here = ref[row, c].astype(jnp.float32)
                gx = 0.5 * (ref[above, c].astype(jnp.float32) - ref[below, c].astype(jnp.float32))
                gz = 0.5 * (pltpu.roll(here, nz - 1, 1) - pltpu.roll(here, 1, 1))
                gx = gx.astype(jnp.bfloat16).astype(jnp.float32)
                gz = gz.astype(jnp.bfloat16).astype(jnp.float32)
                wts[r, block, pl.ds(c * nz, nz)] = (weight * here).astype(jnp.bfloat16)
                for j in range(JB):
                    total = phi[0][j : j + 1] * gx + phi[2][j : j + 1] * gz
                    adv[r, pl.ds((2 * j + half) * nk, nk), pl.ds(c * nz, nz)] = total.astype(jnp.bfloat16)
    total = dot_nt(adv[0], wts[0])
    for r in range(1, rows):
        total = total + dot_nt(adv[r], wts[r])
    acc_ref[...] = total
    quarter = rows // 2
    for r in range(quarter):
        w0_ref[r] = wts[quarter * q + r]


def same_core_rows(planes, first_ref, second_ref):
    x_came = x_first(jnp.bitwise_xor(lax.axis_index("space"), 1), planes)
    return (
        lambda rows: jnp.where(x_came, first_ref[rows, :], second_ref[rows, :]),
        lambda rows: jnp.where(x_came, second_ref[rows, :], first_ref[rows, :]),
    )


def sign_of_plane():
    return jnp.where(lax.rem(lax.axis_index("space"), 2) == 0, 0.5, -0.5)


def early_kernel(
    planes, own_ref, other_ref, first_ref, second_ref, xc_ref, w0_ref, jb_ref, acc_ref, out_ref, w1_ref, adv
):
    xs_rows, _ = same_core_rows(planes, first_ref, second_ref)
    m = lax.axis_index("modes")
    q = lax.rem(lax.axis_index("space"), 2)
    nx, comps, nk, nz = own_ref.shape
    quarter = nx // 4
    pick = picks(jb_ref, m, nk)
    weights = received_weights(xc_ref, quarter * comps * nk, quarter)
    for r in range(quarter):
        row0 = quarter * (2 * m + q) + r
        phi0 = sign_of_plane() * picked(
            pick, lambda at: own_ref[row0, 1, at, :], lambda at: other_ref[row0, 1, at, :]
        )
        phi0 = [spread(phi0[j : j + 1]) for j in range(JB)]
        for c in range(comps):
            at = pl.ds((r * comps + c) * nz, nz)
            src = pl.ds((r * comps + c) * nk, nk)
            for half, f1 in enumerate((xs_rows(src), xc_ref[src, :])):
                w1_ref[pl.ds(half * nk, nk), at] = (weights[r] * f1.astype(jnp.float32)).astype(
                    jnp.bfloat16
                )
                for j in range(JB):
                    adv[r, pl.ds((2 * j + half) * nk, nk), pl.ds(c * nz, nz)] = scaled(phi0[j], f1)
    total = acc_ref[...]
    for r in range(quarter):
        total = total + dot_nt(adv[r], w0_ref[r])
    out_ref[...] = total


def cross_kernel(classes_of, chunk, planes, has_weighted, own_ref, other_ref, *refs):
    first_ref, second_ref, xc_ref, zc_ref, w1_ref, jb_ref, acc_ref, *refs = refs
    xs_rows, zs_rows = same_core_rows(planes, first_ref, second_ref)
    if has_weighted:
        wts, keep_ref, send_ref, adv = refs
    else:
        keep_ref, send_ref, wts, adv = refs
    m = lax.axis_index("modes")
    plane = lax.axis_index("space")
    q = lax.rem(plane, 2)
    inside = jnp.where(jnp.logical_or(plane == 1, plane == planes - 2), 0.0, 1.0)
    nx, comps, nk, nz = own_ref.shape
    quarter = nx // 4
    span = quarter * comps * nz
    pick = picks(jb_ref, m, nk)
    classes = [pl.multiple_of(chunk * cls, chunk) for cls in classes_of(plane)]
    if not has_weighted:
        weights = received_weights(zc_ref, quarter * comps * nk, quarter)
        wts[:, pl.ds(0, span)] = w1_ref[...]
        for r in range(quarter):
            weight = inside * weights[r]
            for c in range(comps):
                src = pl.ds((r * comps + c) * nk, nk)
                for half, f2 in enumerate((zs_rows(src), zc_ref[src, :])):
                    wts[pl.ds(half * nk, nk), pl.ds(span + (r * comps + c) * nz, nz)] = (
                        weight * f2.astype(jnp.float32)
                    ).astype(jnp.bfloat16)
    phis = []
    for r in range(quarter):
        along = (r * comps + 1) * nk

        def moved(at):
            return pl.ds(pl.multiple_of(along + at.start, 16), at.size)

        phi1 = sign_of_plane() * picked(
            pick, lambda at: xs_rows(moved(at)), lambda at: xc_ref[moved(at), :]
        )
        phi2 = -sign_of_plane() * picked(
            pick, lambda at: zs_rows(moved(at)), lambda at: zc_ref[moved(at), :]
        )
        phis.append([[spread(phi[j : j + 1]) for j in range(JB)] for phi in (phi1, phi2)])
    inside = inside.astype(jnp.bfloat16)
    for at, cls in enumerate(classes):
        for r in range(quarter):
            row0 = quarter * (2 * m + q) + r
            phi1, phi2 = phis[r]
            for c in range(comps):
                lane = (r * comps + c) * nz
                src = (r * comps + c) * nk
                rows_at = pl.ds(pl.multiple_of(src + cls, 16), chunk)
                for half, (p0, f1, f2) in enumerate(
                    (
                        (own_ref, xs_rows(rows_at), zs_rows(rows_at)),
                        (other_ref, xc_ref[rows_at, :], zc_ref[rows_at, :]),
                    )
                ):
                    f0 = p0[row0, c, pl.ds(cls, chunk), :]
                    gy = inside * f2 - f0
                    for j in range(JB):
                        here = pl.ds((half * JB + j) * chunk, chunk)
                        adv[at, here, pl.ds(lane, nz)] = scaled(phi1[j], gy)
                        adv[at, here, pl.ds(span + lane, nz)] = scaled(phi2[j], f1)
        total = dot_nt(adv[at], wts[...])
        for half in range(2):
            level = m if half == 0 else 1 - m
            for j in range(JB):
                first = (half * JB + j) * chunk
                piece = total[first : first + chunk] + acc_ref[pl.ds((2 * j + half) * nk + cls, chunk), :]
                keep_ref[at, level, j] = piece[:, :nk]
                row = pl.multiple_of(((2 * at + level) * JB + j) * chunk, chunk)
                send_ref[pl.ds(row, chunk), :] = piece[:, nk:].astype(jnp.bfloat16)


def level_of():
    return lax.div(lax.axis_index("space"), NEAR)


def chip_sum(keep_ref, got_ref, at, level):
    rows = JB * keep_ref.shape[3]
    row = pl.multiple_of((2 * at + level) * rows, rows)
    got = got_ref[pl.ds(row, rows), :].astype(jnp.float32)
    return keep_ref[at, level] + got.reshape(keep_ref.shape[2:])


def put(ref, value):
    ref[...] = value.astype(ref.dtype).reshape(ref.shape)


def plus(total, refs):
    for ref in refs:
        total = total + ref[...].astype(jnp.float32).reshape(total.shape)
    return total


def away_kernel(keep_ref, got_ref, first_ref, second_ref):
    put(first_ref, chip_sum(keep_ref, got_ref, 0, 1 - level_of()))
    put(second_ref, chip_sum(keep_ref, got_ref, 1, 1 - level_of()))


def mine_kernel(keep_ref, got_ref, mine_ref, up_ref):
    for level in range(2):
        mine_ref[level] = chip_sum(keep_ref, got_ref, 0, level)
    put(up_ref, chip_sum(keep_ref, got_ref, 1, 1 - level_of()))


def here_kernel(keep_ref, got_ref, _, first_ref, second_ref):
    put(first_ref, chip_sum(keep_ref, got_ref, 0, level_of()))
    put(second_ref, chip_sum(keep_ref, got_ref, 1, level_of()))


def far_kernel(mine_ref, p0_ref, p1_ref, p2_ref, send_ref):
    put(send_ref, plus(mine_ref[1 - level_of()], (p0_ref, p1_ref, p2_ref)))


def last_kernel(keep_ref, got_ref, _, up_ref):
    put(up_ref, chip_sum(keep_ref, got_ref, 1, level_of()))


def total_kernel(mine_ref, p0_ref, p1_ref, p2_ref, p3_ref, out_ref):
    total = plus(mine_ref[level_of()], (p0_ref, p1_ref, p2_ref, p3_ref))
    for j in range(JB):
        out_ref[:, j, :] = total[j]


def on_device(n, modes, weight_ids, weight_table, j_block):
    nk, comps, _, nx, nz = modes.shape
    bf16, f32 = jnp.bfloat16, jnp.float32
    vmem = pl.BlockSpec(memory_space=pltpu.VMEM)
    smem = pl.BlockSpec(memory_space=pltpu.SMEM)
    params = pltpu.CompilerParams(vmem_limit_bytes=VMEM_LIMIT)
    quarter = nx // 4
    body = quarter * comps * nk
    own, first, second = pl.pallas_call(
        functools.partial(prep_kernel, n),
        out_shape=[jax.ShapeDtypeStruct((nx, comps, nk, nz), bf16)]
        + [jax.ShapeDtypeStruct((body + PADROWS, nz), bf16)] * 2,
        in_specs=[pl.BlockSpec(memory_space=pltpu.HBM)],
        out_specs=[vmem] * 3,
        scratch_shapes=[pltpu.VMEM(modes.shape, bf16), pltpu.SemaphoreType.DMA((LOADS,))],
        compiler_params=pltpu.CompilerParams(vmem_limit_bytes=PREP_LIMIT),
        cost_estimate=pl.CostEstimate(flops=1_500_000_000, bytes_accessed=2_800_000, transcendentals=0),
        name="prep",
    )(modes)

    both = ("space", "modes")
    x_to = lambda s: s ^ 1
    z_to = lambda s: s + 2 if s % 2 else s - 2
    x_now = [n != 8 or X_FIRST >> s & 1 for s in range(n)]
    firsts = [(s, x_to(s) if x_now[s] else z_to(s)) for s in range(n)]
    seconds = [(s, z_to(s) % n if x_now[s] else x_to(s)) for s in range(n)]
    same = lambda pairs: [(2 * a + m, 2 * b + m) for a, b in pairs for m in range(2)]
    cross = lambda pairs: [(2 * a + m, 2 * b + 1 - m) for a, b in pairs for m in range(2)]
    other = lax.ppermute(own, "modes", [(0, 1), (1, 0)])
    first = lax.ppermute(first, both, same(firsts))
    second = lax.ppermute(second, both, same(seconds))
    weight, xc, zc = pl.pallas_call(
        weights_kernel,
        out_shape=[jax.ShapeDtypeStruct((nx, nz), f32)]
        + [jax.ShapeDtypeStruct((body + 8 * quarter, nz), bf16)] * 2,
        in_specs=[vmem] * 3 + [pl.BlockSpec(memory_space=pl.ANY)],
        out_specs=[vmem] * 3,
        compiler_params=params,
        name="weights",
    )(weight_ids, jnp.broadcast_to(weight_table[None], (8, NW)), own, other)
    xc = lax.ppermute(xc, both, cross([(s, x_to(s)) for s in range(n)]))
    zc = lax.ppermute(zc, both, cross([(s, z_to(s)) for s in range(n) if 0 <= z_to(s) < n]))

    depth = nx // 4 * comps * nz
    depth = quarter * comps * nz
    acc, w0 = pl.pallas_call(
        local_kernel,
        out_shape=[
            jax.ShapeDtypeStruct((JB * 2 * nk, 2 * nk), f32),
            jax.ShapeDtypeStruct((quarter, 2 * nk, comps * nz), bf16),
        ],
        in_specs=[vmem, vmem, vmem, smem],
        out_specs=[vmem] * 2,
        scratch_shapes=[
            pltpu.VMEM((2 * quarter, JB * 2 * nk, comps * nz), bf16),
            pltpu.VMEM((2 * quarter, 2 * nk, comps * nz), bf16),
        ],
        compiler_params=params,
        cost_estimate=pl.CostEstimate(flops=900_000_000, bytes_accessed=2_400_000, transcendentals=0),
        name="local",
    )(own, other, weight, j_block)

    acc, w1 = pl.pallas_call(
        functools.partial(early_kernel, n),
        out_shape=[
            jax.ShapeDtypeStruct((JB * 2 * nk, 2 * nk), f32),
            jax.ShapeDtypeStruct((2 * nk, depth), bf16),
        ],
        in_specs=[vmem] * 6 + [smem, vmem],
        out_specs=[vmem] * 2,
        scratch_shapes=[pltpu.VMEM((quarter, JB * 2 * nk, comps * nz), bf16)],
        compiler_params=params,
        cost_estimate=pl.CostEstimate(flops=600_000_000, bytes_accessed=2_400_000, transcendentals=0),
        name="early",
    )(own, other, first, second, xc, w0, j_block, acc)

    per_target = 2 * nk // n
    chunk = max(16, per_target)

    def crossed(count, classes_of, weighted):
        piece = (count, 2, JB, chunk, nk)
        out_shape = [
            jax.ShapeDtypeStruct(piece, f32),
            jax.ShapeDtypeStruct((count * 2 * JB * chunk, nk), bf16),
        ]
        if not weighted:
            out_shape.append(jax.ShapeDtypeStruct((2 * nk, 2 * depth), bf16))
        return pl.pallas_call(
            functools.partial(cross_kernel, classes_of, chunk, n, bool(weighted)),
            out_shape=out_shape,
            in_specs=[vmem] * 7 + [smem] + [vmem] * (1 + len(weighted)),
            out_specs=[vmem] * len(out_shape),
            scratch_shapes=[pltpu.VMEM((count, 2 * JB * chunk, 2 * depth), bf16)],
            compiler_params=params,
            cost_estimate=pl.CostEstimate(
                flops=900_000_000, bytes_accessed=4_000_000, transcendentals=0
            ),
            name="cross",
        )(own, other, first, second, xc, zc, w1, j_block, acc, *weighted)

    swap = [(0, 1), (1, 0)]
    if n == 2 * NEAR:
        def partners(*steps):
            return lambda s: [jnp.bitwise_xor(lax.rem(s, NEAR), step) for step in steps]

        keep_a, send_a, w2 = crossed(2, partners(3, 1), ())
        got_a = lax.ppermute(send_a, "modes", swap)
        keep_b, send_b = crossed(2, partners(0, 2), (w2,))
        got_b = lax.ppermute(send_b, "modes", swap)
        piece = (JB, chunk, nk)

        def made(body_of, out_shape, operands, order=()):
            return pl.pallas_call(
                body_of,
                out_shape=out_shape,
                in_specs=[vmem] * len(operands) + [pl.BlockSpec(memory_space=pl.ANY)] * len(order),
                out_specs=jax.tree.map(lambda _: vmem, out_shape),
                compiler_params=params,
                name=body_of.__name__.removesuffix("_kernel"),
            )(*operands, *order)

        def to_chip(value, step):
            return lax.ppermute(value, "space", [(s, s ^ step) for s in range(n)])

        kept = jax.ShapeDtypeStruct((2, *piece), f32)
        sent = jax.ShapeDtypeStruct((JB * chunk, nk), bf16)
        away_3, away_1 = made(away_kernel, [sent, sent], (keep_a, got_a))
        mine, away_2 = made(mine_kernel, [kept, sent], (keep_b, got_b))
        here_3, here_1 = made(here_kernel, [sent, sent], (keep_a, got_a), (away_2,))
        away = [to_chip(part, step) for part, step in ((away_3, 3), (away_1, 1), (away_2, 2))]
        far = made(far_kernel, sent, (mine, *away))
        here_2 = made(last_kernel, sent, (keep_b, got_b), (far,))
        parts = [
            to_chip(part, step)
            for part, step in ((here_3, 3), (here_1, 1), (far, NEAR), (here_2, 2))
        ]
        return made(total_kernel, jax.ShapeDtypeStruct((chunk, JB, nk), f32), (mine, *parts))

    count = nk // chunk
    keep, send, _ = crossed(count, lambda s: list(range(count)), ())
    share = (keep + lax.ppermute(send, "modes", swap).reshape(keep.shape)).astype(bf16)
    share = share.reshape(count, 2, JB, chunk // per_target, per_target, nk)
    share = share.transpose(1, 0, 3, 2, 4, 5).reshape(n, JB, per_target, nk)
    parts = lax.all_to_all(share, "space", 0, 0, tiled=True)
    return jnp.sum(parts.astype(f32), axis=0).transpose(1, 0, 2)


def solution(mesh):
    return jax.shard_map(
        functools.partial(on_device, mesh.shape["space"]),
        mesh=mesh,
        in_specs=(
            P("modes", None, ("groups", "space"), None, None),
            P(("groups", "space"), None, None),
            P(),
            P("groups"),
        ),
        out_specs=P(("groups", "space"), None, "modes"),
        check_vma=False,
    )
```

```python
import functools

import jax
import jax.numpy as jnp
from jax import lax
from jax.experimental import pallas as pl
from jax.experimental.pallas import tpu as pltpu
from jax.sharding import PartitionSpec as P

JB = 4
NW = 16
PADROWS = 16
LOADS = 4
X_FIRST = 0b10011111
NEAR = 4
VMEM_LIMIT = 48 * 1024 * 1024
PREP_LIMIT = 53_600 * 1024


def x_first(s, planes):
    if planes != 8:
        return s >= 0
    return lax.rem(lax.shift_right_logical(X_FIRST, s), 2) == 1


def copy_rows(ref, tr, at):
    nx, comps, nk, _ = tr.shape
    for row in range(nx // 4):
        for c in range(comps):
            ref[pl.ds((row * comps + c) * nk, nk), :] = tr[at * (nx // 4) + row, c]


def prep_kernel(planes, modes_hbm, tr, first_ref, second_ref, modes_ref, sems):
    m = lax.axis_index("modes")
    s = lax.axis_index("space")
    q = lax.rem(s, 2)
    nk, comps, _, nx, nz = modes_hbm.shape
    step = nk // LOADS
    copies = [
        pltpu.make_async_copy(
            modes_hbm.at[pl.ds(p * step, step)], modes_ref.at[pl.ds(p * step, step)], sems.at[p]
        )
        for p in range(LOADS)
    ]
    for copy in copies:
        copy.start()
    for p in range(LOADS):
        copies[p].wait()
        block = pl.ds(p * step, step)
        for c in range(comps):
            value = modes_ref[block, c, 0].astype(jnp.float32)
            tr[:, c, block] = jnp.swapaxes(value, 0, 1).astype(jnp.bfloat16)
    body = nx // 4 * comps * nk
    to_x, to_z = 2 * m + 1 - q, 2 * m + q
    x_now = x_first(s, planes)
    for ref, at in (
        (first_ref, jnp.where(x_now, to_x, to_z)),
        (second_ref, jnp.where(x_now, to_z, to_x)),
    ):
        copy_rows(ref, tr, at)
        ref[pl.ds(body, PADROWS), :] = jnp.zeros((PADROWS, nz), jnp.bfloat16)


def weights_kernel(ids_ref, table_ref, tr, _, weight_ref, xc_ref, zc_ref):
    m = lax.axis_index("modes")
    q = lax.rem(lax.axis_index("space"), 2)
    nx, comps, nk, nz = tr.shape
    quarter = nx // 4
    table = table_ref[...]
    weight = jnp.zeros((nx, nz), jnp.float32)
    for entry in range(NW):
        weight = jnp.where(ids_ref[0] == entry, table[0:1, entry : entry + 1], weight)
    weight_ref[...] = weight
    for ref, at in ((xc_ref, 2 * (1 - m) + 1 - q), (zc_ref, 2 * (1 - m) + q)):
        copy_rows(ref, tr, at)
        rest = jnp.concatenate(
            [
                jnp.broadcast_to(weight_ref[pl.ds(at * quarter + row, 1), :], (8, nz))
                for row in range(quarter)
            ],
            axis=0,
        )
        piece_of = lax.rem(lax.broadcasted_iota(jnp.int32, rest.shape, 0), 8)
        pieces = jnp.zeros(rest.shape, jnp.float32)
        for piece in range(3):
            rounded = rest.astype(jnp.bfloat16).astype(jnp.float32)
            pieces = jnp.where(piece_of == piece, rounded, pieces)
            rest = rest - rounded
        ref[pl.ds(quarter * comps * nk, 8 * quarter), :] = pieces.astype(jnp.bfloat16)


def received_weights(ref, first, quarter):
    pieces = ref[pl.ds(first, 8 * quarter), :].astype(jnp.float32)
    return [
        pieces[8 * r : 8 * r + 1] + pieces[8 * r + 1 : 8 * r + 2] + pieces[8 * r + 2 : 8 * r + 3]
        for r in range(quarter)
    ]


def picks(jb_ref, m, nk):
    first = jb_ref[0] * JB
    owner = (first >= nk).astype(jnp.int32)
    row = first - owner * nk
    within = lax.rem(row, 16)
    return owner == m, pl.multiple_of(row - within, 16), within


def picked(pick, own, other):
    mine, block, within = pick
    rows = pl.ds(block, 16)
    rows = jnp.where(mine, own(rows).astype(jnp.float32), other(rows).astype(jnp.float32))
    result = rows[0:JB]
    for start in range(JB, 16, JB):
        result = jnp.where(within == start, rows[start : start + JB], result)
    return result


def spread(row):
    return jnp.broadcast_to(row, (16, row.shape[1])).astype(jnp.bfloat16)[None]


def scaled(tile, field):
    rows, lanes = field.shape
    return (tile * field.reshape(rows // 16, 16, lanes)).reshape(rows, lanes)


def dot_nt(a, b):
    return lax.dot_general(a, b, (((1,), (1,)), ((), ())), preferred_element_type=jnp.float32)


def local_kernel(own_ref, other_ref, weight_ref, jb_ref, acc_ref, w0_ref, adv, wts):
    m = lax.axis_index("modes")
    q = lax.rem(lax.axis_index("space"), 2)
    nx, comps, nk, nz = own_ref.shape
    rows = nx // 2
    pick = picks(jb_ref, m, nk)
    for r in range(rows):
        row = rows * m + r
        below, above = lax.rem(row + nx - 1, nx), lax.rem(row + 1, nx)
        phi = [picked(pick, lambda at: own_ref[row, d, at, :], lambda at: other_ref[row, d, at, :]) for d in range(comps)]
        weight = weight_ref[pl.ds(row, 1), :]
        for c in range(comps):
            for half, ref in enumerate((own_ref, other_ref)):
                block = pl.ds(half * nk, nk)
                here = ref[row, c].astype(jnp.float32)
                gx = 0.5 * (ref[above, c].astype(jnp.float32) - ref[below, c].astype(jnp.float32))
                gz = 0.5 * (pltpu.roll(here, nz - 1, 1) - pltpu.roll(here, 1, 1))
                gx = gx.astype(jnp.bfloat16).astype(jnp.float32)
                gz = gz.astype(jnp.bfloat16).astype(jnp.float32)
                wts[r, block, pl.ds(c * nz, nz)] = (weight * here).astype(jnp.bfloat16)
                for j in range(JB):
                    total = phi[0][j : j + 1] * gx + phi[2][j : j + 1] * gz
                    adv[r, pl.ds((2 * j + half) * nk, nk), pl.ds(c * nz, nz)] = total.astype(jnp.bfloat16)
    total = dot_nt(adv[0], wts[0])
    for r in range(1, rows):
        total = total + dot_nt(adv[r], wts[r])
    acc_ref[...] = total
    quarter = rows // 2
    for r in range(quarter):
        w0_ref[r] = wts[quarter * q + r]


def same_core_rows(planes, first_ref, second_ref):
    x_came = x_first(jnp.bitwise_xor(lax.axis_index("space"), 1), planes)
    return (
        lambda rows: jnp.where(x_came, first_ref[rows, :], second_ref[rows, :]),
        lambda rows: jnp.where(x_came, second_ref[rows, :], first_ref[rows, :]),
    )


def sign_of_plane():
    return jnp.where(lax.rem(lax.axis_index("space"), 2) == 0, 0.5, -0.5)


def early_kernel(
    planes, own_ref, other_ref, first_ref, second_ref, xc_ref, w0_ref, jb_ref, acc_ref, out_ref, w1_ref, adv
):
    xs_rows, _ = same_core_rows(planes, first_ref, second_ref)
    m = lax.axis_index("modes")
    q = lax.rem(lax.axis_index("space"), 2)
    nx, comps, nk, nz = own_ref.shape
    quarter = nx // 4
    pick = picks(jb_ref, m, nk)
    weights = received_weights(xc_ref, quarter * comps * nk, quarter)
    for r in range(quarter):
        row0 = quarter * (2 * m + q) + r
        phi0 = sign_of_plane() * picked(
            pick, lambda at: own_ref[row0, 1, at, :], lambda at: other_ref[row0, 1, at, :]
        )
        phi0 = [spread(phi0[j : j + 1]) for j in range(JB)]
        for c in range(comps):
            at = pl.ds((r * comps + c) * nz, nz)
            src = pl.ds((r * comps + c) * nk, nk)
            for half, f1 in enumerate((xs_rows(src), xc_ref[src, :])):
                w1_ref[pl.ds(half * nk, nk), at] = (weights[r] * f1.astype(jnp.float32)).astype(
                    jnp.bfloat16
                )
                for j in range(JB):
                    adv[r, pl.ds((2 * j + half) * nk, nk), pl.ds(c * nz, nz)] = scaled(phi0[j], f1)
    total = acc_ref[...]
    for r in range(quarter):
        total = total + dot_nt(adv[r], w0_ref[r])
    out_ref[...] = total


def cross_kernel(classes_of, chunk, planes, has_weighted, own_ref, other_ref, *refs):
    first_ref, second_ref, xc_ref, zc_ref, w1_ref, jb_ref, acc_ref, *refs = refs
    xs_rows, zs_rows = same_core_rows(planes, first_ref, second_ref)
    if has_weighted:
        wts, keep_ref, send_ref, adv = refs
    else:
        keep_ref, send_ref, wts, adv = refs
    m = lax.axis_index("modes")
    plane = lax.axis_index("space")
    q = lax.rem(plane, 2)
    inside = jnp.where(jnp.logical_or(plane == 1, plane == planes - 2), 0.0, 1.0)
    nx, comps, nk, nz = own_ref.shape
    quarter = nx // 4
    span = quarter * comps * nz
    pick = picks(jb_ref, m, nk)
    classes = [pl.multiple_of(chunk * cls, chunk) for cls in classes_of(plane)]
    if not has_weighted:
        weights = received_weights(zc_ref, quarter * comps * nk, quarter)
        wts[:, pl.ds(0, span)] = w1_ref[...]
        for r in range(quarter):
            weight = inside * weights[r]
            for c in range(comps):
                src = pl.ds((r * comps + c) * nk, nk)
                for half, f2 in enumerate((zs_rows(src), zc_ref[src, :])):
                    wts[pl.ds(half * nk, nk), pl.ds(span + (r * comps + c) * nz, nz)] = (
                        weight * f2.astype(jnp.float32)
                    ).astype(jnp.bfloat16)
    phis = []
    for r in range(quarter):
        along = (r * comps + 1) * nk

        def moved(at):
            return pl.ds(pl.multiple_of(along + at.start, 16), at.size)

        phi1 = sign_of_plane() * picked(
            pick, lambda at: xs_rows(moved(at)), lambda at: xc_ref[moved(at), :]
        )
        phi2 = -sign_of_plane() * picked(
            pick, lambda at: zs_rows(moved(at)), lambda at: zc_ref[moved(at), :]
        )
        phis.append([[spread(phi[j : j + 1]) for j in range(JB)] for phi in (phi1, phi2)])
    inside = inside.astype(jnp.bfloat16)
    for at, cls in enumerate(classes):
        for r in range(quarter):
            row0 = quarter * (2 * m + q) + r
            phi1, phi2 = phis[r]
            for c in range(comps):
                lane = (r * comps + c) * nz
                src = (r * comps + c) * nk
                rows_at = pl.ds(pl.multiple_of(src + cls, 16), chunk)
                for half, (p0, f1, f2) in enumerate(
                    (
                        (own_ref, xs_rows(rows_at), zs_rows(rows_at)),
                        (other_ref, xc_ref[rows_at, :], zc_ref[rows_at, :]),
                    )
                ):
                    f0 = p0[row0, c, pl.ds(cls, chunk), :]
                    gy = inside * f2 - f0
                    for j in range(JB):
                        here = pl.ds((half * JB + j) * chunk, chunk)
                        adv[at, here, pl.ds(lane, nz)] = scaled(phi1[j], gy)
                        adv[at, here, pl.ds(span + lane, nz)] = scaled(phi2[j], f1)
        total = dot_nt(adv[at], wts[...])
        for half in range(2):
            level = m if half == 0 else 1 - m
            for j in range(JB):
                first = (half * JB + j) * chunk
                piece = total[first : first + chunk] + acc_ref[pl.ds((2 * j + half) * nk + cls, chunk), :]
                keep_ref[at, level, j] = piece[:, :nk]
                row = pl.multiple_of(((2 * at + level) * JB + j) * chunk, chunk)
                send_ref[pl.ds(row, chunk), :] = piece[:, nk:].astype(jnp.bfloat16)


def near_kernel(keep_ref, got_ref, *out_refs):
    got = got_ref[...].astype(jnp.float32).reshape(keep_ref.shape)
    for at, ref in enumerate(out_refs):
        ref[...] = (keep_ref[at] + got[at]).astype(ref.dtype).reshape(ref.shape)


def far_kernel(mine_ref, *refs):
    *parts, keep_ref, send_ref = refs
    level = lax.div(lax.axis_index("space"), NEAR)
    rows = send_ref.shape[0]
    for ref, at in ((keep_ref, level), (send_ref, 1 - level)):
        total = mine_ref[at]
        for part in parts:
            piece = part[pl.ds(pl.multiple_of(at * rows, rows), rows), :]
            total = total + piece.astype(jnp.float32).reshape(total.shape)
        ref[...] = total.astype(ref.dtype).reshape(ref.shape)


def total_kernel(keep_ref, got_ref, out_ref):
    total = keep_ref[...] + got_ref[...].astype(jnp.float32).reshape(keep_ref.shape)
    for j in range(JB):
        out_ref[:, j, :] = total[j]


def on_device(n, modes, weight_ids, weight_table, j_block):
    nk, comps, _, nx, nz = modes.shape
    bf16, f32 = jnp.bfloat16, jnp.float32
    vmem = pl.BlockSpec(memory_space=pltpu.VMEM)
    smem = pl.BlockSpec(memory_space=pltpu.SMEM)
    params = pltpu.CompilerParams(vmem_limit_bytes=VMEM_LIMIT)
    quarter = nx // 4
    body = quarter * comps * nk
    own, first, second = pl.pallas_call(
        functools.partial(prep_kernel, n),
        out_shape=[jax.ShapeDtypeStruct((nx, comps, nk, nz), bf16)]
        + [jax.ShapeDtypeStruct((body + PADROWS, nz), bf16)] * 2,
        in_specs=[pl.BlockSpec(memory_space=pltpu.HBM)],
        out_specs=[vmem] * 3,
        scratch_shapes=[pltpu.VMEM(modes.shape, bf16), pltpu.SemaphoreType.DMA((LOADS,))],
        compiler_params=pltpu.CompilerParams(vmem_limit_bytes=PREP_LIMIT),
        cost_estimate=pl.CostEstimate(flops=1_500_000_000, bytes_accessed=2_800_000, transcendentals=0),
        name="prep",
    )(modes)

    both = ("space", "modes")
    x_to = lambda s: s ^ 1
    z_to = lambda s: s + 2 if s % 2 else s - 2
    x_now = [n != 8 or X_FIRST >> s & 1 for s in range(n)]
    firsts = [(s, x_to(s) if x_now[s] else z_to(s)) for s in range(n)]
    seconds = [(s, z_to(s) % n if x_now[s] else x_to(s)) for s in range(n)]
    same = lambda pairs: [(2 * a + m, 2 * b + m) for a, b in pairs for m in range(2)]
    cross = lambda pairs: [(2 * a + m, 2 * b + 1 - m) for a, b in pairs for m in range(2)]
    other = lax.ppermute(own, "modes", [(0, 1), (1, 0)])
    first = lax.ppermute(first, both, same(firsts))
    second = lax.ppermute(second, both, same(seconds))
    weight, xc, zc = pl.pallas_call(
        weights_kernel,
        out_shape=[jax.ShapeDtypeStruct((nx, nz), f32)]
        + [jax.ShapeDtypeStruct((body + 8 * quarter, nz), bf16)] * 2,
        in_specs=[vmem] * 3 + [pl.BlockSpec(memory_space=pl.ANY)],
        out_specs=[vmem] * 3,
        compiler_params=params,
        name="weights",
    )(weight_ids, jnp.broadcast_to(weight_table[None], (8, NW)), own, other)
    xc = lax.ppermute(xc, both, cross([(s, x_to(s)) for s in range(n)]))
    zc = lax.ppermute(zc, both, cross([(s, z_to(s) % n) for s in range(n)]))

    depth = nx // 4 * comps * nz
    depth = quarter * comps * nz
    acc, w0 = pl.pallas_call(
        local_kernel,
        out_shape=[
            jax.ShapeDtypeStruct((JB * 2 * nk, 2 * nk), f32),
            jax.ShapeDtypeStruct((quarter, 2 * nk, comps * nz), bf16),
        ],
        in_specs=[vmem, vmem, vmem, smem],
        out_specs=[vmem] * 2,
        scratch_shapes=[
            pltpu.VMEM((2 * quarter, JB * 2 * nk, comps * nz), bf16),
            pltpu.VMEM((2 * quarter, 2 * nk, comps * nz), bf16),
        ],
        compiler_params=params,
        cost_estimate=pl.CostEstimate(flops=900_000_000, bytes_accessed=2_400_000, transcendentals=0),
        name="local",
    )(own, other, weight, j_block)

    acc, w1 = pl.pallas_call(
        functools.partial(early_kernel, n),
        out_shape=[
            jax.ShapeDtypeStruct((JB * 2 * nk, 2 * nk), f32),
            jax.ShapeDtypeStruct((2 * nk, depth), bf16),
        ],
        in_specs=[vmem] * 6 + [smem, vmem],
        out_specs=[vmem] * 2,
        scratch_shapes=[pltpu.VMEM((quarter, JB * 2 * nk, comps * nz), bf16)],
        compiler_params=params,
        cost_estimate=pl.CostEstimate(flops=600_000_000, bytes_accessed=2_400_000, transcendentals=0),
        name="early",
    )(own, other, first, second, xc, w0, j_block, acc)

    per_target = 2 * nk // n
    chunk = max(16, per_target)

    def crossed(count, classes_of, weighted):
        piece = (count, 2, JB, chunk, nk)
        out_shape = [
            jax.ShapeDtypeStruct(piece, f32),
            jax.ShapeDtypeStruct((count * 2 * JB * chunk, nk), bf16),
        ]
        if not weighted:
            out_shape.append(jax.ShapeDtypeStruct((2 * nk, 2 * depth), bf16))
        return pl.pallas_call(
            functools.partial(cross_kernel, classes_of, chunk, n, bool(weighted)),
            out_shape=out_shape,
            in_specs=[vmem] * 7 + [smem] + [vmem] * (1 + len(weighted)),
            out_specs=[vmem] * len(out_shape),
            scratch_shapes=[pltpu.VMEM((count, 2 * JB * chunk, 2 * depth), bf16)],
            compiler_params=params,
            cost_estimate=pl.CostEstimate(
                flops=900_000_000, bytes_accessed=4_000_000, transcendentals=0
            ),
            name="cross",
        )(own, other, first, second, xc, zc, w1, j_block, acc, *weighted)

    swap = [(0, 1), (1, 0)]
    if n == 2 * NEAR:
        def partners(*steps):
            return lambda s: [jnp.bitwise_xor(lax.rem(s, NEAR), step) for step in steps]

        keep_a, send_a, w2 = crossed(2, partners(3, 1), ())
        got_a = lax.ppermute(send_a, "modes", swap)
        keep_b, send_b = crossed(2, partners(0, 2), (w2,))
        got_b = lax.ppermute(send_b, "modes", swap)
        piece = (JB, chunk, nk)

        def summed(out_shape, keep, got):
            return pl.pallas_call(
                near_kernel,
                out_shape=out_shape,
                in_specs=[vmem] * 2,
                out_specs=[vmem] * 2,
                compiler_params=params,
                name="near",
            )(keep, got)

        kept = jax.ShapeDtypeStruct((2, *piece), f32)
        sent = jax.ShapeDtypeStruct((2 * JB * chunk, nk), bf16)
        part_3, part_1 = summed([sent, sent], keep_a, got_a)
        mine, part_2 = summed([kept, sent], keep_b, got_b)
        parts = [
            lax.ppermute(part, "space", [(s, s ^ step) for s in range(n)])
            for part, step in ((part_3, 3), (part_1, 1), (part_2, 2))
        ]
        keep, send = pl.pallas_call(
            far_kernel,
            out_shape=[
                jax.ShapeDtypeStruct(piece, f32),
                jax.ShapeDtypeStruct((JB * chunk, nk), bf16),
            ],
            in_specs=[vmem] * NEAR,
            out_specs=[vmem] * 2,
            compiler_params=params,
            name="far",
        )(mine, *parts)
        got = lax.ppermute(send, "space", [(s, s ^ NEAR) for s in range(n)])
        return pl.pallas_call(
            total_kernel,
            out_shape=jax.ShapeDtypeStruct((chunk, JB, nk), f32),
            in_specs=[vmem] * 2,
            out_specs=vmem,
            compiler_params=params,
            name="total",
        )(keep, got)

    count = nk // chunk
    keep, send, _ = crossed(count, lambda s: list(range(count)), ())
    share = (keep + lax.ppermute(send, "modes", swap).reshape(keep.shape)).astype(bf16)
    share = share.reshape(count, 2, JB, chunk // per_target, per_target, nk)
    share = share.transpose(1, 0, 3, 2, 4, 5).reshape(n, JB, per_target, nk)
    parts = lax.all_to_all(share, "space", 0, 0, tiled=True)
    return jnp.sum(parts.astype(f32), axis=0).transpose(1, 0, 2)


def solution(mesh):
    return jax.shard_map(
        functools.partial(on_device, mesh.shape["space"]),
        mesh=mesh,
        in_specs=(
            P("modes", None, ("groups", "space"), None, None),
            P(("groups", "space"), None, None),
            P(),
            P("groups"),
        ),
        out_specs=P(("groups", "space"), None, "modes"),
        check_vma=False,
    )
```

```python
import functools

import jax
import jax.numpy as jnp
from jax import lax
from jax.experimental import pallas as pl
from jax.experimental.pallas import tpu as pltpu
from jax.sharding import PartitionSpec as P

JB = 4
NW = 16
PADROWS = 16
LOADS = 4
X_FIRST = 0b10011111
NEAR = 4
VMEM_LIMIT = 48 * 1024 * 1024
PREP_LIMIT = 53_600 * 1024


def x_first(s, planes):
    if planes != 8:
        return s >= 0
    return lax.rem(lax.shift_right_logical(X_FIRST, s), 2) == 1


def copy_rows(ref, tr, at):
    nx, comps, nk, _ = tr.shape
    for row in range(nx // 4):
        for c in range(comps):
            ref[pl.ds((row * comps + c) * nk, nk), :] = tr[at * (nx // 4) + row, c]


def prep_kernel(planes, modes_hbm, tr, first_ref, second_ref, modes_ref, sems):
    m = lax.axis_index("modes")
    s = lax.axis_index("space")
    q = lax.rem(s, 2)
    nk, comps, _, nx, nz = modes_hbm.shape
    step = nk // LOADS
    copies = [
        pltpu.make_async_copy(
            modes_hbm.at[pl.ds(p * step, step)], modes_ref.at[pl.ds(p * step, step)], sems.at[p]
        )
        for p in range(LOADS)
    ]
    for copy in copies:
        copy.start()
    for p in range(LOADS):
        copies[p].wait()
        block = pl.ds(p * step, step)
        for c in range(comps):
            value = modes_ref[block, c, 0].astype(jnp.float32)
            tr[:, c, block] = jnp.swapaxes(value, 0, 1).astype(jnp.bfloat16)
    body = nx // 4 * comps * nk
    to_x, to_z = 2 * m + 1 - q, 2 * m + q
    x_now = x_first(s, planes)
    for ref, at in (
        (first_ref, jnp.where(x_now, to_x, to_z)),
        (second_ref, jnp.where(x_now, to_z, to_x)),
    ):
        copy_rows(ref, tr, at)
        ref[pl.ds(body, 2 * PADROWS), :] = jnp.zeros((2 * PADROWS, nz), jnp.bfloat16)


def weights_kernel(ids_ref, table_ref, tr, _, weight_ref, zc_ref, xc_ref):
    m = lax.axis_index("modes")
    q = lax.rem(lax.axis_index("space"), 2)
    nx, comps, nk, nz = tr.shape
    quarter = nx // 4
    table = table_ref[...]
    weight = jnp.zeros((nx, nz), jnp.float32)
    for entry in range(NW):
        weight = jnp.where(ids_ref[0] == entry, table[0:1, entry : entry + 1], weight)
    weight_ref[...] = weight
    pad = quarter * comps * nk + 8 * quarter
    zc_ref[pl.ds(pad, PADROWS), :] = jnp.zeros((PADROWS, nz), jnp.bfloat16)
    for ref, at in ((xc_ref, 2 * (1 - m) + 1 - q), (zc_ref, 2 * (1 - m) + q)):
        copy_rows(ref, tr, at)
        rest = jnp.concatenate(
            [
                jnp.broadcast_to(weight_ref[pl.ds(at * quarter + row, 1), :], (8, nz))
                for row in range(quarter)
            ],
            axis=0,
        )
        piece_of = lax.rem(lax.broadcasted_iota(jnp.int32, rest.shape, 0), 8)
        pieces = jnp.zeros(rest.shape, jnp.float32)
        for piece in range(3):
            rounded = rest.astype(jnp.bfloat16).astype(jnp.float32)
            pieces = jnp.where(piece_of == piece, rounded, pieces)
            rest = rest - rounded
        ref[pl.ds(quarter * comps * nk, 8 * quarter), :] = pieces.astype(jnp.bfloat16)


def received_weights(ref, first, quarter):
    pieces = ref[pl.ds(first, 8 * quarter), :].astype(jnp.float32)
    return [
        pieces[8 * r : 8 * r + 1] + pieces[8 * r + 1 : 8 * r + 2] + pieces[8 * r + 2 : 8 * r + 3]
        for r in range(quarter)
    ]


def picks(jb_ref, m, nk):
    first = jb_ref[0] * JB
    owner = (first >= nk).astype(jnp.int32)
    row = first - owner * nk
    within = lax.rem(row, 16)
    return owner == m, pl.multiple_of(row - within, 16), within


def picked(pick, own, other):
    mine, block, within = pick
    rows = pl.ds(block, 16)
    rows = jnp.where(mine, own(rows).astype(jnp.float32), other(rows).astype(jnp.float32))
    result = rows[0:JB]
    for start in range(JB, 16, JB):
        result = jnp.where(within == start, rows[start : start + JB], result)
    return result


def spread(row):
    return jnp.broadcast_to(row, (16, row.shape[1])).astype(jnp.bfloat16)[None]


def scaled(tile, field):
    rows, lanes = field.shape
    return (tile * field.reshape(rows // 16, 16, lanes)).reshape(rows, lanes)


def dot_nt(a, b):
    return lax.dot_general(a, b, (((1,), (1,)), ((), ())), preferred_element_type=jnp.float32)


def local_kernel(own_ref, other_ref, weight_ref, jb_ref, acc_ref, w0_ref, adv, wts):
    m = lax.axis_index("modes")
    q = lax.rem(lax.axis_index("space"), 2)
    nx, comps, nk, nz = own_ref.shape
    rows = nx // 2
    pick = picks(jb_ref, m, nk)
    for r in range(rows):
        row = rows * m + r
        below, above = lax.rem(row + nx - 1, nx), lax.rem(row + 1, nx)
        phi = [picked(pick, lambda at: own_ref[row, d, at, :], lambda at: other_ref[row, d, at, :]) for d in range(comps)]
        weight = weight_ref[pl.ds(row, 1), :]
        for c in range(comps):
            for half, ref in enumerate((own_ref, other_ref)):
                block = pl.ds(half * nk, nk)
                here = ref[row, c].astype(jnp.float32)
                gx = 0.5 * (ref[above, c].astype(jnp.float32) - ref[below, c].astype(jnp.float32))
                gz = 0.5 * (pltpu.roll(here, nz - 1, 1) - pltpu.roll(here, 1, 1))
                gx = gx.astype(jnp.bfloat16).astype(jnp.float32)
                gz = gz.astype(jnp.bfloat16).astype(jnp.float32)
                wts[r, block, pl.ds(c * nz, nz)] = (weight * here).astype(jnp.bfloat16)
                for j in range(JB):
                    total = phi[0][j : j + 1] * gx + phi[2][j : j + 1] * gz
                    adv[r, pl.ds((2 * j + half) * nk, nk), pl.ds(c * nz, nz)] = total.astype(jnp.bfloat16)
    total = dot_nt(adv[0], wts[0])
    for r in range(1, rows):
        total = total + dot_nt(adv[r], wts[r])
    acc_ref[...] = total
    quarter = rows // 2
    for r in range(quarter):
        w0_ref[r] = wts[quarter * q + r]


def same_core_rows(planes, first_ref, second_ref):
    x_came = x_first(jnp.bitwise_xor(lax.axis_index("space"), 1), planes)
    return (
        lambda rows: jnp.where(x_came, first_ref[rows, :], second_ref[rows, :]),
        lambda rows: jnp.where(x_came, second_ref[rows, :], first_ref[rows, :]),
    )


def sign_of_plane():
    return jnp.where(lax.rem(lax.axis_index("space"), 2) == 0, 0.5, -0.5)


def early_kernel(
    planes, own_ref, other_ref, first_ref, second_ref, xc_ref, w0_ref, jb_ref, acc_ref, out_ref, w1_ref, adv
):
    xs_rows, _ = same_core_rows(planes, first_ref, second_ref)
    m = lax.axis_index("modes")
    q = lax.rem(lax.axis_index("space"), 2)
    nx, comps, nk, nz = own_ref.shape
    quarter = nx // 4
    pick = picks(jb_ref, m, nk)
    weights = received_weights(xc_ref, quarter * comps * nk, quarter)
    for r in range(quarter):
        row0 = quarter * (2 * m + q) + r
        phi0 = sign_of_plane() * picked(
            pick, lambda at: own_ref[row0, 1, at, :], lambda at: other_ref[row0, 1, at, :]
        )
        phi0 = [spread(phi0[j : j + 1]) for j in range(JB)]
        for c in range(comps):
            at = pl.ds((r * comps + c) * nz, nz)
            src = pl.ds((r * comps + c) * nk, nk)
            for half, f1 in enumerate((xs_rows(src), xc_ref[src, :])):
                w1_ref[pl.ds(half * nk, nk), at] = (weights[r] * f1.astype(jnp.float32)).astype(
                    jnp.bfloat16
                )
                for j in range(JB):
                    adv[r, pl.ds((2 * j + half) * nk, nk), pl.ds(c * nz, nz)] = scaled(phi0[j], f1)
    total = acc_ref[...]
    for r in range(quarter):
        total = total + dot_nt(adv[r], w0_ref[r])
    out_ref[...] = total


def cross_kernel(classes_of, chunk, planes, has_weighted, own_ref, other_ref, *refs):
    first_ref, second_ref, xc_ref, zc_ref, w1_ref, jb_ref, acc_ref, *refs = refs
    xs_rows, zs_rows = same_core_rows(planes, first_ref, second_ref)
    if has_weighted:
        wts, keep_ref, send_ref, adv = refs
    else:
        keep_ref, send_ref, wts, adv = refs
    m = lax.axis_index("modes")
    plane = lax.axis_index("space")
    q = lax.rem(plane, 2)
    inside = jnp.where(jnp.logical_or(plane == 1, plane == planes - 2), 0.0, 1.0)
    nx, comps, nk, nz = own_ref.shape
    quarter = nx // 4
    span = quarter * comps * nz
    pick = picks(jb_ref, m, nk)
    classes = [pl.multiple_of(chunk * cls, chunk) for cls in classes_of(plane)]
    if not has_weighted:
        weights = received_weights(zc_ref, quarter * comps * nk, quarter)
        wts[:, pl.ds(0, span)] = w1_ref[...]
        for r in range(quarter):
            weight = inside * weights[r]
            for c in range(comps):
                src = pl.ds((r * comps + c) * nk, nk)
                for half, f2 in enumerate((zs_rows(src), zc_ref[src, :])):
                    wts[pl.ds(half * nk, nk), pl.ds(span + (r * comps + c) * nz, nz)] = (
                        weight * f2.astype(jnp.float32)
                    ).astype(jnp.bfloat16)
    phis = []
    for r in range(quarter):
        along = (r * comps + 1) * nk

        def moved(at):
            return pl.ds(pl.multiple_of(along + at.start, 16), at.size)

        phi1 = sign_of_plane() * picked(
            pick, lambda at: xs_rows(moved(at)), lambda at: xc_ref[moved(at), :]
        )
        phi2 = -sign_of_plane() * picked(
            pick, lambda at: zs_rows(moved(at)), lambda at: zc_ref[moved(at), :]
        )
        phis.append([[spread(phi[j : j + 1]) for j in range(JB)] for phi in (phi1, phi2)])
    inside = inside.astype(jnp.bfloat16)
    for at, cls in enumerate(classes):
        for r in range(quarter):
            row0 = quarter * (2 * m + q) + r
            phi1, phi2 = phis[r]
            for c in range(comps):
                lane = (r * comps + c) * nz
                src = (r * comps + c) * nk
                rows_at = pl.ds(pl.multiple_of(src + cls, 16), chunk)
                for half, (p0, f1, f2) in enumerate(
                    (
                        (own_ref, xs_rows(rows_at), zs_rows(rows_at)),
                        (other_ref, xc_ref[rows_at, :], zc_ref[rows_at, :]),
                    )
                ):
                    f0 = p0[row0, c, pl.ds(cls, chunk), :]
                    gy = inside * f2 - f0
                    for j in range(JB):
                        here = pl.ds((half * JB + j) * chunk, chunk)
                        adv[at, here, pl.ds(lane, nz)] = scaled(phi1[j], gy)
                        adv[at, here, pl.ds(span + lane, nz)] = scaled(phi2[j], f1)
        total = dot_nt(adv[at], wts[...])
        for half in range(2):
            level = m if half == 0 else 1 - m
            for j in range(JB):
                first = (half * JB + j) * chunk
                piece = total[first : first + chunk] + acc_ref[pl.ds((2 * j + half) * nk + cls, chunk), :]
                keep_ref[at, level, j] = piece[:, :nk]
                row = pl.multiple_of(((2 * at + level) * JB + j) * chunk, chunk)
                send_ref[pl.ds(row, chunk), :] = piece[:, nk:].astype(jnp.bfloat16)


def near_kernel(keep_ref, got_ref, *out_refs):
    got = got_ref[...].astype(jnp.float32).reshape(keep_ref.shape)
    for at, ref in enumerate(out_refs):
        ref[...] = (keep_ref[at] + got[at]).astype(ref.dtype).reshape(ref.shape)


def far_kernel(mine_ref, *refs):
    *parts, keep_ref, send_ref = refs
    level = lax.div(lax.axis_index("space"), NEAR)
    rows = send_ref.shape[0]
    for ref, at in ((keep_ref, level), (send_ref, 1 - level)):
        total = mine_ref[at]
        for part in parts:
            piece = part[pl.ds(pl.multiple_of(at * rows, rows), rows), :]
            total = total + piece.astype(jnp.float32).reshape(total.shape)
        ref[...] = total.astype(ref.dtype).reshape(ref.shape)


def total_kernel(keep_ref, got_ref, out_ref):
    total = keep_ref[...] + got_ref[...].astype(jnp.float32).reshape(keep_ref.shape)
    for j in range(JB):
        out_ref[:, j, :] = total[j]


def on_device(n, modes, weight_ids, weight_table, j_block):
    nk, comps, _, nx, nz = modes.shape
    bf16, f32 = jnp.bfloat16, jnp.float32
    vmem = pl.BlockSpec(memory_space=pltpu.VMEM)
    smem = pl.BlockSpec(memory_space=pltpu.SMEM)
    params = pltpu.CompilerParams(vmem_limit_bytes=VMEM_LIMIT)
    quarter = nx // 4
    body = quarter * comps * nk
    own, first, second = pl.pallas_call(
        functools.partial(prep_kernel, n),
        out_shape=[jax.ShapeDtypeStruct((nx, comps, nk, nz), bf16)]
        + [jax.ShapeDtypeStruct((body + 2 * PADROWS, nz), bf16)] * 2,
        in_specs=[pl.BlockSpec(memory_space=pltpu.HBM)],
        out_specs=[vmem] * 3,
        scratch_shapes=[pltpu.VMEM(modes.shape, bf16), pltpu.SemaphoreType.DMA((LOADS,))],
        compiler_params=pltpu.CompilerParams(vmem_limit_bytes=PREP_LIMIT),
        cost_estimate=pl.CostEstimate(flops=1_500_000_000, bytes_accessed=2_800_000, transcendentals=0),
        name="prep",
    )(modes)

    both = ("space", "modes")
    x_to = lambda s: s ^ 1
    z_to = lambda s: s + 2 if s % 2 else s - 2
    x_now = [n != 8 or X_FIRST >> s & 1 for s in range(n)]
    firsts = [(s, x_to(s) if x_now[s] else z_to(s)) for s in range(n)]
    seconds = [(s, z_to(s) % n if x_now[s] else x_to(s)) for s in range(n)]
    same = lambda pairs: [(2 * a + m, 2 * b + m) for a, b in pairs for m in range(2)]
    cross = lambda pairs: [(2 * a + m, 2 * b + 1 - m) for a, b in pairs for m in range(2)]
    other = lax.ppermute(own, "modes", [(0, 1), (1, 0)])
    first = lax.ppermute(first, both, same(firsts))
    second = lax.ppermute(second, both, same(seconds))
    weight, zc, xc = pl.pallas_call(
        weights_kernel,
        out_shape=[jax.ShapeDtypeStruct((nx, nz), f32)]
        + [
            jax.ShapeDtypeStruct((body + 8 * quarter + PADROWS, nz), bf16),
            jax.ShapeDtypeStruct((body + 8 * quarter, nz), bf16),
        ],
        in_specs=[vmem] * 3 + [pl.BlockSpec(memory_space=pl.ANY)],
        out_specs=[vmem] * 3,
        compiler_params=params,
        name="weights",
    )(weight_ids, jnp.broadcast_to(weight_table[None], (8, NW)), own, other)
    xc = lax.ppermute(xc, both, cross([(s, x_to(s)) for s in range(n)]))
    zc = lax.ppermute(zc, both, cross([(s, z_to(s)) for s in range(n) if 0 <= z_to(s) < n]))

    depth = nx // 4 * comps * nz
    depth = quarter * comps * nz
    acc, w0 = pl.pallas_call(
        local_kernel,
        out_shape=[
            jax.ShapeDtypeStruct((JB * 2 * nk, 2 * nk), f32),
            jax.ShapeDtypeStruct((quarter, 2 * nk, comps * nz), bf16),
        ],
        in_specs=[vmem, vmem, vmem, smem],
        out_specs=[vmem] * 2,
        scratch_shapes=[
            pltpu.VMEM((2 * quarter, JB * 2 * nk, comps * nz), bf16),
            pltpu.VMEM((2 * quarter, 2 * nk, comps * nz), bf16),
        ],
        compiler_params=params,
        cost_estimate=pl.CostEstimate(flops=900_000_000, bytes_accessed=2_400_000, transcendentals=0),
        name="local",
    )(own, other, weight, j_block)

    acc, w1 = pl.pallas_call(
        functools.partial(early_kernel, n),
        out_shape=[
            jax.ShapeDtypeStruct((JB * 2 * nk, 2 * nk), f32),
            jax.ShapeDtypeStruct((2 * nk, depth), bf16),
        ],
        in_specs=[vmem] * 6 + [smem, vmem],
        out_specs=[vmem] * 2,
        scratch_shapes=[pltpu.VMEM((quarter, JB * 2 * nk, comps * nz), bf16)],
        compiler_params=params,
        cost_estimate=pl.CostEstimate(flops=1_000_000, bytes_accessed=10_000, transcendentals=0),
        name="early",
    )(own, other, first, second, xc, w0, j_block, acc)

    per_target = 2 * nk // n
    chunk = max(16, per_target)

    def crossed(count, classes_of, weighted):
        piece = (count, 2, JB, chunk, nk)
        out_shape = [
            jax.ShapeDtypeStruct(piece, f32),
            jax.ShapeDtypeStruct((count * 2 * JB * chunk, nk), bf16),
        ]
        if not weighted:
            out_shape.append(jax.ShapeDtypeStruct((2 * nk, 2 * depth), bf16))
        return pl.pallas_call(
            functools.partial(cross_kernel, classes_of, chunk, n, bool(weighted)),
            out_shape=out_shape,
            in_specs=[vmem] * 7 + [smem] + [vmem] * (1 + len(weighted)),
            out_specs=[vmem] * len(out_shape),
            scratch_shapes=[pltpu.VMEM((count, 2 * JB * chunk, 2 * depth), bf16)],
            compiler_params=params,
            cost_estimate=pl.CostEstimate(
                flops=900_000_000, bytes_accessed=4_000_000, transcendentals=0
            ),
            name="cross",
        )(own, other, first, second, xc, zc, w1, j_block, acc, *weighted)

    swap = [(0, 1), (1, 0)]
    if n == 2 * NEAR:
        def partners(*steps):
            return lambda s: [jnp.bitwise_xor(lax.rem(s, NEAR), step) for step in steps]

        keep_a, send_a, w2 = crossed(2, partners(3, 1), ())
        got_a = lax.ppermute(send_a, "modes", swap)
        keep_b, send_b = crossed(2, partners(0, 2), (w2,))
        got_b = lax.ppermute(send_b, "modes", swap)
        piece = (JB, chunk, nk)

        def summed(out_shape, keep, got):
            return pl.pallas_call(
                near_kernel,
                out_shape=out_shape,
                in_specs=[vmem] * 2,
                out_specs=[vmem] * 2,
                compiler_params=params,
                name="near",
            )(keep, got)

        kept = jax.ShapeDtypeStruct((2, *piece), f32)
        sent = jax.ShapeDtypeStruct((2 * JB * chunk, nk), bf16)
        part_3, part_1 = summed([sent, sent], keep_a, got_a)
        mine, part_2 = summed([kept, sent], keep_b, got_b)
        parts = [
            lax.ppermute(part, "space", [(s, s ^ step) for s in range(n)])
            for part, step in ((part_3, 3), (part_1, 1), (part_2, 2))
        ]
        keep, send = pl.pallas_call(
            far_kernel,
            out_shape=[
                jax.ShapeDtypeStruct(piece, f32),
                jax.ShapeDtypeStruct((JB * chunk, nk), bf16),
            ],
            in_specs=[vmem] * NEAR,
            out_specs=[vmem] * 2,
            compiler_params=params,
            name="far",
        )(mine, *parts)
        got = lax.ppermute(send, "space", [(s, s ^ NEAR) for s in range(n)])
        return pl.pallas_call(
            total_kernel,
            out_shape=jax.ShapeDtypeStruct((chunk, JB, nk), f32),
            in_specs=[vmem] * 2,
            out_specs=vmem,
            compiler_params=params,
            name="total",
        )(keep, got)

    count = nk // chunk
    keep, send, _ = crossed(count, lambda s: list(range(count)), ())
    share = (keep + lax.ppermute(send, "modes", swap).reshape(keep.shape)).astype(bf16)
    share = share.reshape(count, 2, JB, chunk // per_target, per_target, nk)
    share = share.transpose(1, 0, 3, 2, 4, 5).reshape(n, JB, per_target, nk)
    parts = lax.all_to_all(share, "space", 0, 0, tiled=True)
    return jnp.sum(parts.astype(f32), axis=0).transpose(1, 0, 2)


def solution(mesh):
    return jax.shard_map(
        functools.partial(on_device, mesh.shape["space"]),
        mesh=mesh,
        in_specs=(
            P("modes", None, ("groups", "space"), None, None),
            P(("groups", "space"), None, None),
            P(),
            P("groups"),
        ),
        out_specs=P(("groups", "space"), None, "modes"),
        check_vma=False,
    )
```

```python
import functools

import jax
import jax.numpy as jnp
from jax import lax
from jax.experimental import pallas as pl
from jax.experimental.pallas import tpu as pltpu
from jax.sharding import PartitionSpec as P

JB = 4
NW = 16
PADROWS = 16
LOADS = 4
X_FIRST = 0b10011111
NEAR = 4
VMEM_LIMIT = 48 * 1024 * 1024
PREP_LIMIT = 53_600 * 1024


def x_first(s, planes):
    if planes != 8:
        return s >= 0
    return lax.rem(lax.shift_right_logical(X_FIRST, s), 2) == 1


def copy_rows(ref, tr, at):
    nx, comps, nk, _ = tr.shape
    for row in range(nx // 4):
        for c in range(comps):
            ref[pl.ds((row * comps + c) * nk, nk), :] = tr[at * (nx // 4) + row, c]


def prep_kernel(planes, modes_hbm, tr, first_ref, second_ref, modes_ref, sems):
    m = lax.axis_index("modes")
    s = lax.axis_index("space")
    q = lax.rem(s, 2)
    nk, comps, _, nx, nz = modes_hbm.shape
    step = nk // LOADS
    copies = [
        pltpu.make_async_copy(
            modes_hbm.at[pl.ds(p * step, step)], modes_ref.at[pl.ds(p * step, step)], sems.at[p]
        )
        for p in range(LOADS)
    ]
    for copy in copies:
        copy.start()
    for p in range(LOADS):
        copies[p].wait()
        block = pl.ds(p * step, step)
        for c in range(comps):
            value = modes_ref[block, c, 0].astype(jnp.float32)
            tr[:, c, block] = jnp.swapaxes(value, 0, 1).astype(jnp.bfloat16)
    body = nx // 4 * comps * nk
    to_x, to_z = 2 * m + 1 - q, 2 * m + q
    x_now = x_first(s, planes)
    for ref, at in (
        (first_ref, jnp.where(x_now, to_x, to_z)),
        (second_ref, jnp.where(x_now, to_z, to_x)),
    ):
        copy_rows(ref, tr, at)
        ref[pl.ds(body, PADROWS), :] = jnp.zeros((PADROWS, nz), jnp.bfloat16)


def weights_kernel(ids_ref, table_ref, tr, _, weight_ref, xc_ref, zc_ref):
    m = lax.axis_index("modes")
    q = lax.rem(lax.axis_index("space"), 2)
    nx, comps, nk, nz = tr.shape
    quarter = nx // 4
    table = table_ref[...]
    weight = jnp.zeros((nx, nz), jnp.float32)
    for entry in range(NW):
        weight = jnp.where(ids_ref[0] == entry, table[0:1, entry : entry + 1], weight)
    weight_ref[...] = weight
    for ref, at in ((xc_ref, 2 * (1 - m) + 1 - q), (zc_ref, 2 * (1 - m) + q)):
        copy_rows(ref, tr, at)
        rest = jnp.concatenate(
            [
                jnp.broadcast_to(weight_ref[pl.ds(at * quarter + row, 1), :], (8, nz))
                for row in range(quarter)
            ],
            axis=0,
        )
        piece_of = lax.rem(lax.broadcasted_iota(jnp.int32, rest.shape, 0), 8)
        pieces = jnp.zeros(rest.shape, jnp.float32)
        for piece in range(3):
            rounded = rest.astype(jnp.bfloat16).astype(jnp.float32)
            pieces = jnp.where(piece_of == piece, rounded, pieces)
            rest = rest - rounded
        ref[pl.ds(quarter * comps * nk, 8 * quarter), :] = pieces.astype(jnp.bfloat16)


def received_weights(ref, first, quarter):
    pieces = ref[pl.ds(first, 8 * quarter), :].astype(jnp.float32)
    return [
        pieces[8 * r : 8 * r + 1] + pieces[8 * r + 1 : 8 * r + 2] + pieces[8 * r + 2 : 8 * r + 3]
        for r in range(quarter)
    ]


def picks(jb_ref, m, nk):
    first = jb_ref[0] * JB
    owner = (first >= nk).astype(jnp.int32)
    row = first - owner * nk
    within = lax.rem(row, 16)
    return owner == m, pl.multiple_of(row - within, 16), within


def picked(pick, own, other):
    mine, block, within = pick
    rows = pl.ds(block, 16)
    rows = jnp.where(mine, own(rows).astype(jnp.float32), other(rows).astype(jnp.float32))
    result = rows[0:JB]
    for start in range(JB, 16, JB):
        result = jnp.where(within == start, rows[start : start + JB], result)
    return result


def spread(row):
    return jnp.broadcast_to(row, (16, row.shape[1])).astype(jnp.bfloat16)[None]


def scaled(tile, field):
    rows, lanes = field.shape
    return (tile * field.reshape(rows // 16, 16, lanes)).reshape(rows, lanes)


def dot_nt(a, b):
    return lax.dot_general(a, b, (((1,), (1,)), ((), ())), preferred_element_type=jnp.float32)


def local_kernel(own_ref, other_ref, weight_ref, jb_ref, acc_ref, w0_ref, adv, wts):
    m = lax.axis_index("modes")
    q = lax.rem(lax.axis_index("space"), 2)
    nx, comps, nk, nz = own_ref.shape
    rows = nx // 2
    pick = picks(jb_ref, m, nk)
    for r in range(rows):
        row = rows * m + r
        below, above = lax.rem(row + nx - 1, nx), lax.rem(row + 1, nx)
        phi = [picked(pick, lambda at: own_ref[row, d, at, :], lambda at: other_ref[row, d, at, :]) for d in range(comps)]
        weight = weight_ref[pl.ds(row, 1), :]
        for c in range(comps):
            for half, ref in enumerate((own_ref, other_ref)):
                block = pl.ds(half * nk, nk)
                here = ref[row, c].astype(jnp.float32)
                gx = 0.5 * (ref[above, c].astype(jnp.float32) - ref[below, c].astype(jnp.float32))
                gz = 0.5 * (pltpu.roll(here, nz - 1, 1) - pltpu.roll(here, 1, 1))
                gx = gx.astype(jnp.bfloat16).astype(jnp.float32)
                gz = gz.astype(jnp.bfloat16).astype(jnp.float32)
                wts[r, block, pl.ds(c * nz, nz)] = (weight * here).astype(jnp.bfloat16)
                for j in range(JB):
                    total = phi[0][j : j + 1] * gx + phi[2][j : j + 1] * gz
                    adv[r, pl.ds((2 * j + half) * nk, nk), pl.ds(c * nz, nz)] = total.astype(jnp.bfloat16)
    total = dot_nt(adv[0], wts[0])
    for r in range(1, rows):
        total = total + dot_nt(adv[r], wts[r])
    acc_ref[...] = total
    quarter = rows // 2
    for r in range(quarter):
        w0_ref[r] = wts[quarter * q + r]


def same_core_rows(planes, first_ref, second_ref):
    x_came = x_first(jnp.bitwise_xor(lax.axis_index("space"), 1), planes)
    return (
        lambda rows: jnp.where(x_came, first_ref[rows, :], second_ref[rows, :]),
        lambda rows: jnp.where(x_came, second_ref[rows, :], first_ref[rows, :]),
    )


def sign_of_plane():
    return jnp.where(lax.rem(lax.axis_index("space"), 2) == 0, 0.5, -0.5)


def early_kernel(
    planes, own_ref, other_ref, first_ref, second_ref, xc_ref, w0_ref, jb_ref, acc_ref, out_ref, w1_ref, adv
):
    xs_rows, _ = same_core_rows(planes, first_ref, second_ref)
    m = lax.axis_index("modes")
    q = lax.rem(lax.axis_index("space"), 2)
    nx, comps, nk, nz = own_ref.shape
    quarter = nx // 4
    pick = picks(jb_ref, m, nk)
    weights = received_weights(xc_ref, quarter * comps * nk, quarter)
    for r in range(quarter):
        row0 = quarter * (2 * m + q) + r
        phi0 = sign_of_plane() * picked(
            pick, lambda at: own_ref[row0, 1, at, :], lambda at: other_ref[row0, 1, at, :]
        )
        phi0 = [spread(phi0[j : j + 1]) for j in range(JB)]
        for c in range(comps):
            at = pl.ds((r * comps + c) * nz, nz)
            src = pl.ds((r * comps + c) * nk, nk)
            for half, f1 in enumerate((xs_rows(src), xc_ref[src, :])):
                w1_ref[pl.ds(half * nk, nk), at] = (weights[r] * f1.astype(jnp.float32)).astype(
                    jnp.bfloat16
                )
                for j in range(JB):
                    adv[r, pl.ds((2 * j + half) * nk, nk), pl.ds(c * nz, nz)] = scaled(phi0[j], f1)
    total = acc_ref[...]
    for r in range(quarter):
        total = total + dot_nt(adv[r], w0_ref[r])
    out_ref[...] = total


def cross_kernel(classes_of, chunk, planes, has_weighted, own_ref, other_ref, *refs):
    first_ref, second_ref, xc_ref, zc_ref, w1_ref, jb_ref, acc_ref, *refs = refs
    xs_rows, zs_rows = same_core_rows(planes, first_ref, second_ref)
    if has_weighted:
        wts, keep_ref, send_ref, adv = refs
    else:
        keep_ref, send_ref, wts, adv = refs
    m = lax.axis_index("modes")
    plane = lax.axis_index("space")
    q = lax.rem(plane, 2)
    inside = jnp.where(jnp.logical_or(plane == 1, plane == planes - 2), 0.0, 1.0)
    nx, comps, nk, nz = own_ref.shape
    quarter = nx // 4
    span = quarter * comps * nz
    pick = picks(jb_ref, m, nk)
    classes = [pl.multiple_of(chunk * cls, chunk) for cls in classes_of(plane)]
    if not has_weighted:
        weights = received_weights(zc_ref, quarter * comps * nk, quarter)
        wts[:, pl.ds(0, span)] = w1_ref[...]
        for r in range(quarter):
            weight = inside * weights[r]
            for c in range(comps):
                src = pl.ds((r * comps + c) * nk, nk)
                for half, f2 in enumerate((zs_rows(src), zc_ref[src, :])):
                    wts[pl.ds(half * nk, nk), pl.ds(span + (r * comps + c) * nz, nz)] = (
                        weight * f2.astype(jnp.float32)
                    ).astype(jnp.bfloat16)
    phis = []
    for r in range(quarter):
        along = (r * comps + 1) * nk

        def moved(at):
            return pl.ds(pl.multiple_of(along + at.start, 16), at.size)

        phi1 = sign_of_plane() * picked(
            pick, lambda at: xs_rows(moved(at)), lambda at: xc_ref[moved(at), :]
        )
        phi2 = -sign_of_plane() * picked(
            pick, lambda at: zs_rows(moved(at)), lambda at: zc_ref[moved(at), :]
        )
        phis.append([[spread(phi[j : j + 1]) for j in range(JB)] for phi in (phi1, phi2)])
    inside = inside.astype(jnp.bfloat16)
    for at, cls in enumerate(classes):
        for r in range(quarter):
            row0 = quarter * (2 * m + q) + r
            phi1, phi2 = phis[r]
            for c in range(comps):
                lane = (r * comps + c) * nz
                src = (r * comps + c) * nk
                rows_at = pl.ds(pl.multiple_of(src + cls, 16), chunk)
                for half, (p0, f1, f2) in enumerate(
                    (
                        (own_ref, xs_rows(rows_at), zs_rows(rows_at)),
                        (other_ref, xc_ref[rows_at, :], zc_ref[rows_at, :]),
                    )
                ):
                    f0 = p0[row0, c, pl.ds(cls, chunk), :]
                    gy = inside * f2 - f0
                    for j in range(JB):
                        here = pl.ds((half * JB + j) * chunk, chunk)
                        adv[at, here, pl.ds(lane, nz)] = scaled(phi1[j], gy)
                        adv[at, here, pl.ds(span + lane, nz)] = scaled(phi2[j], f1)
        total = dot_nt(adv[at], wts[...])
        for half in range(2):
            level = m if half == 0 else 1 - m
            for j in range(JB):
                first = (half * JB + j) * chunk
                piece = total[first : first + chunk] + acc_ref[pl.ds((2 * j + half) * nk + cls, chunk), :]
                keep_ref[at, level, j] = piece[:, :nk]
                row = pl.multiple_of(((2 * at + level) * JB + j) * chunk, chunk)
                send_ref[pl.ds(row, chunk), :] = piece[:, nk:].astype(jnp.bfloat16)


def near_kernel(by_level, keep_ref, got_ref, *out_refs):
    got = got_ref[...].astype(jnp.float32).reshape(keep_ref.shape)
    totals = [keep_ref[at] + got[at] for at in range(2)]
    lower = lax.div(lax.axis_index("space"), NEAR) == 0
    for at, ref in enumerate(out_refs):
        total = jnp.where(lower, totals[at], totals[1 - at]) if by_level else totals[at]
        ref[...] = total.astype(ref.dtype).reshape(ref.shape)


def far_kernel(mine_ref, *refs):
    *parts, keep_ref, send_ref = refs
    level = lax.div(lax.axis_index("space"), NEAR)
    rows = send_ref.shape[0]
    for ref, at in ((keep_ref, level), (send_ref, 1 - level)):
        total = mine_ref[at]
        for part in parts:
            piece = part[pl.ds(pl.multiple_of(at * rows, rows), rows), :]
            total = total + piece.astype(jnp.float32).reshape(total.shape)
        ref[...] = total.astype(ref.dtype).reshape(ref.shape)


def total_kernel(keep_ref, got_ref, out_ref):
    total = keep_ref[...] + got_ref[...].astype(jnp.float32).reshape(keep_ref.shape)
    for j in range(JB):
        out_ref[:, j, :] = total[j]


def on_device(n, modes, weight_ids, weight_table, j_block):
    nk, comps, _, nx, nz = modes.shape
    bf16, f32 = jnp.bfloat16, jnp.float32
    vmem = pl.BlockSpec(memory_space=pltpu.VMEM)
    smem = pl.BlockSpec(memory_space=pltpu.SMEM)
    params = pltpu.CompilerParams(vmem_limit_bytes=VMEM_LIMIT)
    quarter = nx // 4
    body = quarter * comps * nk
    own, first, second = pl.pallas_call(
        functools.partial(prep_kernel, n),
        out_shape=[jax.ShapeDtypeStruct((nx, comps, nk, nz), bf16)]
        + [jax.ShapeDtypeStruct((body + PADROWS, nz), bf16)] * 2,
        in_specs=[pl.BlockSpec(memory_space=pltpu.HBM)],
        out_specs=[vmem] * 3,
        scratch_shapes=[pltpu.VMEM(modes.shape, bf16), pltpu.SemaphoreType.DMA((LOADS,))],
        compiler_params=pltpu.CompilerParams(vmem_limit_bytes=PREP_LIMIT),
        cost_estimate=pl.CostEstimate(flops=1_500_000_000, bytes_accessed=2_800_000, transcendentals=0),
        name="prep",
    )(modes)

    both = ("space", "modes")
    x_to = lambda s: s ^ 1
    z_to = lambda s: s + 2 if s % 2 else s - 2
    x_now = [n != 8 or X_FIRST >> s & 1 for s in range(n)]
    firsts = [(s, x_to(s) if x_now[s] else z_to(s)) for s in range(n)]
    seconds = [(s, z_to(s) % n if x_now[s] else x_to(s)) for s in range(n)]
    same = lambda pairs: [(2 * a + m, 2 * b + m) for a, b in pairs for m in range(2)]
    cross = lambda pairs: [(2 * a + m, 2 * b + 1 - m) for a, b in pairs for m in range(2)]
    other = lax.ppermute(own, "modes", [(0, 1), (1, 0)])
    first = lax.ppermute(first, both, same(firsts))
    second = lax.ppermute(second, both, same(seconds))
    weight, xc, zc = pl.pallas_call(
        weights_kernel,
        out_shape=[jax.ShapeDtypeStruct((nx, nz), f32)]
        + [jax.ShapeDtypeStruct((body + 8 * quarter, nz), bf16)] * 2,
        in_specs=[vmem] * 3 + [pl.BlockSpec(memory_space=pl.ANY)],
        out_specs=[vmem] * 3,
        compiler_params=params,
        name="weights",
    )(weight_ids, jnp.broadcast_to(weight_table[None], (8, NW)), own, other)
    xc = lax.ppermute(xc, both, cross([(s, x_to(s)) for s in range(n)]))
    zc = lax.ppermute(zc, both, cross([(s, z_to(s) % n) for s in range(n)]))

    depth = nx // 4 * comps * nz
    depth = quarter * comps * nz
    acc, w0 = pl.pallas_call(
        local_kernel,
        out_shape=[
            jax.ShapeDtypeStruct((JB * 2 * nk, 2 * nk), f32),
            jax.ShapeDtypeStruct((quarter, 2 * nk, comps * nz), bf16),
        ],
        in_specs=[vmem, vmem, vmem, smem],
        out_specs=[vmem] * 2,
        scratch_shapes=[
            pltpu.VMEM((2 * quarter, JB * 2 * nk, comps * nz), bf16),
            pltpu.VMEM((2 * quarter, 2 * nk, comps * nz), bf16),
        ],
        compiler_params=params,
        cost_estimate=pl.CostEstimate(flops=900_000_000, bytes_accessed=2_400_000, transcendentals=0),
        name="local",
    )(own, other, weight, j_block)

    acc, w1 = pl.pallas_call(
        functools.partial(early_kernel, n),
        out_shape=[
            jax.ShapeDtypeStruct((JB * 2 * nk, 2 * nk), f32),
            jax.ShapeDtypeStruct((2 * nk, depth), bf16),
        ],
        in_specs=[vmem] * 6 + [smem, vmem],
        out_specs=[vmem] * 2,
        scratch_shapes=[pltpu.VMEM((quarter, JB * 2 * nk, comps * nz), bf16)],
        compiler_params=params,
        cost_estimate=pl.CostEstimate(flops=600_000_000, bytes_accessed=2_400_000, transcendentals=0),
        name="early",
    )(own, other, first, second, xc, w0, j_block, acc)

    per_target = 2 * nk // n
    chunk = max(16, per_target)

    def crossed(count, classes_of, weighted):
        piece = (count, 2, JB, chunk, nk)
        out_shape = [
            jax.ShapeDtypeStruct(piece, f32),
            jax.ShapeDtypeStruct((count * 2 * JB * chunk, nk), bf16),
        ]
        if not weighted:
            out_shape.append(jax.ShapeDtypeStruct((2 * nk, 2 * depth), bf16))
        return pl.pallas_call(
            functools.partial(cross_kernel, classes_of, chunk, n, bool(weighted)),
            out_shape=out_shape,
            in_specs=[vmem] * 7 + [smem] + [vmem] * (1 + len(weighted)),
            out_specs=[vmem] * len(out_shape),
            scratch_shapes=[pltpu.VMEM((count, 2 * JB * chunk, 2 * depth), bf16)],
            compiler_params=params,
            cost_estimate=pl.CostEstimate(
                flops=900_000_000, bytes_accessed=4_000_000, transcendentals=0
            ),
            name="cross",
        )(own, other, first, second, xc, zc, w1, j_block, acc, *weighted)

    swap = [(0, 1), (1, 0)]
    if n == 2 * NEAR:
        def partners(*steps):
            return lambda s: [jnp.bitwise_xor(lax.rem(s, NEAR), step) for step in steps]

        keep_a, send_a, w2 = crossed(2, partners(3, 1), ())
        got_a = lax.ppermute(send_a, "modes", swap)
        keep_b, send_b = crossed(2, partners(0, 2), (w2,))
        got_b = lax.ppermute(send_b, "modes", swap)
        piece = (JB, chunk, nk)

        def summed(by_level, out_shape, keep, got):
            return pl.pallas_call(
                functools.partial(near_kernel, by_level),
                out_shape=out_shape,
                in_specs=[vmem] * 2,
                out_specs=[vmem] * 2,
                compiler_params=params,
                name="near",
            )(keep, got)

        kept = jax.ShapeDtypeStruct((2, *piece), f32)
        sent = jax.ShapeDtypeStruct((2 * JB * chunk, nk), bf16)
        out_0, out_1 = summed(True, [sent, sent], keep_a, got_a)
        mine, out_2 = summed(False, [kept, sent], keep_b, got_b)
        parts = [
            lax.ppermute(out, "space", [(s, s ^ steps[s // NEAR]) for s in range(n)])
            for out, steps in ((out_0, (3, 1)), (out_1, (1, 3)), (out_2, (2, 2)))
        ]
        keep, send = pl.pallas_call(
            far_kernel,
            out_shape=[
                jax.ShapeDtypeStruct(piece, f32),
                jax.ShapeDtypeStruct((JB * chunk, nk), bf16),
            ],
            in_specs=[vmem] * NEAR,
            out_specs=[vmem] * 2,
            compiler_params=params,
            name="far",
        )(mine, *parts)
        got = lax.ppermute(send, "space", [(s, s ^ NEAR) for s in range(n)])
        return pl.pallas_call(
            total_kernel,
            out_shape=jax.ShapeDtypeStruct((chunk, JB, nk), f32),
            in_specs=[vmem] * 2,
            out_specs=vmem,
            compiler_params=params,
            name="total",
        )(keep, got)

    count = nk // chunk
    keep, send, _ = crossed(count, lambda s: list(range(count)), ())
    share = (keep + lax.ppermute(send, "modes", swap).reshape(keep.shape)).astype(bf16)
    share = share.reshape(count, 2, JB, chunk // per_target, per_target, nk)
    share = share.transpose(1, 0, 3, 2, 4, 5).reshape(n, JB, per_target, nk)
    parts = lax.all_to_all(share, "space", 0, 0, tiled=True)
    return jnp.sum(parts.astype(f32), axis=0).transpose(1, 0, 2)


def solution(mesh):
    return jax.shard_map(
        functools.partial(on_device, mesh.shape["space"]),
        mesh=mesh,
        in_specs=(
            P("modes", None, ("groups", "space"), None, None),
            P(("groups", "space"), None, None),
            P(),
            P("groups"),
        ),
        out_specs=P(("groups", "space"), None, "modes"),
        check_vma=False,
    )
```

```python
import functools

import jax
import jax.numpy as jnp
from jax import lax
from jax.experimental import pallas as pl
from jax.experimental.pallas import tpu as pltpu
from jax.sharding import PartitionSpec as P

JB = 4
NW = 16
PADROWS = 16
LOADS = 4
X_FIRST = 0b10011111
NEAR = 4
VMEM_LIMIT = 48 * 1024 * 1024
PREP_LIMIT = 53_600 * 1024


def x_first(s, planes):
    if planes != 8:
        return s >= 0
    return lax.rem(lax.shift_right_logical(X_FIRST, s), 2) == 1


def copy_rows(ref, tr, at):
    nx, comps, nk, _ = tr.shape
    for row in range(nx // 4):
        for c in range(comps):
            ref[pl.ds((row * comps + c) * nk, nk), :] = tr[at * (nx // 4) + row, c]


def prep_kernel(planes, modes_hbm, tr, first_ref, second_ref, modes_ref, sems):
    m = lax.axis_index("modes")
    s = lax.axis_index("space")
    q = lax.rem(s, 2)
    nk, comps, _, nx, nz = modes_hbm.shape
    step = nk // LOADS
    copies = [
        pltpu.make_async_copy(
            modes_hbm.at[pl.ds(p * step, step)], modes_ref.at[pl.ds(p * step, step)], sems.at[p]
        )
        for p in range(LOADS)
    ]
    for copy in copies:
        copy.start()
    for p in range(LOADS):
        copies[p].wait()
        block = pl.ds(p * step, step)
        for c in range(comps):
            value = modes_ref[block, c, 0].astype(jnp.float32)
            tr[:, c, block] = jnp.swapaxes(value, 0, 1).astype(jnp.bfloat16)
    body = nx // 4 * comps * nk
    to_x, to_z = 2 * m + 1 - q, 2 * m + q
    x_now = x_first(s, planes)
    for ref, at in (
        (first_ref, jnp.where(x_now, to_x, to_z)),
        (second_ref, jnp.where(x_now, to_z, to_x)),
    ):
        copy_rows(ref, tr, at)
        ref[pl.ds(body, PADROWS), :] = jnp.zeros((PADROWS, nz), jnp.bfloat16)


def weights_kernel(ids_ref, table_ref, tr, _, weight_ref, xc_ref, zc_ref):
    m = lax.axis_index("modes")
    q = lax.rem(lax.axis_index("space"), 2)
    nx, comps, nk, nz = tr.shape
    quarter = nx // 4
    table = table_ref[...]
    weight = jnp.zeros((nx, nz), jnp.float32)
    for entry in range(NW):
        weight = jnp.where(ids_ref[0] == entry, table[0:1, entry : entry + 1], weight)
    weight_ref[...] = weight
    for ref, at in ((xc_ref, 2 * (1 - m) + 1 - q), (zc_ref, 2 * (1 - m) + q)):
        copy_rows(ref, tr, at)
        rest = jnp.concatenate(
            [
                jnp.broadcast_to(weight_ref[pl.ds(at * quarter + row, 1), :], (8, nz))
                for row in range(quarter)
            ],
            axis=0,
        )
        piece_of = lax.rem(lax.broadcasted_iota(jnp.int32, rest.shape, 0), 8)
        pieces = jnp.zeros(rest.shape, jnp.float32)
        for piece in range(3):
            rounded = rest.astype(jnp.bfloat16).astype(jnp.float32)
            pieces = jnp.where(piece_of == piece, rounded, pieces)
            rest = rest - rounded
        ref[pl.ds(quarter * comps * nk, 8 * quarter), :] = pieces.astype(jnp.bfloat16)


def received_weights(ref, first, quarter):
    pieces = ref[pl.ds(first, 8 * quarter), :].astype(jnp.float32)
    return [
        pieces[8 * r : 8 * r + 1] + pieces[8 * r + 1 : 8 * r + 2] + pieces[8 * r + 2 : 8 * r + 3]
        for r in range(quarter)
    ]


def picks(jb_ref, m, nk):
    first = jb_ref[0] * JB
    owner = (first >= nk).astype(jnp.int32)
    row = first - owner * nk
    within = lax.rem(row, 16)
    return owner == m, pl.multiple_of(row - within, 16), within


def picked(pick, own, other):
    mine, block, within = pick
    rows = pl.ds(block, 16)
    rows = jnp.where(mine, own(rows).astype(jnp.float32), other(rows).astype(jnp.float32))
    result = rows[0:JB]
    for start in range(JB, 16, JB):
        result = jnp.where(within == start, rows[start : start + JB], result)
    return result


def spread(row):
    return jnp.broadcast_to(row, (16, row.shape[1])).astype(jnp.bfloat16)[None]


def scaled(tile, field):
    rows, lanes = field.shape
    return (tile * field.reshape(rows // 16, 16, lanes)).reshape(rows, lanes)


def dot_nt(a, b):
    return lax.dot_general(a, b, (((1,), (1,)), ((), ())), preferred_element_type=jnp.float32)


def local_kernel(own_ref, other_ref, weight_ref, jb_ref, acc_ref, w0_ref, adv, wts):
    m = lax.axis_index("modes")
    q = lax.rem(lax.axis_index("space"), 2)
    nx, comps, nk, nz = own_ref.shape
    rows = nx // 2
    pick = picks(jb_ref, m, nk)
    for r in range(rows):
        row = rows * m + r
        below, above = lax.rem(row + nx - 1, nx), lax.rem(row + 1, nx)
        phi = [picked(pick, lambda at: own_ref[row, d, at, :], lambda at: other_ref[row, d, at, :]) for d in range(comps)]
        weight = weight_ref[pl.ds(row, 1), :]
        for c in range(comps):
            for half, ref in enumerate((own_ref, other_ref)):
                block = pl.ds(half * nk, nk)
                here = ref[row, c].astype(jnp.float32)
                gx = 0.5 * (ref[above, c].astype(jnp.float32) - ref[below, c].astype(jnp.float32))
                gz = 0.5 * (pltpu.roll(here, nz - 1, 1) - pltpu.roll(here, 1, 1))
                gx = gx.astype(jnp.bfloat16).astype(jnp.float32)
                gz = gz.astype(jnp.bfloat16).astype(jnp.float32)
                wts[r, block, pl.ds(c * nz, nz)] = (weight * here).astype(jnp.bfloat16)
                for j in range(JB):
                    total = phi[0][j : j + 1] * gx + phi[2][j : j + 1] * gz
                    adv[r, pl.ds((2 * j + half) * nk, nk), pl.ds(c * nz, nz)] = total.astype(jnp.bfloat16)
    total = dot_nt(adv[0], wts[0])
    for r in range(1, rows):
        total = total + dot_nt(adv[r], wts[r])
    acc_ref[...] = total
    quarter = rows // 2
    for r in range(quarter):
        w0_ref[r] = wts[quarter * q + r]


def same_core_rows(planes, first_ref, second_ref):
    x_came = x_first(jnp.bitwise_xor(lax.axis_index("space"), 1), planes)
    return (
        lambda rows: jnp.where(x_came, first_ref[rows, :], second_ref[rows, :]),
        lambda rows: jnp.where(x_came, second_ref[rows, :], first_ref[rows, :]),
    )


def sign_of_plane():
    return jnp.where(lax.rem(lax.axis_index("space"), 2) == 0, 0.5, -0.5)


def early_kernel(
    planes, own_ref, other_ref, first_ref, second_ref, xc_ref, w0_ref, jb_ref, acc_ref, out_ref, w1_ref, adv
):
    xs_rows, _ = same_core_rows(planes, first_ref, second_ref)
    m = lax.axis_index("modes")
    q = lax.rem(lax.axis_index("space"), 2)
    nx, comps, nk, nz = own_ref.shape
    quarter = nx // 4
    pick = picks(jb_ref, m, nk)
    weights = received_weights(xc_ref, quarter * comps * nk, quarter)
    for r in range(quarter):
        row0 = quarter * (2 * m + q) + r
        phi0 = sign_of_plane() * picked(
            pick, lambda at: own_ref[row0, 1, at, :], lambda at: other_ref[row0, 1, at, :]
        )
        phi0 = [spread(phi0[j : j + 1]) for j in range(JB)]
        for c in range(comps):
            at = pl.ds((r * comps + c) * nz, nz)
            src = pl.ds((r * comps + c) * nk, nk)
            for half, f1 in enumerate((xs_rows(src), xc_ref[src, :])):
                w1_ref[pl.ds(half * nk, nk), at] = (weights[r] * f1.astype(jnp.float32)).astype(
                    jnp.bfloat16
                )
                for j in range(JB):
                    adv[r, pl.ds((2 * j + half) * nk, nk), pl.ds(c * nz, nz)] = scaled(phi0[j], f1)
    total = acc_ref[...]
    for r in range(quarter):
        total = total + dot_nt(adv[r], w0_ref[r])
    out_ref[...] = total


def cross_kernel(classes_of, chunk, planes, has_weighted, own_ref, other_ref, *refs):
    first_ref, second_ref, xc_ref, zc_ref, w1_ref, jb_ref, acc_ref, *refs = refs
    xs_rows, zs_rows = same_core_rows(planes, first_ref, second_ref)
    if has_weighted:
        wts, keep_ref, send_ref, adv = refs
    else:
        keep_ref, send_ref, wts, adv = refs
    m = lax.axis_index("modes")
    plane = lax.axis_index("space")
    q = lax.rem(plane, 2)
    inside = jnp.where(jnp.logical_or(plane == 1, plane == planes - 2), 0.0, 1.0)
    nx, comps, nk, nz = own_ref.shape
    quarter = nx // 4
    span = quarter * comps * nz
    pick = picks(jb_ref, m, nk)
    classes = [pl.multiple_of(chunk * cls, chunk) for cls in classes_of(plane)]
    if not has_weighted:
        weights = received_weights(zc_ref, quarter * comps * nk, quarter)
        wts[:, pl.ds(0, span)] = w1_ref[...]
        for r in range(quarter):
            weight = inside * weights[r]
            for c in range(comps):
                src = pl.ds((r * comps + c) * nk, nk)
                for half, f2 in enumerate((zs_rows(src), zc_ref[src, :])):
                    wts[pl.ds(half * nk, nk), pl.ds(span + (r * comps + c) * nz, nz)] = (
                        weight * f2.astype(jnp.float32)
                    ).astype(jnp.bfloat16)
    phis = []
    for r in range(quarter):
        along = (r * comps + 1) * nk

        def moved(at):
            return pl.ds(pl.multiple_of(along + at.start, 16), at.size)

        phi1 = sign_of_plane() * picked(
            pick, lambda at: xs_rows(moved(at)), lambda at: xc_ref[moved(at), :]
        )
        phi2 = -sign_of_plane() * picked(
            pick, lambda at: zs_rows(moved(at)), lambda at: zc_ref[moved(at), :]
        )
        phis.append([[spread(phi[j : j + 1]) for j in range(JB)] for phi in (phi1, phi2)])
    inside = inside.astype(jnp.bfloat16)
    for at, cls in enumerate(classes):
        for r in range(quarter):
            row0 = quarter * (2 * m + q) + r
            phi1, phi2 = phis[r]
            for c in range(comps):
                lane = (r * comps + c) * nz
                src = (r * comps + c) * nk
                rows_at = pl.ds(pl.multiple_of(src + cls, 16), chunk)
                for half, (p0, f1, f2) in enumerate(
                    (
                        (own_ref, xs_rows(rows_at), zs_rows(rows_at)),
                        (other_ref, xc_ref[rows_at, :], zc_ref[rows_at, :]),
                    )
                ):
                    f0 = p0[row0, c, pl.ds(cls, chunk), :]
                    gy = inside * f2 - f0
                    for j in range(JB):
                        here = pl.ds((half * JB + j) * chunk, chunk)
                        adv[at, here, pl.ds(lane, nz)] = scaled(phi1[j], gy)
                        adv[at, here, pl.ds(span + lane, nz)] = scaled(phi2[j], f1)
        total = dot_nt(adv[at], wts[...])
        for half in range(2):
            level = m if half == 0 else 1 - m
            for j in range(JB):
                first = (half * JB + j) * chunk
                piece = total[first : first + chunk] + acc_ref[pl.ds((2 * j + half) * nk + cls, chunk), :]
                keep_ref[at, level, j] = piece[:, :nk]
                row = pl.multiple_of(((2 * at + level) * JB + j) * chunk, chunk)
                send_ref[pl.ds(row, chunk), :] = piece[:, nk:].astype(jnp.bfloat16)


def near_kernel(keep_ref, got_ref, *out_refs):
    got = got_ref[...].astype(jnp.float32).reshape(keep_ref.shape)
    for at, ref in enumerate(out_refs):
        ref[...] = (keep_ref[at] + got[at]).astype(ref.dtype).reshape(ref.shape)


def far_kernel(mine_ref, *refs):
    *parts, keep_ref, send_ref = refs
    level = lax.div(lax.axis_index("space"), NEAR)
    rows = send_ref.shape[0]
    for ref, at in ((keep_ref, level), (send_ref, 1 - level)):
        total = mine_ref[at]
        for part in parts:
            piece = part[pl.ds(pl.multiple_of(at * rows, rows), rows), :]
            total = total + piece.astype(jnp.float32).reshape(total.shape)
        ref[...] = total.astype(ref.dtype).reshape(ref.shape)


def total_kernel(keep_ref, got_ref, out_ref):
    total = keep_ref[...] + got_ref[...].astype(jnp.float32).reshape(keep_ref.shape)
    for j in range(JB):
        out_ref[:, j, :] = total[j]


def on_device(n, modes, weight_ids, weight_table, j_block):
    nk, comps, _, nx, nz = modes.shape
    bf16, f32 = jnp.bfloat16, jnp.float32
    vmem = pl.BlockSpec(memory_space=pltpu.VMEM)
    smem = pl.BlockSpec(memory_space=pltpu.SMEM)
    params = pltpu.CompilerParams(vmem_limit_bytes=VMEM_LIMIT)
    quarter = nx // 4
    body = quarter * comps * nk
    own, first, second = pl.pallas_call(
        functools.partial(prep_kernel, n),
        out_shape=[jax.ShapeDtypeStruct((nx, comps, nk, nz), bf16)]
        + [jax.ShapeDtypeStruct((body + PADROWS, nz), bf16)] * 2,
        in_specs=[pl.BlockSpec(memory_space=pltpu.HBM)],
        out_specs=[vmem] * 3,
        scratch_shapes=[pltpu.VMEM(modes.shape, bf16), pltpu.SemaphoreType.DMA((LOADS,))],
        compiler_params=pltpu.CompilerParams(vmem_limit_bytes=PREP_LIMIT),
        cost_estimate=pl.CostEstimate(flops=1_500_000_000, bytes_accessed=2_800_000, transcendentals=0),
        name="prep",
    )(modes)

    both = ("space", "modes")
    x_to = lambda s: s ^ 1
    z_to = lambda s: s + 2 if s % 2 else s - 2
    x_now = [n != 8 or X_FIRST >> s & 1 for s in range(n)]
    firsts = [(s, x_to(s) if x_now[s] else z_to(s)) for s in range(n)]
    seconds = [(s, z_to(s) % n if x_now[s] else x_to(s)) for s in range(n)]
    same = lambda pairs: [(2 * a + m, 2 * b + m) for a, b in pairs for m in range(2)]
    cross = lambda pairs: [(2 * a + m, 2 * b + 1 - m) for a, b in pairs for m in range(2)]
    other = lax.ppermute(own, "modes", [(0, 1), (1, 0)])
    first = lax.ppermute(first, both, same(firsts))
    second = lax.ppermute(second, both, same(seconds))
    weight, xc, zc = pl.pallas_call(
        weights_kernel,
        out_shape=[jax.ShapeDtypeStruct((nx, nz), f32)]
        + [jax.ShapeDtypeStruct((body + 8 * quarter, nz), bf16)] * 2,
        in_specs=[vmem] * 3 + [pl.BlockSpec(memory_space=pl.ANY)],
        out_specs=[vmem] * 3,
        compiler_params=params,
        name="weights",
    )(weight_ids, jnp.broadcast_to(weight_table[None], (8, NW)), own, other)
    xc = lax.ppermute(xc, both, cross([(s, x_to(s)) for s in range(n)]))
    zc = lax.ppermute(zc, both, cross([(s, z_to(s) % n) for s in range(n)]))

    depth = nx // 4 * comps * nz
    depth = quarter * comps * nz
    acc, w0 = pl.pallas_call(
        local_kernel,
        out_shape=[
            jax.ShapeDtypeStruct((JB * 2 * nk, 2 * nk), f32),
            jax.ShapeDtypeStruct((quarter, 2 * nk, comps * nz), bf16),
        ],
        in_specs=[vmem, vmem, vmem, smem],
        out_specs=[vmem] * 2,
        scratch_shapes=[
            pltpu.VMEM((2 * quarter, JB * 2 * nk, comps * nz), bf16),
            pltpu.VMEM((2 * quarter, 2 * nk, comps * nz), bf16),
        ],
        compiler_params=params,
        cost_estimate=pl.CostEstimate(flops=900_000_000, bytes_accessed=2_400_000, transcendentals=0),
        name="local",
    )(own, other, weight, j_block)

    acc, w1 = pl.pallas_call(
        functools.partial(early_kernel, n),
        out_shape=[
            jax.ShapeDtypeStruct((JB * 2 * nk, 2 * nk), f32),
            jax.ShapeDtypeStruct((2 * nk, depth), bf16),
        ],
        in_specs=[vmem] * 6 + [smem, vmem],
        out_specs=[vmem] * 2,
        scratch_shapes=[pltpu.VMEM((quarter, JB * 2 * nk, comps * nz), bf16)],
        compiler_params=params,
        cost_estimate=pl.CostEstimate(flops=600_000_000, bytes_accessed=2_400_000, transcendentals=0),
        name="early",
    )(own, other, first, second, xc, w0, j_block, acc)

    per_target = 2 * nk // n
    chunk = max(16, per_target)

    def crossed(count, classes_of, weighted):
        piece = (count, 2, JB, chunk, nk)
        out_shape = [
            jax.ShapeDtypeStruct(piece, f32),
            jax.ShapeDtypeStruct((count * 2 * JB * chunk, nk), bf16),
        ]
        if not weighted:
            out_shape.append(jax.ShapeDtypeStruct((2 * nk, 2 * depth), bf16))
        return pl.pallas_call(
            functools.partial(cross_kernel, classes_of, chunk, n, bool(weighted)),
            out_shape=out_shape,
            in_specs=[vmem] * 7 + [smem] + [vmem] * (1 + len(weighted)),
            out_specs=[vmem] * len(out_shape),
            scratch_shapes=[pltpu.VMEM((count, 2 * JB * chunk, 2 * depth), bf16)],
            compiler_params=params,
            cost_estimate=pl.CostEstimate(
                flops=900_000_000, bytes_accessed=4_000_000, transcendentals=0
            ),
            name="cross",
        )(own, other, first, second, xc, zc, w1, j_block, acc, *weighted)

    swap = [(0, 1), (1, 0)]
    if n == 2 * NEAR:
        def partners(*steps):
            return lambda s: [
                jnp.bitwise_xor(lax.rem(s, NEAR), jnp.where(s < NEAR, low, high)) for low, high in steps
            ]

        keep_a, send_a, w2 = crossed(2, partners((3, 1), (1, 2)), ())
        got_a = lax.ppermute(send_a, "modes", swap)
        keep_b, send_b = crossed(2, partners((0, 0), (2, 3)), (w2,))
        got_b = lax.ppermute(send_b, "modes", swap)
        piece = (JB, chunk, nk)

        def summed(out_shape, keep, got):
            return pl.pallas_call(
                near_kernel,
                out_shape=out_shape,
                in_specs=[vmem] * 2,
                out_specs=[vmem] * 2,
                compiler_params=params,
                name="near",
            )(keep, got)

        kept = jax.ShapeDtypeStruct((2, *piece), f32)
        sent = jax.ShapeDtypeStruct((2 * JB * chunk, nk), bf16)
        out_0, out_1 = summed([sent, sent], keep_a, got_a)
        mine, out_2 = summed([kept, sent], keep_b, got_b)
        parts = [
            lax.ppermute(out, "space", [(s, s ^ steps[s // NEAR]) for s in range(n)])
            for out, steps in ((out_0, (3, 1)), (out_1, (1, 2)), (out_2, (2, 3)))
        ]
        keep, send = pl.pallas_call(
            far_kernel,
            out_shape=[
                jax.ShapeDtypeStruct(piece, f32),
                jax.ShapeDtypeStruct((JB * chunk, nk), bf16),
            ],
            in_specs=[vmem] * NEAR,
            out_specs=[vmem] * 2,
            compiler_params=params,
            name="far",
        )(mine, *parts)
        got = lax.ppermute(send, "space", [(s, s ^ NEAR) for s in range(n)])
        return pl.pallas_call(
            total_kernel,
            out_shape=jax.ShapeDtypeStruct((chunk, JB, nk), f32),
            in_specs=[vmem] * 2,
            out_specs=vmem,
            compiler_params=params,
            name="total",
        )(keep, got)

    count = nk // chunk
    keep, send, _ = crossed(count, lambda s: list(range(count)), ())
    share = (keep + lax.ppermute(send, "modes", swap).reshape(keep.shape)).astype(bf16)
    share = share.reshape(count, 2, JB, chunk // per_target, per_target, nk)
    share = share.transpose(1, 0, 3, 2, 4, 5).reshape(n, JB, per_target, nk)
    parts = lax.all_to_all(share, "space", 0, 0, tiled=True)
    return jnp.sum(parts.astype(f32), axis=0).transpose(1, 0, 2)


def solution(mesh):
    return jax.shard_map(
        functools.partial(on_device, mesh.shape["space"]),
        mesh=mesh,
        in_specs=(
            P("modes", None, ("groups", "space"), None, None),
            P(("groups", "space"), None, None),
            P(),
            P("groups"),
        ),
        out_specs=P(("groups", "space"), None, "modes"),
        check_vma=False,
    )
```

```python
import functools

import jax
import jax.numpy as jnp
from jax import lax
from jax.experimental import pallas as pl
from jax.experimental.pallas import tpu as pltpu
from jax.sharding import PartitionSpec as P

JB = 4
NW = 16
PADROWS = 16
LOADS = 8
X_FIRST = 0b10011111
NEAR = 4
VMEM_LIMIT = 48 * 1024 * 1024
PREP_LIMIT = 53_600 * 1024


def x_first(s, planes):
    if planes != 8:
        return s >= 0
    return lax.rem(lax.shift_right_logical(X_FIRST, s), 2) == 1


def copy_rows(ref, tr, at):
    nx, comps, nk, _ = tr.shape
    for row in range(nx // 4):
        for c in range(comps):
            ref[pl.ds((row * comps + c) * nk, nk), :] = tr[at * (nx // 4) + row, c]


def prep_kernel(planes, modes_hbm, tr, first_ref, second_ref, modes_ref, sems):
    m = lax.axis_index("modes")
    s = lax.axis_index("space")
    q = lax.rem(s, 2)
    nk, comps, _, nx, nz = modes_hbm.shape
    step = nk // LOADS
    copies = [
        pltpu.make_async_copy(
            modes_hbm.at[pl.ds(p * step, step)], modes_ref.at[pl.ds(p * step, step)], sems.at[p]
        )
        for p in range(LOADS)
    ]
    for copy in copies:
        copy.start()
    for p in range(LOADS):
        copies[p].wait()
        block = pl.ds(p * step, step)
        for c in range(comps):
            value = modes_ref[block, c, 0].astype(jnp.float32)
            tr[:, c, block] = jnp.swapaxes(value, 0, 1).astype(jnp.bfloat16)
    body = nx // 4 * comps * nk
    to_x, to_z = 2 * m + 1 - q, 2 * m + q
    x_now = x_first(s, planes)
    for ref, at in (
        (first_ref, jnp.where(x_now, to_x, to_z)),
        (second_ref, jnp.where(x_now, to_z, to_x)),
    ):
        copy_rows(ref, tr, at)
        ref[pl.ds(body, PADROWS), :] = jnp.zeros((PADROWS, nz), jnp.bfloat16)


def weights_kernel(ids_ref, table_ref, tr, _, weight_ref, xc_ref, zc_ref):
    m = lax.axis_index("modes")
    q = lax.rem(lax.axis_index("space"), 2)
    nx, comps, nk, nz = tr.shape
    quarter = nx // 4
    table = table_ref[...]
    weight = jnp.zeros((nx, nz), jnp.float32)
    for entry in range(NW):
        weight = jnp.where(ids_ref[0] == entry, table[0:1, entry : entry + 1], weight)
    weight_ref[...] = weight
    for ref, at in ((xc_ref, 2 * (1 - m) + 1 - q), (zc_ref, 2 * (1 - m) + q)):
        copy_rows(ref, tr, at)
        rest = jnp.concatenate(
            [
                jnp.broadcast_to(weight_ref[pl.ds(at * quarter + row, 1), :], (8, nz))
                for row in range(quarter)
            ],
            axis=0,
        )
        piece_of = lax.rem(lax.broadcasted_iota(jnp.int32, rest.shape, 0), 8)
        pieces = jnp.zeros(rest.shape, jnp.float32)
        for piece in range(3):
            rounded = rest.astype(jnp.bfloat16).astype(jnp.float32)
            pieces = jnp.where(piece_of == piece, rounded, pieces)
            rest = rest - rounded
        ref[pl.ds(quarter * comps * nk, 8 * quarter), :] = pieces.astype(jnp.bfloat16)


def received_weights(ref, first, quarter):
    pieces = ref[pl.ds(first, 8 * quarter), :].astype(jnp.float32)
    return [
        pieces[8 * r : 8 * r + 1] + pieces[8 * r + 1 : 8 * r + 2] + pieces[8 * r + 2 : 8 * r + 3]
        for r in range(quarter)
    ]


def picks(jb_ref, m, nk):
    first = jb_ref[0] * JB
    owner = (first >= nk).astype(jnp.int32)
    row = first - owner * nk
    within = lax.rem(row, 16)
    return owner == m, pl.multiple_of(row - within, 16), within


def picked(pick, own, other):
    mine, block, within = pick
    rows = pl.ds(block, 16)
    rows = jnp.where(mine, own(rows).astype(jnp.float32), other(rows).astype(jnp.float32))
    result = rows[0:JB]
    for start in range(JB, 16, JB):
        result = jnp.where(within == start, rows[start : start + JB], result)
    return result


def spread(row):
    return jnp.broadcast_to(row, (16, row.shape[1])).astype(jnp.bfloat16)[None]


def scaled(tile, field):
    rows, lanes = field.shape
    return (tile * field.reshape(rows // 16, 16, lanes)).reshape(rows, lanes)


def dot_nt(a, b):
    return lax.dot_general(a, b, (((1,), (1,)), ((), ())), preferred_element_type=jnp.float32)


def local_kernel(own_ref, other_ref, weight_ref, jb_ref, acc_ref, w0_ref, adv, wts):
    m = lax.axis_index("modes")
    q = lax.rem(lax.axis_index("space"), 2)
    nx, comps, nk, nz = own_ref.shape
    rows = nx // 2
    pick = picks(jb_ref, m, nk)
    for r in range(rows):
        row = rows * m + r
        below, above = lax.rem(row + nx - 1, nx), lax.rem(row + 1, nx)
        phi = [picked(pick, lambda at: own_ref[row, d, at, :], lambda at: other_ref[row, d, at, :]) for d in range(comps)]
        weight = weight_ref[pl.ds(row, 1), :]
        for c in range(comps):
            for half, ref in enumerate((own_ref, other_ref)):
                block = pl.ds(half * nk, nk)
                here = ref[row, c].astype(jnp.float32)
                gx = 0.5 * (ref[above, c].astype(jnp.float32) - ref[below, c].astype(jnp.float32))
                gz = 0.5 * (pltpu.roll(here, nz - 1, 1) - pltpu.roll(here, 1, 1))
                gx = gx.astype(jnp.bfloat16).astype(jnp.float32)
                gz = gz.astype(jnp.bfloat16).astype(jnp.float32)
                wts[r, block, pl.ds(c * nz, nz)] = (weight * here).astype(jnp.bfloat16)
                for j in range(JB):
                    total = phi[0][j : j + 1] * gx + phi[2][j : j + 1] * gz
                    adv[r, pl.ds((2 * j + half) * nk, nk), pl.ds(c * nz, nz)] = total.astype(jnp.bfloat16)
    total = dot_nt(adv[0], wts[0])
    for r in range(1, rows):
        total = total + dot_nt(adv[r], wts[r])
    acc_ref[...] = total
    quarter = rows // 2
    for r in range(quarter):
        w0_ref[r] = wts[quarter * q + r]


def same_core_rows(planes, first_ref, second_ref):
    x_came = x_first(jnp.bitwise_xor(lax.axis_index("space"), 1), planes)
    return (
        lambda rows: jnp.where(x_came, first_ref[rows, :], second_ref[rows, :]),
        lambda rows: jnp.where(x_came, second_ref[rows, :], first_ref[rows, :]),
    )


def sign_of_plane():
    return jnp.where(lax.rem(lax.axis_index("space"), 2) == 0, 0.5, -0.5)


def early_kernel(
    planes, own_ref, other_ref, first_ref, second_ref, xc_ref, w0_ref, jb_ref, acc_ref, out_ref, w1_ref, adv
):
    xs_rows, _ = same_core_rows(planes, first_ref, second_ref)
    m = lax.axis_index("modes")
    q = lax.rem(lax.axis_index("space"), 2)
    nx, comps, nk, nz = own_ref.shape
    quarter = nx // 4
    pick = picks(jb_ref, m, nk)
    weights = received_weights(xc_ref, quarter * comps * nk, quarter)
    for r in range(quarter):
        row0 = quarter * (2 * m + q) + r
        phi0 = sign_of_plane() * picked(
            pick, lambda at: own_ref[row0, 1, at, :], lambda at: other_ref[row0, 1, at, :]
        )
        phi0 = [spread(phi0[j : j + 1]) for j in range(JB)]
        for c in range(comps):
            at = pl.ds((r * comps + c) * nz, nz)
            src = pl.ds((r * comps + c) * nk, nk)
            for half, f1 in enumerate((xs_rows(src), xc_ref[src, :])):
                w1_ref[pl.ds(half * nk, nk), at] = (weights[r] * f1.astype(jnp.float32)).astype(
                    jnp.bfloat16
                )
                for j in range(JB):
                    adv[r, pl.ds((2 * j + half) * nk, nk), pl.ds(c * nz, nz)] = scaled(phi0[j], f1)
    total = acc_ref[...]
    for r in range(quarter):
        total = total + dot_nt(adv[r], w0_ref[r])
    out_ref[...] = total


def cross_kernel(classes_of, chunk, planes, has_weighted, own_ref, other_ref, *refs):
    first_ref, second_ref, xc_ref, zc_ref, w1_ref, jb_ref, acc_ref, *refs = refs
    xs_rows, zs_rows = same_core_rows(planes, first_ref, second_ref)
    if has_weighted:
        wts, keep_ref, send_ref, adv = refs
    else:
        keep_ref, send_ref, wts, adv = refs
    m = lax.axis_index("modes")
    plane = lax.axis_index("space")
    q = lax.rem(plane, 2)
    inside = jnp.where(jnp.logical_or(plane == 1, plane == planes - 2), 0.0, 1.0)
    nx, comps, nk, nz = own_ref.shape
    quarter = nx // 4
    span = quarter * comps * nz
    pick = picks(jb_ref, m, nk)
    classes = [pl.multiple_of(chunk * cls, chunk) for cls in classes_of(plane)]
    if not has_weighted:
        weights = received_weights(zc_ref, quarter * comps * nk, quarter)
        wts[:, pl.ds(0, span)] = w1_ref[...]
        for r in range(quarter):
            weight = inside * weights[r]
            for c in range(comps):
                src = pl.ds((r * comps + c) * nk, nk)
                for half, f2 in enumerate((zs_rows(src), zc_ref[src, :])):
                    wts[pl.ds(half * nk, nk), pl.ds(span + (r * comps + c) * nz, nz)] = (
                        weight * f2.astype(jnp.float32)
                    ).astype(jnp.bfloat16)
    phis = []
    for r in range(quarter):
        along = (r * comps + 1) * nk

        def moved(at):
            return pl.ds(pl.multiple_of(along + at.start, 16), at.size)

        phi1 = sign_of_plane() * picked(
            pick, lambda at: xs_rows(moved(at)), lambda at: xc_ref[moved(at), :]
        )
        phi2 = -sign_of_plane() * picked(
            pick, lambda at: zs_rows(moved(at)), lambda at: zc_ref[moved(at), :]
        )
        phis.append([[spread(phi[j : j + 1]) for j in range(JB)] for phi in (phi1, phi2)])
    inside = inside.astype(jnp.bfloat16)
    for at, cls in enumerate(classes):
        for r in range(quarter):
            row0 = quarter * (2 * m + q) + r
            phi1, phi2 = phis[r]
            for c in range(comps):
                lane = (r * comps + c) * nz
                src = (r * comps + c) * nk
                rows_at = pl.ds(pl.multiple_of(src + cls, 16), chunk)
                for half, (p0, f1, f2) in enumerate(
                    (
                        (own_ref, xs_rows(rows_at), zs_rows(rows_at)),
                        (other_ref, xc_ref[rows_at, :], zc_ref[rows_at, :]),
                    )
                ):
                    f0 = p0[row0, c, pl.ds(cls, chunk), :]
                    gy = inside * f2 - f0
                    for j in range(JB):
                        here = pl.ds((half * JB + j) * chunk, chunk)
                        adv[at, here, pl.ds(lane, nz)] = scaled(phi1[j], gy)
                        adv[at, here, pl.ds(span + lane, nz)] = scaled(phi2[j], f1)
        total = dot_nt(adv[at], wts[...])
        for half in range(2):
            level = m if half == 0 else 1 - m
            for j in range(JB):
                first = (half * JB + j) * chunk
                piece = total[first : first + chunk] + acc_ref[pl.ds((2 * j + half) * nk + cls, chunk), :]
                keep_ref[at, level, j] = piece[:, :nk]
                row = pl.multiple_of(((2 * at + level) * JB + j) * chunk, chunk)
                send_ref[pl.ds(row, chunk), :] = piece[:, nk:].astype(jnp.bfloat16)


def near_kernel(by_level, keep_ref, got_ref, *out_refs):
    got = got_ref[...].astype(jnp.float32).reshape(keep_ref.shape)
    totals = [keep_ref[at] + got[at] for at in range(2)]
    lower = lax.div(lax.axis_index("space"), NEAR) == 0
    for at, ref in enumerate(out_refs):
        total = jnp.where(lower, totals[at], totals[1 - at]) if by_level else totals[at]
        ref[...] = total.astype(ref.dtype).reshape(ref.shape)


def far_kernel(mine_ref, *refs):
    *parts, keep_ref, send_ref = refs
    level = lax.div(lax.axis_index("space"), NEAR)
    rows = send_ref.shape[0]
    for ref, at in ((keep_ref, level), (send_ref, 1 - level)):
        total = mine_ref[at]
        for part in parts:
            piece = part[pl.ds(pl.multiple_of(at * rows, rows), rows), :]
            total = total + piece.astype(jnp.float32).reshape(total.shape)
        ref[...] = total.astype(ref.dtype).reshape(ref.shape)


def total_kernel(keep_ref, got_ref, out_ref):
    total = keep_ref[...] + got_ref[...].astype(jnp.float32).reshape(keep_ref.shape)
    for j in range(JB):
        out_ref[:, j, :] = total[j]


def on_device(n, modes, weight_ids, weight_table, j_block):
    nk, comps, _, nx, nz = modes.shape
    bf16, f32 = jnp.bfloat16, jnp.float32
    vmem = pl.BlockSpec(memory_space=pltpu.VMEM)
    smem = pl.BlockSpec(memory_space=pltpu.SMEM)
    params = pltpu.CompilerParams(vmem_limit_bytes=VMEM_LIMIT)
    quarter = nx // 4
    body = quarter * comps * nk
    own, first, second = pl.pallas_call(
        functools.partial(prep_kernel, n),
        out_shape=[jax.ShapeDtypeStruct((nx, comps, nk, nz), bf16)]
        + [jax.ShapeDtypeStruct((body + PADROWS, nz), bf16)] * 2,
        in_specs=[pl.BlockSpec(memory_space=pltpu.HBM)],
        out_specs=[vmem] * 3,
        scratch_shapes=[pltpu.VMEM(modes.shape, bf16), pltpu.SemaphoreType.DMA((LOADS,))],
        compiler_params=pltpu.CompilerParams(vmem_limit_bytes=PREP_LIMIT),
        cost_estimate=pl.CostEstimate(flops=1_500_000_000, bytes_accessed=2_800_000, transcendentals=0),
        name="prep",
    )(modes)

    both = ("space", "modes")
    x_to = lambda s: s ^ 1
    z_to = lambda s: s + 2 if s % 2 else s - 2
    x_now = [n != 8 or X_FIRST >> s & 1 for s in range(n)]
    firsts = [(s, x_to(s) if x_now[s] else z_to(s)) for s in range(n)]
    seconds = [(s, z_to(s) % n if x_now[s] else x_to(s)) for s in range(n)]
    same = lambda pairs: [(2 * a + m, 2 * b + m) for a, b in pairs for m in range(2)]
    cross = lambda pairs: [(2 * a + m, 2 * b + 1 - m) for a, b in pairs for m in range(2)]
    other = lax.ppermute(own, "modes", [(0, 1), (1, 0)])
    first = lax.ppermute(first, both, same(firsts))
    second = lax.ppermute(second, both, same(seconds))
    weight, xc, zc = pl.pallas_call(
        weights_kernel,
        out_shape=[jax.ShapeDtypeStruct((nx, nz), f32)]
        + [jax.ShapeDtypeStruct((body + 8 * quarter, nz), bf16)] * 2,
        in_specs=[vmem] * 3 + [pl.BlockSpec(memory_space=pl.ANY)],
        out_specs=[vmem] * 3,
        compiler_params=params,
        name="weights",
    )(weight_ids, jnp.broadcast_to(weight_table[None], (8, NW)), own, other)
    xc = lax.ppermute(xc, both, cross([(s, x_to(s)) for s in range(n)]))
    zc = lax.ppermute(zc, both, cross([(s, z_to(s) % n) for s in range(n)]))

    depth = nx // 4 * comps * nz
    depth = quarter * comps * nz
    acc, w0 = pl.pallas_call(
        local_kernel,
        out_shape=[
            jax.ShapeDtypeStruct((JB * 2 * nk, 2 * nk), f32),
            jax.ShapeDtypeStruct((quarter, 2 * nk, comps * nz), bf16),
        ],
        in_specs=[vmem, vmem, vmem, smem],
        out_specs=[vmem] * 2,
        scratch_shapes=[
            pltpu.VMEM((2 * quarter, JB * 2 * nk, comps * nz), bf16),
            pltpu.VMEM((2 * quarter, 2 * nk, comps * nz), bf16),
        ],
        compiler_params=params,
        cost_estimate=pl.CostEstimate(flops=900_000_000, bytes_accessed=2_400_000, transcendentals=0),
        name="local",
    )(own, other, weight, j_block)

    acc, w1 = pl.pallas_call(
        functools.partial(early_kernel, n),
        out_shape=[
            jax.ShapeDtypeStruct((JB * 2 * nk, 2 * nk), f32),
            jax.ShapeDtypeStruct((2 * nk, depth), bf16),
        ],
        in_specs=[vmem] * 6 + [smem, vmem],
        out_specs=[vmem] * 2,
        scratch_shapes=[pltpu.VMEM((quarter, JB * 2 * nk, comps * nz), bf16)],
        compiler_params=params,
        cost_estimate=pl.CostEstimate(flops=600_000_000, bytes_accessed=2_400_000, transcendentals=0),
        name="early",
    )(own, other, first, second, xc, w0, j_block, acc)

    per_target = 2 * nk // n
    chunk = max(16, per_target)

    def crossed(count, classes_of, weighted):
        piece = (count, 2, JB, chunk, nk)
        out_shape = [
            jax.ShapeDtypeStruct(piece, f32),
            jax.ShapeDtypeStruct((count * 2 * JB * chunk, nk), bf16),
        ]
        if not weighted:
            out_shape.append(jax.ShapeDtypeStruct((2 * nk, 2 * depth), bf16))
        return pl.pallas_call(
            functools.partial(cross_kernel, classes_of, chunk, n, bool(weighted)),
            out_shape=out_shape,
            in_specs=[vmem] * 7 + [smem] + [vmem] * (1 + len(weighted)),
            out_specs=[vmem] * len(out_shape),
            scratch_shapes=[pltpu.VMEM((count, 2 * JB * chunk, 2 * depth), bf16)],
            compiler_params=params,
            cost_estimate=pl.CostEstimate(
                flops=900_000_000, bytes_accessed=4_000_000, transcendentals=0
            ),
            name="cross",
        )(own, other, first, second, xc, zc, w1, j_block, acc, *weighted)

    swap = [(0, 1), (1, 0)]
    if n == 2 * NEAR:
        def partners(*steps):
            return lambda s: [jnp.bitwise_xor(lax.rem(s, NEAR), step) for step in steps]

        keep_a, send_a, w2 = crossed(2, partners(3, 1), ())
        got_a = lax.ppermute(send_a, "modes", swap)
        keep_b, send_b = crossed(2, partners(0, 2), (w2,))
        got_b = lax.ppermute(send_b, "modes", swap)
        piece = (JB, chunk, nk)

        def summed(by_level, out_shape, keep, got):
            return pl.pallas_call(
                functools.partial(near_kernel, by_level),
                out_shape=out_shape,
                in_specs=[vmem] * 2,
                out_specs=[vmem] * 2,
                compiler_params=params,
                name="near",
            )(keep, got)

        kept = jax.ShapeDtypeStruct((2, *piece), f32)
        sent = jax.ShapeDtypeStruct((2 * JB * chunk, nk), bf16)
        out_0, out_1 = summed(True, [sent, sent], keep_a, got_a)
        mine, out_2 = summed(False, [kept, sent], keep_b, got_b)
        parts = [
            lax.ppermute(out, "space", [(s, s ^ steps[s // NEAR]) for s in range(n)])
            for out, steps in ((out_0, (3, 1)), (out_1, (1, 3)), (out_2, (2, 2)))
        ]
        keep, send = pl.pallas_call(
            far_kernel,
            out_shape=[
                jax.ShapeDtypeStruct(piece, f32),
                jax.ShapeDtypeStruct((JB * chunk, nk), bf16),
            ],
            in_specs=[vmem] * NEAR,
            out_specs=[vmem] * 2,
            compiler_params=params,
            name="far",
        )(mine, *parts)
        got = lax.ppermute(send, "space", [(s, s ^ NEAR) for s in range(n)])
        return pl.pallas_call(
            total_kernel,
            out_shape=jax.ShapeDtypeStruct((chunk, JB, nk), f32),
            in_specs=[vmem] * 2,
            out_specs=vmem,
            compiler_params=params,
            name="total",
        )(keep, got)

    count = nk // chunk
    keep, send, _ = crossed(count, lambda s: list(range(count)), ())
    share = (keep + lax.ppermute(send, "modes", swap).reshape(keep.shape)).astype(bf16)
    share = share.reshape(count, 2, JB, chunk // per_target, per_target, nk)
    share = share.transpose(1, 0, 3, 2, 4, 5).reshape(n, JB, per_target, nk)
    parts = lax.all_to_all(share, "space", 0, 0, tiled=True)
    return jnp.sum(parts.astype(f32), axis=0).transpose(1, 0, 2)


def solution(mesh):
    return jax.shard_map(
        functools.partial(on_device, mesh.shape["space"]),
        mesh=mesh,
        in_specs=(
            P("modes", None, ("groups", "space"), None, None),
            P(("groups", "space"), None, None),
            P(),
            P("groups"),
        ),
        out_specs=P(("groups", "space"), None, "modes"),
        check_vma=False,
    )
```

```python
import functools

import jax
import jax.numpy as jnp
from jax import lax
from jax.experimental import pallas as pl
from jax.experimental.pallas import tpu as pltpu
from jax.sharding import PartitionSpec as P

JB = 4
NW = 16
PADROWS = 16
LOADS = 2
X_FIRST = 0b10011111
NEAR = 4
VMEM_LIMIT = 48 * 1024 * 1024
PREP_LIMIT = 53_600 * 1024


def x_first(s, planes):
    if planes != 8:
        return s >= 0
    return lax.rem(lax.shift_right_logical(X_FIRST, s), 2) == 1


def copy_rows(ref, tr, at):
    nx, comps, nk, _ = tr.shape
    for row in range(nx // 4):
        for c in range(comps):
            ref[pl.ds((row * comps + c) * nk, nk), :] = tr[at * (nx // 4) + row, c]


def prep_kernel(planes, modes_hbm, tr, first_ref, second_ref, modes_ref, sems):
    m = lax.axis_index("modes")
    s = lax.axis_index("space")
    q = lax.rem(s, 2)
    nk, comps, _, nx, nz = modes_hbm.shape
    step = nk // LOADS
    copies = [
        pltpu.make_async_copy(
            modes_hbm.at[pl.ds(p * step, step)], modes_ref.at[pl.ds(p * step, step)], sems.at[p]
        )
        for p in range(LOADS)
    ]
    for copy in copies:
        copy.start()
    for p in range(LOADS):
        copies[p].wait()
        block = pl.ds(p * step, step)
        for c in range(comps):
            value = modes_ref[block, c, 0].astype(jnp.float32)
            tr[:, c, block] = jnp.swapaxes(value, 0, 1).astype(jnp.bfloat16)
    body = nx // 4 * comps * nk
    to_x, to_z = 2 * m + 1 - q, 2 * m + q
    x_now = x_first(s, planes)
    for ref, at in (
        (first_ref, jnp.where(x_now, to_x, to_z)),
        (second_ref, jnp.where(x_now, to_z, to_x)),
    ):
        copy_rows(ref, tr, at)
        ref[pl.ds(body, PADROWS), :] = jnp.zeros((PADROWS, nz), jnp.bfloat16)


def weights_kernel(ids_ref, table_ref, tr, _, weight_ref, xc_ref, zc_ref):
    m = lax.axis_index("modes")
    q = lax.rem(lax.axis_index("space"), 2)
    nx, comps, nk, nz = tr.shape
    quarter = nx // 4
    table = table_ref[...]
    weight = jnp.zeros((nx, nz), jnp.float32)
    for entry in range(NW):
        weight = jnp.where(ids_ref[0] == entry, table[0:1, entry : entry + 1], weight)
    weight_ref[...] = weight
    for ref, at in ((xc_ref, 2 * (1 - m) + 1 - q), (zc_ref, 2 * (1 - m) + q)):
        copy_rows(ref, tr, at)
        rest = jnp.concatenate(
            [
                jnp.broadcast_to(weight_ref[pl.ds(at * quarter + row, 1), :], (8, nz))
                for row in range(quarter)
            ],
            axis=0,
        )
        piece_of = lax.rem(lax.broadcasted_iota(jnp.int32, rest.shape, 0), 8)
        pieces = jnp.zeros(rest.shape, jnp.float32)
        for piece in range(3):
            rounded = rest.astype(jnp.bfloat16).astype(jnp.float32)
            pieces = jnp.where(piece_of == piece, rounded, pieces)
            rest = rest - rounded
        ref[pl.ds(quarter * comps * nk, 8 * quarter), :] = pieces.astype(jnp.bfloat16)


def received_weights(ref, first, quarter):
    pieces = ref[pl.ds(first, 8 * quarter), :].astype(jnp.float32)
    return [
        pieces[8 * r : 8 * r + 1] + pieces[8 * r + 1 : 8 * r + 2] + pieces[8 * r + 2 : 8 * r + 3]
        for r in range(quarter)
    ]


def picks(jb_ref, m, nk):
    first = jb_ref[0] * JB
    owner = (first >= nk).astype(jnp.int32)
    row = first - owner * nk
    within = lax.rem(row, 16)
    return owner == m, pl.multiple_of(row - within, 16), within


def picked(pick, own, other):
    mine, block, within = pick
    rows = pl.ds(block, 16)
    rows = jnp.where(mine, own(rows).astype(jnp.float32), other(rows).astype(jnp.float32))
    result = rows[0:JB]
    for start in range(JB, 16, JB):
        result = jnp.where(within == start, rows[start : start + JB], result)
    return result


def spread(row):
    return jnp.broadcast_to(row, (16, row.shape[1])).astype(jnp.bfloat16)[None]


def scaled(tile, field):
    rows, lanes = field.shape
    return (tile * field.reshape(rows // 16, 16, lanes)).reshape(rows, lanes)


def dot_nt(a, b):
    return lax.dot_general(a, b, (((1,), (1,)), ((), ())), preferred_element_type=jnp.float32)


def local_kernel(own_ref, other_ref, weight_ref, jb_ref, acc_ref, w0_ref, adv, wts):
    m = lax.axis_index("modes")
    q = lax.rem(lax.axis_index("space"), 2)
    nx, comps, nk, nz = own_ref.shape
    rows = nx // 2
    pick = picks(jb_ref, m, nk)
    for r in range(rows):
        row = rows * m + r
        below, above = lax.rem(row + nx - 1, nx), lax.rem(row + 1, nx)
        phi = [picked(pick, lambda at: own_ref[row, d, at, :], lambda at: other_ref[row, d, at, :]) for d in range(comps)]
        weight = weight_ref[pl.ds(row, 1), :]
        for c in range(comps):
            for half, ref in enumerate((own_ref, other_ref)):
                block = pl.ds(half * nk, nk)
                here = ref[row, c].astype(jnp.float32)
                gx = 0.5 * (ref[above, c].astype(jnp.float32) - ref[below, c].astype(jnp.float32))
                gz = 0.5 * (pltpu.roll(here, nz - 1, 1) - pltpu.roll(here, 1, 1))
                gx = gx.astype(jnp.bfloat16).astype(jnp.float32)
                gz = gz.astype(jnp.bfloat16).astype(jnp.float32)
                wts[r, block, pl.ds(c * nz, nz)] = (weight * here).astype(jnp.bfloat16)
                for j in range(JB):
                    total = phi[0][j : j + 1] * gx + phi[2][j : j + 1] * gz
                    adv[r, pl.ds((2 * j + half) * nk, nk), pl.ds(c * nz, nz)] = total.astype(jnp.bfloat16)
    total = dot_nt(adv[0], wts[0])
    for r in range(1, rows):
        total = total + dot_nt(adv[r], wts[r])
    acc_ref[...] = total
    quarter = rows // 2
    for r in range(quarter):
        w0_ref[r] = wts[quarter * q + r]


def same_core_rows(planes, first_ref, second_ref):
    x_came = x_first(jnp.bitwise_xor(lax.axis_index("space"), 1), planes)
    return (
        lambda rows: jnp.where(x_came, first_ref[rows, :], second_ref[rows, :]),
        lambda rows: jnp.where(x_came, second_ref[rows, :], first_ref[rows, :]),
    )


def sign_of_plane():
    return jnp.where(lax.rem(lax.axis_index("space"), 2) == 0, 0.5, -0.5)


def early_kernel(
    planes, own_ref, other_ref, first_ref, second_ref, xc_ref, w0_ref, jb_ref, acc_ref, out_ref, w1_ref, adv
):
    xs_rows, _ = same_core_rows(planes, first_ref, second_ref)
    m = lax.axis_index("modes")
    q = lax.rem(lax.axis_index("space"), 2)
    nx, comps, nk, nz = own_ref.shape
    quarter = nx // 4
    pick = picks(jb_ref, m, nk)
    weights = received_weights(xc_ref, quarter * comps * nk, quarter)
    for r in range(quarter):
        row0 = quarter * (2 * m + q) + r
        phi0 = sign_of_plane() * picked(
            pick, lambda at: own_ref[row0, 1, at, :], lambda at: other_ref[row0, 1, at, :]
        )
        phi0 = [spread(phi0[j : j + 1]) for j in range(JB)]
        for c in range(comps):
            at = pl.ds((r * comps + c) * nz, nz)
            src = pl.ds((r * comps + c) * nk, nk)
            for half, f1 in enumerate((xs_rows(src), xc_ref[src, :])):
                w1_ref[pl.ds(half * nk, nk), at] = (weights[r] * f1.astype(jnp.float32)).astype(
                    jnp.bfloat16
                )
                for j in range(JB):
                    adv[r, pl.ds((2 * j + half) * nk, nk), pl.ds(c * nz, nz)] = scaled(phi0[j], f1)
    total = acc_ref[...]
    for r in range(quarter):
        total = total + dot_nt(adv[r], w0_ref[r])
    out_ref[...] = total


def cross_kernel(classes_of, chunk, planes, has_weighted, own_ref, other_ref, *refs):
    first_ref, second_ref, xc_ref, zc_ref, w1_ref, jb_ref, acc_ref, *refs = refs
    xs_rows, zs_rows = same_core_rows(planes, first_ref, second_ref)
    if has_weighted:
        wts, keep_ref, send_ref, adv = refs
    else:
        keep_ref, send_ref, wts, adv = refs
    m = lax.axis_index("modes")
    plane = lax.axis_index("space")
    q = lax.rem(plane, 2)
    inside = jnp.where(jnp.logical_or(plane == 1, plane == planes - 2), 0.0, 1.0)
    nx, comps, nk, nz = own_ref.shape
    quarter = nx // 4
    span = quarter * comps * nz
    pick = picks(jb_ref, m, nk)
    classes = [pl.multiple_of(chunk * cls, chunk) for cls in classes_of(plane)]
    if not has_weighted:
        weights = received_weights(zc_ref, quarter * comps * nk, quarter)
        wts[:, pl.ds(0, span)] = w1_ref[...]
        for r in range(quarter):
            weight = inside * weights[r]
            for c in range(comps):
                src = pl.ds((r * comps + c) * nk, nk)
                for half, f2 in enumerate((zs_rows(src), zc_ref[src, :])):
                    wts[pl.ds(half * nk, nk), pl.ds(span + (r * comps + c) * nz, nz)] = (
                        weight * f2.astype(jnp.float32)
                    ).astype(jnp.bfloat16)
    phis = []
    for r in range(quarter):
        along = (r * comps + 1) * nk

        def moved(at):
            return pl.ds(pl.multiple_of(along + at.start, 16), at.size)

        phi1 = sign_of_plane() * picked(
            pick, lambda at: xs_rows(moved(at)), lambda at: xc_ref[moved(at), :]
        )
        phi2 = -sign_of_plane() * picked(
            pick, lambda at: zs_rows(moved(at)), lambda at: zc_ref[moved(at), :]
        )
        phis.append([[spread(phi[j : j + 1]) for j in range(JB)] for phi in (phi1, phi2)])
    inside = inside.astype(jnp.bfloat16)
    for at, cls in enumerate(classes):
        for r in range(quarter):
            row0 = quarter * (2 * m + q) + r
            phi1, phi2 = phis[r]
            for c in range(comps):
                lane = (r * comps + c) * nz
                src = (r * comps + c) * nk
                rows_at = pl.ds(pl.multiple_of(src + cls, 16), chunk)
                for half, (p0, f1, f2) in enumerate(
                    (
                        (own_ref, xs_rows(rows_at), zs_rows(rows_at)),
                        (other_ref, xc_ref[rows_at, :], zc_ref[rows_at, :]),
                    )
                ):
                    f0 = p0[row0, c, pl.ds(cls, chunk), :]
                    gy = inside * f2 - f0
                    for j in range(JB):
                        here = pl.ds((half * JB + j) * chunk, chunk)
                        adv[at, here, pl.ds(lane, nz)] = scaled(phi1[j], gy)
                        adv[at, here, pl.ds(span + lane, nz)] = scaled(phi2[j], f1)
        total = dot_nt(adv[at], wts[...])
        for half in range(2):
            level = m if half == 0 else 1 - m
            for j in range(JB):
                first = (half * JB + j) * chunk
                piece = total[first : first + chunk] + acc_ref[pl.ds((2 * j + half) * nk + cls, chunk), :]
                keep_ref[at, level, j] = piece[:, :nk]
                row = pl.multiple_of(((2 * at + level) * JB + j) * chunk, chunk)
                send_ref[pl.ds(row, chunk), :] = piece[:, nk:].astype(jnp.bfloat16)


def near_kernel(by_level, keep_ref, got_ref, *out_refs):
    got = got_ref[...].astype(jnp.float32).reshape(keep_ref.shape)
    totals = [keep_ref[at] + got[at] for at in range(2)]
    lower = lax.div(lax.axis_index("space"), NEAR) == 0
    for at, ref in enumerate(out_refs):
        total = jnp.where(lower, totals[at], totals[1 - at]) if by_level else totals[at]
        ref[...] = total.astype(ref.dtype).reshape(ref.shape)


def far_kernel(mine_ref, *refs):
    *parts, keep_ref, send_ref = refs
    level = lax.div(lax.axis_index("space"), NEAR)
    rows = send_ref.shape[0]
    for ref, at in ((keep_ref, level), (send_ref, 1 - level)):
        total = mine_ref[at]
        for part in parts:
            piece = part[pl.ds(pl.multiple_of(at * rows, rows), rows), :]
            total = total + piece.astype(jnp.float32).reshape(total.shape)
        ref[...] = total.astype(ref.dtype).reshape(ref.shape)


def total_kernel(keep_ref, got_ref, out_ref):
    total = keep_ref[...] + got_ref[...].astype(jnp.float32).reshape(keep_ref.shape)
    for j in range(JB):
        out_ref[:, j, :] = total[j]


def on_device(n, modes, weight_ids, weight_table, j_block):
    nk, comps, _, nx, nz = modes.shape
    bf16, f32 = jnp.bfloat16, jnp.float32
    vmem = pl.BlockSpec(memory_space=pltpu.VMEM)
    smem = pl.BlockSpec(memory_space=pltpu.SMEM)
    params = pltpu.CompilerParams(vmem_limit_bytes=VMEM_LIMIT)
    quarter = nx // 4
    body = quarter * comps * nk
    own, first, second = pl.pallas_call(
        functools.partial(prep_kernel, n),
        out_shape=[jax.ShapeDtypeStruct((nx, comps, nk, nz), bf16)]
        + [jax.ShapeDtypeStruct((body + PADROWS, nz), bf16)] * 2,
        in_specs=[pl.BlockSpec(memory_space=pltpu.HBM)],
        out_specs=[vmem] * 3,
        scratch_shapes=[pltpu.VMEM(modes.shape, bf16), pltpu.SemaphoreType.DMA((LOADS,))],
        compiler_params=pltpu.CompilerParams(vmem_limit_bytes=PREP_LIMIT),
        cost_estimate=pl.CostEstimate(flops=1_500_000_000, bytes_accessed=2_800_000, transcendentals=0),
        name="prep",
    )(modes)

    both = ("space", "modes")
    x_to = lambda s: s ^ 1
    z_to = lambda s: s + 2 if s % 2 else s - 2
    x_now = [n != 8 or X_FIRST >> s & 1 for s in range(n)]
    firsts = [(s, x_to(s) if x_now[s] else z_to(s)) for s in range(n)]
    seconds = [(s, z_to(s) % n if x_now[s] else x_to(s)) for s in range(n)]
    same = lambda pairs: [(2 * a + m, 2 * b + m) for a, b in pairs for m in range(2)]
    cross = lambda pairs: [(2 * a + m, 2 * b + 1 - m) for a, b in pairs for m in range(2)]
    other = lax.ppermute(own, "modes", [(0, 1), (1, 0)])
    first = lax.ppermute(first, both, same(firsts))
    second = lax.ppermute(second, both, same(seconds))
    weight, xc, zc = pl.pallas_call(
        weights_kernel,
        out_shape=[jax.ShapeDtypeStruct((nx, nz), f32)]
        + [jax.ShapeDtypeStruct((body + 8 * quarter, nz), bf16)] * 2,
        in_specs=[vmem] * 3 + [pl.BlockSpec(memory_space=pl.ANY)],
        out_specs=[vmem] * 3,
        compiler_params=params,
        name="weights",
    )(weight_ids, jnp.broadcast_to(weight_table[None], (8, NW)), own, other)
    xc = lax.ppermute(xc, both, cross([(s, x_to(s)) for s in range(n)]))
    zc = lax.ppermute(zc, both, cross([(s, z_to(s) % n) for s in range(n)]))

    depth = nx // 4 * comps * nz
    depth = quarter * comps * nz
    acc, w0 = pl.pallas_call(
        local_kernel,
        out_shape=[
            jax.ShapeDtypeStruct((JB * 2 * nk, 2 * nk), f32),
            jax.ShapeDtypeStruct((quarter, 2 * nk, comps * nz), bf16),
        ],
        in_specs=[vmem, vmem, vmem, smem],
        out_specs=[vmem] * 2,
        scratch_shapes=[
            pltpu.VMEM((2 * quarter, JB * 2 * nk, comps * nz), bf16),
            pltpu.VMEM((2 * quarter, 2 * nk, comps * nz), bf16),
        ],
        compiler_params=params,
        cost_estimate=pl.CostEstimate(flops=900_000_000, bytes_accessed=2_400_000, transcendentals=0),
        name="local",
    )(own, other, weight, j_block)

    acc, w1 = pl.pallas_call(
        functools.partial(early_kernel, n),
        out_shape=[
            jax.ShapeDtypeStruct((JB * 2 * nk, 2 * nk), f32),
            jax.ShapeDtypeStruct((2 * nk, depth), bf16),
        ],
        in_specs=[vmem] * 6 + [smem, vmem],
        out_specs=[vmem] * 2,
        scratch_shapes=[pltpu.VMEM((quarter, JB * 2 * nk, comps * nz), bf16)],
        compiler_params=params,
        cost_estimate=pl.CostEstimate(flops=600_000_000, bytes_accessed=2_400_000, transcendentals=0),
        name="early",
    )(own, other, first, second, xc, w0, j_block, acc)

    per_target = 2 * nk // n
    chunk = max(16, per_target)

    def crossed(count, classes_of, weighted):
        piece = (count, 2, JB, chunk, nk)
        out_shape = [
            jax.ShapeDtypeStruct(piece, f32),
            jax.ShapeDtypeStruct((count * 2 * JB * chunk, nk), bf16),
        ]
        if not weighted:
            out_shape.append(jax.ShapeDtypeStruct((2 * nk, 2 * depth), bf16))
        return pl.pallas_call(
            functools.partial(cross_kernel, classes_of, chunk, n, bool(weighted)),
            out_shape=out_shape,
            in_specs=[vmem] * 7 + [smem] + [vmem] * (1 + len(weighted)),
            out_specs=[vmem] * len(out_shape),
            scratch_shapes=[pltpu.VMEM((count, 2 * JB * chunk, 2 * depth), bf16)],
            compiler_params=params,
            cost_estimate=pl.CostEstimate(
                flops=900_000_000, bytes_accessed=4_000_000, transcendentals=0
            ),
            name="cross",
        )(own, other, first, second, xc, zc, w1, j_block, acc, *weighted)

    swap = [(0, 1), (1, 0)]
    if n == 2 * NEAR:
        def partners(*steps):
            return lambda s: [jnp.bitwise_xor(lax.rem(s, NEAR), step) for step in steps]

        keep_a, send_a, w2 = crossed(2, partners(3, 1), ())
        got_a = lax.ppermute(send_a, "modes", swap)
        keep_b, send_b = crossed(2, partners(0, 2), (w2,))
        got_b = lax.ppermute(send_b, "modes", swap)
        piece = (JB, chunk, nk)

        def summed(by_level, out_shape, keep, got):
            return pl.pallas_call(
                functools.partial(near_kernel, by_level),
                out_shape=out_shape,
                in_specs=[vmem] * 2,
                out_specs=[vmem] * 2,
                compiler_params=params,
                name="near",
            )(keep, got)

        kept = jax.ShapeDtypeStruct((2, *piece), f32)
        sent = jax.ShapeDtypeStruct((2 * JB * chunk, nk), bf16)
        out_0, out_1 = summed(True, [sent, sent], keep_a, got_a)
        mine, out_2 = summed(False, [kept, sent], keep_b, got_b)
        parts = [
            lax.ppermute(out, "space", [(s, s ^ steps[s // NEAR]) for s in range(n)])
            for out, steps in ((out_0, (3, 1)), (out_1, (1, 3)), (out_2, (2, 2)))
        ]
        keep, send = pl.pallas_call(
            far_kernel,
            out_shape=[
                jax.ShapeDtypeStruct(piece, f32),
                jax.ShapeDtypeStruct((JB * chunk, nk), bf16),
            ],
            in_specs=[vmem] * NEAR,
            out_specs=[vmem] * 2,
            compiler_params=params,
            name="far",
        )(mine, *parts)
        got = lax.ppermute(send, "space", [(s, s ^ NEAR) for s in range(n)])
        return pl.pallas_call(
            total_kernel,
            out_shape=jax.ShapeDtypeStruct((chunk, JB, nk), f32),
            in_specs=[vmem] * 2,
            out_specs=vmem,
            compiler_params=params,
            name="total",
        )(keep, got)

    count = nk // chunk
    keep, send, _ = crossed(count, lambda s: list(range(count)), ())
    share = (keep + lax.ppermute(send, "modes", swap).reshape(keep.shape)).astype(bf16)
    share = share.reshape(count, 2, JB, chunk // per_target, per_target, nk)
    share = share.transpose(1, 0, 3, 2, 4, 5).reshape(n, JB, per_target, nk)
    parts = lax.all_to_all(share, "space", 0, 0, tiled=True)
    return jnp.sum(parts.astype(f32), axis=0).transpose(1, 0, 2)


def solution(mesh):
    return jax.shard_map(
        functools.partial(on_device, mesh.shape["space"]),
        mesh=mesh,
        in_specs=(
            P("modes", None, ("groups", "space"), None, None),
            P(("groups", "space"), None, None),
            P(),
            P("groups"),
        ),
        out_specs=P(("groups", "space"), None, "modes"),
        check_vma=False,
    )
```
